32 devices in a mesh: rows: 2 (over core), seq: 16 (over z, y, x).
Axes of the slice: x: 2, y: 2, z: 4, core: 2. Of those that a mesh axis runs over, the one named last changes fastest.
Arguments:
- tokens: bfloat16 [2, 1024, 2, 512], P(None, 'seq', 'rows'), may hold values from -6 to 6
- memory: bfloat16 [2, 1024, 2, 512], P(None, 'seq', 'rows'), may hold values from -6 to 6
- cotangent: bfloat16 [2, 1024, 2, 512], P(None, 'seq', 'rows'), may hold values from -6 to 6
- tgt_lengths: int32 [2, 2, 32], P(None, 'rows'), may hold values from 1 to 993, as said below
- src_lengths: int32 [2, 2, 32], P(None, 'rows'), may hold values from 1 to 993, as said below
- tgt_mask: int32 [2, 1024, 2], P(None, 'seq', 'rows'), may hold values 0 or 1
- src_mask: int32 [2, 1024, 2], P(None, 'seq', 'rows'), may hold values 0 or 1
- attn_in: bfloat16 [2, 3, 512, 512], P(None, None, ('rows', 'seq')), may hold values from -0.25 to 0.25
- attn_out: bfloat16 [2, 512, 512], P(None, ('rows', 'seq')), may hold values from -1 to 1
- w_up: bfloat16 [512, 2048], P(('rows', 'seq')), may hold values from -0.25 to 0.25
- w_down: bfloat16 [2048, 512], P(('rows', 'seq')), may hold values from -0.125 to 0.125
- biases: float32 [7, 512], replicated, may hold values from -1.2 to 1.2
- up_bias: float32 [2048], replicated, may hold values from -1.2 to 1.2
- norm_gain: float32 [3, 512], replicated, may hold values from 0.5 to 1.5
- norm_shift: float32 [3, 512], replicated, may hold values from -0.8 to 0.8
- omega: float32 [3, 512], replicated, may hold values from 0.5 to 1.5
Outputs:
- result: bfloat16 [2, 1024, 2, 512], P(None, 'seq', 'rows')
- grad_tokens: bfloat16 [2, 1024, 2, 512], P(None, 'seq', 'rows')
- grad_memory: bfloat16 [2, 1024, 2, 512], P(None, 'seq', 'rows')
- grad_attn_in: float32 [2, 3, 512, 512], P(None, None, ('rows', 'seq'))
- grad_attn_out: float32 [2, 512, 512], P(None, ('rows', 'seq'))
- grad_w_up: float32 [512, 2048], P(('rows', 'seq'))
- grad_w_down: float32 [2048, 512], P(('rows', 'seq'))
- grad_biases: float32 [7, 512], P(None, ('rows', 'seq'))
- grad_up_bias: float32 [2048], P(('rows', 'seq'))
- grad_norm_gain: float32 [3, 512], P(None, ('rows', 'seq'))
- grad_norm_shift: float32 [3, 512], P(None, ('rows', 'seq'))
- grad_omega: float32 [3, 512], P(None, ('rows', 'seq'))
The draws below stay inside these ranges and needn't reach their ends.
Inputs may be any that keep to these rules, and one draw needn't show every extreme that they name: `tgt_lengths`: each row's 32 lengths sum to 1024. `src_lengths`: each row's 32 lengths sum to 1024.
All inputs are finite; a program needn't handle non-finite values. No bound on the sum of `tgt_mask` or of `src_mask` on one device may be relied on, other than what follows from the above.
Results may differ from the reference program's by a relative error of at most 0.03.
Values may be sent and summed in bfloat16 or wider, within the bound.
A program may use at most 256 MiB of HBM per device.

```python
import math
import jax
import jax.numpy as jnp
from jax import lax

D = 512
FF = 2048
HEADS = 8
ROWS_DEV = 1
MICRO = 2
NSEG = 32
ROW_LEN = 1024
ROWS = 2


def long_rows(key):
    groups = ROWS // ROWS_DEV
    pick_micro = jax.random.randint(jax.random.fold_in(key, 101), (groups,), 0, MICRO)
    pick_row = jax.random.randint(jax.random.fold_in(key, 102), (groups,), 0, ROWS_DEV)
    pick_slot = jax.random.randint(jax.random.fold_in(key, 103), (groups,), 0, NSEG)
    micro_ids = jnp.arange(MICRO, dtype=jnp.int32)[:, None]
    row_ids = jnp.arange(ROWS, dtype=jnp.int32)[None, :]
    group_ids = row_ids // ROWS_DEV
    chosen = (micro_ids == pick_micro[group_ids]) & (row_ids % ROWS_DEV == pick_row[group_ids])
    return (chosen, pick_slot[group_ids])


def compose(key, chosen, slot_pick):
    row_keys = jax.random.split(key, MICRO * ROWS)

    def one_row(row_key):
        cut_points = jnp.sort(jax.random.permutation(row_key, ROW_LEN - 1)[:NSEG - 1] + 1).astype(jnp.int32)
        boundary = jnp.concatenate([jnp.zeros((1,), jnp.int32), cut_points, jnp.full((1,), ROW_LEN, jnp.int32)])
        return boundary[1:] - boundary[:-1]
    spreads = jax.vmap(one_row)(row_keys).reshape(MICRO, ROWS, NSEG)
    slot_ids = jnp.arange(NSEG, dtype=jnp.int32)
    single = jnp.where(slot_ids[None, None, :] == slot_pick[..., None], ROW_LEN - NSEG + 1, 1)
    return jnp.where(chosen[..., None], single, spreads).astype(jnp.int32)


def draw_tgt_lengths(key, part):
    chosen, slot_pick = long_rows(key)
    key = jax.random.fold_in(key, 1)
    return compose(key, chosen, slot_pick)


def draw_src_lengths(key, part):
    chosen, slot_pick = long_rows(key)
    key = jax.random.fold_in(key, 2)
    return compose(key, chosen, slot_pick)


def plant(values, key, low, largest):
    longest = values.shape.index(max(values.shape))
    spots = []
    for shift in (0, 1):
        where = [jax.random.randint(jax.random.fold_in(key, axis), (), 0, length) for axis, length in enumerate(values.shape)]
        where[longest] = (where[longest] + shift) % values.shape[longest]
        spots.append(tuple(where))
    return values.at[spots[0]].set(low).at[spots[1]].set(largest)


def shard_levels(key, dims, cuts, least, largest):
    factor_of = 1.0
    for axis_at, shards_of in cuts:
        draws = jax.random.uniform(jax.random.fold_in(jax.random.fold_in(key, 6), axis_at), (shards_of,), jnp.float32, least / len(cuts), largest / len(cuts))
        factor_of = factor_of * jnp.repeat(jnp.exp(draws), dims[axis_at] // shards_of).reshape((-1,) + (1,) * (len(dims) - 1 - axis_at))
    return factor_of


def noise(own_key, dims, spread, reach, cuts=(), kind=jnp.bfloat16):
    factor_of = shard_levels(own_key, dims, cuts, -0.22, 0.18) if cuts else 1.0
    entries = jax.random.normal(own_key, dims, jnp.float32) * spread * factor_of
    return jnp.minimum(jnp.maximum(entries, -reach), reach).astype(kind)


def setup_inputs(seed: int = 0) -> dict:
    streams_of = jax.random.split(jax.random.key(seed), 17)
    return {
        "tokens": noise(streams_of[0], (MICRO, ROW_LEN, ROWS, D), 1.0, 6.0, ((1, 16), (2, 2))),
        "memory": noise(streams_of[1], (MICRO, ROW_LEN, ROWS, D), 1.0, 6.0, ((1, 16), (2, 2))),
        "cotangent": noise(streams_of[2], (MICRO, ROW_LEN, ROWS, D), 1.0, 6.0, ((1, 16), (2, 2))),
        "tgt_lengths": draw_tgt_lengths(jax.random.fold_in(streams_of[16], 71), 0),
        "src_lengths": draw_src_lengths(jax.random.fold_in(streams_of[16], 71), 0),
        "tgt_mask": plant((jax.random.randint(streams_of[5], (MICRO, ROW_LEN, ROWS), 0, 10) < 9).astype(jnp.int32), jax.random.fold_in(streams_of[5], 1), 0, 1),
        "src_mask": plant((jax.random.randint(streams_of[6], (MICRO, ROW_LEN, ROWS), 0, 10) < 9).astype(jnp.int32), jax.random.fold_in(streams_of[6], 1), 0, 1),
        "attn_in": noise(streams_of[7], (2, 3, D, D), D ** -0.5, 0.25, ((2, 32),)),
        "attn_out": noise(streams_of[8], (2, D, D), (D // 16) ** -0.5, 1.0, ((1, 32),)),
        "w_up": noise(streams_of[9], (D, FF), D ** -0.5, 0.25, ((0, 32),)),
        "w_down": noise(streams_of[10], (FF, D), FF ** -0.5, 0.125, ((0, 32),)),
        "biases": noise(streams_of[11], (7, D), 0.3, 1.2, (), jnp.float32),
        "up_bias": noise(streams_of[12], (FF,), 0.3, 1.2, (), jnp.float32),
        "norm_gain": jnp.clip(1.0 + 0.1 * jax.random.normal(streams_of[13], (3, D), jnp.float32), 0.5, 1.5),
        "norm_shift": noise(streams_of[14], (3, D), 0.2, 0.8, (), jnp.float32),
        "omega": jnp.clip(jax.random.uniform(streams_of[15], (3, D), jnp.float32, 0.5, 1.5), 0.5, 1.5),
    }


@jax.custom_vjp
def low(v):
    return lax.optimization_barrier(v.astype(jnp.bfloat16)).astype(jnp.float32)

@jax.custom_vjp
def low_back(v):
    return v

def low_keep(v):
    return (low(v), None)

def low_pass(kept, grad):
    return (grad,)

def back_keep(v):
    return (v, None)

def back_low(kept, grad):
    return (low(grad),)
low.defvjp(low_keep, low_pass)
low_back.defvjp(back_keep, back_low)

def both_round(value):
    return low(low_back(value))

def product(spec, left, right):
    return jnp.einsum(spec, left, right, precision=lax.Precision.HIGHEST)

def segment_of(positions, lengths):
    ends = jnp.cumsum(lengths)
    return lax.optimization_barrier(jnp.sum((ends[None, :] <= positions[:, None]).astype(jnp.int32), axis=-1))

def segment_start(positions, lengths):
    starts = jnp.cumsum(lengths) - lengths
    return jnp.any(starts[None, :] == positions[:, None], axis=-1)

def norm_block(branch, skip, scale, gain, shift):
    mixed = skip * scale + branch
    centered = mixed - lax.optimization_barrier(jnp.mean(mixed, axis=-1, keepdims=True))
    variance = lax.optimization_barrier(jnp.mean(centered * centered, axis=-1, keepdims=True))
    return centered * lax.rsqrt(variance + 1e-05) * gain + shift

def attention(queries, keys, values, query_seg, key_seg, key_usable, causal):
    length, width = queries.shape
    head_size = width // HEADS
    block = math.gcd(length, 512)
    count = length // block
    key_heads = keys.reshape(length, HEADS, head_size)
    value_heads = values.reshape(length, HEADS, head_size)
    key_pos = jnp.arange(length, dtype=jnp.int32)

    def one_block(pieces):
        query_blk, seg_blk, pos_blk = pieces
        scores = low_back(product('qhd,khd->hqk', query_blk.reshape(block, HEADS, head_size), key_heads) * 0.125)
        same = seg_blk[:, None] == key_seg[None, :]
        if causal:
            permit = same & (key_pos[None, :] <= pos_blk[:, None]) & (key_usable[None, :] | (key_pos[None, :] == pos_blk[:, None]))
        else:
            permit = same & key_usable[None, :]
        weights = jnp.where(permit[None], jnp.exp(scores), 0.0)
        totals = lax.optimization_barrier(jnp.sum(weights, axis=-1))
        summed = low_back(product('hqk,khd->qhd', low(weights), value_heads))
        return (summed / jnp.transpose(totals)[:, :, None]).reshape(block, width)
    outputs = lax.map(jax.checkpoint(one_block), (queries.reshape(count, block, width), query_seg.reshape(count, block), key_pos.reshape(count, block)))
    return outputs.reshape(length, width)

def layer_row(weights, words, sources, tgt_len, src_len, tgt_real, src_real):
    attn_in, attn_out, w_up, w_down, biases, up_bias, norm_gain, norm_shift, omega = weights
    length = words.shape[0]
    positions = jnp.arange(length, dtype=jnp.int32)
    tgt_seg = segment_of(positions, tgt_len)
    src_seg = segment_of(positions, src_len)
    tgt_usable = tgt_real > 0
    src_usable = (src_real > 0) | segment_start(positions, src_len)
    self_query = both_round(product('td,de->te', words, attn_in[0, 0]) + biases[0])
    self_key = both_round(product('td,de->te', words, attn_in[0, 1]))
    self_value = both_round(product('td,de->te', words, attn_in[0, 2]) + biases[1])
    heard = attention(self_query, self_key, self_value, tgt_seg, tgt_seg, tgt_usable, True)
    branch_self = low_back(product('td,de->te', low(heard), attn_out[0]) + biases[2])
    hidden_one = norm_block(branch_self, words, omega[0], norm_gain[0], norm_shift[0])
    cross_query = both_round(product('td,de->te', low(hidden_one), attn_in[1, 0]) + biases[3])
    cross_key = both_round(product('td,de->te', sources, attn_in[1, 1]))
    cross_value = both_round(product('td,de->te', sources, attn_in[1, 2]) + biases[4])
    recalled = attention(cross_query, cross_key, cross_value, tgt_seg, src_seg, src_usable, False)
    branch_cross = low_back(product('td,de->te', low(recalled), attn_out[1]) + biases[5])
    hidden_two = norm_block(branch_cross, hidden_one, omega[1], norm_gain[1], norm_shift[1])
    up_pre = low_back(product('td,df->tf', low(hidden_two), w_up) + up_bias)
    active = low(jax.nn.gelu(up_pre))
    branch_ffn = low_back(product('tf,fd->td', active, w_down) + biases[6])
    return norm_block(branch_ffn, hidden_two, omega[2], norm_gain[2], norm_shift[2])

def reference(tokens, memory, cotangent, tgt_lengths, src_lengths, tgt_mask, src_mask, attn_in, attn_out, w_up, w_down, biases, up_bias, norm_gain, norm_shift, omega):

    def to_rows(array):
        moved = jnp.moveaxis(array, 2, 1)
        return moved.reshape((MICRO * ROWS,) + moved.shape[2:])

    def from_rows(array):
        return jnp.moveaxis(array.reshape((MICRO, ROWS) + array.shape[1:]), 1, 2)
    token_rows = to_rows(tokens.astype(jnp.float32))
    memory_rows = to_rows(memory.astype(jnp.float32))
    grad_rows = to_rows(cotangent.astype(jnp.float32))
    tgt_row_lengths = tgt_lengths.reshape(MICRO * ROWS, NSEG)
    src_row_lengths = src_lengths.reshape(MICRO * ROWS, NSEG)
    tgt_row_mask = to_rows(tgt_mask)
    src_row_mask = to_rows(src_mask)
    params = tuple((item.astype(jnp.float32) for item in (attn_in, attn_out, w_up, w_down, biases, up_bias, norm_gain, norm_shift, omega)))

    def forward(weights, words, sources):

        def one_row(pieces):
            return layer_row(weights, pieces[0], pieces[1], pieces[2], pieces[3], pieces[4], pieces[5])
        return lax.map(jax.checkpoint(one_row), (words, sources, tgt_row_lengths, src_row_lengths, tgt_row_mask, src_row_mask))
    outputs, pull = jax.vjp(forward, params, token_rows, memory_rows)
    grad_params, grad_words, grad_sources = pull(grad_rows)
    return (from_rows(outputs).astype(jnp.bfloat16), from_rows(grad_words).astype(jnp.bfloat16), from_rows(grad_sources).astype(jnp.bfloat16), grad_params[0], grad_params[1], grad_params[2], grad_params[3], grad_params[4], grad_params[5], grad_params[6], grad_params[7], grad_params[8])
```

```python
import functools
import math

import jax
import jax.numpy as jnp
from jax import lax
from jax.experimental import pallas as pl
from jax.experimental.pallas import tpu as pltpu
from jax.sharding import PartitionSpec as P

HEADS = 8


def norm_block(branch, skip, scale, gain, shift):
    mixed = skip * scale + branch
    centered = mixed - jnp.mean(mixed, axis=-1, keepdims=True)
    variance = jnp.mean(centered * centered, axis=-1, keepdims=True)
    return centered * lax.rsqrt(variance + 1e-05) * gain + shift


def project(values, matrix):
    return jnp.einsum("trd,de->tre", values, matrix, preferred_element_type=jnp.float32)


def project_back(grads, matrix):
    return jnp.einsum("tre,de->trd", grads, matrix, preferred_element_type=jnp.float32)


def matrix_grad(values, grads):
    return jnp.einsum("trd,tre->de", values, grads, preferred_element_type=jnp.float32)


def column_sum(grads):
    return jnp.sum(grads.astype(jnp.float32), axis=(0, 1))


def segment_of(positions, ends):
    return jnp.sum((ends[None, :, :] <= positions[:, None, None]).astype(jnp.int32), axis=-1)


def segment_bounds(first, last, ends):
    lowest = jnp.sum((ends <= first).astype(jnp.int32), axis=-1)
    highest = jnp.sum((ends <= last).astype(jnp.int32), axis=-1)
    return (lowest, highest)


def ranges_share(query_bounds, key_bounds):
    return jnp.any((key_bounds[0] <= query_bounds[1]) & (key_bounds[1] >= query_bounds[0]))


def key_status(positions, real_marks, ends, starts, causal):
    segments = segment_of(positions, ends)
    usable = real_marks > 0.5
    if not causal:
        usable = usable | jnp.any(starts[None, :, :] == positions[:, None, None], axis=-1)
    return (segments, usable)


def permitted(query_pos, query_seg, key_pos, key_seg, usable, causal):
    same = jnp.transpose(query_seg)[:, :, None] == jnp.transpose(key_seg)[:, None, :]
    usable_keys = jnp.transpose(usable)[:, None, :]
    if causal:
        before = (key_pos[None, :] <= query_pos[:, None])[None]
        itself = (key_pos[None, :] == query_pos[:, None])[None]
        return same & before & (usable_keys | itself)
    return same & usable_keys


def block_grads(query_heads, grad_heads, lambdas, key_heads, value_heads, permit):
    scores = (
        jnp.einsum("arhd,brhd->rhab", query_heads, key_heads, preferred_element_type=jnp.float32)
        * 0.125
    )
    weights = jnp.where(permit[:, None], jnp.exp(scores), 0.0)
    spread = jnp.einsum(
        "arhd,brhd->rhab", grad_heads, value_heads, preferred_element_type=jnp.float32
    )
    slopes = weights * (spread + jnp.transpose(lambdas, (1, 2, 0))[..., None])
    return (weights.astype(jnp.bfloat16), slopes.astype(jnp.bfloat16))


def local(
    tokens,
    memory,
    cotangent,
    tgt_lengths,
    src_lengths,
    tgt_mask,
    src_mask,
    attn_in,
    attn_out,
    w_up,
    w_down,
    biases,
    up_bias,
    norm_gain,
    norm_shift,
    omega,
):
    micro_count, tokens_here, rows_here, width = tokens.shape
    head_size = width // HEADS
    my_pos = lax.axis_index("seq") * tokens_here + jnp.arange(tokens_here, dtype=jnp.int32)
    my_first = my_pos[0]
    my_last = my_pos[tokens_here - 1]

    def split_heads(values):
        return values.reshape(values.shape[0], rows_here, HEADS, head_size)

    def zero_heads():
        return jnp.zeros((tokens_here, rows_here, HEADS, head_size), jnp.float32)

    results = []
    grads_words = []
    grads_sources = []
    shares_all = None
    for micro_index in range(micro_count):
        in_weights = lax.all_gather(attn_in, ("rows", "seq"), axis=2, tiled=True)
        out_weights = lax.all_gather(attn_out, ("rows", "seq"), axis=1, tiled=True)
        up_weights = lax.all_gather(w_up, ("rows", "seq"), axis=0, tiled=True)
        down_weights = lax.all_gather(w_down, ("rows", "seq"), axis=0, tiled=True)
        words = tokens[micro_index]
        sources = memory[micro_index]
        words_full = words.astype(jnp.float32)
        tgt_len = tgt_lengths[micro_index]
        src_len = src_lengths[micro_index]
        tgt_ends = jnp.cumsum(tgt_len, axis=-1)
        src_ends = jnp.cumsum(src_len, axis=-1)
        src_starts = src_ends - src_len
        query_seg = segment_of(my_pos, tgt_ends)
        query_bounds = segment_bounds(my_first, my_last, tgt_ends)
        tgt_real = tgt_mask[micro_index].astype(jnp.bfloat16)
        src_real = src_mask[micro_index].astype(jnp.bfloat16)

        def attend(queries, keys, values, real_marks, ends, starts, causal):
            full_keys, full_values, full_real = (
                lax.all_gather(keys, "seq", axis=0, tiled=True),
                lax.all_gather(values, "seq", axis=0, tiled=True),
                lax.all_gather(real_marks, "seq", axis=0, tiled=True),
            )
            length = full_keys.shape[0]
            block = math.gcd(length, 512)
            query_heads = split_heads(queries)

            def step(carry, block_index):
                begin = block_index * block
                shares = ranges_share(query_bounds, segment_bounds(begin, begin + block - 1, ends))

                def step_compute(state):
                    totals, accum = state
                    key_heads = split_heads(lax.dynamic_slice_in_dim(full_keys, begin, block, 0))
                    value_heads = split_heads(
                        lax.dynamic_slice_in_dim(full_values, begin, block, 0)
                    )
                    key_pos = begin + jnp.arange(block, dtype=jnp.int32)
                    key_seg, usable = key_status(
                        key_pos,
                        lax.dynamic_slice_in_dim(full_real, begin, block, 0),
                        ends,
                        starts,
                        causal,
                    )
                    permit = permitted(my_pos, query_seg, key_pos, key_seg, usable, causal)
                    scores = (
                        jnp.einsum(
                            "trhd,krhd->rhtk",
                            query_heads,
                            key_heads,
                            preferred_element_type=jnp.float32,
                        )
                        * 0.125
                    )
                    weights = jnp.where(permit[:, None], jnp.exp(scores), 0.0)
                    totals = totals + jnp.sum(weights, axis=-1)
                    accum = accum + jnp.einsum(
                        "rhtk,krhd->trhd",
                        weights.astype(jnp.bfloat16),
                        value_heads,
                        preferred_element_type=jnp.float32,
                    )
                    return (totals, accum)

                return (lax.cond(shares, step_compute, lambda unchanged: unchanged, carry), None)

            start_carry = (jnp.zeros((rows_here, HEADS, tokens_here), jnp.float32), zero_heads())
            (totals, accum), unused = lax.scan(
                step, start_carry, jnp.arange(length // block, dtype=jnp.int32)
            )
            sums = jnp.transpose(totals, (2, 0, 1))
            output = (accum / sums[..., None]).reshape(tokens_here, rows_here, width)
            return (output, sums, (full_keys, full_values, full_real))

        def attention_back(
            grad_out,
            output,
            sums,
            queries,
            keys,
            values,
            real_marks,
            gathered_set,
            ends,
            starts,
            causal,
        ):
            full_keys, full_values, full_real = gathered_set
            grad_heads = split_heads(grad_out)
            lambdas = -jnp.sum(grad_heads * split_heads(output), axis=-1) / sums
            scaled = (grad_heads / sums[..., None]).astype(jnp.bfloat16)
            query_heads = split_heads(queries)
            length = full_keys.shape[0]
            block = math.gcd(length, 512)

            def query_step(accum, block_index):
                begin = block_index * block
                shares = ranges_share(query_bounds, segment_bounds(begin, begin + block - 1, ends))

                def query_compute(state):
                    key_heads = split_heads(lax.dynamic_slice_in_dim(full_keys, begin, block, 0))
                    value_heads = split_heads(
                        lax.dynamic_slice_in_dim(full_values, begin, block, 0)
                    )
                    key_pos = begin + jnp.arange(block, dtype=jnp.int32)
                    key_seg, usable = key_status(
                        key_pos,
                        lax.dynamic_slice_in_dim(full_real, begin, block, 0),
                        ends,
                        starts,
                        causal,
                    )
                    permit = permitted(my_pos, query_seg, key_pos, key_seg, usable, causal)
                    weights, slopes = block_grads(
                        query_heads, scaled, lambdas, key_heads, value_heads, permit
                    )
                    return (
                        state
                        + jnp.einsum(
                            "rhab,brhd->arhd", slopes, key_heads, preferred_element_type=jnp.float32
                        )
                        * 0.125
                    )

                return (lax.cond(shares, query_compute, lambda unchanged: unchanged, accum), None)

            grad_query, unused = lax.scan(
                query_step, zero_heads(), jnp.arange(length // block, dtype=jnp.int32)
            )
            all_lambdas = lax.all_gather(lambdas, "seq", axis=0, tiled=True)
            local_seg, local_usable = key_status(my_pos, real_marks, ends, starts, causal)
            local_bounds = segment_bounds(my_first, my_last, ends)
            local_keys = split_heads(keys)
            local_values = split_heads(values)
            query_piece = lax.all_gather(queries, "seq", axis=0, tiled=True)
            scaled_piece = lax.all_gather(
                scaled.reshape(tokens_here, rows_here, width), "seq", axis=0, tiled=True
            )
            size = query_piece.shape[0]
            inner = math.gcd(size, 512)

            def inner_step(inner_carry, inner_index):
                offset = inner_index * inner
                piece_first = offset
                shares = ranges_share(
                    segment_bounds(piece_first, piece_first + inner - 1, tgt_ends), local_bounds
                )

                def inner_compute(state):
                    acc_key, acc_value = state
                    query_blk = split_heads(lax.dynamic_slice_in_dim(query_piece, offset, inner, 0))
                    scaled_blk = split_heads(
                        lax.dynamic_slice_in_dim(scaled_piece, offset, inner, 0)
                    )
                    lambda_blk = lax.dynamic_slice_in_dim(all_lambdas, piece_first, inner, 0)
                    query_pos = piece_first + jnp.arange(inner, dtype=jnp.int32)
                    permit = permitted(
                        query_pos,
                        segment_of(query_pos, tgt_ends),
                        my_pos,
                        local_seg,
                        local_usable,
                        causal,
                    )
                    weights, slopes = block_grads(
                        query_blk, scaled_blk, lambda_blk, local_keys, local_values, permit
                    )
                    acc_key = (
                        acc_key
                        + jnp.einsum(
                            "rhab,arhd->brhd", slopes, query_blk, preferred_element_type=jnp.float32
                        )
                        * 0.125
                    )
                    acc_value = acc_value + jnp.einsum(
                        "rhab,arhd->brhd", weights, scaled_blk, preferred_element_type=jnp.float32
                    )
                    return (acc_key, acc_value)

                return (
                    lax.cond(shares, inner_compute, lambda unchanged: unchanged, inner_carry),
                    None,
                )

            folded, unused_inner = lax.scan(
                inner_step, (zero_heads(), zero_heads()), jnp.arange(size // inner, dtype=jnp.int32)
            )
            grad_key, grad_value = folded
            grad_key = grad_key.reshape(tokens_here, rows_here, width)
            grad_value = grad_value.reshape(tokens_here, rows_here, width)
            return (grad_query.reshape(tokens_here, rows_here, width), grad_key, grad_value)

        self_query = (project(words, in_weights[0, 0]) + biases[0]).astype(jnp.bfloat16)
        self_key = project(words, in_weights[0, 1]).astype(jnp.bfloat16)
        self_value = (project(words, in_weights[0, 2]) + biases[1]).astype(jnp.bfloat16)
        heard, heard_sums, self_set = attend(
            self_query, self_key, self_value, tgt_real, tgt_ends, None, True
        )
        heard_low = heard.astype(jnp.bfloat16)
        branch_self = project(heard_low, out_weights[0]) + biases[2]
        hidden_one, pull_one = jax.vjp(
            norm_block, branch_self, words_full, omega[0], norm_gain[0], norm_shift[0]
        )
        hidden_one_low = hidden_one.astype(jnp.bfloat16)
        cross_query = (project(hidden_one_low, in_weights[1, 0]) + biases[3]).astype(jnp.bfloat16)
        cross_key = project(sources, in_weights[1, 1]).astype(jnp.bfloat16)
        cross_value = (project(sources, in_weights[1, 2]) + biases[4]).astype(jnp.bfloat16)
        recalled, recalled_sums, cross_set = attend(
            cross_query, cross_key, cross_value, src_real, src_ends, src_starts, False
        )
        recalled_low = recalled.astype(jnp.bfloat16)
        branch_cross = project(recalled_low, out_weights[1]) + biases[5]
        hidden_two, pull_two = jax.vjp(
            norm_block, branch_cross, hidden_one, omega[1], norm_gain[1], norm_shift[1]
        )
        hidden_two_low = hidden_two.astype(jnp.bfloat16)
        up_pre = project(hidden_two_low, up_weights) + up_bias
        active, pull_active = jax.vjp(jax.nn.gelu, up_pre)
        active_low = active.astype(jnp.bfloat16)
        branch_ffn = project(active_low, down_weights) + biases[6]
        outcome, pull_three = jax.vjp(
            norm_block, branch_ffn, hidden_two, omega[2], norm_gain[2], norm_shift[2]
        )
        grad_result = cotangent[micro_index].astype(jnp.float32)
        grad_ffn, grad_two, omega_three, gain_three, shift_three = pull_three(grad_result)
        grad_ffn_low = grad_ffn.astype(jnp.bfloat16)
        grad_down = matrix_grad(active_low, grad_ffn_low)
        bias_ffn = column_sum(grad_ffn_low)
        grad_up_pre = pull_active(project_back(grad_ffn_low, down_weights))[0].astype(jnp.bfloat16)
        grad_up = matrix_grad(hidden_two_low, grad_up_pre)
        bias_up = column_sum(grad_up_pre)
        grad_two = grad_two + project_back(grad_up_pre, up_weights)
        grad_cross, grad_one, omega_two, gain_two, shift_two = pull_two(grad_two)
        grad_cross_low = grad_cross.astype(jnp.bfloat16)
        grad_out_cross = matrix_grad(recalled_low, grad_cross_low)
        bias_out_cross = column_sum(grad_cross_low)
        grad_recalled = project_back(grad_cross_low, out_weights[1])
        cross_gq, cross_gk, cross_gv = attention_back(
            grad_recalled,
            recalled,
            recalled_sums,
            cross_query,
            cross_key,
            cross_value,
            src_real,
            cross_set,
            src_ends,
            src_starts,
            False,
        )
        cross_gq = cross_gq.astype(jnp.bfloat16)
        cross_gk = cross_gk.astype(jnp.bfloat16)
        cross_gv = cross_gv.astype(jnp.bfloat16)
        grad_cross_query = matrix_grad(hidden_one_low, cross_gq)
        grad_cross_key = matrix_grad(sources, cross_gk)
        grad_cross_value = matrix_grad(sources, cross_gv)
        grad_one = grad_one + project_back(cross_gq, in_weights[1, 0])
        grad_sources = project_back(cross_gk, in_weights[1, 1]) + project_back(
            cross_gv, in_weights[1, 2]
        )
        grad_self, grad_words, omega_one, gain_one, shift_one = pull_one(grad_one)
        grad_self_low = grad_self.astype(jnp.bfloat16)
        grad_out_self = matrix_grad(heard_low, grad_self_low)
        bias_out_self = column_sum(grad_self_low)
        grad_heard = project_back(grad_self_low, out_weights[0])
        self_gq, self_gk, self_gv = attention_back(
            grad_heard,
            heard,
            heard_sums,
            self_query,
            self_key,
            self_value,
            tgt_real,
            self_set,
            tgt_ends,
            None,
            True,
        )
        self_gq = self_gq.astype(jnp.bfloat16)
        self_gk = self_gk.astype(jnp.bfloat16)
        self_gv = self_gv.astype(jnp.bfloat16)
        grad_words = (
            grad_words
            + project_back(self_gq, in_weights[0, 0])
            + project_back(self_gk, in_weights[0, 1])
            + project_back(self_gv, in_weights[0, 2])
        )
        grad_in = jnp.stack(
            [
                jnp.stack(
                    [
                        matrix_grad(words, self_gq),
                        matrix_grad(words, self_gk),
                        matrix_grad(words, self_gv),
                    ]
                ),
                jnp.stack([grad_cross_query, grad_cross_key, grad_cross_value]),
            ]
        )
        grad_out = jnp.stack([grad_out_self, grad_out_cross])
        grad_bias = jnp.stack(
            [
                column_sum(self_gq),
                column_sum(self_gv),
                bias_out_self,
                column_sum(cross_gq),
                column_sum(cross_gv),
                bias_out_cross,
                bias_ffn,
            ]
        )
        grad_gain = jnp.stack([gain_one, gain_two, gain_three])
        grad_shift = jnp.stack([shift_one, shift_two, shift_three])
        grad_omega = jnp.stack([omega_one, omega_two, omega_three])
        grads = (
            grad_in,
            grad_out,
            grad_up,
            grad_down,
            grad_bias,
            bias_up,
            grad_gain,
            grad_shift,
            grad_omega,
        )
        outcome, grad_words, grad_sources, grads = (
            outcome.astype(jnp.bfloat16),
            grad_words.astype(jnp.bfloat16),
            grad_sources.astype(jnp.bfloat16),
            grads,
        )
        results.append(outcome)
        grads_words.append(grad_words)
        grads_sources.append(grad_sources)
        part_shares = (
            lax.psum_scatter(grads[0], ("rows", "seq"), scatter_dimension=2, tiled=True),
            lax.psum_scatter(grads[1], ("rows", "seq"), scatter_dimension=1, tiled=True),
            lax.psum_scatter(grads[2], ("rows", "seq"), scatter_dimension=0, tiled=True),
            lax.psum_scatter(grads[3], ("rows", "seq"), scatter_dimension=0, tiled=True),
            lax.psum_scatter(grads[4], ("rows", "seq"), scatter_dimension=1, tiled=True),
            lax.psum_scatter(grads[5], ("rows", "seq"), scatter_dimension=0, tiled=True),
            lax.psum_scatter(grads[6], ("rows", "seq"), scatter_dimension=1, tiled=True),
            lax.psum_scatter(grads[7], ("rows", "seq"), scatter_dimension=1, tiled=True),
            lax.psum_scatter(grads[8], ("rows", "seq"), scatter_dimension=1, tiled=True),
        )
        shares_all = (
            part_shares if shares_all is None else jax.tree.map(jnp.add, shares_all, part_shares)
        )
    return (jnp.stack(results), jnp.stack(grads_words), jnp.stack(grads_sources)) + tuple(
        shares_all
    )


def over(mesh, function):
    return jax.shard_map(
        function,
        mesh=mesh,
        in_specs=(
            P(None, "seq", "rows", None),
            P(None, "seq", "rows", None),
            P(None, "seq", "rows", None),
            P(None, "rows", None),
            P(None, "rows", None),
            P(None, "seq", "rows"),
            P(None, "seq", "rows"),
            P(None, None, ("rows", "seq"), None),
            P(None, ("rows", "seq"), None),
            P(("rows", "seq"), None),
            P(("rows", "seq"), None),
            P(),
            P(),
            P(),
            P(),
            P(),
        ),
        out_specs=(
            P(None, "seq", "rows", None),
            P(None, "seq", "rows", None),
            P(None, "seq", "rows", None),
            P(None, None, ("rows", "seq"), None),
            P(None, ("rows", "seq"), None),
            P(("rows", "seq"), None),
            P(("rows", "seq"), None),
            P(None, ("rows", "seq")),
            P(("rows", "seq")),
            P(None, ("rows", "seq")),
            P(None, ("rows", "seq")),
            P(None, ("rows", "seq")),
        ),
        check_vma=False,
    )


def general(mesh):
    return over(mesh, local)


MESH = pl.DeviceIdType.MESH
F32 = jnp.float32
BF16 = jnp.bfloat16
PLANES, YS, XS, CORES = 4, 2, 2, 2
GROUP = YS * XS * CORES


def nn(left, right):
    return lax.dot_general(left, right, (((1,), (0,)), ((), ())), preferred_element_type=F32)


def nt(left, right):
    return lax.dot_general(left, right, (((1,), (1,)), ((), ())), preferred_element_type=F32)


def tn(left, right):
    return lax.dot_general(left, right, (((0,), (0,)), ((), ())), preferred_element_type=F32)


def flip(value):
    return jnp.transpose(value.astype(F32))


def fused_kernel(
    tok, mem, cot, meta, s_in, s_out, s_up, s_dn, biases, up_bias, gain, shift, omega,
    o_res, o_tok, o_mem, o_in, o_out, o_up, o_dn, o_bias, o_upb, o_gain, o_shift, o_omega,
    w_in, w_out, w_up, w_dn, g_in, g_out, g_up, g_dn,
    c_in, c_out, c_up, c_dn,
    p_in, p_out, p_up, p_dn,
    q_in, q_out, q_up, q_dn,
    z_in, z_out, z_up, z_dn,
    in_tok, in_mem, in_cot, in_meta, all_meta,
    a1, b1, a2, b2, a3, b3, a4, b4, a5, b5, a6, b6, a7, b7, a8, b8, a9, b9,
    out_res, out_tok, out_mem,
    sg0, sg1, sg2, sg3, sg4, sr0, sr1, sr2, sr3,
    code_self, code_cross, key_pos, rows_f,
    qt0, kt0, vt0, k0, v0, pt0, l0, ot0,
    qt1, kt1, vt1, k1, v1, pt1, l1, ot1,
    dnt, acc_k, acc_v, acc_q,
    act, slope, xh0, xh1, xh2, h1_f, h2_f,
    ss, rs,
):
    c = lax.axis_index("rows")
    seq = lax.axis_index("seq")
    z = seq // (YS * XS)
    yx = lax.rem(seq, YS * XS)
    y = yx // XS
    x = lax.rem(yx, XS)
    width = 512
    here = 2 * 64

    def at(zz, yy, xx):
        return zz * (YS * XS) + yy * XS + xx

    def slot(cc, yy, xx):
        return cc * 4 + yy * 2 + xx

    def head(cc, yy, xx):
        return (yy * 2 + xx) * 2 + cc

    me_slot, me_head = slot(c, y, x), head(c, y, x)
    plane_peers = []
    for k in range(1, GROUP):
        cc = 1 - c if k & 4 else c
        yy = 1 - y if k & 2 else y
        xx = 1 - x if k & 1 else x
        plane_peers.append((cc, yy, xx))
    z_peers = [lax.rem(z + k, PLANES) for k in (1, 2, 3)]

    barrier = pltpu.get_barrier_semaphore()
    greet = [(cc, at(z, yy, xx)) for cc, yy, xx in plane_peers]
    greet += [(cc, at(zz, y, x)) for zz in z_peers for cc in (c, 1 - c)]
    for device in greet:
        pl.semaphore_signal(barrier, inc=1, device_id=device, device_id_type=MESH)
    pl.semaphore_wait(barrier, len(greet))

    names = {}
    pending = []

    def sem(name):
        return names.setdefault(name, len(names))

    def wait(semaphore, ref):
        pltpu.make_async_copy(ref, ref, semaphore).wait()

    def send(name, src, dst, device):
        i = sem(name)
        pltpu.make_async_remote_copy(
            src_ref=src, dst_ref=dst, send_sem=ss.at[i], recv_sem=rs.at[i], device_id=device, device_id_type=MESH
        ).start()

    def keep(name, src, dst):
        pltpu.make_async_copy(src, dst, rs.at[sem(name)]).start()

    def landed(name, ref):
        wait(rs.at[sem(name)], ref)

    def sent_later(name, ref):
        pending.append((name, ref))

    def to_plane(name, src, dst):
        for m in range(2):
            plane = 2 * m + c
            core = z // 2
            half = lax.rem(z, 2)
            own = (plane == z) & (core == c)
            part = dst.at[half]

            @pl.when(own)
            def _():
                keep(name, src.at[m], part)

            @pl.when(jnp.logical_not(own))
            def _():
                i = sem(name)
                j = sem(name + str(m))
                pltpu.make_async_remote_copy(
                    src_ref=src.at[m], dst_ref=part, send_sem=ss.at[j], recv_sem=rs.at[i],
                    device_id=(core, at(plane, y, x)), device_id_type=MESH,
                ).start()

            pending.append((name + str(m), src.at[m], jnp.logical_not(own)))

    def from_plane(name, src, dst):
        micro, core = z // 2, lax.rem(z, 2)
        for half in range(2):
            zz = 2 * c + half
            own = (core == c) & (zz == z)
            part = dst.at[micro]

            @pl.when(own)
            def _():
                keep(name, src.at[half], part)

            @pl.when(jnp.logical_not(own))
            def _():
                i = sem(name)
                j = sem(name + str(half))
                pltpu.make_async_remote_copy(
                    src_ref=src.at[half], dst_ref=part, send_sem=ss.at[j], recv_sem=rs.at[i],
                    device_id=(core, at(zz, y, x)), device_id_type=MESH,
                ).start()

            pending.append((name + str(half), src.at[half], jnp.logical_not(own)))

    def to_heads(name, src, dst):
        keep(name, src.at[me_head], dst.at[me_slot])
        for cc, yy, xx in plane_peers:
            send(name, src.at[head(cc, yy, xx)], dst.at[me_slot], (cc, at(z, yy, xx)))
        sent_later(name, src.at[pl.ds(0, GROUP - 1)])

    def to_slots(name, src, dst):
        keep(name, src.at[me_slot], dst.at[me_head])
        for cc, yy, xx in plane_peers:
            send(name, src.at[slot(cc, yy, xx)], dst.at[me_head], (cc, at(z, yy, xx)))
        sent_later(name, src.at[pl.ds(0, GROUP - 1)])

    weights = {
        "in0": (w_in.at[0], s_in.at[0], g_in.at[0], c_in.at[0], p_in.at[0], q_in.at[0], z_in.at[0], o_in.at[0]),
        "in1": (w_in.at[1], s_in.at[1], g_in.at[1], c_in.at[1], p_in.at[1], q_in.at[1], z_in.at[1], o_in.at[1]),
        "out": (w_out, s_out, g_out, c_out, p_out, q_out, z_out, o_out),
        "up": (w_up, s_up, g_up, c_up, p_up, q_up, z_up, o_up),
        "dn": (w_dn, s_dn, g_dn, c_dn, p_dn, q_dn, z_dn, o_dn),
    }

    def halves(ref):
        cols = ref.shape[-1] // 2
        return pl.ds(0, cols), pl.ds(cols, cols)

    x_next, y_next, core_next = (c, at(z, y, 1 - x)), (c, at(z, 1 - y, x)), (1 - c, seq)

    def gather_z(g):
        full, shard = weights[g][:2]
        keep(g + "z", shard, full.at[:, c, z, y, x])
        for zz in z_peers:
            send(g + "z", shard, full.at[:, c, z, y, x], (c, at(zz, y, x)))
        sent_later(g + "z", full.at[:, c, pl.ds(0, 3), y, x])

    def gather_1(g):
        full = weights[g][0]
        first, second = halves(full)
        landed(g + "z", full.at[:, c, :, y, x])
        part = full.at[:, c, :, y, x, :, first]
        send(g + "1a", part, part, x_next)
        sent_later(g + "1a", part)
        part = full.at[:, c, :, y, x, :, second]
        send(g + "1b", part, part, y_next)
        sent_later(g + "1b", part)

    def gather_2(g):
        full = weights[g][0]
        first, second = halves(full)
        landed(g + "1a", full.at[:, c, :, y, 1 - x, :, first])
        part = full.at[:, c, :, y, :, :, first]
        send(g + "2a", part, part, y_next)
        sent_later(g + "2a", part)
        landed(g + "1b", full.at[:, c, :, 1 - y, x, :, second])
        part = full.at[:, c, :, :, x, :, second]
        send(g + "2b", part, part, x_next)
        sent_later(g + "2b", part)

    def gather_3(g):
        full = weights[g][0]
        first, second = halves(full)
        landed(g + "2a", full.at[:, c, :, 1 - y, :, :, first])
        landed(g + "2b", full.at[:, c, :, :, 1 - x, :, second])
        send(g + "3", full.at[:, c], full.at[:, c], core_next)
        sent_later(g + "3", full.at[:, c])

    def gathered(g):
        landed(g + "3", weights[g][0].at[:, 1 - c])

    def add(target, other):
        target[...] = (target[...].astype(F32) + other[...].astype(F32)).astype(BF16)

    def scatter_0(g):
        grad, across = weights[g][2:4]
        send(g + "r0", grad.at[:, 1 - c], across, core_next)
        sent_later(g + "r0", across)

    def scatter_1(g):
        grad, across, part = weights[g][2:5]
        first, second = halves(grad)
        landed(g + "r0", across)
        for lead in range(grad.shape[0]):

            @pl.loop(0, PLANES)
            def _(zz):
                add(grad.at[lead, c, zz], across.at[lead, zz])

        send(g + "r1a", grad.at[:, c, :, 1 - y, :, :, first], part.at[0], y_next)
        sent_later(g + "r1a", part.at[0])
        send(g + "r1b", grad.at[:, c, :, :, 1 - x, :, second], part.at[1], x_next)
        sent_later(g + "r1b", part.at[1])

    def scatter_2(g):
        grad, _, part, piece = weights[g][2:6]
        first, second = halves(grad)
        landed(g + "r1a", part.at[0])
        landed(g + "r1b", part.at[1])
        for lead in range(grad.shape[0]):

            @pl.loop(0, PLANES)
            def _(zz):
                add(grad.at[lead, c, zz, y, :, :, first], part.at[0, lead, zz])
                add(grad.at[lead, c, zz, :, x, :, second], part.at[1, lead, zz])

        send(g + "r2a", grad.at[:, c, :, y, 1 - x, :, first], piece.at[0], x_next)
        sent_later(g + "r2a", piece.at[0])
        send(g + "r2b", grad.at[:, c, :, 1 - y, x, :, second], piece.at[1], y_next)
        sent_later(g + "r2b", piece.at[1])

    def scatter_3(g):
        grad, _, _, piece, line = weights[g][2:7]
        first, second = halves(grad)
        landed(g + "r2a", piece.at[0])
        landed(g + "r2b", piece.at[1])
        for lead in range(grad.shape[0]):

            @pl.loop(0, PLANES)
            def _(zz):
                add(grad.at[lead, c, zz, y, x, :, first], piece.at[0, lead, zz])
                add(grad.at[lead, c, zz, y, x, :, second], piece.at[1, lead, zz])

        for k in range(3):
            send(g + "r3", grad.at[:, c, z_peers[k], y, x], line.at[2 - k], (c, at(z_peers[k], y, x)))
        sent_later(g + "r3", line)

    def scattered(g):
        grad, _, _, _, line, result = weights[g][2:8]
        landed(g + "r3", line)
        total = grad[:, c, z, y, x].astype(F32)
        for k in range(3):
            total = total + line[k].astype(F32)
        result[...] = total

    def matrix(ref):
        return ref[...].reshape(-1, ref.shape[-1])

    def put(ref, value):
        ref[...] = value.astype(BF16).reshape(ref.shape)

    def norm(r, i, kept):
        centered = r - jnp.mean(r, axis=1, keepdims=True)
        scale = lax.rsqrt(jnp.mean(centered * centered, axis=1, keepdims=True) + 1e-05)
        xhat = centered * scale
        kept[...] = xhat
        return xhat * gain[i : i + 1, :] + shift[i : i + 1, :], scale

    def column(row, value):
        sg0[row : row + 1, :] = jnp.sum(value, axis=0, keepdims=True)

    def norm_back(grad, i, kept, scale, skip):
        xhat = kept[...]
        column(11 + i, grad * xhat)
        column(14 + i, grad)
        dxhat = grad * gain[i : i + 1, :]
        dr = dxhat - jnp.mean(dxhat, axis=1, keepdims=True)
        dr = (dr - xhat * jnp.mean(dxhat * xhat, axis=1, keepdims=True)) * scale
        column(17 + i, dr * skip)
        return dr, dr * omega[i : i + 1, :]

    def take(index, buffer, queries, keys, keys_t, values, values_t, which):
        for s in range(GROUP):
            cols = slice(s * here, (s + 1) * here)
            if "q" in which:
                queries[:, cols] = (buffer[(s,) + index["q"]].astype(F32) * 0.125).astype(BF16)
            if "k" in which:
                block = buffer[(s,) + index["k"]]
                keys_t[:, cols] = block
                keys[cols, :] = flip(block).astype(BF16)
                block = buffer[(s,) + index["v"]]
                values_t[:, cols] = block
                values[cols, :] = flip(block).astype(BF16)

    BLOCK = 256

    def attend(queries, keys, values_t, weights_t, sums, outputs, causal, target):
        def make(extent):
            def body(b):
                cols = pl.ds(pl.multiple_of(b * BLOCK, BLOCK), BLOCK)
                scores = nn(keys[:extent, :], queries[:, cols])
                seg = rows_f[0:1, cols]
                code = (code_self if causal else code_cross)[:extent, :]
                permit = jnp.concatenate([code, code], axis=1) == seg
                if causal:
                    pos = key_pos[:extent, :]
                    pos = jnp.concatenate([pos, pos], axis=1)
                    mine = rows_f[1:2, cols]
                    permit = (permit & (pos <= mine)) | (pos == mine)
                weight = jnp.where(permit, jnp.exp(scores), 0.0)
                total = jnp.sum(weight, axis=0, keepdims=True)
                low = weight.astype(BF16)
                weights_t[:extent, cols] = low
                out = nn(values_t[:, :extent], low) / total
                sums[0:1, cols] = total
                outputs[:, cols] = out

            return body

        if causal:
            pl.loop(0, 2)(make(512))
            pl.loop(2, 4)(make(1024))
        else:
            pl.loop(0, 4)(make(1024))
        for s in range(GROUP):
            target[s] = outputs[:, s * here : (s + 1) * here].astype(BF16)

    def attend_back(buffer, queries, keys_t, values, weights_t, sums, outputs, causal, target):
        acc_k[...] = jnp.zeros_like(acc_k)
        acc_v[...] = jnp.zeros_like(acc_v)
        for s in range(GROUP):
            cols = slice(s * here, (s + 1) * here)
            grad = buffer[s].astype(F32)
            inverse = 1.0 / sums[0:1, cols]
            dnt[:, cols] = (grad * inverse).astype(BF16)
            rows_f[2:3, cols] = -jnp.sum(grad * outputs[:, cols], axis=0, keepdims=True) * inverse

        def make(extent):
            def body(b):
                cols = pl.ds(pl.multiple_of(b * BLOCK, BLOCK), BLOCK)
                low = weights_t[:extent, cols]
                dn = dnt[:, cols]
                spread = nn(values[:extent, :], dn)
                slopes = (low.astype(F32) * (spread + rows_f[2:3, cols])).astype(BF16)
                acc_q[:, cols] = nn(keys_t[:, :extent], slopes) * 0.125
                acc_k[:, :extent] += nt(queries[:, cols], slopes)
                acc_v[:, :extent] += nt(dn, low)

            return body

        if causal:
            pl.loop(0, 2)(make(512))
            pl.loop(2, 4)(make(1024))
        else:
            pl.loop(0, 4)(make(1024))
        for s in range(GROUP):
            cols = slice(s * here, (s + 1) * here)
            target[s, 0] = acc_q[:, cols].astype(BF16)
            target[s, 1] = acc_k[:, cols].astype(BF16)
            target[s, 2] = acc_v[:, cols].astype(BF16)

    def by_head(target, index, value):
        low = flip(value).astype(BF16).reshape(GROUP, 64, here)
        target[(slice(None),) + index] = low

    def bias(i):
        return biases[i : i + 1, :]

    to_plane("meta", meta, in_meta)
    to_plane("tok", tok, in_tok)
    gather_z("in0")
    to_plane("mem", mem, in_mem)
    gather_z("in1")
    gather_z("out")
    to_plane("cot", cot, in_cot)
    gather_z("up")
    gather_z("dn")

    landed("meta", in_meta)
    lane = lax.broadcasted_iota(jnp.int32, (8, 128), 1)
    all_meta[me_slot] = jnp.where(lane < 64, in_meta[0], in_meta[1])
    for cc, yy, xx in plane_peers:
        send("marks", all_meta.at[me_slot], all_meta.at[me_slot], (cc, at(z, yy, xx)))
    sent_later("marks", all_meta.at[pl.ds(0, 7)])
    gather_1("in0")
    gather_1("in1")
    gather_2("in0")
    gather_1("out")
    gather_2("in1")
    gather_3("in0")
    gather_1("up")
    gathered("in0")
    landed("tok", in_tok)

    words = in_tok[...].reshape(here, width)
    for j, extra in ((0, 0), (1, None), (2, 1)):
        value = nn(words, matrix(w_in.at[0, j]))
        by_head(a1, (j,), value if extra is None else value + bias(extra))
    to_heads("x1", a1, b1)
    gather_3("in1")
    gather_2("out")
    gather_1("dn")
    gathered("in1")
    landed("mem", in_mem)
    sources = in_mem[...].reshape(here, width)
    by_head(a2, (0,), nn(sources, matrix(w_in.at[1, 1])))
    by_head(a2, (1,), nn(sources, matrix(w_in.at[1, 2])) + bias(4))
    to_heads("x2", a2, b2)
    gather_3("out")

    landed("marks", all_meta.at[pl.ds(0, 7)])
    order = lax.broadcasted_iota(jnp.int32, (1, 1024), 1)
    place = (order // 512) * 512 + lax.rem(order // 64, 2) * 256 + lax.rem(order // 128, 4) * 64 + lax.rem(order, 64)
    place = place.astype(F32)
    marks = [all_meta[s].astype(F32) for s in range(GROUP)]
    tgt_real = jnp.concatenate([mark[0:1, :] for mark in marks], axis=1)
    src_real = jnp.concatenate([mark[1:2, :] for mark in marks], axis=1)
    lower = lax.broadcasted_iota(jnp.int32, (32, 128), 1)
    later = lax.broadcasted_iota(jnp.int32, (32, 128), 0)

    def ends_of(row):
        lengths = jnp.broadcast_to(row, (32, 128))
        ends = jnp.sum(jnp.where(lower <= later, lengths, 0.0), axis=1, keepdims=True)
        starts = jnp.sum(jnp.where(lower < later, lengths, 0.0), axis=1, keepdims=True)
        return ends, starts

    def count(flags):
        return jnp.sum(jnp.where(flags, 1.0, 0.0), axis=0, keepdims=True)

    tgt_ends, _ = ends_of(marks[0][2:3, :])
    src_ends, src_starts = ends_of(marks[0][3:4, :])
    tgt_seg = count(tgt_ends <= place)
    src_seg = count(src_ends <= place)
    src_first = count(src_starts == place)
    self_row = jnp.where(tgt_real > 0.5, tgt_seg, -1.0)
    cross_row = jnp.where((src_real > 0.5) | (src_first > 0.5), src_seg, -1.0)
    rows_f[0:1, :] = tgt_seg
    rows_f[1:2, :] = place
    code_self[...] = jnp.transpose(jnp.broadcast_to(self_row, (128, 1024)))
    code_cross[...] = jnp.transpose(jnp.broadcast_to(cross_row, (128, 1024)))
    key_pos[...] = jnp.transpose(jnp.broadcast_to(place, (128, 1024)))

    landed("x1", b1)
    take({"q": (0,), "k": (1,), "v": (2,)}, b1, qt0, k0, kt0, v0, vt0, "qk")
    attend(qt0, k0, vt0, pt0, l0, ot0, True, a3)
    to_slots("x3", a3, b3)
    gather_2("up")
    gather_2("dn")
    gathered("out")
    landed("x2", b2)
    take({"k": (0,), "v": (1,)}, b2, qt1, k1, kt1, v1, vt1, "k")

    landed("x3", b3)
    words_f = words.astype(F32)
    branch = tn(b3[...].reshape(width, here), matrix(w_out.at[0])) + bias(2)
    h1, scale0 = norm(words_f * omega[0:1, :] + branch, 0, xh0)
    h1_f[...] = h1
    h1_low = h1.astype(BF16)
    by_head(a4, (), nn(h1_low, matrix(w_in.at[1, 0])) + bias(3))
    to_heads("x4", a4, b4)

    landed("x4", b4)
    take({"q": ()}, b4, qt1, k1, kt1, v1, vt1, "q")
    attend(qt1, k1, vt1, pt1, l1, ot1, False, a5)
    to_slots("x5", a5, b5)
    gather_3("up")
    gather_3("dn")

    landed("x5", b5)
    branch = tn(b5[...].reshape(width, here), matrix(w_out.at[1])) + bias(5)
    h2, scale1 = norm(h1_f[...] * omega[1:2, :] + branch, 1, xh1)
    h2_f[...] = h2
    h2_low = h2.astype(BF16)

    gathered("up")
    for k in range(4):
        cols = slice(k * width, (k + 1) * width)
        u = nn(h2_low, matrix(w_up.at[0, :, :, :, :, :, cols])) + up_bias[0:1, cols]
        square = u * u
        t = jnp.tanh(u * (0.7978845608028654 + 0.035677408136300125 * square))
        act[:, cols] = (0.5 * u * (1.0 + t)).astype(BF16)
        inner = 0.7978845608028654 + 0.10703222440890037 * square
        slope[:, cols] = 0.5 * (1.0 + t) + 0.5 * u * (1.0 - t * t) * inner
    gathered("dn")
    branch = bias(6)
    for k in range(4):
        rows = w_dn.at[0, k // 2, pl.ds(2 * (k % 2), 2)]
        branch = branch + nn(act[:, k * width : (k + 1) * width], matrix(rows))
    h3, scale2 = norm(h2_f[...] * omega[2:3, :] + branch, 2, xh2)
    out_res[...] = h3.astype(BF16).reshape(2, 64, width)
    from_plane("res", out_res, o_res)

    landed("cot", in_cot)
    grad = in_cot[...].reshape(here, width).astype(F32)
    dr, skip = norm_back(grad, 2, xh2, scale2, h2_f[...])
    gf = dr.astype(BF16)
    column(6, gf.astype(F32))
    back = skip
    for k in range(4):
        cols = slice(k * width, (k + 1) * width)
        part = act[:, cols]
        put(g_dn.at[0, k // 2, pl.ds(2 * (k % 2), 2)], tn(part, gf))
        gu = nt(gf, matrix(w_dn.at[0, k // 2, pl.ds(2 * (k % 2), 2)])) * slope[:, cols]
        gu = gu.astype(BF16)
        column(7 + k, gu.astype(F32))
        put(g_up.at[0, :, :, :, :, :, cols], tn(h2_low, gu))
        back = back + nt(gu, matrix(w_up.at[0, :, :, :, :, :, cols]))
    scatter_0("dn")
    scatter_0("up")

    dr, skip = norm_back(back, 1, xh1, scale1, h1_f[...])
    gc = dr.astype(BF16)
    column(5, gc.astype(F32))
    by_head(a6, (), nt(gc, matrix(w_out.at[1])))
    to_heads("x6", a6, b6)
    back = skip
    put(g_out.at[1], nn(b5[...].reshape(width, here), gc))
    scatter_1("dn")
    scatter_1("up")

    landed("x6", b6)
    attend_back(b6, qt1, kt1, v1, pt1, l1, ot1, False, a7)
    to_slots("x7", a7, b7)
    scatter_2("dn")
    scatter_2("up")

    landed("x7", b7)
    dq, dk, dv = (b7[:, j].reshape(width, here) for j in range(3))
    dq_row, dv_row = flip(dq), flip(dv)
    column(3, dq_row)
    column(4, dv_row)
    back = back + nt(dq_row.astype(BF16), matrix(w_in.at[1, 0]))
    dr, skip = norm_back(back, 0, xh0, scale0, words_f)
    ga = dr.astype(BF16)
    column(2, ga.astype(F32))
    by_head(a8, (), nt(ga, matrix(w_out.at[0])))
    to_heads("x8", a8, b8)
    back = skip
    put(g_out.at[0], nn(b3[...].reshape(width, here), ga))
    scatter_0("out")
    h1_t = flip(h1_low).astype(BF16)
    put(g_in.at[1, 0], nt(h1_t, dq))
    sources_t = flip(sources).astype(BF16)
    put(g_in.at[1, 1], nt(sources_t, dk))
    put(g_in.at[1, 2], nt(sources_t, dv))
    scatter_0("in1")
    grad_mem = nt(flip(dk).astype(BF16), matrix(w_in.at[1, 1])) + nt(dv_row.astype(BF16), matrix(w_in.at[1, 2]))
    out_mem[...] = grad_mem.astype(BF16).reshape(2, 64, width)
    from_plane("gmem", out_mem, o_mem)
    scatter_3("dn")
    scatter_3("up")
    scatter_1("out")
    scatter_1("in1")

    landed("x8", b8)
    attend_back(b8, qt0, kt0, v0, pt0, l0, ot0, True, a9)
    to_slots("x9", a9, b9)
    scatter_2("out")
    scatter_2("in1")
    scattered("dn")
    scattered("up")

    landed("x9", b9)
    dq, dk, dv = (b9[:, j].reshape(width, here) for j in range(3))
    words_t = flip(words).astype(BF16)
    for j, value in enumerate((dq, dk, dv)):
        put(g_in.at[0, j], nt(words_t, value))
    scatter_0("in0")
    for j, value in enumerate((dq, dk, dv)):
        value = flip(value)
        if j != 1:
            column(j // 2, value)
        back = back + nt(value.astype(BF16), matrix(w_in.at[0, j]))
    out_tok[...] = back.astype(BF16).reshape(2, 64, width)
    from_plane("gtok", out_tok, o_tok)

    send("s0", sg0, sr0, core_next)
    sent_later("s0", sr0)
    scatter_1("in0")
    scatter_3("out")
    landed("s0", sr0)
    sg1[...] = sg0[...] + sr0[...]
    send("s1", sg1, sr1, y_next)
    sent_later("s1", sr1)
    scatter_3("in1")
    landed("s1", sr1)
    sg2[...] = sg1[...] + sr1[...]
    send("s2", sg2, sr2, x_next)
    sent_later("s2", sr2)
    scatter_2("in0")
    landed("s2", sr2)
    sg3[...] = sg2[...] + sr2[...]
    for k in range(3):
        send("s3", sg3, sr3.at[2 - k], (c, at(z_peers[k], y, x)))
    sent_later("s3", sr3)
    scatter_3("in0")
    scattered("out")
    scattered("in1")
    landed("s3", sr3)
    sg0_total = sg3[...] + sr3[0] + sr3[1] + sr3[2]
    sg4[...] = sg0_total
    block = c * 16 + seq
    tile = sg4[:, pl.ds(pl.multiple_of((block // 8) * 128, 128), 128)]
    turned = pltpu.roll(tile, lax.rem(128 - lax.rem(block, 8) * 16, 128), 1)
    o_bias[...] = turned[0:7, 0:16]
    o_gain[...] = turned[11:14, 0:16]
    o_shift[...] = turned[14:17, 0:16]
    o_omega[...] = turned[17:20, 0:16]
    tile = sg4[:, pl.ds(pl.multiple_of((lax.rem(block, 8) // 2) * 128, 128), 128)]
    turned = pltpu.roll(tile, lax.rem(block, 2) * 64, 1)
    wanted = block // 8
    row = jnp.zeros((1, 64), F32)
    for k in range(4):
        row = row + turned[7 + k : 8 + k, 0:64] * (wanted == k).astype(F32)
    o_upb[...] = row
    scattered("in0")

    landed("res", o_res)
    landed("gmem", o_mem)
    landed("gtok", o_tok)
    for entry in pending:
        if len(entry) == 2:
            wait(ss.at[sem(entry[0])], entry[1])
        else:

            @pl.when(entry[2])
            def _():
                wait(ss.at[sem(entry[0])], entry[1])

    assert len(names) <= ss.shape[0], len(names)


def fused_local(
    tokens, memory, cotangent, tgt_lengths, src_lengths, tgt_mask, src_mask, attn_in, attn_out, w_up, w_down,
    biases, up_bias, norm_gain, norm_shift, omega,
):
    tgt_row = jnp.transpose(tgt_mask, (0, 2, 1))
    src_row = jnp.transpose(src_mask, (0, 2, 1))
    meta = jnp.concatenate(
        [
            jnp.concatenate([tgt_row, tgt_row], axis=2),
            jnp.concatenate([src_row, src_row], axis=2),
            jnp.pad(tgt_lengths, ((0, 0), (0, 0), (0, 96))),
            jnp.pad(src_lengths, ((0, 0), (0, 0), (0, 96))),
            jnp.zeros((2, 4, 128), jnp.int32),
        ],
        axis=1,
    )
    any_space = pl.BlockSpec(memory_space=pl.ANY)
    vmem = pl.BlockSpec(memory_space=pltpu.VMEM)
    lines = (CORES, PLANES, YS, XS)
    leads = {"in": (2, 3), "out": (2,), "up": (1,), "dn": (1,)}
    shards = {"in": (16, 512), "out": (16, 512), "up": (16, 2048), "dn": (64, 512)}
    kinds = tuple(leads)

    def half(shape):
        return shape[:-1] + (shape[-1] // 2,)

    def split_lead(lead, extra):
        return lead[:-1] + extra + lead[-1:]

    def low(shape):
        return pltpu.VMEM(shape, BF16)

    full = [low(leads[k] + lines + shards[k]) for k in kinds]
    across = [low(leads[k] + lines[1:] + shards[k]) for k in kinds]
    part = [low(split_lead(leads[k], (2,)) + (PLANES, 2) + half(shards[k])) for k in kinds]
    piece = [low(split_lead(leads[k], (2,)) + (PLANES,) + half(shards[k])) for k in kinds]
    line = [low(split_lead(leads[k], (3,)) + shards[k]) for k in kinds]
    local_rows = low((2, 64, 512))
    one = low((GROUP, 64, 128))
    many = lambda n: low((GROUP, n, 64, 128))
    small = pltpu.VMEM((24, 512), F32)
    attn = [low((64, 1024))] * 3 + [low((1024, 64))] * 2 + [low((1024, 1024))]
    attn += [pltpu.VMEM((1, 1024), F32), pltpu.VMEM((64, 1024), F32)]
    wide = pltpu.VMEM((128, 512), F32)
    scratch = full + full + across + part + piece + line
    scratch += [local_rows] * 3 + [pltpu.VMEM((2, 8, 128), jnp.int32), pltpu.VMEM((GROUP, 8, 128), jnp.int32)]
    for n in (3, 2, 1, 1, 1, 1, 3, 1, 3):
        scratch += [one if n == 1 else many(n)] * 2
    scratch += [local_rows] * 3
    scratch += [small] * 8 + [pltpu.VMEM((3, 24, 512), F32)]
    scratch += [pltpu.VMEM((1024, 128), F32)] * 3 + [pltpu.VMEM((8, 1024), F32)]
    scratch += attn + attn
    scratch += [low((64, 1024))] + [pltpu.VMEM((64, 1024), F32)] * 3
    scratch += [low((128, 2048)), pltpu.VMEM((128, 2048), F32)] + [wide] * 5
    scratch += [pltpu.SemaphoreType.DMA((96,)), pltpu.SemaphoreType.DMA((96,))]
    rows = jax.ShapeDtypeStruct((2, 64, 512), BF16)

    def wide_out(*shape):
        return jax.ShapeDtypeStruct(shape, F32)

    outs = pl.pallas_call(
        fused_kernel,
        name="layer",
        out_shape=(
            rows, rows, rows, wide_out(2, 3, 16, 512), wide_out(2, 16, 512), wide_out(1, 16, 2048),
            wide_out(1, 64, 512), wide_out(7, 16), wide_out(1, 64), wide_out(3, 16), wide_out(3, 16), wide_out(3, 16),
        ),
        in_specs=[any_space] * 3 + [any_space] + [any_space] * 4 + [vmem] * 5,
        out_specs=(any_space,) * 3 + (vmem,) * 9,
        scratch_shapes=scratch,
        compiler_params=pltpu.CompilerParams(collective_id=0, has_side_effects=True, vmem_limit_bytes=60 * 1024 * 1024),
    )(
        tokens.reshape(2, 64, 512), memory.reshape(2, 64, 512), cotangent.reshape(2, 64, 512), meta,
        attn_in, attn_out, w_up.reshape(1, 16, 2048), w_down.reshape(1, 64, 512),
        biases, up_bias.reshape(1, 2048), norm_gain, norm_shift, omega,
    )
    shaped = [out.reshape(2, 64, 1, 512) for out in outs[:3]]
    return (
        *shaped, outs[3], outs[4], outs[5].reshape(16, 2048), outs[6].reshape(64, 512), outs[7], outs[8].reshape(64),
        outs[9], outs[10], outs[11],
    )


def solution(mesh):
    if mesh.shape["seq"] != PLANES * YS * XS or mesh.shape["rows"] != CORES:
        return general(mesh)
    return over(mesh, fused_local)
```

```python
import functools
import math

import jax
import jax.numpy as jnp
from jax import lax
from jax.experimental import pallas as pl
from jax.experimental.pallas import tpu as pltpu
from jax.sharding import PartitionSpec as P

HEADS = 8


def norm_block(branch, skip, scale, gain, shift):
    mixed = skip * scale + branch
    centered = mixed - jnp.mean(mixed, axis=-1, keepdims=True)
    variance = jnp.mean(centered * centered, axis=-1, keepdims=True)
    return centered * lax.rsqrt(variance + 1e-05) * gain + shift


def project(values, matrix):
    return jnp.einsum("trd,de->tre", values, matrix, preferred_element_type=jnp.float32)


def project_back(grads, matrix):
    return jnp.einsum("tre,de->trd", grads, matrix, preferred_element_type=jnp.float32)


def matrix_grad(values, grads):
    return jnp.einsum("trd,tre->de", values, grads, preferred_element_type=jnp.float32)


def column_sum(grads):
    return jnp.sum(grads.astype(jnp.float32), axis=(0, 1))


def segment_of(positions, ends):
    return jnp.sum((ends[None, :, :] <= positions[:, None, None]).astype(jnp.int32), axis=-1)


def segment_bounds(first, last, ends):
    lowest = jnp.sum((ends <= first).astype(jnp.int32), axis=-1)
    highest = jnp.sum((ends <= last).astype(jnp.int32), axis=-1)
    return (lowest, highest)


def ranges_share(query_bounds, key_bounds):
    return jnp.any((key_bounds[0] <= query_bounds[1]) & (key_bounds[1] >= query_bounds[0]))


def key_status(positions, real_marks, ends, starts, causal):
    segments = segment_of(positions, ends)
    usable = real_marks > 0.5
    if not causal:
        usable = usable | jnp.any(starts[None, :, :] == positions[:, None, None], axis=-1)
    return (segments, usable)


def permitted(query_pos, query_seg, key_pos, key_seg, usable, causal):
    same = jnp.transpose(query_seg)[:, :, None] == jnp.transpose(key_seg)[:, None, :]
    usable_keys = jnp.transpose(usable)[:, None, :]
    if causal:
        before = (key_pos[None, :] <= query_pos[:, None])[None]
        itself = (key_pos[None, :] == query_pos[:, None])[None]
        return same & before & (usable_keys | itself)
    return same & usable_keys


def block_grads(query_heads, grad_heads, lambdas, key_heads, value_heads, permit):
    scores = (
        jnp.einsum("arhd,brhd->rhab", query_heads, key_heads, preferred_element_type=jnp.float32)
        * 0.125
    )
    weights = jnp.where(permit[:, None], jnp.exp(scores), 0.0)
    spread = jnp.einsum(
        "arhd,brhd->rhab", grad_heads, value_heads, preferred_element_type=jnp.float32
    )
    slopes = weights * (spread + jnp.transpose(lambdas, (1, 2, 0))[..., None])
    return (weights.astype(jnp.bfloat16), slopes.astype(jnp.bfloat16))


def local(
    tokens,
    memory,
    cotangent,
    tgt_lengths,
    src_lengths,
    tgt_mask,
    src_mask,
    attn_in,
    attn_out,
    w_up,
    w_down,
    biases,
    up_bias,
    norm_gain,
    norm_shift,
    omega,
):
    micro_count, tokens_here, rows_here, width = tokens.shape
    head_size = width // HEADS
    my_pos = lax.axis_index("seq") * tokens_here + jnp.arange(tokens_here, dtype=jnp.int32)
    my_first = my_pos[0]
    my_last = my_pos[tokens_here - 1]

    def split_heads(values):
        return values.reshape(values.shape[0], rows_here, HEADS, head_size)

    def zero_heads():
        return jnp.zeros((tokens_here, rows_here, HEADS, head_size), jnp.float32)

    results = []
    grads_words = []
    grads_sources = []
    shares_all = None
    for micro_index in range(micro_count):
        in_weights = lax.all_gather(attn_in, ("rows", "seq"), axis=2, tiled=True)
        out_weights = lax.all_gather(attn_out, ("rows", "seq"), axis=1, tiled=True)
        up_weights = lax.all_gather(w_up, ("rows", "seq"), axis=0, tiled=True)
        down_weights = lax.all_gather(w_down, ("rows", "seq"), axis=0, tiled=True)
        words = tokens[micro_index]
        sources = memory[micro_index]
        words_full = words.astype(jnp.float32)
        tgt_len = tgt_lengths[micro_index]
        src_len = src_lengths[micro_index]
        tgt_ends = jnp.cumsum(tgt_len, axis=-1)
        src_ends = jnp.cumsum(src_len, axis=-1)
        src_starts = src_ends - src_len
        query_seg = segment_of(my_pos, tgt_ends)
        query_bounds = segment_bounds(my_first, my_last, tgt_ends)
        tgt_real = tgt_mask[micro_index].astype(jnp.bfloat16)
        src_real = src_mask[micro_index].astype(jnp.bfloat16)

        def attend(queries, keys, values, real_marks, ends, starts, causal):
            full_keys, full_values, full_real = (
                lax.all_gather(keys, "seq", axis=0, tiled=True),
                lax.all_gather(values, "seq", axis=0, tiled=True),
                lax.all_gather(real_marks, "seq", axis=0, tiled=True),
            )
            length = full_keys.shape[0]
            block = math.gcd(length, 512)
            query_heads = split_heads(queries)

            def step(carry, block_index):
                begin = block_index * block
                shares = ranges_share(query_bounds, segment_bounds(begin, begin + block - 1, ends))

                def step_compute(state):
                    totals, accum = state
                    key_heads = split_heads(lax.dynamic_slice_in_dim(full_keys, begin, block, 0))
                    value_heads = split_heads(
                        lax.dynamic_slice_in_dim(full_values, begin, block, 0)
                    )
                    key_pos = begin + jnp.arange(block, dtype=jnp.int32)
                    key_seg, usable = key_status(
                        key_pos,
                        lax.dynamic_slice_in_dim(full_real, begin, block, 0),
                        ends,
                        starts,
                        causal,
                    )
                    permit = permitted(my_pos, query_seg, key_pos, key_seg, usable, causal)
                    scores = (
                        jnp.einsum(
                            "trhd,krhd->rhtk",
                            query_heads,
                            key_heads,
                            preferred_element_type=jnp.float32,
                        )
                        * 0.125
                    )
                    weights = jnp.where(permit[:, None], jnp.exp(scores), 0.0)
                    totals = totals + jnp.sum(weights, axis=-1)
                    accum = accum + jnp.einsum(
                        "rhtk,krhd->trhd",
                        weights.astype(jnp.bfloat16),
                        value_heads,
                        preferred_element_type=jnp.float32,
                    )
                    return (totals, accum)

                return (lax.cond(shares, step_compute, lambda unchanged: unchanged, carry), None)

            start_carry = (jnp.zeros((rows_here, HEADS, tokens_here), jnp.float32), zero_heads())
            (totals, accum), unused = lax.scan(
                step, start_carry, jnp.arange(length // block, dtype=jnp.int32)
            )
            sums = jnp.transpose(totals, (2, 0, 1))
            output = (accum / sums[..., None]).reshape(tokens_here, rows_here, width)
            return (output, sums, (full_keys, full_values, full_real))

        def attention_back(
            grad_out,
            output,
            sums,
            queries,
            keys,
            values,
            real_marks,
            gathered_set,
            ends,
            starts,
            causal,
        ):
            full_keys, full_values, full_real = gathered_set
            grad_heads = split_heads(grad_out)
            lambdas = -jnp.sum(grad_heads * split_heads(output), axis=-1) / sums
            scaled = (grad_heads / sums[..., None]).astype(jnp.bfloat16)
            query_heads = split_heads(queries)
            length = full_keys.shape[0]
            block = math.gcd(length, 512)

            def query_step(accum, block_index):
                begin = block_index * block
                shares = ranges_share(query_bounds, segment_bounds(begin, begin + block - 1, ends))

                def query_compute(state):
                    key_heads = split_heads(lax.dynamic_slice_in_dim(full_keys, begin, block, 0))
                    value_heads = split_heads(
                        lax.dynamic_slice_in_dim(full_values, begin, block, 0)
                    )
                    key_pos = begin + jnp.arange(block, dtype=jnp.int32)
                    key_seg, usable = key_status(
                        key_pos,
                        lax.dynamic_slice_in_dim(full_real, begin, block, 0),
                        ends,
                        starts,
                        causal,
                    )
                    permit = permitted(my_pos, query_seg, key_pos, key_seg, usable, causal)
                    weights, slopes = block_grads(
                        query_heads, scaled, lambdas, key_heads, value_heads, permit
                    )
                    return (
                        state
                        + jnp.einsum(
                            "rhab,brhd->arhd", slopes, key_heads, preferred_element_type=jnp.float32
                        )
                        * 0.125
                    )

                return (lax.cond(shares, query_compute, lambda unchanged: unchanged, accum), None)

            grad_query, unused = lax.scan(
                query_step, zero_heads(), jnp.arange(length // block, dtype=jnp.int32)
            )
            all_lambdas = lax.all_gather(lambdas, "seq", axis=0, tiled=True)
            local_seg, local_usable = key_status(my_pos, real_marks, ends, starts, causal)
            local_bounds = segment_bounds(my_first, my_last, ends)
            local_keys = split_heads(keys)
            local_values = split_heads(values)
            query_piece = lax.all_gather(queries, "seq", axis=0, tiled=True)
            scaled_piece = lax.all_gather(
                scaled.reshape(tokens_here, rows_here, width), "seq", axis=0, tiled=True
            )
            size = query_piece.shape[0]
            inner = math.gcd(size, 512)

            def inner_step(inner_carry, inner_index):
                offset = inner_index * inner
                piece_first = offset
                shares = ranges_share(
                    segment_bounds(piece_first, piece_first + inner - 1, tgt_ends), local_bounds
                )

                def inner_compute(state):
                    acc_key, acc_value = state
                    query_blk = split_heads(lax.dynamic_slice_in_dim(query_piece, offset, inner, 0))
                    scaled_blk = split_heads(
                        lax.dynamic_slice_in_dim(scaled_piece, offset, inner, 0)
                    )
                    lambda_blk = lax.dynamic_slice_in_dim(all_lambdas, piece_first, inner, 0)
                    query_pos = piece_first + jnp.arange(inner, dtype=jnp.int32)
                    permit = permitted(
                        query_pos,
                        segment_of(query_pos, tgt_ends),
                        my_pos,
                        local_seg,
                        local_usable,
                        causal,
                    )
                    weights, slopes = block_grads(
                        query_blk, scaled_blk, lambda_blk, local_keys, local_values, permit
                    )
                    acc_key = (
                        acc_key
                        + jnp.einsum(
                            "rhab,arhd->brhd", slopes, query_blk, preferred_element_type=jnp.float32
                        )
                        * 0.125
                    )
                    acc_value = acc_value + jnp.einsum(
                        "rhab,arhd->brhd", weights, scaled_blk, preferred_element_type=jnp.float32
                    )
                    return (acc_key, acc_value)

                return (
                    lax.cond(shares, inner_compute, lambda unchanged: unchanged, inner_carry),
                    None,
                )

            folded, unused_inner = lax.scan(
                inner_step, (zero_heads(), zero_heads()), jnp.arange(size // inner, dtype=jnp.int32)
            )
            grad_key, grad_value = folded
            grad_key = grad_key.reshape(tokens_here, rows_here, width)
            grad_value = grad_value.reshape(tokens_here, rows_here, width)
            return (grad_query.reshape(tokens_here, rows_here, width), grad_key, grad_value)

        self_query = (project(words, in_weights[0, 0]) + biases[0]).astype(jnp.bfloat16)
        self_key = project(words, in_weights[0, 1]).astype(jnp.bfloat16)
        self_value = (project(words, in_weights[0, 2]) + biases[1]).astype(jnp.bfloat16)
        heard, heard_sums, self_set = attend(
            self_query, self_key, self_value, tgt_real, tgt_ends, None, True
        )
        heard_low = heard.astype(jnp.bfloat16)
        branch_self = project(heard_low, out_weights[0]) + biases[2]
        hidden_one, pull_one = jax.vjp(
            norm_block, branch_self, words_full, omega[0], norm_gain[0], norm_shift[0]
        )
        hidden_one_low = hidden_one.astype(jnp.bfloat16)
        cross_query = (project(hidden_one_low, in_weights[1, 0]) + biases[3]).astype(jnp.bfloat16)
        cross_key = project(sources, in_weights[1, 1]).astype(jnp.bfloat16)
        cross_value = (project(sources, in_weights[1, 2]) + biases[4]).astype(jnp.bfloat16)
        recalled, recalled_sums, cross_set = attend(
            cross_query, cross_key, cross_value, src_real, src_ends, src_starts, False
        )
        recalled_low = recalled.astype(jnp.bfloat16)
        branch_cross = project(recalled_low, out_weights[1]) + biases[5]
        hidden_two, pull_two = jax.vjp(
            norm_block, branch_cross, hidden_one, omega[1], norm_gain[1], norm_shift[1]
        )
        hidden_two_low = hidden_two.astype(jnp.bfloat16)
        up_pre = project(hidden_two_low, up_weights) + up_bias
        active, pull_active = jax.vjp(jax.nn.gelu, up_pre)
        active_low = active.astype(jnp.bfloat16)
        branch_ffn = project(active_low, down_weights) + biases[6]
        outcome, pull_three = jax.vjp(
            norm_block, branch_ffn, hidden_two, omega[2], norm_gain[2], norm_shift[2]
        )
        grad_result = cotangent[micro_index].astype(jnp.float32)
        grad_ffn, grad_two, omega_three, gain_three, shift_three = pull_three(grad_result)
        grad_ffn_low = grad_ffn.astype(jnp.bfloat16)
        grad_down = matrix_grad(active_low, grad_ffn_low)
        bias_ffn = column_sum(grad_ffn_low)
        grad_up_pre = pull_active(project_back(grad_ffn_low, down_weights))[0].astype(jnp.bfloat16)
        grad_up = matrix_grad(hidden_two_low, grad_up_pre)
        bias_up = column_sum(grad_up_pre)
        grad_two = grad_two + project_back(grad_up_pre, up_weights)
        grad_cross, grad_one, omega_two, gain_two, shift_two = pull_two(grad_two)
        grad_cross_low = grad_cross.astype(jnp.bfloat16)
        grad_out_cross = matrix_grad(recalled_low, grad_cross_low)
        bias_out_cross = column_sum(grad_cross_low)
        grad_recalled = project_back(grad_cross_low, out_weights[1])
        cross_gq, cross_gk, cross_gv = attention_back(
            grad_recalled,
            recalled,
            recalled_sums,
            cross_query,
            cross_key,
            cross_value,
            src_real,
            cross_set,
            src_ends,
            src_starts,
            False,
        )
        cross_gq = cross_gq.astype(jnp.bfloat16)
        cross_gk = cross_gk.astype(jnp.bfloat16)
        cross_gv = cross_gv.astype(jnp.bfloat16)
        grad_cross_query = matrix_grad(hidden_one_low, cross_gq)
        grad_cross_key = matrix_grad(sources, cross_gk)
        grad_cross_value = matrix_grad(sources, cross_gv)
        grad_one = grad_one + project_back(cross_gq, in_weights[1, 0])
        grad_sources = project_back(cross_gk, in_weights[1, 1]) + project_back(
            cross_gv, in_weights[1, 2]
        )
        grad_self, grad_words, omega_one, gain_one, shift_one = pull_one(grad_one)
        grad_self_low = grad_self.astype(jnp.bfloat16)
        grad_out_self = matrix_grad(heard_low, grad_self_low)
        bias_out_self = column_sum(grad_self_low)
        grad_heard = project_back(grad_self_low, out_weights[0])
        self_gq, self_gk, self_gv = attention_back(
            grad_heard,
            heard,
            heard_sums,
            self_query,
            self_key,
            self_value,
            tgt_real,
            self_set,
            tgt_ends,
            None,
            True,
        )
        self_gq = self_gq.astype(jnp.bfloat16)
        self_gk = self_gk.astype(jnp.bfloat16)
        self_gv = self_gv.astype(jnp.bfloat16)
        grad_words = (
            grad_words
            + project_back(self_gq, in_weights[0, 0])
            + project_back(self_gk, in_weights[0, 1])
            + project_back(self_gv, in_weights[0, 2])
        )
        grad_in = jnp.stack(
            [
                jnp.stack(
                    [
                        matrix_grad(words, self_gq),
                        matrix_grad(words, self_gk),
                        matrix_grad(words, self_gv),
                    ]
                ),
                jnp.stack([grad_cross_query, grad_cross_key, grad_cross_value]),
            ]
        )
        grad_out = jnp.stack([grad_out_self, grad_out_cross])
        grad_bias = jnp.stack(
            [
                column_sum(self_gq),
                column_sum(self_gv),
                bias_out_self,
                column_sum(cross_gq),
                column_sum(cross_gv),
                bias_out_cross,
                bias_ffn,
            ]
        )
        grad_gain = jnp.stack([gain_one, gain_two, gain_three])
        grad_shift = jnp.stack([shift_one, shift_two, shift_three])
        grad_omega = jnp.stack([omega_one, omega_two, omega_three])
        grads = (
            grad_in,
            grad_out,
            grad_up,
            grad_down,
            grad_bias,
            bias_up,
            grad_gain,
            grad_shift,
            grad_omega,
        )
        outcome, grad_words, grad_sources, grads = (
            outcome.astype(jnp.bfloat16),
            grad_words.astype(jnp.bfloat16),
            grad_sources.astype(jnp.bfloat16),
            grads,
        )
        results.append(outcome)
        grads_words.append(grad_words)
        grads_sources.append(grad_sources)
        part_shares = (
            lax.psum_scatter(grads[0], ("rows", "seq"), scatter_dimension=2, tiled=True),
            lax.psum_scatter(grads[1], ("rows", "seq"), scatter_dimension=1, tiled=True),
            lax.psum_scatter(grads[2], ("rows", "seq"), scatter_dimension=0, tiled=True),
            lax.psum_scatter(grads[3], ("rows", "seq"), scatter_dimension=0, tiled=True),
            lax.psum_scatter(grads[4], ("rows", "seq"), scatter_dimension=1, tiled=True),
            lax.psum_scatter(grads[5], ("rows", "seq"), scatter_dimension=0, tiled=True),
            lax.psum_scatter(grads[6], ("rows", "seq"), scatter_dimension=1, tiled=True),
            lax.psum_scatter(grads[7], ("rows", "seq"), scatter_dimension=1, tiled=True),
            lax.psum_scatter(grads[8], ("rows", "seq"), scatter_dimension=1, tiled=True),
        )
        shares_all = (
            part_shares if shares_all is None else jax.tree.map(jnp.add, shares_all, part_shares)
        )
    return (jnp.stack(results), jnp.stack(grads_words), jnp.stack(grads_sources)) + tuple(
        shares_all
    )


def over(mesh, function):
    return jax.shard_map(
        function,
        mesh=mesh,
        in_specs=(
            P(None, "seq", "rows", None),
            P(None, "seq", "rows", None),
            P(None, "seq", "rows", None),
            P(None, "rows", None),
            P(None, "rows", None),
            P(None, "seq", "rows"),
            P(None, "seq", "rows"),
            P(None, None, ("rows", "seq"), None),
            P(None, ("rows", "seq"), None),
            P(("rows", "seq"), None),
            P(("rows", "seq"), None),
            P(),
            P(),
            P(),
            P(),
            P(),
        ),
        out_specs=(
            P(None, "seq", "rows", None),
            P(None, "seq", "rows", None),
            P(None, "seq", "rows", None),
            P(None, None, ("rows", "seq"), None),
            P(None, ("rows", "seq"), None),
            P(("rows", "seq"), None),
            P(("rows", "seq"), None),
            P(None, ("rows", "seq")),
            P(("rows", "seq")),
            P(None, ("rows", "seq")),
            P(None, ("rows", "seq")),
            P(None, ("rows", "seq")),
        ),
        check_vma=False,
    )


def general(mesh):
    return over(mesh, local)


MESH = pl.DeviceIdType.MESH
F32 = jnp.float32
BF16 = jnp.bfloat16
PLANES, YS, XS, CORES = 4, 2, 2, 2
GROUP = YS * XS * CORES


def nn(left, right):
    return lax.dot_general(left, right, (((1,), (0,)), ((), ())), preferred_element_type=F32)


def nt(left, right):
    return lax.dot_general(left, right, (((1,), (1,)), ((), ())), preferred_element_type=F32)


def tn(left, right):
    return lax.dot_general(left, right, (((0,), (0,)), ((), ())), preferred_element_type=F32)


def flip(value):
    return jnp.transpose(value.astype(F32))


def fused_kernel(
    tok, mem, cot, tgt_len, src_len, tgt_msk, src_msk, s_in, s_out, s_up, s_dn, biases, up_bias, gain, shift, omega,
    o_res, o_tok, o_mem, o_in, o_out, o_up, o_dn, o_bias, o_upb, o_gain, o_shift, o_omega,
    w_q, w_out, w_up, w_dn, g_q, g_out, g_up, g_dn,
    c_q, c_out, c_up, c_dn,
    p_q, p_out, p_up, p_dn,
    q_q, q_out, q_up, q_dn,
    z_q, z_out, z_up, z_dn,
    ws0, ws1, gs0, gs1, cs0, cs1, zs0, zs1, fs0, fs1,
    all_tok, all_mem, in_cot, raw_tl, raw_sl, raw_tm, raw_sm, meta, in_meta, all_meta,
    dx0, dx1, dc0, dc1, dp0, dp1,
    a3, b3, a4, b4, a5, b5, a6, b6, a7, b7, a8, b8,
    out_res, out_tok, out_mem,
    sg0, sg1, sg2, sg3, sg4, sr0, sr1, sr2, sr3,
    code_self, code_cross, key_pos, rows_f,
    qt0, kt0, vt0, k0, v0, pt0, l0, ot0,
    qt1, kt1, vt1, k1, v1, pt1, l1, ot1,
    dnt, acc_k, acc_v, acc_q,
    act, slope, gul, xh0, xh1, xh2, h1_f, h2_f,
    wt, bias_cols, wz, dt0, dt1, col_sums,
    ss, rs,
):
    c = lax.axis_index("rows")
    seq = lax.axis_index("seq")
    z = seq // (YS * XS)
    yx = lax.rem(seq, YS * XS)
    y = yx // XS
    x = lax.rem(yx, XS)
    width = 512
    here = 2 * 64

    def at(zz, yy, xx):
        return zz * (YS * XS) + yy * XS + xx

    def slot(cc, yy, xx):
        return cc * 4 + yy * 2 + xx

    def head(cc, yy, xx):
        return (yy * 2 + xx) * 2 + cc

    me_slot, me_head = slot(c, y, x), head(c, y, x)
    plane_peers = []
    for k in range(1, GROUP):
        cc = 1 - c if k & 4 else c
        yy = 1 - y if k & 2 else y
        xx = 1 - x if k & 1 else x
        plane_peers.append((cc, yy, xx))
    trio = [(1 - y, x), (y, 1 - x), (1 - y, 1 - x)]
    z_peers = [lax.rem(z + k, PLANES) for k in (1, 2, 3)]

    names = {}
    pending = []

    def sem(name):
        return names.setdefault(name, len(names))

    def wait(semaphore, ref):
        pltpu.make_async_copy(ref, ref, semaphore).wait()

    def send(name, src, dst, device):
        i = sem(name)
        pltpu.make_async_remote_copy(
            src_ref=src, dst_ref=dst, send_sem=ss.at[i], recv_sem=rs.at[i], device_id=device, device_id_type=MESH
        ).start()

    def keep(name, src, dst):
        pltpu.make_async_copy(src, dst, rs.at[sem(name)]).start()

    def landed(name, ref):
        wait(rs.at[sem(name)], ref)

    def sent_later(name, ref):
        pending.append((name, ref))

    def to_plane(name, src, dst, slotted=False):
        for m in range(2):
            plane = 2 * m + c
            core = z // 2
            half = lax.rem(z, 2)
            own = (plane == z) & (core == c)
            part = dst.at[slot(core, y, x), half] if slotted else dst.at[half]

            @pl.when(own)
            def _():
                keep(name, src.at[m], part)

            @pl.when(jnp.logical_not(own))
            def _():
                i = sem(name)
                j = sem(name + str(m))
                pltpu.make_async_remote_copy(
                    src_ref=src.at[m], dst_ref=part, send_sem=ss.at[j], recv_sem=rs.at[i],
                    device_id=(core, at(plane, y, x)), device_id_type=MESH,
                ).start()

            pending.append((name + str(m), src.at[m], jnp.logical_not(own)))

    def from_plane(name, src, dst):
        micro, core = z // 2, lax.rem(z, 2)
        for half in range(2):
            zz = 2 * c + half
            own = (core == c) & (zz == z)
            part = dst.at[micro]

            @pl.when(own)
            def _():
                keep(name, src.at[half], part)

            @pl.when(jnp.logical_not(own))
            def _():
                i = sem(name)
                j = sem(name + str(half))
                pltpu.make_async_remote_copy(
                    src_ref=src.at[half], dst_ref=part, send_sem=ss.at[j], recv_sem=rs.at[i],
                    device_id=(core, at(zz, y, x)), device_id_type=MESH,
                ).start()

            pending.append((name + str(half), src.at[half], jnp.logical_not(own)))

    def to_heads(name, src, dst):
        keep(name, src.at[me_head], dst.at[me_slot])
        for cc, yy, xx in plane_peers:
            send(name, src.at[head(cc, yy, xx)], dst.at[me_slot], (cc, at(z, yy, xx)))
        sent_later(name, src.at[pl.ds(0, GROUP - 1)])

    def to_slots(name, src, dst):
        keep(name, src.at[me_slot], dst.at[me_head])
        for cc, yy, xx in plane_peers:
            send(name, src.at[slot(cc, yy, xx)], dst.at[me_head], (cc, at(z, yy, xx)))
        sent_later(name, src.at[pl.ds(0, GROUP - 1)])

    weights = {
        "q": (w_q, s_in.at[1, pl.ds(0, 1)], g_q, c_q, p_q, q_q, z_q, o_in.at[1, pl.ds(0, 1)]),
        "out": (w_out, s_out, g_out, c_out, p_out, q_out, z_out, o_out),
        "up": (w_up, s_up, g_up, c_up, p_up, q_up, z_up, o_up),
        "dn": (w_dn, s_dn, g_dn, c_dn, p_dn, q_dn, z_dn, o_dn),
    }

    def halves(ref):
        cols = ref.shape[-1] // 2
        return pl.ds(0, cols), pl.ds(cols, cols)

    x_next, y_next, core_next = (c, at(z, y, 1 - x)), (c, at(z, 1 - y, x)), (1 - c, seq)

    def gather_z(g):
        full, shard = weights[g][:2]
        keep(g + "z", shard, full.at[:, c, z, y, x])
        for zz in z_peers:
            send(g + "z", shard, full.at[:, c, z, y, x], (c, at(zz, y, x)))
        sent_later(g + "z", full.at[:, c, pl.ds(0, 3), y, x])

    def gather_1(g):
        full = weights[g][0]
        first, second = halves(full)
        landed(g + "z", full.at[:, c, :, y, x])
        part = full.at[:, c, :, y, x, :, first]
        send(g + "1a", part, part, x_next)
        sent_later(g + "1a", part)
        part = full.at[:, c, :, y, x, :, second]
        send(g + "1b", part, part, y_next)
        sent_later(g + "1b", part)

    def gather_2(g):
        full = weights[g][0]
        first, second = halves(full)
        landed(g + "1a", full.at[:, c, :, y, 1 - x, :, first])
        part = full.at[:, c, :, y, :, :, first]
        send(g + "2a", part, part, y_next)
        sent_later(g + "2a", part)
        landed(g + "1b", full.at[:, c, :, 1 - y, x, :, second])
        part = full.at[:, c, :, :, x, :, second]
        send(g + "2b", part, part, x_next)
        sent_later(g + "2b", part)

    def gather_3(g):
        full = weights[g][0]
        first, second = halves(full)
        landed(g + "2a", full.at[:, c, :, 1 - y, :, :, first])
        landed(g + "2b", full.at[:, c, :, :, 1 - x, :, second])
        send(g + "3", full.at[:, c], full.at[:, c], core_next)
        sent_later(g + "3", full.at[:, c])

    def gathered(g):
        landed(g + "3", weights[g][0].at[:, 1 - c])

    def add(target, other):
        target[...] = (target[...].astype(F32) + other[...].astype(F32)).astype(BF16)

    def scatter_0(g):
        grad, across = weights[g][2:4]
        send(g + "r0", grad.at[:, 1 - c], across, core_next)
        sent_later(g + "r0", across)

    def scatter_1(g):
        grad, across, part = weights[g][2:5]
        first, second = halves(grad)
        landed(g + "r0", across)
        for lead in range(grad.shape[0]):

            @pl.loop(0, PLANES)
            def _(zz):
                add(grad.at[lead, c, zz], across.at[lead, zz])

        send(g + "r1a", grad.at[:, c, :, 1 - y, :, :, first], part.at[0], y_next)
        sent_later(g + "r1a", part.at[0])
        send(g + "r1b", grad.at[:, c, :, :, 1 - x, :, second], part.at[1], x_next)
        sent_later(g + "r1b", part.at[1])

    def scatter_2(g):
        grad, _, part, piece = weights[g][2:6]
        first, second = halves(grad)
        landed(g + "r1a", part.at[0])
        landed(g + "r1b", part.at[1])
        for lead in range(grad.shape[0]):

            @pl.loop(0, PLANES)
            def _(zz):
                add(grad.at[lead, c, zz, y, :, :, first], part.at[0, lead, zz])
                add(grad.at[lead, c, zz, :, x, :, second], part.at[1, lead, zz])

        send(g + "r2a", grad.at[:, c, :, y, 1 - x, :, first], piece.at[0], x_next)
        sent_later(g + "r2a", piece.at[0])
        send(g + "r2b", grad.at[:, c, :, 1 - y, x, :, second], piece.at[1], y_next)
        sent_later(g + "r2b", piece.at[1])

    def scatter_3(g):
        grad, _, _, piece, line = weights[g][2:7]
        first, second = halves(grad)
        landed(g + "r2a", piece.at[0])
        landed(g + "r2b", piece.at[1])
        for lead in range(grad.shape[0]):

            @pl.loop(0, PLANES)
            def _(zz):
                add(grad.at[lead, c, zz, y, x, :, first], piece.at[0, lead, zz])
                add(grad.at[lead, c, zz, y, x, :, second], piece.at[1, lead, zz])

        for k in range(3):
            send(g + "r3", grad.at[:, c, z_peers[k], y, x], line.at[2 - k], (c, at(z_peers[k], y, x)))
        sent_later(g + "r3", line)

    def scattered(g):
        grad, _, _, _, line, result = weights[g][2:8]
        landed(g + "r3", line)
        total = grad[:, c, z, y, x].astype(F32)
        for k in range(3):
            total = total + line[k].astype(F32)
        result[...] = total

    def spread_1(name, full):
        own = full.at[me_slot]
        for yy, xx in trio:
            send(name + "p", own, own, (c, at(z, yy, xx)))
        sent_later(name + "p", full.at[pl.ds(0, 3)])
        send(name + "c", own, own, core_next)
        sent_later(name + "c", own)

    def spread_2(name, full):
        landed(name + "p", full.at[pl.ds(0, 3)])
        for yy, xx in trio:
            part = full.at[slot(c, yy, xx)]
            send(name + "d", part, part, core_next)
        sent_later(name + "d", full.at[pl.ds(0, 3)])

    def spread_3(name, full):
        landed(name + "c", full.at[0])
        landed(name + "d", full.at[pl.ds(0, 3)])

    def merge_0(name, full, across):
        send(name + "c", full.at[pl.ds((1 - c) * 4, 4)], across, core_next)
        sent_later(name + "c", across)

    def merge_1(name, full, across, parts):
        landed(name + "c", across)

        @pl.loop(0, 4)
        def _(i):
            add(full.at[c * 4 + i], across.at[i])

        for k, (yy, xx) in enumerate(trio):
            send(name + "p", full.at[slot(c, yy, xx)], parts.at[k], (c, at(z, yy, xx)))
        sent_later(name + "p", parts)

    def merge_2(name, full, parts):
        landed(name + "p", parts)
        total = full[me_slot].astype(F32)
        for k in range(3):
            total = total + parts[k].astype(F32)
        return total.reshape(here, width)

    def tile(index):
        return pl.ds(pl.multiple_of(index * 128, 128), 128)

    def slice_1(name, shard, full):
        keep(name + "p", shard.at[:, :, tile(yx)], full.at[:, c, z, yx])
        for yy, xx in trio:
            send(name + "p", shard.at[:, :, tile(yy * 2 + xx)], full.at[:, c, z, yx], (c, at(z, yy, xx)))
        sent_later(name + "p", full.at[:, c, z, pl.ds(0, 3)])

    def slice_2(name, full):
        landed(name + "p", full.at[:, c, z])
        for zz in z_peers:
            send(name + "z", full.at[:, c, z], full.at[:, c, z], (c, at(zz, y, x)))
        sent_later(name + "z", full.at[:, c, pl.ds(0, 3)])

    def slice_3(name, full):
        landed(name + "z", full.at[:, c, pl.ds(0, 3)])
        send(name + "c", full.at[:, c], full.at[:, c], core_next)
        sent_later(name + "c", full.at[:, c])

    def slice_4(name, full):
        landed(name + "c", full.at[:, 1 - c])

    def unslice_0(name, grad, across):
        send(name + "c", grad.at[:, 1 - c], across, core_next)
        sent_later(name + "c", across)

    def unslice_1(name, grad, across, line):
        landed(name + "c", across)
        for lead in range(grad.shape[0]):
            add(grad.at[lead, c], across.at[lead])
        for k in range(3):
            send(name + "z", grad.at[:, c, z_peers[k]], line.at[2 - k], (c, at(z_peers[k], y, x)))
        sent_later(name + "z", line)

    def unslice_2(name, grad, line, total, result):
        landed(name + "z", line)
        value = grad[:, c, z].astype(F32)
        for k in range(3):
            value = value + line[k].astype(F32)
        total[...] = value
        for yy, xx in trio:
            send(name + "p", total.at[:, yy * 2 + xx], result.at[:, :, tile(yx)], (c, at(z, yy, xx)))
        sent_later(name + "p", total.at[:, pl.ds(0, 3)])
        result[:, :, tile(yx)] = total[:, yx]

    def unslice_3(name, result):
        landed(name + "p", result.at[:, :, pl.ds(0, 384)])

    def matrix(ref):
        return ref[...].reshape(-1, ref.shape[-1])

    def put(ref, value):
        ref[...] = value.astype(BF16).reshape(ref.shape)

    def norm(r, i, kept):
        centered = r - jnp.mean(r, axis=1, keepdims=True)
        scale = lax.rsqrt(jnp.mean(centered * centered, axis=1, keepdims=True) + 1e-05)
        xhat = centered * scale
        kept[...] = xhat
        return xhat * gain[i : i + 1, :] + shift[i : i + 1, :], scale

    def column(row, value):
        sg0[row : row + 1, :] = jnp.sum(value, axis=0, keepdims=True)

    def norm_back(grad, i, kept, scale, skip):
        xhat = kept[...]
        column(11 + i, grad * xhat)
        column(14 + i, grad)
        dxhat = grad * gain[i : i + 1, :]
        dr = dxhat - jnp.mean(dxhat, axis=1, keepdims=True)
        dr = (dr - xhat * jnp.mean(dxhat * xhat, axis=1, keepdims=True)) * scale
        column(17 + i, dr * skip)
        return dr, dr * omega[i : i + 1, :]

    BLOCK = 256

    def attend(queries, keys, values_t, weights_t, sums, outputs, causal, target):
        def make(extent):
            def body(b):
                cols = pl.ds(pl.multiple_of(b * BLOCK, BLOCK), BLOCK)
                scores = nn(keys[:extent, :], queries[:, cols])
                seg = rows_f[0:1, cols]
                code = (code_self if causal else code_cross)[:extent, :]
                permit = jnp.concatenate([code, code], axis=1) == seg
                if causal:
                    pos = key_pos[:extent, :]
                    pos = jnp.concatenate([pos, pos], axis=1)
                    mine = rows_f[1:2, cols]
                    permit = (permit & (pos <= mine)) | (pos == mine)
                weight = jnp.where(permit, jnp.exp(scores), 0.0)
                total = jnp.sum(weight, axis=0, keepdims=True)
                low = weight.astype(BF16)
                weights_t[:extent, cols] = low
                out = nn(values_t[:, :extent], low) / total
                sums[0:1, cols] = total
                outputs[:, cols] = out

            return body

        if causal:
            pl.loop(0, 2)(make(512))
            pl.loop(2, 4)(make(1024))
        else:
            pl.loop(0, 4)(make(1024))
        for s in range(GROUP):
            target[s] = outputs[:, s * here : (s + 1) * here].astype(BF16)

    def attend_back(buffer, queries, keys_t, values, weights_t, sums, outputs, causal):
        acc_k[...] = jnp.zeros_like(acc_k)
        acc_v[...] = jnp.zeros_like(acc_v)
        for s in range(GROUP):
            cols = slice(s * here, (s + 1) * here)
            grad = buffer[s].astype(F32)
            inverse = 1.0 / sums[0:1, cols]
            dnt[:, cols] = (grad * inverse).astype(BF16)
            rows_f[2:3, cols] = -jnp.sum(grad * outputs[:, cols], axis=0, keepdims=True) * inverse

        def make(extent):
            def body(b):
                cols = pl.ds(pl.multiple_of(b * BLOCK, BLOCK), BLOCK)
                low = weights_t[:extent, cols]
                dn = dnt[:, cols]
                spread = nn(values[:extent, :], dn)
                slopes = (low.astype(F32) * (spread + rows_f[2:3, cols])).astype(BF16)
                acc_q[:, cols] = nn(keys_t[:, :extent], slopes) * 0.125
                acc_k[:, :extent] += nt(queries[:, cols], slopes)
                acc_v[:, :extent] += nt(dn, low)

            return body

        if causal:
            pl.loop(0, 2)(make(512))
            pl.loop(2, 4)(make(1024))
        else:
            pl.loop(0, 4)(make(1024))
    def by_head(target, value):
        target[...] = flip(value).astype(BF16).reshape(GROUP, 64, here)

    def heads_weights(first, full):
        for j in range(full.shape[0]):
            wt[first + j] = flip(matrix(full.at[j])).astype(BF16)

    own_rows = pl.ds(pl.multiple_of(c * 64, 64), 64)
    own_head = pl.ds(pl.multiple_of(me_head * 64, 64), 64)

    def own_weights(first, count):
        return jnp.concatenate([wt[first + j, own_rows, :] for j in range(count)], axis=0)

    def wide_bias(i):
        col = bias_cols[i, own_head, :]
        return jnp.concatenate([col, col], axis=1)

    def project_heads(rows, first, queries, keys, keys_t, values, values_t):
        count = 2 if queries is None else 3
        own = own_weights(first, count)
        for b in range(4):
            cols = slice(b * 256, (b + 1) * 256)
            out = nt(own, rows[2 * b : 2 * b + 2].reshape(256, width))
            if queries is not None:
                queries[:, cols] = ((out[0:64] + wide_bias(0)).astype(BF16).astype(F32) * 0.125).astype(BF16)
            at_k = 64 * (count - 2)
            block = out[at_k : at_k + 64].astype(BF16)
            keys_t[:, cols] = block
            keys[cols, :] = flip(block).astype(BF16)
            block = (out[at_k + 64 : at_k + 128] + wide_bias(1 if count == 3 else 2)).astype(BF16)
            values_t[:, cols] = block
            values[cols, :] = flip(block).astype(BF16)

    def rows_back(grads_t, first, target, core):
        count = grads_t.shape[0] // 64
        own = own_weights(first, count)
        for b in range(2):
            cols = pl.ds(pl.multiple_of(core * 512 + b * 256, 256), 256)
            out = tn(grads_t[:, cols], own)
            target[pl.ds(core * 4 + b * 2, 2)] = out.astype(BF16).reshape(2, 2, 64, width)

    def slices_back(grads_t, rows, grad):
        count = grads_t.shape[0] // 64
        out = nn(grads_t[...], rows[...].reshape(1024, width))
        wz[...] = jnp.zeros_like(wz)
        for j in range(count):
            wz[j, own_rows, :] = out[j * 64 : (j + 1) * 64]
            put(grad.at[j], jnp.transpose(wz[j]))

    def bias(i):
        return biases[i : i + 1, :]

    raw = ((raw_tm, tgt_msk), (raw_sm, src_msk), (raw_tl, tgt_len), (raw_sl, src_len))
    for i, (ref, given) in enumerate(raw):
        keep("raw" + str(i), given, ref)
    barrier = pltpu.get_barrier_semaphore()
    greet = [(cc, at(z, yy, xx)) for cc, yy, xx in plane_peers]
    greet += [(cc, at(zz, y, x)) for zz in z_peers for cc in (c, 1 - c)]
    for device in greet:
        pl.semaphore_signal(barrier, inc=1, device_id=device, device_id_type=MESH)
    pl.semaphore_wait(barrier, len(greet))

    to_plane("tok", tok, all_tok, True)
    slice_1("w0", s_in.at[0], ws0)
    slice_1("w1", s_in.at[1, pl.ds(1, 2)], ws1)
    for i, (ref, _) in enumerate(raw):
        landed("raw" + str(i), ref)
        span = ref.shape[2]
        for m in range(2):
            for start in (0, 64):
                meta[m, i : i + 1, start : start + span] = ref[m]
    to_plane("meta", meta, in_meta)
    slice_2("w0", ws0)
    gather_z("out")
    to_plane("mem", mem, all_mem, True)
    landed("tok", all_tok.at[me_slot])
    spread_1("x", all_tok)
    slice_2("w1", ws1)
    gather_z("q")
    gather_z("up")
    gather_z("dn")
    to_plane("cot", cot, in_cot)
    landed("meta", in_meta)
    lane = lax.broadcasted_iota(jnp.int32, (8, 128), 1)
    all_meta[me_slot] = jnp.where(lane < 64, in_meta[0], in_meta[1])
    for cc, yy, xx in plane_peers:
        send("marks", all_meta.at[me_slot], all_meta.at[me_slot], (cc, at(z, yy, xx)))
    sent_later("marks", all_meta.at[pl.ds(0, 7)])
    for i, row in enumerate((0, 1, 4)):
        bias_cols[i] = jnp.transpose(jnp.broadcast_to(bias(row), (128, width)))

    landed("marks", all_meta.at[pl.ds(0, 7)])
    order = lax.broadcasted_iota(jnp.int32, (1, 1024), 1)
    place = (order // 512) * 512 + lax.rem(order // 64, 2) * 256 + lax.rem(order // 128, 4) * 64 + lax.rem(order, 64)
    place = place.astype(F32)
    marks = [all_meta[s].astype(F32) for s in range(GROUP)]
    tgt_real = jnp.concatenate([mark[0:1, :] for mark in marks], axis=1)
    src_real = jnp.concatenate([mark[1:2, :] for mark in marks], axis=1)
    lower = lax.broadcasted_iota(jnp.int32, (32, 128), 1)
    later = lax.broadcasted_iota(jnp.int32, (32, 128), 0)

    def ends_of(row):
        lengths = jnp.broadcast_to(row, (32, 128))
        ends = jnp.sum(jnp.where(lower <= later, lengths, 0.0), axis=1, keepdims=True)
        starts = jnp.sum(jnp.where(lower < later, lengths, 0.0), axis=1, keepdims=True)
        return ends, starts

    def count(flags):
        return jnp.sum(jnp.where(flags, 1.0, 0.0), axis=0, keepdims=True)

    tgt_ends, _ = ends_of(marks[0][2:3, :])
    src_ends, src_starts = ends_of(marks[0][3:4, :])
    tgt_seg = count(tgt_ends <= place)
    src_seg = count(src_ends <= place)
    src_first = count(src_starts == place)
    self_row = jnp.where(tgt_real > 0.5, tgt_seg, -1.0)
    cross_row = jnp.where((src_real > 0.5) | (src_first > 0.5), src_seg, -1.0)
    rows_f[0:1, :] = tgt_seg
    rows_f[1:2, :] = place
    code_self[...] = jnp.transpose(jnp.broadcast_to(self_row, (128, 1024)))
    code_cross[...] = jnp.transpose(jnp.broadcast_to(cross_row, (128, 1024)))
    key_pos[...] = jnp.transpose(jnp.broadcast_to(place, (128, 1024)))

    slice_3("w0", ws0)
    gather_1("out")
    spread_2("x", all_tok)
    slice_4("w0", ws0)
    heads_weights(0, ws0)
    landed("mem", all_mem.at[me_slot])
    spread_1("m", all_mem)
    gather_2("out")
    spread_3("x", all_tok)

    project_heads(all_tok, 0, qt0, k0, kt0, v0, vt0)
    attend(qt0, k0, vt0, pt0, l0, ot0, True, a3)
    to_slots("x3", a3, b3)
    gather_3("out")
    slice_3("w1", ws1)
    gather_1("q")
    spread_2("m", all_mem)
    gather_2("q")
    gather_1("up")
    slice_4("w1", ws1)
    heads_weights(3, ws1)
    spread_3("m", all_mem)
    project_heads(all_mem, 3, None, k1, kt1, v1, vt1)
    gather_3("q")
    gathered("out")

    landed("x3", b3)
    words_f = all_tok[me_slot].reshape(here, width).astype(F32)
    branch = tn(b3[...].reshape(width, here), matrix(w_out.at[0])) + bias(2)
    h1, scale0 = norm(words_f * omega[0:1, :] + branch, 0, xh0)
    h1_f[...] = h1
    h1_low = h1.astype(BF16)
    gathered("q")
    by_head(a4, nn(h1_low, matrix(w_q.at[0])) + bias(3))
    to_heads("x4", a4, b4)
    gather_1("dn")
    gather_2("up")

    landed("x4", b4)
    for s in range(GROUP):
        qt1[:, s * here : (s + 1) * here] = (b4[s].astype(F32) * 0.125).astype(BF16)
    attend(qt1, k1, vt1, pt1, l1, ot1, False, a5)
    to_slots("x5", a5, b5)
    gather_2("dn")
    gather_3("up")

    landed("x5", b5)
    branch = tn(b5[...].reshape(width, here), matrix(w_out.at[1])) + bias(5)
    h2, scale1 = norm(h1_f[...] * omega[1:2, :] + branch, 1, xh1)
    h2_f[...] = h2
    h2_low = h2.astype(BF16)
    gather_3("dn")

    gathered("up")
    for k in range(4):
        cols = slice(k * width, (k + 1) * width)
        u = nn(h2_low, matrix(w_up.at[0, :, :, :, :, :, cols])) + up_bias[0:1, cols]
        square = u * u
        t = jnp.tanh(u * (0.7978845608028654 + 0.035677408136300125 * square))
        act[:, cols] = (0.5 * u * (1.0 + t)).astype(BF16)
        inner = 0.7978845608028654 + 0.10703222440890037 * square
        slope[:, cols] = 0.5 * (1.0 + t) + 0.5 * u * (1.0 - t * t) * inner
    gathered("dn")
    branch = bias(6)
    for k in range(4):
        rows = w_dn.at[0, k // 2, pl.ds(2 * (k % 2), 2)]
        branch = branch + nn(act[:, k * width : (k + 1) * width], matrix(rows))
    h3, scale2 = norm(h2_f[...] * omega[2:3, :] + branch, 2, xh2)
    out_res[...] = h3.astype(BF16).reshape(2, 64, width)
    from_plane("res", out_res, o_res)

    landed("cot", in_cot)
    grad = in_cot[...].reshape(here, width).astype(F32)
    dr, skip = norm_back(grad, 2, xh2, scale2, h2_f[...])
    gf = dr.astype(BF16)
    column(6, gf.astype(F32))
    back = skip
    for k in range(4):
        cols = slice(k * width, (k + 1) * width)
        gu = nt(gf, matrix(w_dn.at[0, k // 2, pl.ds(2 * (k % 2), 2)])) * slope[:, cols]
        gu = gu.astype(BF16)
        gul[:, cols] = gu
        column(7 + k, gu.astype(F32))
        back = back + nt(gu, matrix(w_up.at[0, :, :, :, :, :, cols]))

    dr, skip = norm_back(back, 1, xh1, scale1, h1_f[...])
    gc = dr.astype(BF16)
    column(5, gc.astype(F32))
    by_head(a6, nt(gc, matrix(w_out.at[1])))
    to_heads("x6", a6, b6)
    back = skip
    for k in range(4):
        put(g_dn.at[0, k // 2, pl.ds(2 * (k % 2), 2)], tn(act[:, k * width : (k + 1) * width], gf))
    scatter_0("dn")
    for k in range(4):
        cols = slice(k * width, (k + 1) * width)
        put(g_up.at[0, :, :, :, :, :, cols], tn(h2_low, gul[:, cols]))
    scatter_0("up")
    scatter_1("dn")

    landed("x6", b6)
    attend_back(b6, qt1, kt1, v1, pt1, l1, ot1, False)
    for s in range(GROUP):
        a7[s] = acc_q[:, s * here : (s + 1) * here].astype(BF16)
    to_slots("x7", a7, b7)
    scatter_1("up")
    dt1[0:64, :] = acc_k[...].astype(BF16)
    dt1[64:128, :] = acc_v[...].astype(BF16)
    rows_back(dt1, 3, dx1, 1 - c)
    merge_0("dm", dx1, dc1)
    rows_back(dt1, 3, dx1, c)
    slices_back(dt1, all_mem, gs1)
    unslice_0("u1", gs1, cs1)
    col_sums[0] = jnp.broadcast_to(jnp.sum(dt1[64:128, :].astype(F32), axis=1, keepdims=True), (64, 128))
    put(g_out.at[1], nn(b5[...].reshape(width, here), gc))

    landed("x7", b7)
    dq = b7[...].reshape(width, here)
    dq_row = flip(dq)
    column(3, dq_row)
    back = back + nt(dq_row.astype(BF16), matrix(w_q.at[0]))
    dr, skip = norm_back(back, 0, xh0, scale0, words_f)
    ga = dr.astype(BF16)
    column(2, ga.astype(F32))
    by_head(a8, nt(ga, matrix(w_out.at[0])))
    to_heads("x8", a8, b8)
    back = skip
    scatter_2("dn")
    merge_1("dm", dx1, dc1, dp1)
    put(g_out.at[0], nn(b3[...].reshape(width, here), ga))
    scatter_0("out")
    put(g_q.at[0], nt(flip(h1_low).astype(BF16), dq))
    scatter_0("q")
    unslice_1("u1", gs1, cs1, zs1)
    scatter_2("up")
    scatter_3("dn")

    landed("x8", b8)
    attend_back(b8, qt0, kt0, v0, pt0, l0, ot0, True)
    dt0[0:64, :] = acc_q[...].astype(BF16)
    dt0[64:128, :] = acc_k[...].astype(BF16)
    dt0[128:192, :] = acc_v[...].astype(BF16)
    rows_back(dt0, 0, dx0, 1 - c)
    merge_0("dx", dx0, dc0)
    rows_back(dt0, 0, dx0, c)
    merge_1("dx", dx0, dc0, dp0)
    slices_back(dt0, all_tok, gs0)
    unslice_0("u0", gs0, cs0)
    lanes = lax.broadcasted_iota(jnp.int32, (64, 128), 1)
    dq_sum = jnp.sum(dt0[0:64, :].astype(F32), axis=1, keepdims=True)
    dv_sum = jnp.sum(dt0[128:192, :].astype(F32), axis=1, keepdims=True)
    bias_cols[0] = jnp.zeros((width, 128), F32)
    bias_cols[0, own_head, :] = jnp.where(lanes == 0, dq_sum, jnp.where(lanes == 1, dv_sum, col_sums[0]))
    turned = jnp.transpose(bias_cols[0])
    sg0[0:2, :] = turned[0:2, :]
    sg0[4:5, :] = turned[2:3, :]

    send("s0", sg0, sr0, core_next)
    sent_later("s0", sr0)
    scatter_1("out")
    scatter_1("q")
    out_mem[...] = merge_2("dm", dx1, dp1).astype(BF16).reshape(2, 64, width)
    from_plane("gmem", out_mem, o_mem)
    unslice_2("u1", gs1, zs1, fs1, o_in.at[1, pl.ds(1, 2)])
    scatter_3("up")
    unslice_1("u0", gs0, cs0, zs0)
    landed("s0", sr0)
    sg1[...] = sg0[...] + sr0[...]
    send("s1", sg1, sr1, y_next)
    sent_later("s1", sr1)
    scatter_2("out")
    scatter_2("q")
    out_tok[...] = (merge_2("dx", dx0, dp0) + back).astype(BF16).reshape(2, 64, width)
    from_plane("gtok", out_tok, o_tok)
    landed("s1", sr1)
    sg2[...] = sg1[...] + sr1[...]
    send("s2", sg2, sr2, x_next)
    sent_later("s2", sr2)
    scatter_3("out")
    scatter_3("q")
    unslice_2("u0", gs0, zs0, fs0, o_in.at[0])
    scattered("dn")
    scattered("up")
    landed("s2", sr2)
    sg3[...] = sg2[...] + sr2[...]
    for k in range(3):
        send("s3", sg3, sr3.at[2 - k], (c, at(z_peers[k], y, x)))
    sent_later("s3", sr3)
    scattered("out")
    scattered("q")
    unslice_3("u1", o_in.at[1, pl.ds(1, 2)])
    unslice_3("u0", o_in.at[0])
    landed("s3", sr3)
    sg0_total = sg3[...] + sr3[0] + sr3[1] + sr3[2]
    sg4[...] = sg0_total
    block = c * 16 + seq
    tile = sg4[:, pl.ds(pl.multiple_of((block // 8) * 128, 128), 128)]
    turned = pltpu.roll(tile, lax.rem(128 - lax.rem(block, 8) * 16, 128), 1)
    o_bias[...] = turned[0:7, 0:16]
    o_gain[...] = turned[11:14, 0:16]
    o_shift[...] = turned[14:17, 0:16]
    o_omega[...] = turned[17:20, 0:16]
    tile = sg4[:, pl.ds(pl.multiple_of((lax.rem(block, 8) // 2) * 128, 128), 128)]
    turned = pltpu.roll(tile, lax.rem(block, 2) * 64, 1)
    wanted = block // 8
    row = jnp.zeros((1, 64), F32)
    for k in range(4):
        row = row + turned[7 + k : 8 + k, 0:64] * (wanted == k).astype(F32)
    o_upb[...] = row

    landed("res", o_res)
    landed("gmem", o_mem)
    landed("gtok", o_tok)
    for entry in pending:
        if len(entry) == 2:
            wait(ss.at[sem(entry[0])], entry[1])
        else:

            @pl.when(entry[2])
            def _():
                wait(ss.at[sem(entry[0])], entry[1])

    assert len(names) <= ss.shape[0], len(names)


def copy_kernel(*refs):
    count = len(refs) // 2
    for i in range(count):
        refs[count + i][...] = refs[i][...]


def fused_local(
    tokens, memory, cotangent, tgt_lengths, src_lengths, tgt_mask, src_mask, attn_in, attn_out, w_up, w_down,
    biases, up_bias, norm_gain, norm_shift, omega,
):
    any_space = pl.BlockSpec(memory_space=pl.ANY)
    vmem = pl.BlockSpec(memory_space=pltpu.VMEM)
    lines = (CORES, PLANES, YS, XS)
    leads = {"q": 1, "out": 2, "up": 1, "dn": 1}
    shards = {"q": (16, 512), "out": (16, 512), "up": (16, 2048), "dn": (64, 512)}
    kinds = tuple(leads)

    def low(*shape):
        return pltpu.VMEM(shape, BF16)

    def full(*shape):
        return pltpu.VMEM(shape, F32)

    def whole(k):
        return low(leads[k], *lines, *shards[k])

    def halved(k, *middle):
        return low(2, leads[k], *middle, shards[k][0], shards[k][1] // 2)

    scratch = [whole(k) for k in kinds] * 2
    scratch += [low(leads[k], *lines[1:], *shards[k]) for k in kinds]
    scratch += [halved(k, PLANES, 2) for k in kinds] + [halved(k, PLANES) for k in kinds]
    scratch += [low(3, leads[k], *shards[k]) for k in kinds]
    scratch += [low(n, CORES, PLANES, 4, 16, 128) for n in (3, 2)] * 2
    scratch += [low(n, PLANES, 4, 16, 128) for n in (3, 2)] + [low(3, n, 4, 16, 128) for n in (3, 2)]
    scratch += [full(n, 4, 16, 128) for n in (3, 2)]
    local_rows = low(2, 64, 512)
    marks = [pltpu.VMEM((2, 1, n), jnp.int32) for n in (32, 32, 64, 64)] + [pltpu.VMEM((2, 8, 128), jnp.int32)] * 2
    scratch += [low(GROUP, 2, 64, 512)] * 2 + [local_rows] + marks + [pltpu.VMEM((GROUP, 8, 128), jnp.int32)]
    scratch += [low(GROUP, 2, 64, 512)] * 2 + [low(4, 2, 64, 512)] * 2 + [low(3, 2, 64, 512)] * 2
    scratch += [low(GROUP, 64, 128)] * 12 + [local_rows] * 3
    scratch += [full(24, 512)] * 8 + [full(3, 24, 512)]
    scratch += [full(1024, 128)] * 3 + [full(8, 1024)]
    scratch += ([low(64, 1024)] * 3 + [low(1024, 64)] * 2 + [low(1024, 1024), full(1, 1024), full(64, 1024)]) * 2
    scratch += [low(64, 1024)] + [full(64, 1024)] * 3
    scratch += [low(128, 2048), full(128, 2048), low(128, 2048)] + [full(128, 512)] * 5
    scratch += [low(5, 128, 512), full(3, 512, 128), full(3, 128, 512), low(192, 1024), low(128, 1024), full(1, 64, 128)]
    scratch += [pltpu.SemaphoreType.DMA((128,)), pltpu.SemaphoreType.DMA((128,))]
    rows = jax.ShapeDtypeStruct((2, 64, 512), BF16)

    def wide_out(*shape):
        return jax.ShapeDtypeStruct(shape, F32)

    outs = pl.pallas_call(
        fused_kernel,
        name="layer",
        out_shape=(
            rows, rows, rows, wide_out(2, 3, 16, 512), wide_out(2, 16, 512), wide_out(1, 16, 2048),
            wide_out(1, 64, 512), wide_out(7, 16), wide_out(1, 64), wide_out(3, 16), wide_out(3, 16), wide_out(3, 16),
        ),
        in_specs=[any_space] * 11 + [vmem] * 5,
        out_specs=(any_space,) * 3 + (vmem,) * 9,
        scratch_shapes=scratch,
        compiler_params=pltpu.CompilerParams(collective_id=0, has_side_effects=True, vmem_limit_bytes=60 * 1024 * 1024),
    )(
        tokens.reshape(2, 64, 512), memory.reshape(2, 64, 512), cotangent.reshape(2, 64, 512),
        tgt_lengths, src_lengths, jnp.transpose(tgt_mask, (0, 2, 1)), jnp.transpose(src_mask, (0, 2, 1)),
        attn_in, attn_out, w_up.reshape(1, 16, 2048), w_down.reshape(1, 64, 512),
        biases, up_bias.reshape(1, 2048), norm_gain, norm_shift, omega,
    )
    outs = pl.pallas_call(
        copy_kernel,
        name="hand_over",
        out_shape=tuple(jax.ShapeDtypeStruct(out.shape, out.dtype) for out in outs),
        in_specs=[vmem] * len(outs),
        out_specs=(vmem,) * len(outs),
    )(*outs)
    shaped = [out.reshape(2, 64, 1, 512) for out in outs[:3]]
    return (
        *shaped, outs[3], outs[4], outs[5].reshape(16, 2048), outs[6].reshape(64, 512), outs[7], outs[8].reshape(64),
        outs[9], outs[10], outs[11],
    )


def solution(mesh):
    if mesh.shape["seq"] != PLANES * YS * XS or mesh.shape["rows"] != CORES:
        return general(mesh)
    return over(mesh, fused_local)
```

```python
import functools
import math

import jax
import jax.numpy as jnp
from jax import lax
from jax.experimental import pallas as pl
from jax.experimental.pallas import tpu as pltpu
from jax.sharding import PartitionSpec as P

HEADS = 8


def norm_block(branch, skip, scale, gain, shift):
    mixed = skip * scale + branch
    centered = mixed - jnp.mean(mixed, axis=-1, keepdims=True)
    variance = jnp.mean(centered * centered, axis=-1, keepdims=True)
    return centered * lax.rsqrt(variance + 1e-05) * gain + shift


def project(values, matrix):
    return jnp.einsum("trd,de->tre", values, matrix, preferred_element_type=jnp.float32)


def project_back(grads, matrix):
    return jnp.einsum("tre,de->trd", grads, matrix, preferred_element_type=jnp.float32)


def matrix_grad(values, grads):
    return jnp.einsum("trd,tre->de", values, grads, preferred_element_type=jnp.float32)


def column_sum(grads):
    return jnp.sum(grads.astype(jnp.float32), axis=(0, 1))


def segment_of(positions, ends):
    return jnp.sum((ends[None, :, :] <= positions[:, None, None]).astype(jnp.int32), axis=-1)


def segment_bounds(first, last, ends):
    lowest = jnp.sum((ends <= first).astype(jnp.int32), axis=-1)
    highest = jnp.sum((ends <= last).astype(jnp.int32), axis=-1)
    return (lowest, highest)


def ranges_share(query_bounds, key_bounds):
    return jnp.any((key_bounds[0] <= query_bounds[1]) & (key_bounds[1] >= query_bounds[0]))


def key_status(positions, real_marks, ends, starts, causal):
    segments = segment_of(positions, ends)
    usable = real_marks > 0.5
    if not causal:
        usable = usable | jnp.any(starts[None, :, :] == positions[:, None, None], axis=-1)
    return (segments, usable)


def permitted(query_pos, query_seg, key_pos, key_seg, usable, causal):
    same = jnp.transpose(query_seg)[:, :, None] == jnp.transpose(key_seg)[:, None, :]
    usable_keys = jnp.transpose(usable)[:, None, :]
    if causal:
        before = (key_pos[None, :] <= query_pos[:, None])[None]
        itself = (key_pos[None, :] == query_pos[:, None])[None]
        return same & before & (usable_keys | itself)
    return same & usable_keys


def block_grads(query_heads, grad_heads, lambdas, key_heads, value_heads, permit):
    scores = (
        jnp.einsum("arhd,brhd->rhab", query_heads, key_heads, preferred_element_type=jnp.float32)
        * 0.125
    )
    weights = jnp.where(permit[:, None], jnp.exp(scores), 0.0)
    spread = jnp.einsum(
        "arhd,brhd->rhab", grad_heads, value_heads, preferred_element_type=jnp.float32
    )
    slopes = weights * (spread + jnp.transpose(lambdas, (1, 2, 0))[..., None])
    return (weights.astype(jnp.bfloat16), slopes.astype(jnp.bfloat16))


def local(
    tokens,
    memory,
    cotangent,
    tgt_lengths,
    src_lengths,
    tgt_mask,
    src_mask,
    attn_in,
    attn_out,
    w_up,
    w_down,
    biases,
    up_bias,
    norm_gain,
    norm_shift,
    omega,
):
    micro_count, tokens_here, rows_here, width = tokens.shape
    head_size = width // HEADS
    my_pos = lax.axis_index("seq") * tokens_here + jnp.arange(tokens_here, dtype=jnp.int32)
    my_first = my_pos[0]
    my_last = my_pos[tokens_here - 1]

    def split_heads(values):
        return values.reshape(values.shape[0], rows_here, HEADS, head_size)

    def zero_heads():
        return jnp.zeros((tokens_here, rows_here, HEADS, head_size), jnp.float32)

    results = []
    grads_words = []
    grads_sources = []
    shares_all = None
    for micro_index in range(micro_count):
        in_weights = lax.all_gather(attn_in, ("rows", "seq"), axis=2, tiled=True)
        out_weights = lax.all_gather(attn_out, ("rows", "seq"), axis=1, tiled=True)
        up_weights = lax.all_gather(w_up, ("rows", "seq"), axis=0, tiled=True)
        down_weights = lax.all_gather(w_down, ("rows", "seq"), axis=0, tiled=True)
        words = tokens[micro_index]
        sources = memory[micro_index]
        words_full = words.astype(jnp.float32)
        tgt_len = tgt_lengths[micro_index]
        src_len = src_lengths[micro_index]
        tgt_ends = jnp.cumsum(tgt_len, axis=-1)
        src_ends = jnp.cumsum(src_len, axis=-1)
        src_starts = src_ends - src_len
        query_seg = segment_of(my_pos, tgt_ends)
        query_bounds = segment_bounds(my_first, my_last, tgt_ends)
        tgt_real = tgt_mask[micro_index].astype(jnp.bfloat16)
        src_real = src_mask[micro_index].astype(jnp.bfloat16)

        def attend(queries, keys, values, real_marks, ends, starts, causal):
            full_keys, full_values, full_real = (
                lax.all_gather(keys, "seq", axis=0, tiled=True),
                lax.all_gather(values, "seq", axis=0, tiled=True),
                lax.all_gather(real_marks, "seq", axis=0, tiled=True),
            )
            length = full_keys.shape[0]
            block = math.gcd(length, 512)
            query_heads = split_heads(queries)

            def step(carry, block_index):
                begin = block_index * block
                shares = ranges_share(query_bounds, segment_bounds(begin, begin + block - 1, ends))

                def step_compute(state):
                    totals, accum = state
                    key_heads = split_heads(lax.dynamic_slice_in_dim(full_keys, begin, block, 0))
                    value_heads = split_heads(
                        lax.dynamic_slice_in_dim(full_values, begin, block, 0)
                    )
                    key_pos = begin + jnp.arange(block, dtype=jnp.int32)
                    key_seg, usable = key_status(
                        key_pos,
                        lax.dynamic_slice_in_dim(full_real, begin, block, 0),
                        ends,
                        starts,
                        causal,
                    )
                    permit = permitted(my_pos, query_seg, key_pos, key_seg, usable, causal)
                    scores = (
                        jnp.einsum(
                            "trhd,krhd->rhtk",
                            query_heads,
                            key_heads,
                            preferred_element_type=jnp.float32,
                        )
                        * 0.125
                    )
                    weights = jnp.where(permit[:, None], jnp.exp(scores), 0.0)
                    totals = totals + jnp.sum(weights, axis=-1)
                    accum = accum + jnp.einsum(
                        "rhtk,krhd->trhd",
                        weights.astype(jnp.bfloat16),
                        value_heads,
                        preferred_element_type=jnp.float32,
                    )
                    return (totals, accum)

                return (lax.cond(shares, step_compute, lambda unchanged: unchanged, carry), None)

            start_carry = (jnp.zeros((rows_here, HEADS, tokens_here), jnp.float32), zero_heads())
            (totals, accum), unused = lax.scan(
                step, start_carry, jnp.arange(length // block, dtype=jnp.int32)
            )
            sums = jnp.transpose(totals, (2, 0, 1))
            output = (accum / sums[..., None]).reshape(tokens_here, rows_here, width)
            return (output, sums, (full_keys, full_values, full_real))

        def attention_back(
            grad_out,
            output,
            sums,
            queries,
            keys,
            values,
            real_marks,
            gathered_set,
            ends,
            starts,
            causal,
        ):
            full_keys, full_values, full_real = gathered_set
            grad_heads = split_heads(grad_out)
            lambdas = -jnp.sum(grad_heads * split_heads(output), axis=-1) / sums
            scaled = (grad_heads / sums[..., None]).astype(jnp.bfloat16)
            query_heads = split_heads(queries)
            length = full_keys.shape[0]
            block = math.gcd(length, 512)

            def query_step(accum, block_index):
                begin = block_index * block
                shares = ranges_share(query_bounds, segment_bounds(begin, begin + block - 1, ends))

                def query_compute(state):
                    key_heads = split_heads(lax.dynamic_slice_in_dim(full_keys, begin, block, 0))
                    value_heads = split_heads(
                        lax.dynamic_slice_in_dim(full_values, begin, block, 0)
                    )
                    key_pos = begin + jnp.arange(block, dtype=jnp.int32)
                    key_seg, usable = key_status(
                        key_pos,
                        lax.dynamic_slice_in_dim(full_real, begin, block, 0),
                        ends,
                        starts,
                        causal,
                    )
                    permit = permitted(my_pos, query_seg, key_pos, key_seg, usable, causal)
                    weights, slopes = block_grads(
                        query_heads, scaled, lambdas, key_heads, value_heads, permit
                    )
                    return (
                        state
                        + jnp.einsum(
                            "rhab,brhd->arhd", slopes, key_heads, preferred_element_type=jnp.float32
                        )
                        * 0.125
                    )

                return (lax.cond(shares, query_compute, lambda unchanged: unchanged, accum), None)

            grad_query, unused = lax.scan(
                query_step, zero_heads(), jnp.arange(length // block, dtype=jnp.int32)
            )
            all_lambdas = lax.all_gather(lambdas, "seq", axis=0, tiled=True)
            local_seg, local_usable = key_status(my_pos, real_marks, ends, starts, causal)
            local_bounds = segment_bounds(my_first, my_last, ends)
            local_keys = split_heads(keys)
            local_values = split_heads(values)
            query_piece = lax.all_gather(queries, "seq", axis=0, tiled=True)
            scaled_piece = lax.all_gather(
                scaled.reshape(tokens_here, rows_here, width), "seq", axis=0, tiled=True
            )
            size = query_piece.shape[0]
            inner = math.gcd(size, 512)

            def inner_step(inner_carry, inner_index):
                offset = inner_index * inner
                piece_first = offset
                shares = ranges_share(
                    segment_bounds(piece_first, piece_first + inner - 1, tgt_ends), local_bounds
                )

                def inner_compute(state):
                    acc_key, acc_value = state
                    query_blk = split_heads(lax.dynamic_slice_in_dim(query_piece, offset, inner, 0))
                    scaled_blk = split_heads(
                        lax.dynamic_slice_in_dim(scaled_piece, offset, inner, 0)
                    )
                    lambda_blk = lax.dynamic_slice_in_dim(all_lambdas, piece_first, inner, 0)
                    query_pos = piece_first + jnp.arange(inner, dtype=jnp.int32)
                    permit = permitted(
                        query_pos,
                        segment_of(query_pos, tgt_ends),
                        my_pos,
                        local_seg,
                        local_usable,
                        causal,
                    )
                    weights, slopes = block_grads(
                        query_blk, scaled_blk, lambda_blk, local_keys, local_values, permit
                    )
                    acc_key = (
                        acc_key
                        + jnp.einsum(
                            "rhab,arhd->brhd", slopes, query_blk, preferred_element_type=jnp.float32
                        )
                        * 0.125
                    )
                    acc_value = acc_value + jnp.einsum(
                        "rhab,arhd->brhd", weights, scaled_blk, preferred_element_type=jnp.float32
                    )
                    return (acc_key, acc_value)

                return (
                    lax.cond(shares, inner_compute, lambda unchanged: unchanged, inner_carry),
                    None,
                )

            folded, unused_inner = lax.scan(
                inner_step, (zero_heads(), zero_heads()), jnp.arange(size // inner, dtype=jnp.int32)
            )
            grad_key, grad_value = folded
            grad_key = grad_key.reshape(tokens_here, rows_here, width)
            grad_value = grad_value.reshape(tokens_here, rows_here, width)
            return (grad_query.reshape(tokens_here, rows_here, width), grad_key, grad_value)

        self_query = (project(words, in_weights[0, 0]) + biases[0]).astype(jnp.bfloat16)
        self_key = project(words, in_weights[0, 1]).astype(jnp.bfloat16)
        self_value = (project(words, in_weights[0, 2]) + biases[1]).astype(jnp.bfloat16)
        heard, heard_sums, self_set = attend(
            self_query, self_key, self_value, tgt_real, tgt_ends, None, True
        )
        heard_low = heard.astype(jnp.bfloat16)
        branch_self = project(heard_low, out_weights[0]) + biases[2]
        hidden_one, pull_one = jax.vjp(
            norm_block, branch_self, words_full, omega[0], norm_gain[0], norm_shift[0]
        )
        hidden_one_low = hidden_one.astype(jnp.bfloat16)
        cross_query = (project(hidden_one_low, in_weights[1, 0]) + biases[3]).astype(jnp.bfloat16)
        cross_key = project(sources, in_weights[1, 1]).astype(jnp.bfloat16)
        cross_value = (project(sources, in_weights[1, 2]) + biases[4]).astype(jnp.bfloat16)
        recalled, recalled_sums, cross_set = attend(
            cross_query, cross_key, cross_value, src_real, src_ends, src_starts, False
        )
        recalled_low = recalled.astype(jnp.bfloat16)
        branch_cross = project(recalled_low, out_weights[1]) + biases[5]
        hidden_two, pull_two = jax.vjp(
            norm_block, branch_cross, hidden_one, omega[1], norm_gain[1], norm_shift[1]
        )
        hidden_two_low = hidden_two.astype(jnp.bfloat16)
        up_pre = project(hidden_two_low, up_weights) + up_bias
        active, pull_active = jax.vjp(jax.nn.gelu, up_pre)
        active_low = active.astype(jnp.bfloat16)
        branch_ffn = project(active_low, down_weights) + biases[6]
        outcome, pull_three = jax.vjp(
            norm_block, branch_ffn, hidden_two, omega[2], norm_gain[2], norm_shift[2]
        )
        grad_result = cotangent[micro_index].astype(jnp.float32)
        grad_ffn, grad_two, omega_three, gain_three, shift_three = pull_three(grad_result)
        grad_ffn_low = grad_ffn.astype(jnp.bfloat16)
        grad_down = matrix_grad(active_low, grad_ffn_low)
        bias_ffn = column_sum(grad_ffn_low)
        grad_up_pre = pull_active(project_back(grad_ffn_low, down_weights))[0].astype(jnp.bfloat16)
        grad_up = matrix_grad(hidden_two_low, grad_up_pre)
        bias_up = column_sum(grad_up_pre)
        grad_two = grad_two + project_back(grad_up_pre, up_weights)
        grad_cross, grad_one, omega_two, gain_two, shift_two = pull_two(grad_two)
        grad_cross_low = grad_cross.astype(jnp.bfloat16)
        grad_out_cross = matrix_grad(recalled_low, grad_cross_low)
        bias_out_cross = column_sum(grad_cross_low)
        grad_recalled = project_back(grad_cross_low, out_weights[1])
        cross_gq, cross_gk, cross_gv = attention_back(
            grad_recalled,
            recalled,
            recalled_sums,
            cross_query,
            cross_key,
            cross_value,
            src_real,
            cross_set,
            src_ends,
            src_starts,
            False,
        )
        cross_gq = cross_gq.astype(jnp.bfloat16)
        cross_gk = cross_gk.astype(jnp.bfloat16)
        cross_gv = cross_gv.astype(jnp.bfloat16)
        grad_cross_query = matrix_grad(hidden_one_low, cross_gq)
        grad_cross_key = matrix_grad(sources, cross_gk)
        grad_cross_value = matrix_grad(sources, cross_gv)
        grad_one = grad_one + project_back(cross_gq, in_weights[1, 0])
        grad_sources = project_back(cross_gk, in_weights[1, 1]) + project_back(
            cross_gv, in_weights[1, 2]
        )
        grad_self, grad_words, omega_one, gain_one, shift_one = pull_one(grad_one)
        grad_self_low = grad_self.astype(jnp.bfloat16)
        grad_out_self = matrix_grad(heard_low, grad_self_low)
        bias_out_self = column_sum(grad_self_low)
        grad_heard = project_back(grad_self_low, out_weights[0])
        self_gq, self_gk, self_gv = attention_back(
            grad_heard,
            heard,
            heard_sums,
            self_query,
            self_key,
            self_value,
            tgt_real,
            self_set,
            tgt_ends,
            None,
            True,
        )
        self_gq = self_gq.astype(jnp.bfloat16)
        self_gk = self_gk.astype(jnp.bfloat16)
        self_gv = self_gv.astype(jnp.bfloat16)
        grad_words = (
            grad_words
            + project_back(self_gq, in_weights[0, 0])
            + project_back(self_gk, in_weights[0, 1])
            + project_back(self_gv, in_weights[0, 2])
        )
        grad_in = jnp.stack(
            [
                jnp.stack(
                    [
                        matrix_grad(words, self_gq),
                        matrix_grad(words, self_gk),
                        matrix_grad(words, self_gv),
                    ]
                ),
                jnp.stack([grad_cross_query, grad_cross_key, grad_cross_value]),
            ]
        )
        grad_out = jnp.stack([grad_out_self, grad_out_cross])
        grad_bias = jnp.stack(
            [
                column_sum(self_gq),
                column_sum(self_gv),
                bias_out_self,
                column_sum(cross_gq),
                column_sum(cross_gv),
                bias_out_cross,
                bias_ffn,
            ]
        )
        grad_gain = jnp.stack([gain_one, gain_two, gain_three])
        grad_shift = jnp.stack([shift_one, shift_two, shift_three])
        grad_omega = jnp.stack([omega_one, omega_two, omega_three])
        grads = (
            grad_in,
            grad_out,
            grad_up,
            grad_down,
            grad_bias,
            bias_up,
            grad_gain,
            grad_shift,
            grad_omega,
        )
        outcome, grad_words, grad_sources, grads = (
            outcome.astype(jnp.bfloat16),
            grad_words.astype(jnp.bfloat16),
            grad_sources.astype(jnp.bfloat16),
            grads,
        )
        results.append(outcome)
        grads_words.append(grad_words)
        grads_sources.append(grad_sources)
        part_shares = (
            lax.psum_scatter(grads[0], ("rows", "seq"), scatter_dimension=2, tiled=True),
            lax.psum_scatter(grads[1], ("rows", "seq"), scatter_dimension=1, tiled=True),
            lax.psum_scatter(grads[2], ("rows", "seq"), scatter_dimension=0, tiled=True),
            lax.psum_scatter(grads[3], ("rows", "seq"), scatter_dimension=0, tiled=True),
            lax.psum_scatter(grads[4], ("rows", "seq"), scatter_dimension=1, tiled=True),
            lax.psum_scatter(grads[5], ("rows", "seq"), scatter_dimension=0, tiled=True),
            lax.psum_scatter(grads[6], ("rows", "seq"), scatter_dimension=1, tiled=True),
            lax.psum_scatter(grads[7], ("rows", "seq"), scatter_dimension=1, tiled=True),
            lax.psum_scatter(grads[8], ("rows", "seq"), scatter_dimension=1, tiled=True),
        )
        shares_all = (
            part_shares if shares_all is None else jax.tree.map(jnp.add, shares_all, part_shares)
        )
    return (jnp.stack(results), jnp.stack(grads_words), jnp.stack(grads_sources)) + tuple(
        shares_all
    )


def over(mesh, function):
    return jax.shard_map(
        function,
        mesh=mesh,
        in_specs=(
            P(None, "seq", "rows", None),
            P(None, "seq", "rows", None),
            P(None, "seq", "rows", None),
            P(None, "rows", None),
            P(None, "rows", None),
            P(None, "seq", "rows"),
            P(None, "seq", "rows"),
            P(None, None, ("rows", "seq"), None),
            P(None, ("rows", "seq"), None),
            P(("rows", "seq"), None),
            P(("rows", "seq"), None),
            P(),
            P(),
            P(),
            P(),
            P(),
        ),
        out_specs=(
            P(None, "seq", "rows", None),
            P(None, "seq", "rows", None),
            P(None, "seq", "rows", None),
            P(None, None, ("rows", "seq"), None),
            P(None, ("rows", "seq"), None),
            P(("rows", "seq"), None),
            P(("rows", "seq"), None),
            P(None, ("rows", "seq")),
            P(("rows", "seq")),
            P(None, ("rows", "seq")),
            P(None, ("rows", "seq")),
            P(None, ("rows", "seq")),
        ),
        check_vma=False,
    )


def general(mesh):
    return over(mesh, local)


MESH = pl.DeviceIdType.MESH
UNIT = 16 * 1024
BINS = 16
NAMES = 168
ODD = ("marks", "w0p", "w1p", "u0p")
F32 = jnp.float32
BF16 = jnp.bfloat16
PLANES, YS, XS, CORES = 4, 2, 2, 2
GROUP = YS * XS * CORES


def nn(left, right):
    return lax.dot_general(left, right, (((1,), (0,)), ((), ())), preferred_element_type=F32)


def nt(left, right):
    return lax.dot_general(left, right, (((1,), (1,)), ((), ())), preferred_element_type=F32)


def tn(left, right):
    return lax.dot_general(left, right, (((0,), (0,)), ((), ())), preferred_element_type=F32)


def flip(value):
    return jnp.transpose(value.astype(F32))


def fused_kernel(
    tok, mem, cot, tgt_len, src_len, tgt_msk, src_msk, s_in, s_out, s_up, s_dn, h_biases, h_up_bias, h_gain, h_shift, h_omega,
    o_res, o_tok, o_mem, h_in, h_out, h_up, h_dn, h_bias, h_upb, h_gain_o, h_shift_o, h_omega_o,
    biases, up_bias, gain, shift, omega, o_in, o_out, o_up, o_dn, o_bias, o_upb, o_gain, o_shift, o_omega,
    w_q, w_out, w_up, w_dn, g_q, g_out, g_up, g_dn,
    c_q, c_out, c_up, c_dn,
    p_q, p_out, p_up, p_dn,
    q_q, q_out, q_up, q_dn,
    z_q, z_out, z_up, z_dn,
    ws0, ws1, gs0, gs1, cs0, cs1, zs0, zs1, fs0, fs1,
    all_tok, all_mem, in_cot, raw_tl, raw_sl, raw_tm, raw_sm, meta, in_meta, all_meta,
    dx0, dx1, dc0, dc1, dp0, dp1,
    a3, b3, a4, b4, a5, b5, a6, b6, a7, b7, a8, b8,
    out_res, out_tok, out_mem,
    sg0, sg1, sg2, sg3, sg4, sr0, sr1, sr2, sr3,
    tg0, tg1, tg2, tg3, tr0, tr1, tr2, tr3,
    code_self, code_cross, key_pos, rows_f,
    qt0, kt0, vt0, k0, v0, pt0, l0, ot0,
    qt1, kt1, vt1, k1, v1, pt1, l1, ot1,
    dnt, acc_k, acc_v,
    act, slope, gul, xh0, xh1, xh2, h1_f, h2_f,
    wt, bias_cols, wz, dt0, dt1, gauge,
    ss, rs,
):
    c = lax.axis_index("rows")
    seq = lax.axis_index("seq")
    z = seq // (YS * XS)
    yx = lax.rem(seq, YS * XS)
    y = yx // XS
    x = lax.rem(yx, XS)
    width = 512
    here = 2 * 64

    def at(zz, yy, xx):
        return zz * (YS * XS) + yy * XS + xx

    def slot(cc, yy, xx):
        return cc * 4 + yy * 2 + xx

    def head(cc, yy, xx):
        return (yy * 2 + xx) * 2 + cc

    me_slot, me_head = slot(c, y, x), head(c, y, x)
    plane_peers = []
    for k in range(1, GROUP):
        cc = 1 - c if k & 4 else c
        yy = 1 - y if k & 2 else y
        xx = 1 - x if k & 1 else x
        plane_peers.append((cc, yy, xx))
    trio = [(1 - y, x), (y, 1 - x), (1 - y, 1 - x)]
    z_peers = [lax.rem(z + k, PLANES) for k in (1, 2, 3)]

    names, expected_bytes = {}, {}
    pending = []
    edge = (z == 0) | (z == PLANES - 1)

    def sem(name):
        return names.setdefault(name, len(names))

    def wait(semaphore, ref):
        pltpu.make_async_copy(ref, ref, semaphore).wait()

    def size(ref):
        return math.prod(ref.shape) * jnp.dtype(ref.dtype).itemsize

    bins = [0]
    odd = {}

    def out_sem(name):
        return ss.at[odd.setdefault(name, BINS + 1 + len(odd))] if name in ODD else ss.at[len(bins) - 1]

    def send(name, src, dst, device, recv=None):
        pltpu.make_async_remote_copy(
            src_ref=src, dst_ref=dst, send_sem=out_sem(name), recv_sem=rs.at[sem(name)] if recv is None else recv,
            device_id=device, device_id_type=MESH,
        ).start()

    def keep(name, src, dst):
        pltpu.make_async_copy(src, dst, rs.at[sem(name)]).start()

    def landed(name, ref):
        wait(rs.at[sem(name)], ref)

    def sent_later(name, ref):
        if name in ODD:
            pending.append((ss.at[odd[name]], ref, None))
            return
        bins[-1] += size(ref)
        assert size(ref) % UNIT == 0, (name, size(ref))
        if bins[-1] > 1024 * UNIT // 16:
            bins.append(0)

    line_bytes = [0]

    def along_z(name, src, block):
        i, j = sem(name + "z"), sem(name + "f")
        for step in (1, -1, 2, -2):
            to = z + step
            far = (z == 0) if step == 2 else (z == PLANES - 1) if step == -2 else None

            @pl.when((to >= 0) & (to < PLANES))
            def _():
                pltpu.make_async_remote_copy(
                    src_ref=src, dst_ref=block(z), send_sem=ss.at[BINS],
                    recv_sem=rs.at[i] if far is None else rs.at[jnp.where(far, j, i)],
                    device_id=(c, at(to, y, x)), device_id_type=MESH,
                ).start()

        line_bytes[0] += size(src)

    def pass_on(name, block):
        for mine, origin, to in ((1, 3, 0), (2, 0, 3)):

            @pl.when(z == mine)
            def _():
                landed(name + "f", block(origin))
                pltpu.make_async_remote_copy(
                    src_ref=block(origin), dst_ref=block(origin), send_sem=ss.at[BINS], recv_sem=rs.at[sem(name + "z")],
                    device_id=(c, at(to, y, x)), device_id_type=MESH,
                ).start()

    def line_landed(name, blocks, own):
        @pl.when(edge)
        def _():
            landed(name + "z", blocks(3 + own))

        @pl.when(jnp.logical_not(edge))
        def _():
            landed(name + "z", blocks(2 + own))

    def to_plane(name, src, dst, slotted=False):
        half = lax.rem(z, 2)
        core = z // 2
        if slotted:
            recv = rs.at[jnp.where(half == 0, sem(name + "h0"), sem(name + "h1"))]
            part = dst.at[slot(core, y, x), half]
        else:
            recv = rs.at[sem(name)]
            part = dst.at[half]
        for m in range(2):
            plane = 2 * m + c
            own = (plane == z) & (core == c)
            out = ss.at[odd.setdefault(name + str(m), BINS + 1 + len(odd))]

            @pl.when(own)
            def _():
                pltpu.make_async_copy(src.at[m], part, recv).start()

            @pl.when(jnp.logical_not(own))
            def _():
                pltpu.make_async_remote_copy(
                    src_ref=src.at[m], dst_ref=part, send_sem=out, recv_sem=recv,
                    device_id=(core, at(plane, y, x)), device_id_type=MESH,
                ).start()

            pending.append((out, src.at[m], jnp.logical_not(own)))

    def from_plane(name, src, dst):
        micro, core = z // 2, lax.rem(z, 2)
        recv = rs.at[sem(name)]
        for half in range(2):
            zz = 2 * c + half
            own = (core == c) & (zz == z)
            part = dst.at[micro]
            out = ss.at[odd.setdefault(name + str(half), BINS + 1 + len(odd))]

            @pl.when(own)
            def _():
                pltpu.make_async_copy(src.at[half], part, recv).start()

            @pl.when(jnp.logical_not(own))
            def _():
                pltpu.make_async_remote_copy(
                    src_ref=src.at[half], dst_ref=part, send_sem=out, recv_sem=recv,
                    device_id=(core, at(zz, y, x)), device_id_type=MESH,
                ).start()

            pending.append((out, src.at[half], jnp.logical_not(own)))

    def to_heads(name, src, dst):
        keep(name, src.at[me_head], dst.at[me_slot])
        for cc, yy, xx in plane_peers:
            send(name, src.at[head(cc, yy, xx)], dst.at[me_slot], (cc, at(z, yy, xx)))
        sent_later(name, src.at[pl.ds(0, GROUP - 1)])

    def to_slot(name, src, dst, s):
        device = (s // 4, at(z, lax.rem(s, 4) // 2, lax.rem(s, 2)))
        i = sem(name)
        out = out_sem(name)

        @pl.when(s == me_slot)
        def _():
            pltpu.make_async_copy(src.at[s], dst.at[me_head], rs.at[i]).start()

        @pl.when(s != me_slot)
        def _():
            pltpu.make_async_remote_copy(
                src_ref=src.at[s], dst_ref=dst.at[me_head], send_sem=out, recv_sem=rs.at[i],
                device_id=device, device_id_type=MESH,
            ).start()

    weights = {
        "q": (w_q, s_in.at[1, pl.ds(0, 1)], g_q, c_q, p_q, q_q, z_q, o_in.at[1, pl.ds(0, 1)]),
    }

    for i in range(2):
        one = pl.ds(i, 1)
        refs = (w_out, s_out, g_out, c_out, p_out, q_out, z_out, o_out)
        weights["out" + str(i)] = tuple(
            ref.at[:, one] if ref is p_out or ref is q_out or ref is z_out else ref.at[one] for ref in refs
        )
        refs = (w_up, s_up, g_up, c_up, p_up, q_up, z_up, o_up)
        cols = pl.ds(i * 1024, 1024)
        weights["up" + str(i)] = tuple(
            ref.at[:, one] if ref is p_up or ref is q_up or ref is z_up
            else ref.at[:, :, cols] if ref is s_up or ref is o_up else ref.at[one]
            for ref in refs
        )
        refs = (w_dn, s_dn, g_dn, c_dn, p_dn, q_dn, z_dn, o_dn)
        cols = pl.ds(i * 256, 256)
        weights["dn" + str(i)] = tuple(
            ref.at[:, one] if ref is p_dn or ref is q_dn or ref is z_dn
            else ref.at[:, :, cols] if ref is s_dn or ref is o_dn else ref.at[one]
            for ref in refs
        )

    def halves(ref):
        cols = ref.shape[-1] // 2
        return pl.ds(0, cols), pl.ds(cols, cols)

    x_next, y_next, core_next = (c, at(z, y, 1 - x)), (c, at(z, 1 - y, x)), (1 - c, seq)

    def gather_z(g):
        full, shard = weights[g][:2]
        keep(g + "z", shard, full.at[:, c, z, y, x])
        along_z(g, shard, lambda zz: full.at[:, c, zz, y, x])

    def gather_f(g):
        full = weights[g][0]
        pass_on(g, lambda zz: full.at[:, c, zz, y, x])

    def gather_1(g):
        full = weights[g][0]
        first, second = halves(full)
        line_landed(g, lambda n: full.at[:, c, pl.ds(0, n), y, x], 1)
        part = full.at[:, c, :, y, x, :, first]
        send(g + "1a", part, part, x_next)
        sent_later(g + "1a", part)
        part = full.at[:, c, :, y, x, :, second]
        send(g + "1b", part, part, y_next)
        sent_later(g + "1b", part)

    def gather_2(g):
        full = weights[g][0]
        first, second = halves(full)
        landed(g + "1a", full.at[:, c, :, y, 1 - x, :, first])
        part = full.at[:, c, :, y, :, :, first]
        send(g + "2a", part, part, y_next)
        sent_later(g + "2a", part)
        landed(g + "1b", full.at[:, c, :, 1 - y, x, :, second])
        part = full.at[:, c, :, :, x, :, second]
        send(g + "2b", part, part, x_next)
        sent_later(g + "2b", part)

    def gather_3(g):
        full = weights[g][0]
        first, second = halves(full)
        landed(g + "2a", full.at[:, c, :, 1 - y, :, :, first])
        landed(g + "2b", full.at[:, c, :, :, 1 - x, :, second])
        send(g + "3", full.at[:, c], full.at[:, c], core_next)
        sent_later(g + "3", full.at[:, c])

    def gathered(g):
        landed(g + "3", weights[g][0].at[:, 1 - c])

    def add(target, other):
        target[...] = (target[...].astype(F32) + other[...].astype(F32)).astype(BF16)

    def scatter_0(g):
        grad, across = weights[g][2:4]
        send(g + "r0", grad.at[:, 1 - c], across, core_next)
        sent_later(g + "r0", across)

    def scatter_1(g):
        grad, across, part = weights[g][2:5]
        first, second = halves(grad)
        landed(g + "r0", across)
        for lead in range(grad.shape[0]):

            @pl.loop(0, PLANES)
            def _(zz):
                add(grad.at[lead, c, zz], across.at[lead, zz])

        send(g + "r1a", grad.at[:, c, :, 1 - y, :, :, first], part.at[0], y_next)
        sent_later(g + "r1a", part.at[0])
        send(g + "r1b", grad.at[:, c, :, :, 1 - x, :, second], part.at[1], x_next)
        sent_later(g + "r1b", part.at[1])

    def scatter_2(g):
        grad, _, part, piece = weights[g][2:6]
        first, second = halves(grad)
        landed(g + "r1a", part.at[0])
        landed(g + "r1b", part.at[1])
        for lead in range(grad.shape[0]):

            @pl.loop(0, PLANES)
            def _(zz):
                add(grad.at[lead, c, zz, y, :, :, first], part.at[0, lead, zz])
                add(grad.at[lead, c, zz, :, x, :, second], part.at[1, lead, zz])

        send(g + "r2a", grad.at[:, c, :, y, 1 - x, :, first], piece.at[0], x_next)
        sent_later(g + "r2a", piece.at[0])
        send(g + "r2b", grad.at[:, c, :, 1 - y, x, :, second], piece.at[1], y_next)
        sent_later(g + "r2b", piece.at[1])

    def scatter_3(g):
        grad, _, _, piece, line = weights[g][2:7]
        first, second = halves(grad)
        landed(g + "r2a", piece.at[0])
        landed(g + "r2b", piece.at[1])
        for lead in range(grad.shape[0]):

            @pl.loop(0, PLANES)
            def _(zz):
                add(grad.at[lead, c, zz, y, x, :, first], piece.at[0, lead, zz])
                add(grad.at[lead, c, zz, y, x, :, second], piece.at[1, lead, zz])

        for k in range(3):
            send(g + "r3", grad.at[:, c, z_peers[k], y, x], line.at[2 - k], (c, at(z_peers[k], y, x)))
        sent_later(g + "r3", line)

    def scattered(g):
        grad, _, _, _, line, result = weights[g][2:8]
        landed(g + "r3", line)
        total = grad[:, c, z, y, x].astype(F32)
        for k in range(3):
            total = total + line[k].astype(F32)
        result[...] = total

    def spread_1(name, full, half):
        own = full.at[me_slot, half]
        landed(name + "h" + str(half), own)
        for k, (yy, xx) in enumerate(trio):
            send(name + "p" + str(half) + str(k), own, own, (c, at(z, yy, xx)))
            sent_later(name + "p" + str(half) + str(k), own)
        send(name + "c", own, own, core_next)
        sent_later(name + "c", own)

    def spread_2(name, full, half):
        for k, (yy, xx) in enumerate(trio):
            part = full.at[slot(c, yy, xx), half]
            landed(name + "p" + str(half) + str(k), part)
            send(name + "d", part, part, core_next)
            sent_later(name + "d", part)

    def spread_3(name, full):
        landed(name + "c", full.at[0])
        landed(name + "d", full.at[pl.ds(0, 3)])

    def merge_0(name, full, across):
        send(name + "c", full.at[pl.ds((1 - c) * 4, 4)], across, core_next)
        sent_later(name + "c", across)

    def merge_1(name, full, across, parts):
        landed(name + "c", across)
        for k, (yy, xx) in enumerate(trio):
            place = slot(c, yy, xx)
            add(full.at[place], across.at[yy * 2 + xx])
            send(name + "p", full.at[place], parts.at[k], (c, at(z, yy, xx)))
        sent_later(name + "p", parts)
        add(full.at[me_slot], across.at[yx])

    def merge_2(name, full, parts):
        landed(name + "p", parts)
        total = full[me_slot].astype(F32)
        for k in range(3):
            total = total + parts[k].astype(F32)
        return total.reshape(here, width)

    def tile(index):
        return pl.ds(pl.multiple_of(index * 128, 128), 128)

    def slice_1(name, shard, full):
        keep(name + "p", shard.at[:, :, tile(yx)], full.at[:, c, z, yx])
        for yy, xx in trio:
            send(name + "p", shard.at[:, :, tile(yy * 2 + xx)], full.at[:, c, z, yx], (c, at(z, yy, xx)))
        sent_later(name + "p", full.at[:, c, z, pl.ds(0, 3)])

    def slice_2(name, full):
        landed(name + "p", full.at[:, c, z])
        along_z(name, full.at[:, c, z], lambda zz: full.at[:, c, zz])

    def slice_f(name, full):
        pass_on(name, lambda zz: full.at[:, c, zz])

    def slice_3(name, full):
        line_landed(name, lambda n: full.at[:, c, pl.ds(0, n)], 0)
        send(name + "c", full.at[:, c], full.at[:, c], core_next)
        sent_later(name + "c", full.at[:, c])

    def slice_4(name, full):
        landed(name + "c", full.at[:, 1 - c])

    def unslice_0(name, grad, across):
        send(name + "c", grad.at[:, 1 - c], across, core_next)
        sent_later(name + "c", across)

    def unslice_1(name, grad, across, line):
        landed(name + "c", across)
        for lead in range(grad.shape[0]):
            add(grad.at[lead, c], across.at[lead])
        for k in range(3):
            send(name + "z", grad.at[:, c, z_peers[k]], line.at[2 - k], (c, at(z_peers[k], y, x)))
        sent_later(name + "z", line)

    def unslice_2(name, grad, line, total, result):
        landed(name + "z", line)
        value = grad[:, c, z].astype(F32)
        for k in range(3):
            value = value + line[k].astype(F32)
        total[...] = value
        for yy, xx in trio:
            send(name + "p", total.at[:, yy * 2 + xx], result.at[:, :, tile(yx)], (c, at(z, yy, xx)))
        sent_later(name + "p", total.at[:, pl.ds(0, 3)])
        result[:, :, tile(yx)] = total[:, yx]

    def unslice_3(name, result):
        landed(name + "p", result.at[:, :, pl.ds(0, 384)])

    def matrix(ref):
        return ref[...].reshape(-1, ref.shape[-1])

    def put(ref, value):
        ref[...] = value.astype(BF16).reshape(ref.shape)

    def norm(r, i, kept):
        centered = r - jnp.mean(r, axis=1, keepdims=True)
        scale = lax.rsqrt(jnp.mean(centered * centered, axis=1, keepdims=True) + 1e-05)
        xhat = centered * scale
        kept[...] = xhat
        return xhat * gain[i : i + 1, :] + shift[i : i + 1, :], scale

    def column(row, value):
        sg0[row : row + 1, :] = jnp.sum(value, axis=0, keepdims=True)

    def norm_back(grad, i, kept, scale, skip):
        xhat = kept[...]
        column(11 + i, grad * xhat)
        column(14 + i, grad)
        dxhat = grad * gain[i : i + 1, :]
        dr = dxhat - jnp.mean(dxhat, axis=1, keepdims=True)
        dr = (dr - xhat * jnp.mean(dxhat * xhat, axis=1, keepdims=True)) * scale
        column(17 + i, dr * skip)
        return dr, dr * omega[i : i + 1, :]

    BLOCK = 256

    def attend(queries, keys, values_t, weights_t, sums, outputs, causal, name, target, arrives):
        def make(extent):
            def body(b):
                cols = pl.ds(pl.multiple_of(b * BLOCK, BLOCK), BLOCK)
                scores = nn(keys[:extent, :], queries[:, cols])
                seg = rows_f[0:1, cols]
                code = (code_self if causal else code_cross)[:extent, :]
                permit = jnp.concatenate([code, code], axis=1) == seg
                if causal:
                    pos = key_pos[:extent, :]
                    pos = jnp.concatenate([pos, pos], axis=1)
                    mine = rows_f[1:2, cols]
                    permit = (permit & (pos <= mine)) | (pos == mine)
                weight = jnp.where(permit, jnp.exp(scores), 0.0)
                total = jnp.sum(weight, axis=0, keepdims=True)
                low = weight.astype(BF16)
                weights_t[:extent, cols] = low
                out = nn(values_t[:, :extent], low) / total
                sums[0:1, cols] = total
                outputs[:, cols] = out
                for k in range(2):
                    target[2 * b + k] = out[:, k * here : (k + 1) * here].astype(BF16)
                    to_slot(name, target, arrives, 2 * b + k)

            return body

        if causal:
            pl.loop(0, 2)(make(512))
            pl.loop(2, 4)(make(1024))
        else:
            pl.loop(0, 4)(make(1024))
        sent_later(name, target.at[pl.ds(0, GROUP - 1)])

    def attend_back(buffer, queries, keys_t, values, weights_t, sums, outputs, causal, name, target, arrives):
        acc_k[...] = jnp.zeros_like(acc_k)
        acc_v[...] = jnp.zeros_like(acc_v)
        for s in range(GROUP):
            cols = slice(s * here, (s + 1) * here)
            grad = buffer[s].astype(F32)
            inverse = 1.0 / sums[0:1, cols]
            dnt[:, cols] = (grad * inverse).astype(BF16)
            rows_f[2:3, cols] = -jnp.sum(grad * outputs[:, cols], axis=0, keepdims=True) * inverse

        def make(extent):
            def body(b):
                cols = pl.ds(pl.multiple_of(b * BLOCK, BLOCK), BLOCK)
                low = weights_t[:extent, cols]
                dn = dnt[:, cols]
                spread = nn(values[:extent, :], dn)
                slopes = (low.astype(F32) * (spread + rows_f[2:3, cols])).astype(BF16)
                block = (nn(keys_t[:, :extent], slopes) * 0.125).astype(BF16)
                if name is None:
                    dt0[0:64, cols] = block
                else:
                    for k in range(2):
                        target[2 * b + k] = block[:, k * here : (k + 1) * here]
                        to_slot(name, target, arrives, 2 * b + k)
                acc_k[:, :extent] += nt(queries[:, cols], slopes)
                acc_v[:, :extent] += nt(dn, low)

            return body

        if causal:
            pl.loop(0, 2)(make(512))
            pl.loop(2, 4)(make(1024))
        else:
            pl.loop(0, 4)(make(1024))
        if name is not None:
            sent_later(name, target.at[pl.ds(0, GROUP - 1)])

    def by_head(target, value):
        target[...] = flip(value).astype(BF16).reshape(GROUP, 64, here)

    def heads_weights(first, full):
        for j in range(full.shape[0]):
            wt[first + j] = flip(matrix(full.at[j])).astype(BF16)

    own_rows = pl.ds(pl.multiple_of(c * 64, 64), 64)
    own_head = pl.ds(pl.multiple_of(me_head * 64, 64), 64)

    def own_weights(first, count):
        return jnp.concatenate([wt[first + j, own_rows, :] for j in range(count)], axis=0)

    def wide_bias(i):
        col = bias_cols[i, own_head, :]
        return jnp.concatenate([col, col], axis=1)

    def project_heads(rows, first, queries, keys, keys_t, values, values_t):
        count = 2 if queries is None else 3
        own = own_weights(first, count)
        for b in range(4):
            cols = slice(b * 256, (b + 1) * 256)
            out = nt(own, rows[2 * b : 2 * b + 2].reshape(256, width))
            if queries is not None:
                queries[:, cols] = ((out[0:64] + wide_bias(0)).astype(BF16).astype(F32) * 0.125).astype(BF16)
            at_k = 64 * (count - 2)
            block = out[at_k : at_k + 64].astype(BF16)
            keys_t[:, cols] = block
            keys[cols, :] = flip(block).astype(BF16)
            block = (out[at_k + 64 : at_k + 128] + wide_bias(1 if count == 3 else 2)).astype(BF16)
            values_t[:, cols] = block
            values[cols, :] = flip(block).astype(BF16)

    def rows_back(grads_t, first, target, core):
        count = grads_t.shape[0] // 64
        own = own_weights(first, count)
        for b in range(2):
            cols = pl.ds(pl.multiple_of(core * 512 + b * 256, 256), 256)
            out = tn(grads_t[:, cols], own)
            target[pl.ds(core * 4 + b * 2, 2)] = out.astype(BF16).reshape(2, 2, 64, width)

    def slices_back(grads_t, rows, grad):
        count = grads_t.shape[0] // 64
        out = nn(grads_t[...], rows[...].reshape(1024, width))
        wz[...] = jnp.zeros_like(wz)
        for j in range(count):
            wz[j, own_rows, :] = out[j * 64 : (j + 1) * 64]
            put(grad.at[j], jnp.transpose(wz[j]))

    def bias(i):
        return biases[i : i + 1, :]

    def make_masks():
        landed("marks", all_meta.at[pl.ds(0, 7)])
        order = lax.broadcasted_iota(jnp.int32, (1, 1024), 1)
        place = (order // 512) * 512 + lax.rem(order // 64, 2) * 256 + lax.rem(order // 128, 4) * 64 + lax.rem(order, 64)
        place = place.astype(F32)
        marks = [all_meta[s].astype(F32) for s in range(GROUP)]
        tgt_real = jnp.concatenate([mark[0:1, :] for mark in marks], axis=1)
        src_real = jnp.concatenate([mark[1:2, :] for mark in marks], axis=1)
        lower = lax.broadcasted_iota(jnp.int32, (32, 128), 1)
        later = lax.broadcasted_iota(jnp.int32, (32, 128), 0)

        def ends_of(row):
            lengths = jnp.broadcast_to(row, (32, 128))
            ends = jnp.sum(jnp.where(lower <= later, lengths, 0.0), axis=1, keepdims=True)
            starts = jnp.sum(jnp.where(lower < later, lengths, 0.0), axis=1, keepdims=True)
            return ends, starts

        def count(flags):
            return jnp.sum(jnp.where(flags, 1.0, 0.0), axis=0, keepdims=True)

        tgt_ends, _ = ends_of(marks[0][2:3, :])
        src_ends, src_starts = ends_of(marks[0][3:4, :])
        tgt_seg = count(tgt_ends <= place)
        src_seg = count(src_ends <= place)
        src_first = count(src_starts == place)
        self_row = jnp.where(tgt_real > 0.5, tgt_seg, -1.0)
        cross_row = jnp.where((src_real > 0.5) | (src_first > 0.5), src_seg, -1.0)
        rows_f[0:1, :] = tgt_seg
        rows_f[1:2, :] = place
        code_self[...] = jnp.transpose(jnp.broadcast_to(self_row, (128, 1024)))
        code_cross[...] = jnp.transpose(jnp.broadcast_to(cross_row, (128, 1024)))
        key_pos[...] = jnp.transpose(jnp.broadcast_to(place, (128, 1024)))

    def feed_up(rows, i):
        for k in (2 * i, 2 * i + 1):
            cols = slice(k * width, (k + 1) * width)
            inner = slice((k % 2) * width, (k % 2 + 1) * width)
            u = nn(rows, matrix(w_up.at[i, :, :, :, :, :, inner])) + up_bias[0:1, cols]
            square = u * u
            t = jnp.tanh(u * (0.7978845608028654 + 0.035677408136300125 * square))
            act[:, cols] = (0.5 * u * (1.0 + t)).astype(BF16)
            inner = 0.7978845608028654 + 0.10703222440890037 * square
            slope[:, cols] = 0.5 * (1.0 + t) + 0.5 * u * (1.0 - t * t) * inner

    def feed_back(gf, back):
        for k in range(4):
            cols = slice(k * width, (k + 1) * width)
            inner = slice((k % 2) * width, (k % 2 + 1) * width)
            rows = pl.ds(2 * (k % 2), 2)
            gu = nt(gf[:, 0:256], matrix(w_dn.at[0, k // 2, rows]))
            gu = gu + nt(gf[:, 256:512], matrix(w_dn.at[1, k // 2, rows]))
            gu = (gu * slope[:, cols]).astype(BF16)
            gul[:, cols] = gu
            column(7 + k, gu.astype(F32))
            back = back + nt(gu, matrix(w_up.at[k // 2, :, :, :, :, :, inner]))
        return back

    def value_sums(grads_t):
        total = jnp.sum(grads_t[64:128, :].astype(F32), axis=1, keepdims=True)
        bias_cols[0] = jnp.zeros((width, 128), F32)
        bias_cols[0, own_head, :] = jnp.broadcast_to(total, (64, 128))
        sg0[4:5, :] = jnp.transpose(bias_cols[0])[0:1, :]

    def head_sums(grads_t):
        lanes = lax.broadcasted_iota(jnp.int32, (64, 128), 1)
        dq_sum = jnp.sum(grads_t[0:64, :].astype(F32), axis=1, keepdims=True)
        dv_sum = jnp.sum(grads_t[128:192, :].astype(F32), axis=1, keepdims=True)
        bias_cols[0] = jnp.zeros((width, 128), F32)
        bias_cols[0, own_head, :] = jnp.where(lanes == 0, dq_sum, dv_sum)
        tg0[...] = jnp.transpose(bias_cols[0])[0:8, :]

    def small(name, src, dst, device):
        send(name, src, dst, device)
        sent_later(name, dst)

    def small_add(name, arrived, mine, total):
        landed(name, arrived)
        total[...] = mine[...] + arrived[...]

    def small_z(name, src, dst):
        for k in range(3):
            send(name, src, dst.at[2 - k], (c, at(z_peers[k], y, x)))
        sent_later(name, dst)

    def small_out():
        landed("s3", sr3)
        sg4[...] = sg3[...] + sr3[0] + sr3[1] + sr3[2]
        landed("t3", tr3)
        sg4[0:2, :] = (tg3[...] + tr3[0] + tr3[1] + tr3[2])[0:2, :]
        block = c * 16 + seq
        tile_of = sg4[:, pl.ds(pl.multiple_of((block // 8) * 128, 128), 128)]
        turned = pltpu.roll(tile_of, lax.rem(128 - lax.rem(block, 8) * 16, 128), 1)
        o_bias[...] = turned[0:7, 0:16]
        o_gain[...] = turned[11:14, 0:16]
        o_shift[...] = turned[14:17, 0:16]
        o_omega[...] = turned[17:20, 0:16]
        tile_of = sg4[:, pl.ds(pl.multiple_of((lax.rem(block, 8) // 2) * 128, 128), 128)]
        turned = pltpu.roll(tile_of, lax.rem(block, 2) * 64, 1)
        wanted = block // 8
        row = jnp.zeros((1, 64), F32)
        for k in range(4):
            row = row + turned[7 + k : 8 + k, 0:64] * (wanted == k).astype(F32)
        o_upb[...] = row
        ends = ((o_bias, h_bias), (o_upb, h_upb), (o_gain, h_gain_o), (o_shift, h_shift_o), (o_omega, h_omega_o))
        for i, (src, dst) in enumerate(ends):
            keep("e" + str(4 + i), src, dst)

    raw = ((raw_tm, tgt_msk), (raw_sm, src_msk), (raw_tl, tgt_len), (raw_sl, src_len))
    for i, (ref, given) in enumerate(raw):
        keep("raw" + str(i), given, ref)
    given = ((h_biases, biases), (h_up_bias, up_bias), (h_gain, gain), (h_shift, shift), (h_omega, omega))
    for i, (src, ref) in enumerate(given):
        keep("given" + str(i), src, ref)
    barrier = pltpu.get_barrier_semaphore()
    greet = [(cc, at(z, yy, xx)) for cc, yy, xx in plane_peers]
    greet += [(cc, at(zz, y, x)) for zz in z_peers for cc in (c, 1 - c)]
    for device in greet:
        pl.semaphore_signal(barrier, inc=1, device_id=device, device_id_type=MESH)
    pl.semaphore_wait(barrier, len(greet))
    to_plane("x", tok, all_tok, True)
    slice_1("w0", s_in.at[0], ws0)
    slice_1("w1", s_in.at[1, pl.ds(1, 2)], ws1)
    for i, (ref, _) in enumerate(raw):
        landed("raw" + str(i), ref)
        span = ref.shape[2]
        for m in range(2):
            for start in (0, 64):
                meta[m, i : i + 1, start : start + span] = ref[m]
    to_plane("meta", meta, in_meta)
    slice_2("w0", ws0)
    gather_z("out0")
    gather_z("q")
    to_plane("m", mem, all_mem, True)
    spread_1("x", all_tok, 0)
    spread_1("x", all_tok, 1)
    slice_2("w1", ws1)
    gather_z("up0")
    gather_z("up1")
    gather_z("dn0")
    gather_z("dn1")
    gather_z("out1")
    to_plane("cot", cot, in_cot)
    for i, (_, ref) in enumerate(given):
        landed("given" + str(i), ref)
    for i, row in enumerate((0, 1, 4)):
        bias_cols[i] = jnp.transpose(jnp.broadcast_to(bias(row), (128, width)))
    landed("meta", in_meta)
    lane = lax.broadcasted_iota(jnp.int32, (8, 128), 1)
    all_meta[me_slot] = jnp.where(lane < 64, in_meta[0], in_meta[1])
    for cc, yy, xx in plane_peers:
        send("marks", all_meta.at[me_slot], all_meta.at[me_slot], (cc, at(z, yy, xx)))
    sent_later("marks", all_meta.at[pl.ds(0, 7)])
    spread_2("x", all_tok, 0)
    slice_f("w0", ws0)
    spread_2("x", all_tok, 1)
    slice_3("w0", ws0)
    gather_f("out0")
    gather_f("q")
    slice_4("w0", ws0)
    heads_weights(0, ws0)
    spread_3("x", all_tok)
    project_heads(all_tok, 0, qt0, k0, kt0, v0, vt0)
    gather_1("out0")
    gather_1("q")
    make_masks()
    gather_2("out0")
    gather_2("q")
    attend(qt0, k0, vt0, pt0, l0, ot0, True, "x3", a3, b3)
    slice_f("w1", ws1)
    gather_3("out0")
    gather_3("q")
    spread_1("m", all_mem, 0)
    spread_1("m", all_mem, 1)
    slice_3("w1", ws1)
    gather_f("up0")
    slice_4("w1", ws1)
    heads_weights(3, ws1)
    gathered("out0")
    landed("x3", b3)
    words_f = all_tok[me_slot].reshape(here, width).astype(F32)
    branch = tn(b3[...].reshape(width, here), matrix(w_out.at[0])) + bias(2)
    h1, scale0 = norm(words_f * omega[0:1, :] + branch, 0, xh0)
    h1_f[...] = h1
    h1_low = h1.astype(BF16)
    gathered("q")
    by_head(a4, nn(h1_low, matrix(w_q.at[0])) + bias(3))
    to_heads("x4", a4, b4)
    spread_2("m", all_mem, 0)
    gather_f("up1")
    gather_1("up0")
    spread_2("m", all_mem, 1)
    gather_f("dn0")
    gather_1("up1")
    spread_3("m", all_mem)
    project_heads(all_mem, 3, None, k1, kt1, v1, vt1)
    landed("x4", b4)
    for s in range(GROUP):
        qt1[:, s * here : (s + 1) * here] = (b4[s].astype(F32) * 0.125).astype(BF16)
    gather_2("up0")
    gather_f("dn1")
    gather_f("out1")
    attend(qt1, k1, vt1, pt1, l1, ot1, False, "x5", a5, b5)
    gather_1("out1")
    gather_2("up1")
    gather_1("dn0")
    gather_3("up0")
    gather_1("dn1")
    gather_2("out1")
    gather_3("up1")
    gather_3("out1")
    gathered("out1")
    landed("x5", b5)
    branch = tn(b5[...].reshape(width, here), matrix(w_out.at[1])) + bias(5)
    h2, scale1 = norm(h1_f[...] * omega[1:2, :] + branch, 1, xh1)
    h2_f[...] = h2
    h2_low = h2.astype(BF16)
    gather_2("dn0")
    gather_2("dn1")
    gathered("up0")
    feed_up(h2_low, 0)
    gathered("up1")
    feed_up(h2_low, 1)
    gather_3("dn0")
    gather_3("dn1")
    gathered("dn0")
    first = nn(act[...], matrix(w_dn.at[0]))
    gathered("dn1")
    second = nn(act[...], matrix(w_dn.at[1]))
    h3, scale2 = norm(h2_f[...] * omega[2:3, :] + jnp.concatenate([first, second], axis=1) + bias(6), 2, xh2)
    out_res[...] = h3.astype(BF16).reshape(2, 64, width)
    from_plane("res", out_res, o_res)
    landed("cot", in_cot)
    grad = in_cot[...].reshape(here, width).astype(F32)
    dr, skip = norm_back(grad, 2, xh2, scale2, h2_f[...])
    gf = dr.astype(BF16)
    column(6, gf.astype(F32))
    put(g_dn.at[0], tn(act[...], gf[:, 0:256]))
    scatter_0("dn0")
    put(g_dn.at[1], tn(act[...], gf[:, 256:512]))
    scatter_0("dn1")
    back = feed_back(gf, skip)
    dr, skip = norm_back(back, 1, xh1, scale1, h1_f[...])
    gc = dr.astype(BF16)
    column(5, gc.astype(F32))
    by_head(a6, nt(gc, matrix(w_out.at[1])))
    to_heads("x6", a6, b6)
    back = skip
    scatter_1("dn0")
    put(g_up.at[0], tn(h2_low, gul[:, 0:1024]))
    scatter_0("up0")
    scatter_1("dn1")
    put(g_up.at[1], tn(h2_low, gul[:, 1024:2048]))
    scatter_0("up1")
    landed("x6", b6)
    attend_back(b6, qt1, kt1, v1, pt1, l1, ot1, False, "x7", a7, b7)
    dt1[0:64, :] = acc_k[...].astype(BF16)
    dt1[64:128, :] = acc_v[...].astype(BF16)
    rows_back(dt1, 3, dx1, 1 - c)
    merge_0("dm", dx1, dc1)
    scatter_1("up0")
    rows_back(dt1, 3, dx1, c)
    slices_back(dt1, all_mem, gs1)
    unslice_0("u1", gs1, cs1)
    value_sums(dt1)
    put(g_out.at[1], nn(b5[...].reshape(width, here), gc))
    scatter_0("out1")
    landed("x7", b7)
    dq = b7[...].reshape(width, here)
    dq_row = flip(dq)
    column(3, dq_row)
    back = back + nt(dq_row.astype(BF16), matrix(w_q.at[0]))
    dr, skip = norm_back(back, 0, xh0, scale0, words_f)
    ga = dr.astype(BF16)
    column(2, ga.astype(F32))
    by_head(a8, nt(ga, matrix(w_out.at[0])))
    to_heads("x8", a8, b8)
    last = skip
    small("s0", sg0, sr0, core_next)
    merge_1("dm", dx1, dc1, dp1)
    put(g_out.at[0], nn(b3[...].reshape(width, here), ga))
    scatter_0("out0")
    put(g_q.at[0], nt(flip(h1_low).astype(BF16), dq))
    scatter_0("q")
    small_add("s0", sr0, sg0, sg1)
    small("s1", sg1, sr1, y_next)
    unslice_1("u1", gs1, cs1, zs1)
    landed("x8", b8)
    scatter_1("up1")
    scatter_2("dn0")
    scatter_2("dn1")
    attend_back(b8, qt0, kt0, v0, pt0, l0, ot0, True, None, None, None)
    dt0[64:128, :] = acc_k[...].astype(BF16)
    dt0[128:192, :] = acc_v[...].astype(BF16)
    rows_back(dt0, 0, dx0, 1 - c)
    merge_0("dx", dx0, dc0)
    head_sums(dt0)
    small("t0", tg0, tr0, core_next)
    rows_back(dt0, 0, dx0, c)
    merge_1("dx", dx0, dc0, dp0)
    small_add("t0", tr0, tg0, tg1)
    small("t1", tg1, tr1, y_next)
    slices_back(dt0, all_tok, gs0)
    unslice_0("u0", gs0, cs0)
    small_add("s1", sr1, sg1, sg2)
    small("s2", sg2, sr2, x_next)
    scatter_1("out1")
    scatter_1("out0")
    scatter_1("q")
    scatter_2("up0")
    scatter_2("up1")
    out_mem[...] = merge_2("dm", dx1, dp1).astype(BF16).reshape(2, 64, width)
    from_plane("gmem", out_mem, o_mem)
    scatter_3("dn0")
    scatter_3("dn1")
    unslice_1("u0", gs0, cs0, zs0)
    small_add("t1", tr1, tg1, tg2)
    small("t2", tg2, tr2, x_next)
    out_tok[...] = (merge_2("dx", dx0, dp0) + last).astype(BF16).reshape(2, 64, width)
    from_plane("gtok", out_tok, o_tok)
    scatter_2("out1")
    scatter_2("out0")
    scatter_2("q")
    unslice_2("u1", gs1, zs1, fs1, o_in.at[1, pl.ds(1, 2)])
    small_add("s2", sr2, sg2, sg3)
    small_z("s3", sg3, sr3)
    small_add("t2", tr2, tg2, tg3)
    small_z("t3", tg3, tr3)
    unslice_2("u0", gs0, zs0, fs0, o_in.at[0])
    scatter_3("up0")
    scatter_3("up1")
    scatter_3("out1")
    scatter_3("out0")
    scatter_3("q")
    scattered("dn0")
    scattered("dn1")
    keep("e3", o_dn, h_dn)
    small_out()
    scattered("up0")
    scattered("up1")
    keep("e2", o_up, h_up)
    scattered("out1")
    scattered("out0")
    scattered("q")
    keep("e1", o_out, h_out)
    unslice_3("u1", o_in.at[1, pl.ds(1, 2)])
    unslice_3("u0", o_in.at[0])
    keep("e0", o_in, h_in)
    landed("res", o_res)
    landed("gmem", o_mem)
    landed("gtok", o_tok)
    for i, ref in enumerate((h_in, h_out, h_up, h_dn, h_bias, h_upb, h_gain_o, h_shift_o, h_omega_o)):
        landed("e" + str(i), ref)
    for semaphore, ref, when in pending:
        if when is None:
            wait(semaphore, ref)
        else:

            @pl.when(when)
            def _():
                wait(semaphore, ref)

    for i, total in enumerate(bins):
        if total:
            wait(ss.at[i], gauge.at[pl.ds(0, total // 1024)])
    units = line_bytes[0] // UNIT
    assert line_bytes[0] % UNIT == 0

    @pl.when(edge)
    def _():
        wait(ss.at[BINS], gauge.at[pl.ds(0, 2 * units * 16)])

    @pl.when(jnp.logical_not(edge))
    def _():
        wait(ss.at[BINS], gauge.at[pl.ds(0, 4 * units * 16)])

    assert len(names) <= NAMES and len(bins) <= BINS and BINS + 1 + len(odd) <= ss.shape[0]


def copy_kernel(*refs):
    count = len(refs) // 2
    for i in range(count):
        refs[count + i][...] = refs[i][...]


def fused_local(
    tokens, memory, cotangent, tgt_lengths, src_lengths, tgt_mask, src_mask, attn_in, attn_out, w_up, w_down,
    biases, up_bias, norm_gain, norm_shift, omega,
):
    any_space = pl.BlockSpec(memory_space=pl.ANY)
    vmem = pl.BlockSpec(memory_space=pltpu.VMEM)
    lines = (CORES, PLANES, YS, XS)
    leads = {"q": 1, "out": 2, "up": 2, "dn": 2}
    shards = {"q": (16, 512), "out": (16, 512), "up": (16, 1024), "dn": (64, 256)}
    kinds = tuple(leads)

    def low(*shape):
        return pltpu.VMEM(shape, BF16)

    def full(*shape):
        return pltpu.VMEM(shape, F32)

    def whole(k):
        return low(leads[k], *lines, *shards[k])

    def halved(k, *middle):
        return low(2, leads[k], *middle, shards[k][0], shards[k][1] // 2)

    params = [full(7, 512), full(1, 2048), full(3, 512), full(3, 512), full(3, 512)]
    results = [(2, 3, 16, 512), (2, 16, 512), (1, 16, 2048), (1, 64, 512), (7, 16), (1, 64), (3, 16), (3, 16), (3, 16)]
    scratch = params + [full(*shape) for shape in results]
    scratch += [whole(k) for k in kinds] * 2
    scratch += [low(leads[k], *lines[1:], *shards[k]) for k in kinds]
    scratch += [halved(k, PLANES, 2) for k in kinds] + [halved(k, PLANES) for k in kinds]
    scratch += [low(3, leads[k], *shards[k]) for k in kinds]
    scratch += [low(n, CORES, PLANES, 4, 16, 128) for n in (3, 2)] * 2
    scratch += [low(n, PLANES, 4, 16, 128) for n in (3, 2)] + [low(3, n, 4, 16, 128) for n in (3, 2)]
    scratch += [full(n, 4, 16, 128) for n in (3, 2)]
    local_rows = low(2, 64, 512)
    marks = [pltpu.VMEM((2, 1, n), jnp.int32) for n in (32, 32, 64, 64)] + [pltpu.VMEM((2, 8, 128), jnp.int32)] * 2
    scratch += [low(GROUP, 2, 64, 512)] * 2 + [local_rows] + marks + [pltpu.VMEM((GROUP, 8, 128), jnp.int32)]
    scratch += [low(GROUP, 2, 64, 512)] * 2 + [low(4, 2, 64, 512)] * 2 + [low(3, 2, 64, 512)] * 2
    scratch += [low(GROUP, 64, 128)] * 12 + [local_rows] * 3
    scratch += [full(24, 512)] * 8 + [full(3, 24, 512)]
    scratch += [full(8, 512)] * 7 + [full(3, 8, 512)]
    scratch += [full(1024, 128)] * 3 + [full(8, 1024)]
    scratch += ([low(64, 1024)] * 3 + [low(1024, 64)] * 2 + [low(1024, 1024), full(1, 1024), full(64, 1024)]) * 2
    scratch += [low(64, 1024)] + [full(64, 1024)] * 2
    scratch += [low(128, 2048), full(128, 2048), low(128, 2048)] + [full(128, 512)] * 5
    scratch += [low(5, 128, 512), full(3, 512, 128), full(3, 128, 512), low(192, 1024), low(128, 1024), low(2048, 512)]
    scratch += [pltpu.SemaphoreType.DMA((36,)), pltpu.SemaphoreType.DMA((NAMES,))]
    rows = jax.ShapeDtypeStruct((2, 64, 512), BF16)

    def wide_out(*shape):
        return jax.ShapeDtypeStruct(shape, F32)

    outs = pl.pallas_call(
        fused_kernel,
        name="layer",
        out_shape=(rows, rows, rows, *(wide_out(*shape) for shape in results)),
        in_specs=[any_space] * 16,
        out_specs=(any_space,) * 12,
        scratch_shapes=scratch,
        compiler_params=pltpu.CompilerParams(collective_id=0, has_side_effects=True, vmem_limit_bytes=60 * 1024 * 1024),
    )(
        tokens.reshape(2, 64, 512), memory.reshape(2, 64, 512), cotangent.reshape(2, 64, 512),
        tgt_lengths, src_lengths, jnp.transpose(tgt_mask, (0, 2, 1)), jnp.transpose(src_mask, (0, 2, 1)),
        attn_in, attn_out, w_up.reshape(1, 16, 2048), w_down.reshape(1, 64, 512),
        biases, up_bias.reshape(1, 2048), norm_gain, norm_shift, omega,
    )
    outs = pl.pallas_call(
        copy_kernel,
        name="hand_over",
        out_shape=tuple(jax.ShapeDtypeStruct(out.shape, out.dtype) for out in outs),
        in_specs=[vmem] * len(outs),
        out_specs=(vmem,) * len(outs),
    )(*outs)
    shaped = [out.reshape(2, 64, 1, 512) for out in outs[:3]]
    return (
        *shaped, outs[3], outs[4], outs[5].reshape(16, 2048), outs[6].reshape(64, 512), outs[7], outs[8].reshape(64),
        outs[9], outs[10], outs[11],
    )


def solution(mesh):
    if mesh.shape["seq"] != PLANES * YS * XS or mesh.shape["rows"] != CORES:
        return general(mesh)
    return over(mesh, fused_local)
```

```python
import functools
import math

import jax
import jax.numpy as jnp
from jax import lax
from jax.experimental import pallas as pl
from jax.experimental.pallas import tpu as pltpu
from jax.sharding import PartitionSpec as P

HEADS = 8


def norm_block(branch, skip, scale, gain, shift):
    mixed = skip * scale + branch
    centered = mixed - jnp.mean(mixed, axis=-1, keepdims=True)
    variance = jnp.mean(centered * centered, axis=-1, keepdims=True)
    return centered * lax.rsqrt(variance + 1e-05) * gain + shift


def project(values, matrix):
    return jnp.einsum("trd,de->tre", values, matrix, preferred_element_type=jnp.float32)


def project_back(grads, matrix):
    return jnp.einsum("tre,de->trd", grads, matrix, preferred_element_type=jnp.float32)


def matrix_grad(values, grads):
    return jnp.einsum("trd,tre->de", values, grads, preferred_element_type=jnp.float32)


def column_sum(grads):
    return jnp.sum(grads.astype(jnp.float32), axis=(0, 1))


def segment_of(positions, ends):
    return jnp.sum((ends[None, :, :] <= positions[:, None, None]).astype(jnp.int32), axis=-1)


def segment_bounds(first, last, ends):
    lowest = jnp.sum((ends <= first).astype(jnp.int32), axis=-1)
    highest = jnp.sum((ends <= last).astype(jnp.int32), axis=-1)
    return (lowest, highest)


def ranges_share(query_bounds, key_bounds):
    return jnp.any((key_bounds[0] <= query_bounds[1]) & (key_bounds[1] >= query_bounds[0]))


def key_status(positions, real_marks, ends, starts, causal):
    segments = segment_of(positions, ends)
    usable = real_marks > 0.5
    if not causal:
        usable = usable | jnp.any(starts[None, :, :] == positions[:, None, None], axis=-1)
    return (segments, usable)


def permitted(query_pos, query_seg, key_pos, key_seg, usable, causal):
    same = jnp.transpose(query_seg)[:, :, None] == jnp.transpose(key_seg)[:, None, :]
    usable_keys = jnp.transpose(usable)[:, None, :]
    if causal:
        before = (key_pos[None, :] <= query_pos[:, None])[None]
        itself = (key_pos[None, :] == query_pos[:, None])[None]
        return same & before & (usable_keys | itself)
    return same & usable_keys


def block_grads(query_heads, grad_heads, lambdas, key_heads, value_heads, permit):
    scores = (
        jnp.einsum("arhd,brhd->rhab", query_heads, key_heads, preferred_element_type=jnp.float32)
        * 0.125
    )
    weights = jnp.where(permit[:, None], jnp.exp(scores), 0.0)
    spread = jnp.einsum(
        "arhd,brhd->rhab", grad_heads, value_heads, preferred_element_type=jnp.float32
    )
    slopes = weights * (spread + jnp.transpose(lambdas, (1, 2, 0))[..., None])
    return (weights.astype(jnp.bfloat16), slopes.astype(jnp.bfloat16))


def local(
    tokens,
    memory,
    cotangent,
    tgt_lengths,
    src_lengths,
    tgt_mask,
    src_mask,
    attn_in,
    attn_out,
    w_up,
    w_down,
    biases,
    up_bias,
    norm_gain,
    norm_shift,
    omega,
):
    micro_count, tokens_here, rows_here, width = tokens.shape
    head_size = width // HEADS
    my_pos = lax.axis_index("seq") * tokens_here + jnp.arange(tokens_here, dtype=jnp.int32)
    my_first = my_pos[0]
    my_last = my_pos[tokens_here - 1]

    def split_heads(values):
        return values.reshape(values.shape[0], rows_here, HEADS, head_size)

    def zero_heads():
        return jnp.zeros((tokens_here, rows_here, HEADS, head_size), jnp.float32)

    results = []
    grads_words = []
    grads_sources = []
    shares_all = None
    for micro_index in range(micro_count):
        in_weights = lax.all_gather(attn_in, ("rows", "seq"), axis=2, tiled=True)
        out_weights = lax.all_gather(attn_out, ("rows", "seq"), axis=1, tiled=True)
        up_weights = lax.all_gather(w_up, ("rows", "seq"), axis=0, tiled=True)
        down_weights = lax.all_gather(w_down, ("rows", "seq"), axis=0, tiled=True)
        words = tokens[micro_index]
        sources = memory[micro_index]
        words_full = words.astype(jnp.float32)
        tgt_len = tgt_lengths[micro_index]
        src_len = src_lengths[micro_index]
        tgt_ends = jnp.cumsum(tgt_len, axis=-1)
        src_ends = jnp.cumsum(src_len, axis=-1)
        src_starts = src_ends - src_len
        query_seg = segment_of(my_pos, tgt_ends)
        query_bounds = segment_bounds(my_first, my_last, tgt_ends)
        tgt_real = tgt_mask[micro_index].astype(jnp.bfloat16)
        src_real = src_mask[micro_index].astype(jnp.bfloat16)

        def attend(queries, keys, values, real_marks, ends, starts, causal):
            full_keys, full_values, full_real = (
                lax.all_gather(keys, "seq", axis=0, tiled=True),
                lax.all_gather(values, "seq", axis=0, tiled=True),
                lax.all_gather(real_marks, "seq", axis=0, tiled=True),
            )
            length = full_keys.shape[0]
            block = math.gcd(length, 512)
            query_heads = split_heads(queries)

            def step(carry, block_index):
                begin = block_index * block
                shares = ranges_share(query_bounds, segment_bounds(begin, begin + block - 1, ends))

                def step_compute(state):
                    totals, accum = state
                    key_heads = split_heads(lax.dynamic_slice_in_dim(full_keys, begin, block, 0))
                    value_heads = split_heads(
                        lax.dynamic_slice_in_dim(full_values, begin, block, 0)
                    )
                    key_pos = begin + jnp.arange(block, dtype=jnp.int32)
                    key_seg, usable = key_status(
                        key_pos,
                        lax.dynamic_slice_in_dim(full_real, begin, block, 0),
                        ends,
                        starts,
                        causal,
                    )
                    permit = permitted(my_pos, query_seg, key_pos, key_seg, usable, causal)
                    scores = (
                        jnp.einsum(
                            "trhd,krhd->rhtk",
                            query_heads,
                            key_heads,
                            preferred_element_type=jnp.float32,
                        )
                        * 0.125
                    )
                    weights = jnp.where(permit[:, None], jnp.exp(scores), 0.0)
                    totals = totals + jnp.sum(weights, axis=-1)
                    accum = accum + jnp.einsum(
                        "rhtk,krhd->trhd",
                        weights.astype(jnp.bfloat16),
                        value_heads,
                        preferred_element_type=jnp.float32,
                    )
                    return (totals, accum)

                return (lax.cond(shares, step_compute, lambda unchanged: unchanged, carry), None)

            start_carry = (jnp.zeros((rows_here, HEADS, tokens_here), jnp.float32), zero_heads())
            (totals, accum), unused = lax.scan(
                step, start_carry, jnp.arange(length // block, dtype=jnp.int32)
            )
            sums = jnp.transpose(totals, (2, 0, 1))
            output = (accum / sums[..., None]).reshape(tokens_here, rows_here, width)
            return (output, sums, (full_keys, full_values, full_real))

        def attention_back(
            grad_out,
            output,
            sums,
            queries,
            keys,
            values,
            real_marks,
            gathered_set,
            ends,
            starts,
            causal,
        ):
            full_keys, full_values, full_real = gathered_set
            grad_heads = split_heads(grad_out)
            lambdas = -jnp.sum(grad_heads * split_heads(output), axis=-1) / sums
            scaled = (grad_heads / sums[..., None]).astype(jnp.bfloat16)
            query_heads = split_heads(queries)
            length = full_keys.shape[0]
            block = math.gcd(length, 512)

            def query_step(accum, block_index):
                begin = block_index * block
                shares = ranges_share(query_bounds, segment_bounds(begin, begin + block - 1, ends))

                def query_compute(state):
                    key_heads = split_heads(lax.dynamic_slice_in_dim(full_keys, begin, block, 0))
                    value_heads = split_heads(
                        lax.dynamic_slice_in_dim(full_values, begin, block, 0)
                    )
                    key_pos = begin + jnp.arange(block, dtype=jnp.int32)
                    key_seg, usable = key_status(
                        key_pos,
                        lax.dynamic_slice_in_dim(full_real, begin, block, 0),
                        ends,
                        starts,
                        causal,
                    )
                    permit = permitted(my_pos, query_seg, key_pos, key_seg, usable, causal)
                    weights, slopes = block_grads(
                        query_heads, scaled, lambdas, key_heads, value_heads, permit
                    )
                    return (
                        state
                        + jnp.einsum(
                            "rhab,brhd->arhd", slopes, key_heads, preferred_element_type=jnp.float32
                        )
                        * 0.125
                    )

                return (lax.cond(shares, query_compute, lambda unchanged: unchanged, accum), None)

            grad_query, unused = lax.scan(
                query_step, zero_heads(), jnp.arange(length // block, dtype=jnp.int32)
            )
            all_lambdas = lax.all_gather(lambdas, "seq", axis=0, tiled=True)
            local_seg, local_usable = key_status(my_pos, real_marks, ends, starts, causal)
            local_bounds = segment_bounds(my_first, my_last, ends)
            local_keys = split_heads(keys)
            local_values = split_heads(values)
            query_piece = lax.all_gather(queries, "seq", axis=0, tiled=True)
            scaled_piece = lax.all_gather(
                scaled.reshape(tokens_here, rows_here, width), "seq", axis=0, tiled=True
            )
            size = query_piece.shape[0]
            inner = math.gcd(size, 512)

            def inner_step(inner_carry, inner_index):
                offset = inner_index * inner
                piece_first = offset
                shares = ranges_share(
                    segment_bounds(piece_first, piece_first + inner - 1, tgt_ends), local_bounds
                )

                def inner_compute(state):
                    acc_key, acc_value = state
                    query_blk = split_heads(lax.dynamic_slice_in_dim(query_piece, offset, inner, 0))
                    scaled_blk = split_heads(
                        lax.dynamic_slice_in_dim(scaled_piece, offset, inner, 0)
                    )
                    lambda_blk = lax.dynamic_slice_in_dim(all_lambdas, piece_first, inner, 0)
                    query_pos = piece_first + jnp.arange(inner, dtype=jnp.int32)
                    permit = permitted(
                        query_pos,
                        segment_of(query_pos, tgt_ends),
                        my_pos,
                        local_seg,
                        local_usable,
                        causal,
                    )
                    weights, slopes = block_grads(
                        query_blk, scaled_blk, lambda_blk, local_keys, local_values, permit
                    )
                    acc_key = (
                        acc_key
                        + jnp.einsum(
                            "rhab,arhd->brhd", slopes, query_blk, preferred_element_type=jnp.float32
                        )
                        * 0.125
                    )
                    acc_value = acc_value + jnp.einsum(
                        "rhab,arhd->brhd", weights, scaled_blk, preferred_element_type=jnp.float32
                    )
                    return (acc_key, acc_value)

                return (
                    lax.cond(shares, inner_compute, lambda unchanged: unchanged, inner_carry),
                    None,
                )

            folded, unused_inner = lax.scan(
                inner_step, (zero_heads(), zero_heads()), jnp.arange(size // inner, dtype=jnp.int32)
            )
            grad_key, grad_value = folded
            grad_key = grad_key.reshape(tokens_here, rows_here, width)
            grad_value = grad_value.reshape(tokens_here, rows_here, width)
            return (grad_query.reshape(tokens_here, rows_here, width), grad_key, grad_value)

        self_query = (project(words, in_weights[0, 0]) + biases[0]).astype(jnp.bfloat16)
        self_key = project(words, in_weights[0, 1]).astype(jnp.bfloat16)
        self_value = (project(words, in_weights[0, 2]) + biases[1]).astype(jnp.bfloat16)
        heard, heard_sums, self_set = attend(
            self_query, self_key, self_value, tgt_real, tgt_ends, None, True
        )
        heard_low = heard.astype(jnp.bfloat16)
        branch_self = project(heard_low, out_weights[0]) + biases[2]
        hidden_one, pull_one = jax.vjp(
            norm_block, branch_self, words_full, omega[0], norm_gain[0], norm_shift[0]
        )
        hidden_one_low = hidden_one.astype(jnp.bfloat16)
        cross_query = (project(hidden_one_low, in_weights[1, 0]) + biases[3]).astype(jnp.bfloat16)
        cross_key = project(sources, in_weights[1, 1]).astype(jnp.bfloat16)
        cross_value = (project(sources, in_weights[1, 2]) + biases[4]).astype(jnp.bfloat16)
        recalled, recalled_sums, cross_set = attend(
            cross_query, cross_key, cross_value, src_real, src_ends, src_starts, False
        )
        recalled_low = recalled.astype(jnp.bfloat16)
        branch_cross = project(recalled_low, out_weights[1]) + biases[5]
        hidden_two, pull_two = jax.vjp(
            norm_block, branch_cross, hidden_one, omega[1], norm_gain[1], norm_shift[1]
        )
        hidden_two_low = hidden_two.astype(jnp.bfloat16)
        up_pre = project(hidden_two_low, up_weights) + up_bias
        active, pull_active = jax.vjp(jax.nn.gelu, up_pre)
        active_low = active.astype(jnp.bfloat16)
        branch_ffn = project(active_low, down_weights) + biases[6]
        outcome, pull_three = jax.vjp(
            norm_block, branch_ffn, hidden_two, omega[2], norm_gain[2], norm_shift[2]
        )
        grad_result = cotangent[micro_index].astype(jnp.float32)
        grad_ffn, grad_two, omega_three, gain_three, shift_three = pull_three(grad_result)
        grad_ffn_low = grad_ffn.astype(jnp.bfloat16)
        grad_down = matrix_grad(active_low, grad_ffn_low)
        bias_ffn = column_sum(grad_ffn_low)
        grad_up_pre = pull_active(project_back(grad_ffn_low, down_weights))[0].astype(jnp.bfloat16)
        grad_up = matrix_grad(hidden_two_low, grad_up_pre)
        bias_up = column_sum(grad_up_pre)
        grad_two = grad_two + project_back(grad_up_pre, up_weights)
        grad_cross, grad_one, omega_two, gain_two, shift_two = pull_two(grad_two)
        grad_cross_low = grad_cross.astype(jnp.bfloat16)
        grad_out_cross = matrix_grad(recalled_low, grad_cross_low)
        bias_out_cross = column_sum(grad_cross_low)
        grad_recalled = project_back(grad_cross_low, out_weights[1])
        cross_gq, cross_gk, cross_gv = attention_back(
            grad_recalled,
            recalled,
            recalled_sums,
            cross_query,
            cross_key,
            cross_value,
            src_real,
            cross_set,
            src_ends,
            src_starts,
            False,
        )
        cross_gq = cross_gq.astype(jnp.bfloat16)
        cross_gk = cross_gk.astype(jnp.bfloat16)
        cross_gv = cross_gv.astype(jnp.bfloat16)
        grad_cross_query = matrix_grad(hidden_one_low, cross_gq)
        grad_cross_key = matrix_grad(sources, cross_gk)
        grad_cross_value = matrix_grad(sources, cross_gv)
        grad_one = grad_one + project_back(cross_gq, in_weights[1, 0])
        grad_sources = project_back(cross_gk, in_weights[1, 1]) + project_back(
            cross_gv, in_weights[1, 2]
        )
        grad_self, grad_words, omega_one, gain_one, shift_one = pull_one(grad_one)
        grad_self_low = grad_self.astype(jnp.bfloat16)
        grad_out_self = matrix_grad(heard_low, grad_self_low)
        bias_out_self = column_sum(grad_self_low)
        grad_heard = project_back(grad_self_low, out_weights[0])
        self_gq, self_gk, self_gv = attention_back(
            grad_heard,
            heard,
            heard_sums,
            self_query,
            self_key,
            self_value,
            tgt_real,
            self_set,
            tgt_ends,
            None,
            True,
        )
        self_gq = self_gq.astype(jnp.bfloat16)
        self_gk = self_gk.astype(jnp.bfloat16)
        self_gv = self_gv.astype(jnp.bfloat16)
        grad_words = (
            grad_words
            + project_back(self_gq, in_weights[0, 0])
            + project_back(self_gk, in_weights[0, 1])
            + project_back(self_gv, in_weights[0, 2])
        )
        grad_in = jnp.stack(
            [
                jnp.stack(
                    [
                        matrix_grad(words, self_gq),
                        matrix_grad(words, self_gk),
                        matrix_grad(words, self_gv),
                    ]
                ),
                jnp.stack([grad_cross_query, grad_cross_key, grad_cross_value]),
            ]
        )
        grad_out = jnp.stack([grad_out_self, grad_out_cross])
        grad_bias = jnp.stack(
            [
                column_sum(self_gq),
                column_sum(self_gv),
                bias_out_self,
                column_sum(cross_gq),
                column_sum(cross_gv),
                bias_out_cross,
                bias_ffn,
            ]
        )
        grad_gain = jnp.stack([gain_one, gain_two, gain_three])
        grad_shift = jnp.stack([shift_one, shift_two, shift_three])
        grad_omega = jnp.stack([omega_one, omega_two, omega_three])
        grads = (
            grad_in,
            grad_out,
            grad_up,
            grad_down,
            grad_bias,
            bias_up,
            grad_gain,
            grad_shift,
            grad_omega,
        )
        outcome, grad_words, grad_sources, grads = (
            outcome.astype(jnp.bfloat16),
            grad_words.astype(jnp.bfloat16),
            grad_sources.astype(jnp.bfloat16),
            grads,
        )
        results.append(outcome)
        grads_words.append(grad_words)
        grads_sources.append(grad_sources)
        part_shares = (
            lax.psum_scatter(grads[0], ("rows", "seq"), scatter_dimension=2, tiled=True),
            lax.psum_scatter(grads[1], ("rows", "seq"), scatter_dimension=1, tiled=True),
            lax.psum_scatter(grads[2], ("rows", "seq"), scatter_dimension=0, tiled=True),
            lax.psum_scatter(grads[3], ("rows", "seq"), scatter_dimension=0, tiled=True),
            lax.psum_scatter(grads[4], ("rows", "seq"), scatter_dimension=1, tiled=True),
            lax.psum_scatter(grads[5], ("rows", "seq"), scatter_dimension=0, tiled=True),
            lax.psum_scatter(grads[6], ("rows", "seq"), scatter_dimension=1, tiled=True),
            lax.psum_scatter(grads[7], ("rows", "seq"), scatter_dimension=1, tiled=True),
            lax.psum_scatter(grads[8], ("rows", "seq"), scatter_dimension=1, tiled=True),
        )
        shares_all = (
            part_shares if shares_all is None else jax.tree.map(jnp.add, shares_all, part_shares)
        )
    return (jnp.stack(results), jnp.stack(grads_words), jnp.stack(grads_sources)) + tuple(
        shares_all
    )


def over(mesh, function):
    return jax.shard_map(
        function,
        mesh=mesh,
        in_specs=(
            P(None, "seq", "rows", None),
            P(None, "seq", "rows", None),
            P(None, "seq", "rows", None),
            P(None, "rows", None),
            P(None, "rows", None),
            P(None, "seq", "rows"),
            P(None, "seq", "rows"),
            P(None, None, ("rows", "seq"), None),
            P(None, ("rows", "seq"), None),
            P(("rows", "seq"), None),
            P(("rows", "seq"), None),
            P(),
            P(),
            P(),
            P(),
            P(),
        ),
        out_specs=(
            P(None, "seq", "rows", None),
            P(None, "seq", "rows", None),
            P(None, "seq", "rows", None),
            P(None, None, ("rows", "seq"), None),
            P(None, ("rows", "seq"), None),
            P(("rows", "seq"), None),
            P(("rows", "seq"), None),
            P(None, ("rows", "seq")),
            P(("rows", "seq")),
            P(None, ("rows", "seq")),
            P(None, ("rows", "seq")),
            P(None, ("rows", "seq")),
        ),
        check_vma=False,
    )


def general(mesh):
    return over(mesh, local)


MESH = pl.DeviceIdType.MESH
UNIT = 16 * 1024
BINS = 16
NAMES = 168
ODD = ("marks", "w0p", "w1p", "u0p")
F32 = jnp.float32
BF16 = jnp.bfloat16
PLANES, YS, XS, CORES = 4, 2, 2, 2
GROUP = YS * XS * CORES


def nn(left, right):
    return lax.dot_general(left, right, (((1,), (0,)), ((), ())), preferred_element_type=F32)


def nt(left, right):
    return lax.dot_general(left, right, (((1,), (1,)), ((), ())), preferred_element_type=F32)


def tn(left, right):
    return lax.dot_general(left, right, (((0,), (0,)), ((), ())), preferred_element_type=F32)


def flip(value):
    return jnp.transpose(value.astype(F32))


def fused_kernel(
    tok, mem, cot, tgt_len, src_len, tgt_msk, src_msk, s_in, s_out, s_up, s_dn, h_biases, h_up_bias, h_gain, h_shift, h_omega,
    o_res, o_tok, o_mem, h_in, h_out, h_up, h_dn, h_bias, h_upb, h_gain_o, h_shift_o, h_omega_o,
    biases, up_bias, gain, shift, omega, o_in, o_out, o_up, o_dn, o_bias, o_upb, o_gain, o_shift, o_omega,
    w_q, w_out, w_up, w_dn, g_q, g_out, g_up, g_dn,
    c_q, c_out, c_up, c_dn,
    p_q, p_out, p_up, p_dn,
    q_q, q_out, q_up, q_dn,
    z_q, z_out, z_up, z_dn,
    ws0, ws1, gs0, gs1, cs0, cs1, zs0, zs1, fs0, fs1,
    all_tok, all_mem, in_cot, raw_tl, raw_sl, raw_tm, raw_sm, meta, in_meta, all_meta,
    dx0, dx1, dc0, dc1, dp0, dp1,
    a3, b3, a4, b4, a5, b5, a6, b6, a7, b7, a8, b8,
    out_res, out_tok, out_mem,
    sg0, sg1, sg2, sg3, sg4, sr0, sr1, sr2, sr3,
    tg0, tg1, tg2, tg3, tr0, tr1, tr2, tr3,
    code_self, code_cross, key_pos, rows_f,
    qt0, kt0, vt0, k0, v0, pt0, l0, ot0,
    qt1, kt1, vt1, k1, v1, pt1, l1, ot1,
    dnt, acc_k, acc_v,
    act, slope, gul, xh0, xh1, xh2, h1_f, h2_f,
    wt, bias_cols, wz, dt0, dt1, gauge,
    ss, rs,
):
    c = lax.axis_index("rows")
    seq = lax.axis_index("seq")
    z = seq // (YS * XS)
    yx = lax.rem(seq, YS * XS)
    y = yx // XS
    x = lax.rem(yx, XS)
    width = 512
    here = 2 * 64

    def at(zz, yy, xx):
        return zz * (YS * XS) + yy * XS + xx

    def slot(cc, yy, xx):
        return cc * 4 + yy * 2 + xx

    def head(cc, yy, xx):
        return (yy * 2 + xx) * 2 + cc

    me_slot, me_head = slot(c, y, x), head(c, y, x)
    plane_peers = []
    for k in range(1, GROUP):
        cc = 1 - c if k & 4 else c
        yy = 1 - y if k & 2 else y
        xx = 1 - x if k & 1 else x
        plane_peers.append((cc, yy, xx))
    trio = [(1 - y, x), (y, 1 - x), (1 - y, 1 - x)]
    z_peers = [lax.rem(z + k, PLANES) for k in (1, 2, 3)]

    names, expected_bytes = {}, {}
    pending = []
    edge = (z == 0) | (z == PLANES - 1)

    def sem(name):
        return names.setdefault(name, len(names))

    def wait(semaphore, ref):
        pltpu.make_async_copy(ref, ref, semaphore).wait()

    def size(ref):
        return math.prod(ref.shape) * jnp.dtype(ref.dtype).itemsize

    bins = [0]
    odd = {}

    def out_sem(name):
        return ss.at[odd.setdefault(name, BINS + 1 + len(odd))] if name in ODD else ss.at[len(bins) - 1]

    def send(name, src, dst, device, recv=None):
        pltpu.make_async_remote_copy(
            src_ref=src, dst_ref=dst, send_sem=out_sem(name), recv_sem=rs.at[sem(name)] if recv is None else recv,
            device_id=device, device_id_type=MESH,
        ).start()

    def keep(name, src, dst):
        pltpu.make_async_copy(src, dst, rs.at[sem(name)]).start()

    def landed(name, ref):
        wait(rs.at[sem(name)], ref)

    def sent_later(name, ref):
        if name in ODD:
            pending.append((ss.at[odd[name]], ref, None))
            return
        bins[-1] += size(ref)
        assert size(ref) % UNIT == 0, (name, size(ref))
        if bins[-1] > 1024 * UNIT // 16:
            bins.append(0)

    line_bytes = [0]

    def along_z(name, src, block):
        i, j = sem(name + "z"), sem(name + "f")
        for step in (1, -1, 2, -2):
            to = z + step
            far = (z == 0) if step == 2 else (z == PLANES - 1) if step == -2 else None

            @pl.when((to >= 0) & (to < PLANES))
            def _():
                pltpu.make_async_remote_copy(
                    src_ref=src, dst_ref=block(z), send_sem=ss.at[BINS],
                    recv_sem=rs.at[i] if far is None else rs.at[jnp.where(far, j, i)],
                    device_id=(c, at(to, y, x)), device_id_type=MESH,
                ).start()

        line_bytes[0] += size(src)

    def pass_on(name, block):
        for mine, origin, to in ((1, 3, 0), (2, 0, 3)):

            @pl.when(z == mine)
            def _():
                landed(name + "f", block(origin))
                pltpu.make_async_remote_copy(
                    src_ref=block(origin), dst_ref=block(origin), send_sem=ss.at[BINS], recv_sem=rs.at[sem(name + "z")],
                    device_id=(c, at(to, y, x)), device_id_type=MESH,
                ).start()

    def line_landed(name, blocks, own):
        @pl.when(edge)
        def _():
            landed(name + "z", blocks(3 + own))

        @pl.when(jnp.logical_not(edge))
        def _():
            landed(name + "z", blocks(2 + own))

    def to_plane(name, src, dst, slotted=False):
        half = lax.rem(z, 2)
        core = z // 2
        if slotted:
            recv = rs.at[jnp.where(half == 0, sem(name + "h0"), sem(name + "h1"))]
            part = dst.at[slot(core, y, x), half]
        else:
            recv = rs.at[sem(name)]
            part = dst.at[half]
        for m in range(2):
            plane = 2 * m + c
            own = (plane == z) & (core == c)
            out = ss.at[odd.setdefault(name + str(m), BINS + 1 + len(odd))]

            @pl.when(own)
            def _():
                pltpu.make_async_copy(src.at[m], part, recv).start()

            @pl.when(jnp.logical_not(own))
            def _():
                pltpu.make_async_remote_copy(
                    src_ref=src.at[m], dst_ref=part, send_sem=out, recv_sem=recv,
                    device_id=(core, at(plane, y, x)), device_id_type=MESH,
                ).start()

            pending.append((out, src.at[m], jnp.logical_not(own)))

    def from_plane(name, src, dst):
        micro, core = z // 2, lax.rem(z, 2)
        recv = rs.at[sem(name)]
        for half in range(2):
            zz = 2 * c + half
            own = (core == c) & (zz == z)
            part = dst.at[micro]
            out = ss.at[odd.setdefault(name + str(half), BINS + 1 + len(odd))]

            @pl.when(own)
            def _():
                pltpu.make_async_copy(src.at[half], part, recv).start()

            @pl.when(jnp.logical_not(own))
            def _():
                pltpu.make_async_remote_copy(
                    src_ref=src.at[half], dst_ref=part, send_sem=out, recv_sem=recv,
                    device_id=(core, at(zz, y, x)), device_id_type=MESH,
                ).start()

            pending.append((out, src.at[half], jnp.logical_not(own)))

    def to_heads(name, src, dst):
        keep(name, src.at[me_head], dst.at[me_slot])
        for cc, yy, xx in plane_peers:
            send(name, src.at[head(cc, yy, xx)], dst.at[me_slot], (cc, at(z, yy, xx)))
        sent_later(name, src.at[pl.ds(0, GROUP - 1)])

    def to_slot(name, src, dst, s):
        device = (s // 4, at(z, lax.rem(s, 4) // 2, lax.rem(s, 2)))
        i = sem(name)
        out = out_sem(name)

        @pl.when(s == me_slot)
        def _():
            pltpu.make_async_copy(src.at[s], dst.at[me_head], rs.at[i]).start()

        @pl.when(s != me_slot)
        def _():
            pltpu.make_async_remote_copy(
                src_ref=src.at[s], dst_ref=dst.at[me_head], send_sem=out, recv_sem=rs.at[i],
                device_id=device, device_id_type=MESH,
            ).start()

    weights = {
        "q": (w_q, s_in.at[1, pl.ds(0, 1)], g_q, c_q, p_q, q_q, z_q, o_in.at[1, pl.ds(0, 1)]),
    }

    for i in range(2):
        one = pl.ds(i, 1)
        refs = (w_out, s_out, g_out, c_out, p_out, q_out, z_out, o_out)
        weights["out" + str(i)] = tuple(
            ref.at[:, one] if ref is p_out or ref is q_out or ref is z_out else ref.at[one] for ref in refs
        )
        refs = (w_up, s_up, g_up, c_up, p_up, q_up, z_up, o_up)
        cols = pl.ds(i * 1024, 1024)
        weights["up" + str(i)] = tuple(
            ref.at[:, one] if ref is p_up or ref is q_up or ref is z_up
            else ref.at[:, :, cols] if ref is s_up or ref is o_up else ref.at[one]
            for ref in refs
        )
        refs = (w_dn, s_dn, g_dn, c_dn, p_dn, q_dn, z_dn, o_dn)
        cols = pl.ds(i * 256, 256)
        weights["dn" + str(i)] = tuple(
            ref.at[:, one] if ref is p_dn or ref is q_dn or ref is z_dn
            else ref.at[:, :, cols] if ref is s_dn or ref is o_dn else ref.at[one]
            for ref in refs
        )

    def halves(ref):
        cols = ref.shape[-1] // 2
        return pl.ds(0, cols), pl.ds(cols, cols)

    x_next, y_next, core_next = (c, at(z, y, 1 - x)), (c, at(z, 1 - y, x)), (1 - c, seq)

    def gather_z(g):
        full, shard = weights[g][:2]
        keep(g + "z", shard, full.at[:, c, z, y, x])
        along_z(g, shard, lambda zz: full.at[:, c, zz, y, x])

    def gather_f(g):
        full = weights[g][0]
        pass_on(g, lambda zz: full.at[:, c, zz, y, x])

    def gather_1(g):
        full = weights[g][0]
        first, second = halves(full)
        line_landed(g, lambda n: full.at[:, c, pl.ds(0, n), y, x], 1)
        part = full.at[:, c, :, y, x, :, first]
        send(g + "1a", part, part, x_next)
        sent_later(g + "1a", part)
        part = full.at[:, c, :, y, x, :, second]
        send(g + "1b", part, part, y_next)
        sent_later(g + "1b", part)

    def gather_2(g):
        full = weights[g][0]
        first, second = halves(full)
        landed(g + "1a", full.at[:, c, :, y, 1 - x, :, first])
        part = full.at[:, c, :, y, :, :, first]
        send(g + "2a", part, part, y_next)
        sent_later(g + "2a", part)
        landed(g + "1b", full.at[:, c, :, 1 - y, x, :, second])
        part = full.at[:, c, :, :, x, :, second]
        send(g + "2b", part, part, x_next)
        sent_later(g + "2b", part)

    def gather_3(g):
        full = weights[g][0]
        first, second = halves(full)
        landed(g + "2a", full.at[:, c, :, 1 - y, :, :, first])
        landed(g + "2b", full.at[:, c, :, :, 1 - x, :, second])
        send(g + "3", full.at[:, c], full.at[:, c], core_next)
        sent_later(g + "3", full.at[:, c])

    def gathered(g):
        landed(g + "3", weights[g][0].at[:, 1 - c])

    def add(target, other):
        target[...] = (target[...].astype(F32) + other[...].astype(F32)).astype(BF16)

    def scatter_0(g):
        grad, across = weights[g][2:4]
        send(g + "r0", grad.at[:, 1 - c], across, core_next)
        sent_later(g + "r0", across)

    def scatter_1(g):
        grad, across, part = weights[g][2:5]
        first, second = halves(grad)
        landed(g + "r0", across)
        for lead in range(grad.shape[0]):

            @pl.loop(0, PLANES)
            def _(zz):
                add(grad.at[lead, c, zz], across.at[lead, zz])

        send(g + "r1a", grad.at[:, c, :, 1 - y, :, :, first], part.at[0], y_next)
        sent_later(g + "r1a", part.at[0])
        send(g + "r1b", grad.at[:, c, :, :, 1 - x, :, second], part.at[1], x_next)
        sent_later(g + "r1b", part.at[1])

    def scatter_2(g):
        grad, _, part, piece = weights[g][2:6]
        first, second = halves(grad)
        landed(g + "r1a", part.at[0])
        landed(g + "r1b", part.at[1])
        for lead in range(grad.shape[0]):

            @pl.loop(0, PLANES)
            def _(zz):
                add(grad.at[lead, c, zz, y, :, :, first], part.at[0, lead, zz])
                add(grad.at[lead, c, zz, :, x, :, second], part.at[1, lead, zz])

        send(g + "r2a", grad.at[:, c, :, y, 1 - x, :, first], piece.at[0], x_next)
        sent_later(g + "r2a", piece.at[0])
        send(g + "r2b", grad.at[:, c, :, 1 - y, x, :, second], piece.at[1], y_next)
        sent_later(g + "r2b", piece.at[1])

    def scatter_3(g):
        grad, _, _, piece, line = weights[g][2:7]
        first, second = halves(grad)
        landed(g + "r2a", piece.at[0])
        landed(g + "r2b", piece.at[1])
        for lead in range(grad.shape[0]):

            @pl.loop(0, PLANES)
            def _(zz):
                add(grad.at[lead, c, zz, y, x, :, first], piece.at[0, lead, zz])
                add(grad.at[lead, c, zz, y, x, :, second], piece.at[1, lead, zz])

        for k in range(3):
            send(g + "r3", grad.at[:, c, z_peers[k], y, x], line.at[2 - k], (c, at(z_peers[k], y, x)))
        sent_later(g + "r3", line)

    def scattered(g):
        grad, _, _, _, line, result = weights[g][2:8]
        landed(g + "r3", line)
        total = grad[:, c, z, y, x].astype(F32)
        for k in range(3):
            total = total + line[k].astype(F32)
        result[...] = total

    def spread_1(name, full, half):
        own = full.at[me_slot, half]
        landed(name + "h" + str(half), own)
        for k, (yy, xx) in enumerate(trio):
            send(name + "p" + str(half) + str(k), own, own, (c, at(z, yy, xx)))
            sent_later(name + "p" + str(half) + str(k), own)
        send(name + "c", own, own, core_next)
        sent_later(name + "c", own)

    def spread_2(name, full, half):
        for k, (yy, xx) in enumerate(trio):
            part = full.at[slot(c, yy, xx), half]
            landed(name + "p" + str(half) + str(k), part)
            send(name + "d", part, part, core_next)
            sent_later(name + "d", part)

    def spread_3(name, full):
        landed(name + "c", full.at[0])
        landed(name + "d", full.at[pl.ds(0, 3)])

    def merge_0(name, full, across):
        send(name + "c", full.at[pl.ds((1 - c) * 4, 4)], across, core_next)
        sent_later(name + "c", across)

    def merge_1(name, full, across, parts):
        landed(name + "c", across)
        for k, (yy, xx) in enumerate(trio):
            place = slot(c, yy, xx)
            add(full.at[place], across.at[yy * 2 + xx])
            send(name + "p", full.at[place], parts.at[k], (c, at(z, yy, xx)))
        sent_later(name + "p", parts)
        add(full.at[me_slot], across.at[yx])

    def merge_2(name, full, parts):
        landed(name + "p", parts)
        total = full[me_slot].astype(F32)
        for k in range(3):
            total = total + parts[k].astype(F32)
        return total.reshape(here, width)

    def tile(index):
        return pl.ds(pl.multiple_of(index * 128, 128), 128)

    def slice_1(name, shard, full):
        keep(name + "p", shard.at[:, :, tile(yx)], full.at[:, c, z, yx])
        for yy, xx in trio:
            send(name + "p", shard.at[:, :, tile(yy * 2 + xx)], full.at[:, c, z, yx], (c, at(z, yy, xx)))
        sent_later(name + "p", full.at[:, c, z, pl.ds(0, 3)])

    def slice_2(name, full):
        landed(name + "p", full.at[:, c, z])
        along_z(name, full.at[:, c, z], lambda zz: full.at[:, c, zz])

    def slice_f(name, full):
        pass_on(name, lambda zz: full.at[:, c, zz])

    def slice_3(name, full):
        line_landed(name, lambda n: full.at[:, c, pl.ds(0, n)], 0)
        send(name + "c", full.at[:, c], full.at[:, c], core_next)
        sent_later(name + "c", full.at[:, c])

    def slice_4(name, full):
        landed(name + "c", full.at[:, 1 - c])

    def unslice_0(name, grad, across):
        send(name + "c", grad.at[:, 1 - c], across, core_next)
        sent_later(name + "c", across)

    def unslice_1(name, grad, across, line):
        landed(name + "c", across)
        for lead in range(grad.shape[0]):
            add(grad.at[lead, c], across.at[lead])
        for k in range(3):
            send(name + "z", grad.at[:, c, z_peers[k]], line.at[2 - k], (c, at(z_peers[k], y, x)))
        sent_later(name + "z", line)

    def unslice_2(name, grad, line, total, result):
        landed(name + "z", line)
        value = grad[:, c, z].astype(F32)
        for k in range(3):
            value = value + line[k].astype(F32)
        total[...] = value
        for yy, xx in trio:
            send(name + "p", total.at[:, yy * 2 + xx], result.at[:, :, tile(yx)], (c, at(z, yy, xx)))
        sent_later(name + "p", total.at[:, pl.ds(0, 3)])
        result[:, :, tile(yx)] = total[:, yx]

    def unslice_3(name, result):
        landed(name + "p", result.at[:, :, pl.ds(0, 384)])

    def matrix(ref):
        return ref[...].reshape(-1, ref.shape[-1])

    def put(ref, value):
        ref[...] = value.astype(BF16).reshape(ref.shape)

    def norm(r, i, kept):
        centered = r - jnp.mean(r, axis=1, keepdims=True)
        scale = lax.rsqrt(jnp.mean(centered * centered, axis=1, keepdims=True) + 1e-05)
        xhat = centered * scale
        kept[...] = xhat
        return xhat * gain[i : i + 1, :] + shift[i : i + 1, :], scale

    def column(row, value):
        sg0[row : row + 1, :] = jnp.sum(value, axis=0, keepdims=True)

    def norm_back(grad, i, kept, scale, skip):
        xhat = kept[...]
        column(11 + i, grad * xhat)
        column(14 + i, grad)
        dxhat = grad * gain[i : i + 1, :]
        dr = dxhat - jnp.mean(dxhat, axis=1, keepdims=True)
        dr = (dr - xhat * jnp.mean(dxhat * xhat, axis=1, keepdims=True)) * scale
        column(17 + i, dr * skip)
        return dr, dr * omega[i : i + 1, :]

    BLOCK = 256

    def attend(queries, keys, values_t, weights_t, sums, outputs, causal, name, target, arrives):
        def make(extent):
            def body(b):
                cols = pl.ds(pl.multiple_of(b * BLOCK, BLOCK), BLOCK)
                scores = nn(keys[:extent, :], queries[:, cols])
                seg = rows_f[0:1, cols]
                code = (code_self if causal else code_cross)[:extent, :]
                permit = jnp.concatenate([code, code], axis=1) == seg
                if causal:
                    pos = key_pos[:extent, :]
                    pos = jnp.concatenate([pos, pos], axis=1)
                    mine = rows_f[1:2, cols]
                    permit = (permit & (pos <= mine)) | (pos == mine)
                weight = jnp.where(permit, jnp.exp(scores), 0.0)
                total = jnp.sum(weight, axis=0, keepdims=True)
                low = weight.astype(BF16)
                weights_t[:extent, cols] = low
                out = nn(values_t[:, :extent], low) / total
                sums[0:1, cols] = total
                outputs[:, cols] = out
                for k in range(2):
                    target[2 * b + k] = out[:, k * here : (k + 1) * here].astype(BF16)
                    to_slot(name, target, arrives, 2 * b + k)

            return body

        if causal:
            pl.loop(0, 2)(make(512))
            pl.loop(2, 4)(make(1024))
        else:
            pl.loop(0, 4)(make(1024))
        sent_later(name, target.at[pl.ds(0, GROUP - 1)])

    def attend_back(buffer, queries, keys_t, values, weights_t, sums, outputs, causal, name, target, arrives):
        acc_k[...] = jnp.zeros_like(acc_k)
        acc_v[...] = jnp.zeros_like(acc_v)
        for s in range(GROUP):
            cols = slice(s * here, (s + 1) * here)
            grad = buffer[s].astype(F32)
            inverse = 1.0 / sums[0:1, cols]
            dnt[:, cols] = (grad * inverse).astype(BF16)
            rows_f[2:3, cols] = -jnp.sum(grad * outputs[:, cols], axis=0, keepdims=True) * inverse

        def make(extent):
            def body(b):
                cols = pl.ds(pl.multiple_of(b * BLOCK, BLOCK), BLOCK)
                low = weights_t[:extent, cols]
                dn = dnt[:, cols]
                spread = nn(values[:extent, :], dn)
                slopes = (low.astype(F32) * (spread + rows_f[2:3, cols])).astype(BF16)
                block = (nn(keys_t[:, :extent], slopes) * 0.125).astype(BF16)
                if name is None:
                    dt0[0:64, cols] = block
                else:
                    for k in range(2):
                        target[2 * b + k] = block[:, k * here : (k + 1) * here]
                        to_slot(name, target, arrives, 2 * b + k)
                acc_k[:, :extent] += nt(queries[:, cols], slopes)
                acc_v[:, :extent] += nt(dn, low)

            return body

        if causal:
            pl.loop(0, 2)(make(512))
            pl.loop(2, 4)(make(1024))
        else:
            pl.loop(0, 4)(make(1024))
        if name is not None:
            sent_later(name, target.at[pl.ds(0, GROUP - 1)])

    def by_head(target, value):
        target[...] = flip(value).astype(BF16).reshape(GROUP, 64, here)

    def heads_weights(first, full):
        for j in range(full.shape[0]):
            wt[first + j] = flip(matrix(full.at[j])).astype(BF16)

    own_rows = pl.ds(pl.multiple_of(c * 64, 64), 64)
    own_head = pl.ds(pl.multiple_of(me_head * 64, 64), 64)

    def own_weights(first, count):
        return jnp.concatenate([wt[first + j, own_rows, :] for j in range(count)], axis=0)

    def wide_bias(i):
        col = bias_cols[i, own_head, :]
        return jnp.concatenate([col, col], axis=1)

    def project_heads(rows, first, queries, keys, keys_t, values, values_t):
        count = 2 if queries is None else 3
        own = own_weights(first, count)
        for b in range(4):
            cols = slice(b * 256, (b + 1) * 256)
            out = nt(own, rows[2 * b : 2 * b + 2].reshape(256, width))
            if queries is not None:
                queries[:, cols] = ((out[0:64] + wide_bias(0)).astype(BF16).astype(F32) * 0.125).astype(BF16)
            at_k = 64 * (count - 2)
            block = out[at_k : at_k + 64].astype(BF16)
            keys_t[:, cols] = block
            keys[cols, :] = flip(block).astype(BF16)
            block = (out[at_k + 64 : at_k + 128] + wide_bias(1 if count == 3 else 2)).astype(BF16)
            values_t[:, cols] = block
            values[cols, :] = flip(block).astype(BF16)

    def rows_back(grads_t, first, target, core):
        count = grads_t.shape[0] // 64
        own = own_weights(first, count)
        for b in range(2):
            cols = pl.ds(pl.multiple_of(core * 512 + b * 256, 256), 256)
            out = tn(grads_t[:, cols], own)
            target[pl.ds(core * 4 + b * 2, 2)] = out.astype(BF16).reshape(2, 2, 64, width)

    def slices_back(grads_t, rows, grad):
        count = grads_t.shape[0] // 64
        out = nn(grads_t[...], rows[...].reshape(1024, width))
        wz[...] = jnp.zeros_like(wz)
        for j in range(count):
            wz[j, own_rows, :] = out[j * 64 : (j + 1) * 64]
            put(grad.at[j], jnp.transpose(wz[j]))

    def bias(i):
        return biases[i : i + 1, :]

    def make_masks():
        landed("marks", all_meta.at[pl.ds(0, 7)])
        order = lax.broadcasted_iota(jnp.int32, (1, 1024), 1)
        place = (order // 512) * 512 + lax.rem(order // 64, 2) * 256 + lax.rem(order // 128, 4) * 64 + lax.rem(order, 64)
        place = place.astype(F32)
        marks = [all_meta[s].astype(F32) for s in range(GROUP)]
        tgt_real = jnp.concatenate([mark[0:1, :] for mark in marks], axis=1)
        src_real = jnp.concatenate([mark[1:2, :] for mark in marks], axis=1)
        lower = lax.broadcasted_iota(jnp.int32, (32, 128), 1)
        later = lax.broadcasted_iota(jnp.int32, (32, 128), 0)

        def ends_of(row):
            lengths = jnp.broadcast_to(row, (32, 128))
            ends = jnp.sum(jnp.where(lower <= later, lengths, 0.0), axis=1, keepdims=True)
            starts = jnp.sum(jnp.where(lower < later, lengths, 0.0), axis=1, keepdims=True)
            return ends, starts

        def count(flags):
            return jnp.sum(jnp.where(flags, 1.0, 0.0), axis=0, keepdims=True)

        tgt_ends, _ = ends_of(marks[0][2:3, :])
        src_ends, src_starts = ends_of(marks[0][3:4, :])
        tgt_seg = count(tgt_ends <= place)
        src_seg = count(src_ends <= place)
        src_first = count(src_starts == place)
        self_row = jnp.where(tgt_real > 0.5, tgt_seg, -1.0)
        cross_row = jnp.where((src_real > 0.5) | (src_first > 0.5), src_seg, -1.0)
        rows_f[0:1, :] = tgt_seg
        rows_f[1:2, :] = place
        code_self[...] = jnp.transpose(jnp.broadcast_to(self_row, (128, 1024)))
        code_cross[...] = jnp.transpose(jnp.broadcast_to(cross_row, (128, 1024)))
        key_pos[...] = jnp.transpose(jnp.broadcast_to(place, (128, 1024)))

    def feed_up(rows, i):
        for k in (2 * i, 2 * i + 1):
            cols = slice(k * width, (k + 1) * width)
            inner = slice((k % 2) * width, (k % 2 + 1) * width)
            u = nn(rows, matrix(w_up.at[i, :, :, :, :, :, inner])) + up_bias[0:1, cols]
            square = u * u
            t = jnp.tanh(u * (0.7978845608028654 + 0.035677408136300125 * square))
            act[:, cols] = (0.5 * u * (1.0 + t)).astype(BF16)
            inner = 0.7978845608028654 + 0.10703222440890037 * square
            slope[:, cols] = 0.5 * (1.0 + t) + 0.5 * u * (1.0 - t * t) * inner

    def feed_back(gf, back):
        for k in range(4):
            cols = slice(k * width, (k + 1) * width)
            inner = slice((k % 2) * width, (k % 2 + 1) * width)
            rows = pl.ds(2 * (k % 2), 2)
            gu = nt(gf[:, 0:256], matrix(w_dn.at[0, k // 2, rows]))
            gu = gu + nt(gf[:, 256:512], matrix(w_dn.at[1, k // 2, rows]))
            gu = (gu * slope[:, cols]).astype(BF16)
            gul[:, cols] = gu
            column(7 + k, gu.astype(F32))
            back = back + nt(gu, matrix(w_up.at[k // 2, :, :, :, :, :, inner]))
        return back

    def value_sums(grads_t):
        total = jnp.sum(grads_t[64:128, :].astype(F32), axis=1, keepdims=True)
        bias_cols[0] = jnp.zeros((width, 128), F32)
        bias_cols[0, own_head, :] = jnp.broadcast_to(total, (64, 128))
        sg0[4:5, :] = jnp.transpose(bias_cols[0])[0:1, :]

    def head_sums(grads_t):
        lanes = lax.broadcasted_iota(jnp.int32, (64, 128), 1)
        dq_sum = jnp.sum(grads_t[0:64, :].astype(F32), axis=1, keepdims=True)
        dv_sum = jnp.sum(grads_t[128:192, :].astype(F32), axis=1, keepdims=True)
        bias_cols[0] = jnp.zeros((width, 128), F32)
        bias_cols[0, own_head, :] = jnp.where(lanes == 0, dq_sum, dv_sum)
        tg0[...] = jnp.transpose(bias_cols[0])[0:8, :]

    def small(name, src, dst, device):
        send(name, src, dst, device)
        sent_later(name, dst)

    def small_add(name, arrived, mine, total):
        landed(name, arrived)
        total[...] = mine[...] + arrived[...]

    def small_z(name, src, dst):
        for k in range(3):
            send(name, src, dst.at[2 - k], (c, at(z_peers[k], y, x)))
        sent_later(name, dst)

    def small_out():
        landed("s3", sr3)
        sg4[...] = sg3[...] + sr3[0] + sr3[1] + sr3[2]
        landed("t3", tr3)
        sg4[0:2, :] = (tg3[...] + tr3[0] + tr3[1] + tr3[2])[0:2, :]
        block = c * 16 + seq
        tile_of = sg4[:, pl.ds(pl.multiple_of((block // 8) * 128, 128), 128)]
        turned = pltpu.roll(tile_of, lax.rem(128 - lax.rem(block, 8) * 16, 128), 1)
        o_bias[...] = turned[0:7, 0:16]
        o_gain[...] = turned[11:14, 0:16]
        o_shift[...] = turned[14:17, 0:16]
        o_omega[...] = turned[17:20, 0:16]
        tile_of = sg4[:, pl.ds(pl.multiple_of((lax.rem(block, 8) // 2) * 128, 128), 128)]
        turned = pltpu.roll(tile_of, lax.rem(block, 2) * 64, 1)
        wanted = block // 8
        row = jnp.zeros((1, 64), F32)
        for k in range(4):
            row = row + turned[7 + k : 8 + k, 0:64] * (wanted == k).astype(F32)
        o_upb[...] = row
        ends = ((o_bias, h_bias), (o_upb, h_upb), (o_gain, h_gain_o), (o_shift, h_shift_o), (o_omega, h_omega_o))
        for i, (src, dst) in enumerate(ends):
            keep("e" + str(4 + i), src, dst)

    raw = ((raw_tm, tgt_msk), (raw_sm, src_msk), (raw_tl, tgt_len), (raw_sl, src_len))
    for i, (ref, given) in enumerate(raw):
        keep("raw" + str(i), given, ref)
    given = ((h_biases, biases), (h_up_bias, up_bias), (h_gain, gain), (h_shift, shift), (h_omega, omega))
    for i, (src, ref) in enumerate(given):
        keep("given" + str(i), src, ref)
    barrier = pltpu.get_barrier_semaphore()
    greet = [(cc, at(z, yy, xx)) for cc, yy, xx in plane_peers]
    greet += [(cc, at(zz, y, x)) for zz in z_peers for cc in (c, 1 - c)]
    for device in greet:
        pl.semaphore_signal(barrier, inc=1, device_id=device, device_id_type=MESH)
    pl.semaphore_wait(barrier, len(greet))
    to_plane("m", mem, all_mem, True)
    for i, (ref, _) in enumerate(raw):
        landed("raw" + str(i), ref)
        span = ref.shape[2]
        for m in range(2):
            for start in (0, 64):
                meta[m, i : i + 1, start : start + span] = ref[m]
    slice_1("w0", s_in.at[0], ws0)
    to_plane("meta", meta, in_meta)
    for i, (_, ref) in enumerate(given):
        landed("given" + str(i), ref)
    gather_z("out0")
    slice_1("w1", s_in.at[1, pl.ds(1, 2)], ws1)
    gather_z("out1")
    for i, row in enumerate((0, 1, 4)):
        bias_cols[i] = jnp.transpose(jnp.broadcast_to(bias(row), (128, width)))
    to_plane("x", tok, all_tok, True)
    gather_z("up1")
    spread_1("m", all_mem, 0)
    gather_z("q")
    gather_f("out0")
    slice_2("w0", ws0)
    spread_1("m", all_mem, 1)
    spread_1("x", all_tok, 0)
    gather_f("out1")
    spread_1("x", all_tok, 1)
    slice_2("w1", ws1)
    spread_2("m", all_mem, 0)
    gather_f("up1")
    landed("meta", in_meta)
    gather_f("q")
    spread_2("x", all_tok, 0)
    slice_f("w0", ws0)
    lane = lax.broadcasted_iota(jnp.int32, (8, 128), 1)
    gather_z("dn0")
    gather_z("up0")
    gather_1("out1")
    all_meta[me_slot] = jnp.where(lane < 64, in_meta[0], in_meta[1])
    gather_1("out0")
    gather_1("up1")
    for cc, yy, xx in plane_peers:
        send("marks", all_meta.at[me_slot], all_meta.at[me_slot], (cc, at(z, yy, xx)))
    spread_2("x", all_tok, 1)
    gather_2("out0")
    slice_3("w0", ws0)
    slice_f("w1", ws1)
    sent_later("marks", all_meta.at[pl.ds(0, 7)])
    gather_f("dn0")
    gather_1("q")
    spread_2("m", all_mem, 1)
    gather_2("out1")
    gather_z("dn1")
    make_masks()
    gather_2("q")
    gather_1("dn0")
    gather_f("dn1")
    slice_4("w0", ws0)
    heads_weights(0, ws0)
    slice_3("w1", ws1)
    gather_3("out1")
    spread_3("x", all_tok)
    to_plane("cot", cot, in_cot)
    gather_2("up1")
    project_heads(all_tok, 0, qt0, k0, kt0, v0, vt0)
    gather_3("out0")
    gather_1("dn1")
    attend(qt0, k0, vt0, pt0, l0, ot0, True, "x3", a3, b3)
    gather_3("up1")
    gather_2("dn0")
    gather_2("dn1")
    gathered("out0")
    spread_3("m", all_mem)
    gather_3("q")
    gathered("q")
    landed("x3", b3)
    words_f = all_tok[me_slot].reshape(here, width).astype(F32)
    gather_f("up0")
    gather_3("dn0")
    branch = tn(b3[...].reshape(width, here), matrix(w_out.at[0])) + bias(2)
    h1, scale0 = norm(words_f * omega[0:1, :] + branch, 0, xh0)
    h1_f[...] = h1
    slice_4("w1", ws1)
    gathered("out1")
    h1_low = h1.astype(BF16)
    by_head(a4, nn(h1_low, matrix(w_q.at[0])) + bias(3))
    gather_1("up0")
    heads_weights(3, ws1)
    project_heads(all_mem, 3, None, k1, kt1, v1, vt1)
    to_heads("x4", a4, b4)
    gather_3("dn1")
    gathered("dn0")
    gather_2("up0")
    landed("x4", b4)
    for s in range(GROUP):
        qt1[:, s * here : (s + 1) * here] = (b4[s].astype(F32) * 0.125).astype(BF16)
    gathered("up1")
    gathered("dn1")
    attend(qt1, k1, vt1, pt1, l1, ot1, False, "x5", a5, b5)
    gather_3("up0")
    landed("x5", b5)
    branch = tn(b5[...].reshape(width, here), matrix(w_out.at[1])) + bias(5)
    h2, scale1 = norm(h1_f[...] * omega[1:2, :] + branch, 1, xh1)
    gathered("up0")
    h2_f[...] = h2
    h2_low = h2.astype(BF16)
    feed_up(h2_low, 0)
    feed_up(h2_low, 1)
    first = nn(act[...], matrix(w_dn.at[0]))
    second = nn(act[...], matrix(w_dn.at[1]))
    h3, scale2 = norm(h2_f[...] * omega[2:3, :] + jnp.concatenate([first, second], axis=1) + bias(6), 2, xh2)
    out_res[...] = h3.astype(BF16).reshape(2, 64, width)
    landed("cot", in_cot)
    grad = in_cot[...].reshape(here, width).astype(F32)
    dr, skip = norm_back(grad, 2, xh2, scale2, h2_f[...])
    gf = dr.astype(BF16)
    put(g_dn.at[0], tn(act[...], gf[:, 0:256]))
    column(6, gf.astype(F32))
    scatter_0("dn0")
    back = feed_back(gf, skip)
    scatter_1("dn0")
    dr, skip = norm_back(back, 1, xh1, scale1, h1_f[...])
    gc = dr.astype(BF16)
    put(g_up.at[0], tn(h2_low, gul[:, 0:1024]))
    put(g_out.at[1], nn(b5[...].reshape(width, here), gc))
    scatter_0("up0")
    scatter_0("out1")
    column(5, gc.astype(F32))
    by_head(a6, nt(gc, matrix(w_out.at[1])))
    to_heads("x6", a6, b6)
    from_plane("res", out_res, o_res)
    put(g_dn.at[1], tn(act[...], gf[:, 256:512]))
    scatter_1("up0")
    scatter_0("dn1")
    scatter_2("dn0")
    back = skip
    put(g_up.at[1], tn(h2_low, gul[:, 1024:2048]))
    scatter_1("out1")
    landed("x6", b6)
    attend_back(b6, qt1, kt1, v1, pt1, l1, ot1, False, "x7", a7, b7)
    dt1[0:64, :] = acc_k[...].astype(BF16)
    scatter_2("up0")
    scatter_3("dn0")
    dt1[64:128, :] = acc_v[...].astype(BF16)
    rows_back(dt1, 3, dx1, 1 - c)
    merge_0("dm", dx1, dc1)
    rows_back(dt1, 3, dx1, c)
    scatter_1("dn1")
    slices_back(dt1, all_mem, gs1)
    landed("x7", b7)
    scatter_2("out1")
    dq = b7[...].reshape(width, here)
    scatter_0("up1")
    dq_row = flip(dq)
    put(g_q.at[0], nt(flip(h1_low).astype(BF16), dq))
    unslice_0("u1", gs1, cs1)
    scatter_3("up0")
    value_sums(dt1)
    column(3, dq_row)
    back = back + nt(dq_row.astype(BF16), matrix(w_q.at[0]))
    dr, skip = norm_back(back, 0, xh0, scale0, words_f)
    ga = dr.astype(BF16)
    column(2, ga.astype(F32))
    small("s0", sg0, sr0, core_next)
    by_head(a8, nt(ga, matrix(w_out.at[0])))
    to_heads("x8", a8, b8)
    scatter_2("dn1")
    put(g_out.at[0], nn(b3[...].reshape(width, here), ga))
    scatter_0("out0")
    scatter_3("out1")
    last = skip
    scatter_1("up1")
    unslice_1("u1", gs1, cs1, zs1)
    small_add("s0", sr0, sg0, sg1)
    landed("x8", b8)
    scatter_0("q")
    scatter_1("out0")
    small("s1", sg1, sr1, y_next)
    attend_back(b8, qt0, kt0, v0, pt0, l0, ot0, True, None, None, None)
    scattered("dn0")
    dt0[64:128, :] = acc_k[...].astype(BF16)
    scatter_1("q")
    scatter_3("dn1")
    dt0[128:192, :] = acc_v[...].astype(BF16)
    slices_back(dt0, all_tok, gs0)
    unslice_0("u0", gs0, cs0)
    rows_back(dt0, 0, dx0, 1 - c)
    landed("res", o_res)
    scatter_2("up1")
    head_sums(dt0)
    small_add("s1", sr1, sg1, sg2)
    unslice_1("u0", gs0, cs0, zs0)
    small("s2", sg2, sr2, x_next)
    small("t0", tg0, tr0, core_next)
    merge_0("dx", dx0, dc0)
    scatter_2("q")
    small_add("t0", tr0, tg0, tg1)
    scatter_2("out0")
    scattered("up0")
    rows_back(dt0, 0, dx0, c)
    small("t1", tg1, tr1, y_next)
    merge_1("dm", dx1, dc1, dp1)
    merge_1("dx", dx0, dc0, dp0)
    scatter_3("out0")
    scatter_3("up1")
    scatter_3("q")
    small_add("s2", sr2, sg2, sg3)
    small_z("s3", sg3, sr3)
    scattered("up1")
    out_mem[...] = merge_2("dm", dx1, dp1).astype(BF16).reshape(2, 64, width)
    from_plane("gmem", out_mem, o_mem)
    unslice_2("u0", gs0, zs0, fs0, o_in.at[0])
    scattered("dn1")
    keep("e3", o_dn, h_dn)
    small_add("t1", tr1, tg1, tg2)
    small("t2", tg2, tr2, x_next)
    unslice_2("u1", gs1, zs1, fs1, o_in.at[1, pl.ds(1, 2)])
    small_add("t2", tr2, tg2, tg3)
    small_z("t3", tg3, tr3)
    out_tok[...] = (merge_2("dx", dx0, dp0) + last).astype(BF16).reshape(2, 64, width)
    from_plane("gtok", out_tok, o_tok)
    small_out()
    scattered("out0")
    landed("gmem", o_mem)
    keep("e2", o_up, h_up)
    unslice_3("u0", o_in.at[0])
    scattered("out1")
    keep("e1", o_out, h_out)
    scattered("q")
    unslice_3("u1", o_in.at[1, pl.ds(1, 2)])
    keep("e0", o_in, h_in)
    landed("gtok", o_tok)
    for i, ref in enumerate((h_in, h_out, h_up, h_dn, h_bias, h_upb, h_gain_o, h_shift_o, h_omega_o)):
        landed("e" + str(i), ref)
    for semaphore, ref, when in pending:
        if when is None:
            wait(semaphore, ref)
        else:

            @pl.when(when)
            def _():
                wait(semaphore, ref)

    for i, total in enumerate(bins):
        if total:
            wait(ss.at[i], gauge.at[pl.ds(0, total // 1024)])
    units = line_bytes[0] // UNIT
    assert line_bytes[0] % UNIT == 0

    @pl.when(edge)
    def _():
        wait(ss.at[BINS], gauge.at[pl.ds(0, 2 * units * 16)])

    @pl.when(jnp.logical_not(edge))
    def _():
        wait(ss.at[BINS], gauge.at[pl.ds(0, 4 * units * 16)])

    assert len(names) <= NAMES and len(bins) <= BINS and BINS + 1 + len(odd) <= ss.shape[0]


def copy_kernel(*refs):
    count = len(refs) // 2
    for i in range(count):
        refs[count + i][...] = refs[i][...]


def fused_local(
    tokens, memory, cotangent, tgt_lengths, src_lengths, tgt_mask, src_mask, attn_in, attn_out, w_up, w_down,
    biases, up_bias, norm_gain, norm_shift, omega,
):
    any_space = pl.BlockSpec(memory_space=pl.ANY)
    vmem = pl.BlockSpec(memory_space=pltpu.VMEM)
    lines = (CORES, PLANES, YS, XS)
    leads = {"q": 1, "out": 2, "up": 2, "dn": 2}
    shards = {"q": (16, 512), "out": (16, 512), "up": (16, 1024), "dn": (64, 256)}
    kinds = tuple(leads)

    def low(*shape):
        return pltpu.VMEM(shape, BF16)

    def full(*shape):
        return pltpu.VMEM(shape, F32)

    def whole(k):
        return low(leads[k], *lines, *shards[k])

    def halved(k, *middle):
        return low(2, leads[k], *middle, shards[k][0], shards[k][1] // 2)

    params = [full(7, 512), full(1, 2048), full(3, 512), full(3, 512), full(3, 512)]
    results = [(2, 3, 16, 512), (2, 16, 512), (1, 16, 2048), (1, 64, 512), (7, 16), (1, 64), (3, 16), (3, 16), (3, 16)]
    scratch = params + [full(*shape) for shape in results]
    scratch += [whole(k) for k in kinds] * 2
    scratch += [low(leads[k], *lines[1:], *shards[k]) for k in kinds]
    scratch += [halved(k, PLANES, 2) for k in kinds] + [halved(k, PLANES) for k in kinds]
    scratch += [low(3, leads[k], *shards[k]) for k in kinds]
    scratch += [low(n, CORES, PLANES, 4, 16, 128) for n in (3, 2)] * 2
    scratch += [low(n, PLANES, 4, 16, 128) for n in (3, 2)] + [low(3, n, 4, 16, 128) for n in (3, 2)]
    scratch += [full(n, 4, 16, 128) for n in (3, 2)]
    local_rows = low(2, 64, 512)
    marks = [pltpu.VMEM((2, 1, n), jnp.int32) for n in (32, 32, 64, 64)] + [pltpu.VMEM((2, 8, 128), jnp.int32)] * 2
    scratch += [low(GROUP, 2, 64, 512)] * 2 + [local_rows] + marks + [pltpu.VMEM((GROUP, 8, 128), jnp.int32)]
    scratch += [low(GROUP, 2, 64, 512)] * 2 + [low(4, 2, 64, 512)] * 2 + [low(3, 2, 64, 512)] * 2
    scratch += [low(GROUP, 64, 128)] * 12 + [local_rows] * 3
    scratch += [full(24, 512)] * 8 + [full(3, 24, 512)]
    scratch += [full(8, 512)] * 7 + [full(3, 8, 512)]
    scratch += [full(1024, 128)] * 3 + [full(8, 1024)]
    scratch += ([low(64, 1024)] * 3 + [low(1024, 64)] * 2 + [low(1024, 1024), full(1, 1024), full(64, 1024)]) * 2
    scratch += [low(64, 1024)] + [full(64, 1024)] * 2
    scratch += [low(128, 2048), full(128, 2048), low(128, 2048)] + [full(128, 512)] * 5
    scratch += [low(5, 128, 512), full(3, 512, 128), full(3, 128, 512), low(192, 1024), low(128, 1024), low(2048, 512)]
    scratch += [pltpu.SemaphoreType.DMA((36,)), pltpu.SemaphoreType.DMA((NAMES,))]
    rows = jax.ShapeDtypeStruct((2, 64, 512), BF16)

    def wide_out(*shape):
        return jax.ShapeDtypeStruct(shape, F32)

    outs = pl.pallas_call(
        fused_kernel,
        name="layer",
        out_shape=(rows, rows, rows, *(wide_out(*shape) for shape in results)),
        in_specs=[any_space] * 16,
        out_specs=(any_space,) * 12,
        scratch_shapes=scratch,
        compiler_params=pltpu.CompilerParams(collective_id=0, has_side_effects=True, vmem_limit_bytes=60 * 1024 * 1024),
    )(
        tokens.reshape(2, 64, 512), memory.reshape(2, 64, 512), cotangent.reshape(2, 64, 512),
        tgt_lengths, src_lengths, jnp.transpose(tgt_mask, (0, 2, 1)), jnp.transpose(src_mask, (0, 2, 1)),
        attn_in, attn_out, w_up.reshape(1, 16, 2048), w_down.reshape(1, 64, 512),
        biases, up_bias.reshape(1, 2048), norm_gain, norm_shift, omega,
    )
    outs = pl.pallas_call(
        copy_kernel,
        name="hand_over",
        out_shape=tuple(jax.ShapeDtypeStruct(out.shape, out.dtype) for out in outs),
        in_specs=[vmem] * len(outs),
        out_specs=(vmem,) * len(outs),
    )(*outs)
    shaped = [out.reshape(2, 64, 1, 512) for out in outs[:3]]
    return (
        *shaped, outs[3], outs[4], outs[5].reshape(16, 2048), outs[6].reshape(64, 512), outs[7], outs[8].reshape(64),
        outs[9], outs[10], outs[11],
    )


def solution(mesh):
    if mesh.shape["seq"] != PLANES * YS * XS or mesh.shape["rows"] != CORES:
        return general(mesh)
    return over(mesh, fused_local)
```

```python
import functools
import math

import jax
import jax.numpy as jnp
from jax import lax
from jax.experimental import pallas as pl
from jax.experimental.pallas import tpu as pltpu
from jax.sharding import PartitionSpec as P

HEADS = 8


def norm_block(branch, skip, scale, gain, shift):
    mixed = skip * scale + branch
    centered = mixed - jnp.mean(mixed, axis=-1, keepdims=True)
    variance = jnp.mean(centered * centered, axis=-1, keepdims=True)
    return centered * lax.rsqrt(variance + 1e-05) * gain + shift


def project(values, matrix):
    return jnp.einsum("trd,de->tre", values, matrix, preferred_element_type=jnp.float32)


def project_back(grads, matrix):
    return jnp.einsum("tre,de->trd", grads, matrix, preferred_element_type=jnp.float32)


def matrix_grad(values, grads):
    return jnp.einsum("trd,tre->de", values, grads, preferred_element_type=jnp.float32)


def column_sum(grads):
    return jnp.sum(grads.astype(jnp.float32), axis=(0, 1))


def segment_of(positions, ends):
    return jnp.sum((ends[None, :, :] <= positions[:, None, None]).astype(jnp.int32), axis=-1)


def segment_bounds(first, last, ends):
    lowest = jnp.sum((ends <= first).astype(jnp.int32), axis=-1)
    highest = jnp.sum((ends <= last).astype(jnp.int32), axis=-1)
    return (lowest, highest)


def ranges_share(query_bounds, key_bounds):
    return jnp.any((key_bounds[0] <= query_bounds[1]) & (key_bounds[1] >= query_bounds[0]))


def key_status(positions, real_marks, ends, starts, causal):
    segments = segment_of(positions, ends)
    usable = real_marks > 0.5
    if not causal:
        usable = usable | jnp.any(starts[None, :, :] == positions[:, None, None], axis=-1)
    return (segments, usable)


def permitted(query_pos, query_seg, key_pos, key_seg, usable, causal):
    same = jnp.transpose(query_seg)[:, :, None] == jnp.transpose(key_seg)[:, None, :]
    usable_keys = jnp.transpose(usable)[:, None, :]
    if causal:
        before = (key_pos[None, :] <= query_pos[:, None])[None]
        itself = (key_pos[None, :] == query_pos[:, None])[None]
        return same & before & (usable_keys | itself)
    return same & usable_keys


def block_grads(query_heads, grad_heads, lambdas, key_heads, value_heads, permit):
    scores = (
        jnp.einsum("arhd,brhd->rhab", query_heads, key_heads, preferred_element_type=jnp.float32)
        * 0.125
    )
    weights = jnp.where(permit[:, None], jnp.exp(scores), 0.0)
    spread = jnp.einsum(
        "arhd,brhd->rhab", grad_heads, value_heads, preferred_element_type=jnp.float32
    )
    slopes = weights * (spread + jnp.transpose(lambdas, (1, 2, 0))[..., None])
    return (weights.astype(jnp.bfloat16), slopes.astype(jnp.bfloat16))


def local(
    tokens,
    memory,
    cotangent,
    tgt_lengths,
    src_lengths,
    tgt_mask,
    src_mask,
    attn_in,
    attn_out,
    w_up,
    w_down,
    biases,
    up_bias,
    norm_gain,
    norm_shift,
    omega,
):
    micro_count, tokens_here, rows_here, width = tokens.shape
    head_size = width // HEADS
    my_pos = lax.axis_index("seq") * tokens_here + jnp.arange(tokens_here, dtype=jnp.int32)
    my_first = my_pos[0]
    my_last = my_pos[tokens_here - 1]

    def split_heads(values):
        return values.reshape(values.shape[0], rows_here, HEADS, head_size)

    def zero_heads():
        return jnp.zeros((tokens_here, rows_here, HEADS, head_size), jnp.float32)

    results = []
    grads_words = []
    grads_sources = []
    shares_all = None
    for micro_index in range(micro_count):
        in_weights = lax.all_gather(attn_in, ("rows", "seq"), axis=2, tiled=True)
        out_weights = lax.all_gather(attn_out, ("rows", "seq"), axis=1, tiled=True)
        up_weights = lax.all_gather(w_up, ("rows", "seq"), axis=0, tiled=True)
        down_weights = lax.all_gather(w_down, ("rows", "seq"), axis=0, tiled=True)
        words = tokens[micro_index]
        sources = memory[micro_index]
        words_full = words.astype(jnp.float32)
        tgt_len = tgt_lengths[micro_index]
        src_len = src_lengths[micro_index]
        tgt_ends = jnp.cumsum(tgt_len, axis=-1)
        src_ends = jnp.cumsum(src_len, axis=-1)
        src_starts = src_ends - src_len
        query_seg = segment_of(my_pos, tgt_ends)
        query_bounds = segment_bounds(my_first, my_last, tgt_ends)
        tgt_real = tgt_mask[micro_index].astype(jnp.bfloat16)
        src_real = src_mask[micro_index].astype(jnp.bfloat16)

        def attend(queries, keys, values, real_marks, ends, starts, causal):
            full_keys, full_values, full_real = (
                lax.all_gather(keys, "seq", axis=0, tiled=True),
                lax.all_gather(values, "seq", axis=0, tiled=True),
                lax.all_gather(real_marks, "seq", axis=0, tiled=True),
            )
            length = full_keys.shape[0]
            block = math.gcd(length, 512)
            query_heads = split_heads(queries)

            def step(carry, block_index):
                begin = block_index * block
                shares = ranges_share(query_bounds, segment_bounds(begin, begin + block - 1, ends))

                def step_compute(state):
                    totals, accum = state
                    key_heads = split_heads(lax.dynamic_slice_in_dim(full_keys, begin, block, 0))
                    value_heads = split_heads(
                        lax.dynamic_slice_in_dim(full_values, begin, block, 0)
                    )
                    key_pos = begin + jnp.arange(block, dtype=jnp.int32)
                    key_seg, usable = key_status(
                        key_pos,
                        lax.dynamic_slice_in_dim(full_real, begin, block, 0),
                        ends,
                        starts,
                        causal,
                    )
                    permit = permitted(my_pos, query_seg, key_pos, key_seg, usable, causal)
                    scores = (
                        jnp.einsum(
                            "trhd,krhd->rhtk",
                            query_heads,
                            key_heads,
                            preferred_element_type=jnp.float32,
                        )
                        * 0.125
                    )
                    weights = jnp.where(permit[:, None], jnp.exp(scores), 0.0)
                    totals = totals + jnp.sum(weights, axis=-1)
                    accum = accum + jnp.einsum(
                        "rhtk,krhd->trhd",
                        weights.astype(jnp.bfloat16),
                        value_heads,
                        preferred_element_type=jnp.float32,
                    )
                    return (totals, accum)

                return (lax.cond(shares, step_compute, lambda unchanged: unchanged, carry), None)

            start_carry = (jnp.zeros((rows_here, HEADS, tokens_here), jnp.float32), zero_heads())
            (totals, accum), unused = lax.scan(
                step, start_carry, jnp.arange(length // block, dtype=jnp.int32)
            )
            sums = jnp.transpose(totals, (2, 0, 1))
            output = (accum / sums[..., None]).reshape(tokens_here, rows_here, width)
            return (output, sums, (full_keys, full_values, full_real))

        def attention_back(
            grad_out,
            output,
            sums,
            queries,
            keys,
            values,
            real_marks,
            gathered_set,
            ends,
            starts,
            causal,
        ):
            full_keys, full_values, full_real = gathered_set
            grad_heads = split_heads(grad_out)
            lambdas = -jnp.sum(grad_heads * split_heads(output), axis=-1) / sums
            scaled = (grad_heads / sums[..., None]).astype(jnp.bfloat16)
            query_heads = split_heads(queries)
            length = full_keys.shape[0]
            block = math.gcd(length, 512)

            def query_step(accum, block_index):
                begin = block_index * block
                shares = ranges_share(query_bounds, segment_bounds(begin, begin + block - 1, ends))

                def query_compute(state):
                    key_heads = split_heads(lax.dynamic_slice_in_dim(full_keys, begin, block, 0))
                    value_heads = split_heads(
                        lax.dynamic_slice_in_dim(full_values, begin, block, 0)
                    )
                    key_pos = begin + jnp.arange(block, dtype=jnp.int32)
                    key_seg, usable = key_status(
                        key_pos,
                        lax.dynamic_slice_in_dim(full_real, begin, block, 0),
                        ends,
                        starts,
                        causal,
                    )
                    permit = permitted(my_pos, query_seg, key_pos, key_seg, usable, causal)
                    weights, slopes = block_grads(
                        query_heads, scaled, lambdas, key_heads, value_heads, permit
                    )
                    return (
                        state
                        + jnp.einsum(
                            "rhab,brhd->arhd", slopes, key_heads, preferred_element_type=jnp.float32
                        )
                        * 0.125
                    )

                return (lax.cond(shares, query_compute, lambda unchanged: unchanged, accum), None)

            grad_query, unused = lax.scan(
                query_step, zero_heads(), jnp.arange(length // block, dtype=jnp.int32)
            )
            all_lambdas = lax.all_gather(lambdas, "seq", axis=0, tiled=True)
            local_seg, local_usable = key_status(my_pos, real_marks, ends, starts, causal)
            local_bounds = segment_bounds(my_first, my_last, ends)
            local_keys = split_heads(keys)
            local_values = split_heads(values)
            query_piece = lax.all_gather(queries, "seq", axis=0, tiled=True)
            scaled_piece = lax.all_gather(
                scaled.reshape(tokens_here, rows_here, width), "seq", axis=0, tiled=True
            )
            size = query_piece.shape[0]
            inner = math.gcd(size, 512)

            def inner_step(inner_carry, inner_index):
                offset = inner_index * inner
                piece_first = offset
                shares = ranges_share(
                    segment_bounds(piece_first, piece_first + inner - 1, tgt_ends), local_bounds
                )

                def inner_compute(state):
                    acc_key, acc_value = state
                    query_blk = split_heads(lax.dynamic_slice_in_dim(query_piece, offset, inner, 0))
                    scaled_blk = split_heads(
                        lax.dynamic_slice_in_dim(scaled_piece, offset, inner, 0)
                    )
                    lambda_blk = lax.dynamic_slice_in_dim(all_lambdas, piece_first, inner, 0)
                    query_pos = piece_first + jnp.arange(inner, dtype=jnp.int32)
                    permit = permitted(
                        query_pos,
                        segment_of(query_pos, tgt_ends),
                        my_pos,
                        local_seg,
                        local_usable,
                        causal,
                    )
                    weights, slopes = block_grads(
                        query_blk, scaled_blk, lambda_blk, local_keys, local_values, permit
                    )
                    acc_key = (
                        acc_key
                        + jnp.einsum(
                            "rhab,arhd->brhd", slopes, query_blk, preferred_element_type=jnp.float32
                        )
                        * 0.125
                    )
                    acc_value = acc_value + jnp.einsum(
                        "rhab,arhd->brhd", weights, scaled_blk, preferred_element_type=jnp.float32
                    )
                    return (acc_key, acc_value)

                return (
                    lax.cond(shares, inner_compute, lambda unchanged: unchanged, inner_carry),
                    None,
                )

            folded, unused_inner = lax.scan(
                inner_step, (zero_heads(), zero_heads()), jnp.arange(size // inner, dtype=jnp.int32)
            )
            grad_key, grad_value = folded
            grad_key = grad_key.reshape(tokens_here, rows_here, width)
            grad_value = grad_value.reshape(tokens_here, rows_here, width)
            return (grad_query.reshape(tokens_here, rows_here, width), grad_key, grad_value)

        self_query = (project(words, in_weights[0, 0]) + biases[0]).astype(jnp.bfloat16)
        self_key = project(words, in_weights[0, 1]).astype(jnp.bfloat16)
        self_value = (project(words, in_weights[0, 2]) + biases[1]).astype(jnp.bfloat16)
        heard, heard_sums, self_set = attend(
            self_query, self_key, self_value, tgt_real, tgt_ends, None, True
        )
        heard_low = heard.astype(jnp.bfloat16)
        branch_self = project(heard_low, out_weights[0]) + biases[2]
        hidden_one, pull_one = jax.vjp(
            norm_block, branch_self, words_full, omega[0], norm_gain[0], norm_shift[0]
        )
        hidden_one_low = hidden_one.astype(jnp.bfloat16)
        cross_query = (project(hidden_one_low, in_weights[1, 0]) + biases[3]).astype(jnp.bfloat16)
        cross_key = project(sources, in_weights[1, 1]).astype(jnp.bfloat16)
        cross_value = (project(sources, in_weights[1, 2]) + biases[4]).astype(jnp.bfloat16)
        recalled, recalled_sums, cross_set = attend(
            cross_query, cross_key, cross_value, src_real, src_ends, src_starts, False
        )
        recalled_low = recalled.astype(jnp.bfloat16)
        branch_cross = project(recalled_low, out_weights[1]) + biases[5]
        hidden_two, pull_two = jax.vjp(
            norm_block, branch_cross, hidden_one, omega[1], norm_gain[1], norm_shift[1]
        )
        hidden_two_low = hidden_two.astype(jnp.bfloat16)
        up_pre = project(hidden_two_low, up_weights) + up_bias
        active, pull_active = jax.vjp(jax.nn.gelu, up_pre)
        active_low = active.astype(jnp.bfloat16)
        branch_ffn = project(active_low, down_weights) + biases[6]
        outcome, pull_three = jax.vjp(
            norm_block, branch_ffn, hidden_two, omega[2], norm_gain[2], norm_shift[2]
        )
        grad_result = cotangent[micro_index].astype(jnp.float32)
        grad_ffn, grad_two, omega_three, gain_three, shift_three = pull_three(grad_result)
        grad_ffn_low = grad_ffn.astype(jnp.bfloat16)
        grad_down = matrix_grad(active_low, grad_ffn_low)
        bias_ffn = column_sum(grad_ffn_low)
        grad_up_pre = pull_active(project_back(grad_ffn_low, down_weights))[0].astype(jnp.bfloat16)
        grad_up = matrix_grad(hidden_two_low, grad_up_pre)
        bias_up = column_sum(grad_up_pre)
        grad_two = grad_two + project_back(grad_up_pre, up_weights)
        grad_cross, grad_one, omega_two, gain_two, shift_two = pull_two(grad_two)
        grad_cross_low = grad_cross.astype(jnp.bfloat16)
        grad_out_cross = matrix_grad(recalled_low, grad_cross_low)
        bias_out_cross = column_sum(grad_cross_low)
        grad_recalled = project_back(grad_cross_low, out_weights[1])
        cross_gq, cross_gk, cross_gv = attention_back(
            grad_recalled,
            recalled,
            recalled_sums,
            cross_query,
            cross_key,
            cross_value,
            src_real,
            cross_set,
            src_ends,
            src_starts,
            False,
        )
        cross_gq = cross_gq.astype(jnp.bfloat16)
        cross_gk = cross_gk.astype(jnp.bfloat16)
        cross_gv = cross_gv.astype(jnp.bfloat16)
        grad_cross_query = matrix_grad(hidden_one_low, cross_gq)
        grad_cross_key = matrix_grad(sources, cross_gk)
        grad_cross_value = matrix_grad(sources, cross_gv)
        grad_one = grad_one + project_back(cross_gq, in_weights[1, 0])
        grad_sources = project_back(cross_gk, in_weights[1, 1]) + project_back(
            cross_gv, in_weights[1, 2]
        )
        grad_self, grad_words, omega_one, gain_one, shift_one = pull_one(grad_one)
        grad_self_low = grad_self.astype(jnp.bfloat16)
        grad_out_self = matrix_grad(heard_low, grad_self_low)
        bias_out_self = column_sum(grad_self_low)
        grad_heard = project_back(grad_self_low, out_weights[0])
        self_gq, self_gk, self_gv = attention_back(
            grad_heard,
            heard,
            heard_sums,
            self_query,
            self_key,
            self_value,
            tgt_real,
            self_set,
            tgt_ends,
            None,
            True,
        )
        self_gq = self_gq.astype(jnp.bfloat16)
        self_gk = self_gk.astype(jnp.bfloat16)
        self_gv = self_gv.astype(jnp.bfloat16)
        grad_words = (
            grad_words
            + project_back(self_gq, in_weights[0, 0])
            + project_back(self_gk, in_weights[0, 1])
            + project_back(self_gv, in_weights[0, 2])
        )
        grad_in = jnp.stack(
            [
                jnp.stack(
                    [
                        matrix_grad(words, self_gq),
                        matrix_grad(words, self_gk),
                        matrix_grad(words, self_gv),
                    ]
                ),
                jnp.stack([grad_cross_query, grad_cross_key, grad_cross_value]),
            ]
        )
        grad_out = jnp.stack([grad_out_self, grad_out_cross])
        grad_bias = jnp.stack(
            [
                column_sum(self_gq),
                column_sum(self_gv),
                bias_out_self,
                column_sum(cross_gq),
                column_sum(cross_gv),
                bias_out_cross,
                bias_ffn,
            ]
        )
        grad_gain = jnp.stack([gain_one, gain_two, gain_three])
        grad_shift = jnp.stack([shift_one, shift_two, shift_three])
        grad_omega = jnp.stack([omega_one, omega_two, omega_three])
        grads = (
            grad_in,
            grad_out,
            grad_up,
            grad_down,
            grad_bias,
            bias_up,
            grad_gain,
            grad_shift,
            grad_omega,
        )
        outcome, grad_words, grad_sources, grads = (
            outcome.astype(jnp.bfloat16),
            grad_words.astype(jnp.bfloat16),
            grad_sources.astype(jnp.bfloat16),
            grads,
        )
        results.append(outcome)
        grads_words.append(grad_words)
        grads_sources.append(grad_sources)
        part_shares = (
            lax.psum_scatter(grads[0], ("rows", "seq"), scatter_dimension=2, tiled=True),
            lax.psum_scatter(grads[1], ("rows", "seq"), scatter_dimension=1, tiled=True),
            lax.psum_scatter(grads[2], ("rows", "seq"), scatter_dimension=0, tiled=True),
            lax.psum_scatter(grads[3], ("rows", "seq"), scatter_dimension=0, tiled=True),
            lax.psum_scatter(grads[4], ("rows", "seq"), scatter_dimension=1, tiled=True),
            lax.psum_scatter(grads[5], ("rows", "seq"), scatter_dimension=0, tiled=True),
            lax.psum_scatter(grads[6], ("rows", "seq"), scatter_dimension=1, tiled=True),
            lax.psum_scatter(grads[7], ("rows", "seq"), scatter_dimension=1, tiled=True),
            lax.psum_scatter(grads[8], ("rows", "seq"), scatter_dimension=1, tiled=True),
        )
        shares_all = (
            part_shares if shares_all is None else jax.tree.map(jnp.add, shares_all, part_shares)
        )
    return (jnp.stack(results), jnp.stack(grads_words), jnp.stack(grads_sources)) + tuple(
        shares_all
    )


def over(mesh, function):
    return jax.shard_map(
        function,
        mesh=mesh,
        in_specs=(
            P(None, "seq", "rows", None),
            P(None, "seq", "rows", None),
            P(None, "seq", "rows", None),
            P(None, "rows", None),
            P(None, "rows", None),
            P(None, "seq", "rows"),
            P(None, "seq", "rows"),
            P(None, None, ("rows", "seq"), None),
            P(None, ("rows", "seq"), None),
            P(("rows", "seq"), None),
            P(("rows", "seq"), None),
            P(),
            P(),
            P(),
            P(),
            P(),
        ),
        out_specs=(
            P(None, "seq", "rows", None),
            P(None, "seq", "rows", None),
            P(None, "seq", "rows", None),
            P(None, None, ("rows", "seq"), None),
            P(None, ("rows", "seq"), None),
            P(("rows", "seq"), None),
            P(("rows", "seq"), None),
            P(None, ("rows", "seq")),
            P(("rows", "seq")),
            P(None, ("rows", "seq")),
            P(None, ("rows", "seq")),
            P(None, ("rows", "seq")),
        ),
        check_vma=False,
    )


def general(mesh):
    return over(mesh, local)


MESH = pl.DeviceIdType.MESH
UNIT = 16 * 1024
BINS = 16
NAMES = 192
ODD = ("marks", "w0p", "w1p", "u0p", "x3", "x5", "x7")
F32 = jnp.float32
BF16 = jnp.bfloat16
PLANES, YS, XS, CORES = 4, 2, 2, 2
GROUP = YS * XS * CORES


def nn(left, right):
    return lax.dot_general(left, right, (((1,), (0,)), ((), ())), preferred_element_type=F32)


def nt(left, right):
    return lax.dot_general(left, right, (((1,), (1,)), ((), ())), preferred_element_type=F32)


def tn(left, right):
    return lax.dot_general(left, right, (((0,), (0,)), ((), ())), preferred_element_type=F32)


def flip(value):
    return jnp.transpose(value.astype(F32))


def fused_kernel(
    tok, mem, cot, tgt_len, src_len, tgt_msk, src_msk, s_in, s_out, s_up, s_dn, h_biases, h_up_bias, h_gain, h_shift, h_omega,
    o_res, o_tok, o_mem, h_in, h_out, h_up, h_dn, h_bias, h_upb, h_gain_o, h_shift_o, h_omega_o,
    biases, up_bias, gain, shift, omega, o_in, o_out, o_up, o_dn, o_bias, o_upb, o_gain, o_shift, o_omega,
    w_q, w_out, w_up, w_dn, g_q, g_out, g_up, g_dn,
    c_q, c_out, c_up, c_dn,
    p_q, p_out, p_up, p_dn,
    q_q, q_out, q_up, q_dn,
    z_q, z_out, z_up, z_dn,
    ws0, ws1, gs0, gs1, cs0, cs1, zs0, zs1, fs0, fs1,
    all_tok, all_mem, in_cot, raw_tl, raw_sl, raw_tm, raw_sm, meta, in_meta, all_meta,
    dx0, dx1, dc0, dc1, dp0, dp1,
    a3, b3, a4, b4, a5, b5, a6, b6, a7, b7, a8, b8,
    out_res, out_tok, out_mem,
    sg0, sg1, sg2, sg3, sg4, sr0, sr1, sr2, sr3,
    tg0, tg1, tg2, tg3, tr0, tr1, tr2, tr3,
    code_self, code_cross, key_pos, rows_f,
    qt0, kt0, vt0, k0, v0, pt0, l0, ot0,
    qt1, kt1, vt1, k1, v1, pt1, l1, ot1,
    dnt, acc_k, acc_v,
    act, slope, gul, xh0, xh1, xh2, h1_f, h2_f,
    wt, bias_cols, wz, dt0, dt1, gauge,
    ss, rs,
):
    c = lax.axis_index("rows")
    seq = lax.axis_index("seq")
    z = seq // (YS * XS)
    yx = lax.rem(seq, YS * XS)
    y = yx // XS
    x = lax.rem(yx, XS)
    width = 512
    here = 2 * 64

    def at(zz, yy, xx):
        return zz * (YS * XS) + yy * XS + xx

    def slot(cc, yy, xx):
        return cc * 4 + yy * 2 + xx

    def head(cc, yy, xx):
        return (yy * 2 + xx) * 2 + cc

    me_slot, me_head = slot(c, y, x), head(c, y, x)
    plane_peers = []
    for k in range(1, GROUP):
        cc = 1 - c if k & 4 else c
        yy = 1 - y if k & 2 else y
        xx = 1 - x if k & 1 else x
        plane_peers.append((cc, yy, xx))
    trio = [(1 - y, x), (y, 1 - x), (1 - y, 1 - x)]
    z_peers = [lax.rem(z + k, PLANES) for k in (1, 2, 3)]

    names, expected_bytes = {}, {}
    pending = []
    edge = (z == 0) | (z == PLANES - 1)

    def sem(name):
        return names.setdefault(name, len(names))

    def wait(semaphore, ref):
        pltpu.make_async_copy(ref, ref, semaphore).wait()

    def size(ref):
        return math.prod(ref.shape) * jnp.dtype(ref.dtype).itemsize

    bins = [0]
    odd = {}

    def out_sem(name):
        return ss.at[odd.setdefault(name, BINS + 1 + len(odd))] if name in ODD else ss.at[len(bins) - 1]

    def send(name, src, dst, device, recv=None):
        pltpu.make_async_remote_copy(
            src_ref=src, dst_ref=dst, send_sem=out_sem(name), recv_sem=rs.at[sem(name)] if recv is None else recv,
            device_id=device, device_id_type=MESH,
        ).start()

    def keep(name, src, dst):
        pltpu.make_async_copy(src, dst, rs.at[sem(name)]).start()

    def landed(name, ref):
        wait(rs.at[sem(name)], ref)

    def sent_later(name, ref):
        if name in ODD:
            pending.append((ss.at[odd[name]], ref, None))
            return
        bins[-1] += size(ref)
        assert size(ref) % UNIT == 0, (name, size(ref))
        if bins[-1] > 1024 * UNIT // 16:
            bins.append(0)

    line_bytes = [0]

    def along_z(name, src, block):
        i, j = sem(name + "z"), sem(name + "f")
        for step in (1, -1, 2, -2):
            to = z + step
            far = (z == 0) if step == 2 else (z == PLANES - 1) if step == -2 else None

            @pl.when((to >= 0) & (to < PLANES))
            def _():
                pltpu.make_async_remote_copy(
                    src_ref=src, dst_ref=block(z), send_sem=ss.at[BINS],
                    recv_sem=rs.at[i] if far is None else rs.at[jnp.where(far, j, i)],
                    device_id=(c, at(to, y, x)), device_id_type=MESH,
                ).start()

        line_bytes[0] += size(src)

    def pass_on(name, block):
        for mine, origin, to in ((1, 3, 0), (2, 0, 3)):

            @pl.when(z == mine)
            def _():
                landed(name + "f", block(origin))
                pltpu.make_async_remote_copy(
                    src_ref=block(origin), dst_ref=block(origin), send_sem=ss.at[BINS], recv_sem=rs.at[sem(name + "z")],
                    device_id=(c, at(to, y, x)), device_id_type=MESH,
                ).start()

    def line_landed(name, blocks, own):
        @pl.when(edge)
        def _():
            landed(name + "z", blocks(3 + own))

        @pl.when(jnp.logical_not(edge))
        def _():
            landed(name + "z", blocks(2 + own))

    def to_plane(name, src, dst, slotted=False):
        half = lax.rem(z, 2)
        core = z // 2
        if slotted:
            recv = rs.at[jnp.where(half == 0, sem(name + "h0"), sem(name + "h1"))]
            part = dst.at[slot(core, y, x), half]
        else:
            recv = rs.at[sem(name)]
            part = dst.at[half]
        for m in range(2):
            plane = 2 * m + c
            own = (plane == z) & (core == c)
            out = ss.at[odd.setdefault(name + str(m), BINS + 1 + len(odd))]

            @pl.when(own)
            def _():
                pltpu.make_async_copy(src.at[m], part, recv).start()

            @pl.when(jnp.logical_not(own))
            def _():
                pltpu.make_async_remote_copy(
                    src_ref=src.at[m], dst_ref=part, send_sem=out, recv_sem=recv,
                    device_id=(core, at(plane, y, x)), device_id_type=MESH,
                ).start()

            pending.append((out, src.at[m], jnp.logical_not(own)))

    def from_plane(name, src, dst):
        micro, core = z // 2, lax.rem(z, 2)
        recv = rs.at[sem(name)]
        for half in range(2):
            zz = 2 * c + half
            own = (core == c) & (zz == z)
            part = dst.at[micro]
            out = ss.at[odd.setdefault(name + str(half), BINS + 1 + len(odd))]

            @pl.when(own)
            def _():
                pltpu.make_async_copy(src.at[half], part, recv).start()

            @pl.when(jnp.logical_not(own))
            def _():
                pltpu.make_async_remote_copy(
                    src_ref=src.at[half], dst_ref=part, send_sem=out, recv_sem=recv,
                    device_id=(core, at(zz, y, x)), device_id_type=MESH,
                ).start()

            pending.append((out, src.at[half], jnp.logical_not(own)))

    def to_heads(name, src, dst):
        keep(name, src.at[me_head], dst.at[me_slot])
        for cc, yy, xx in plane_peers:
            send(name, src.at[head(cc, yy, xx)], dst.at[me_slot], (cc, at(z, yy, xx)))
        sent_later(name, src.at[pl.ds(0, GROUP - 1)])

    def to_slot(name, src, dst, s):
        device = (s // 4, at(z, (s % 4) // 2, s % 2))
        i = sem(name)
        out = out_sem(name)

        @pl.when(me_slot == s)
        def _():
            pltpu.make_async_copy(src.at[s], dst.at[me_head], rs.at[i]).start()

        @pl.when(me_slot != s)
        def _():
            pltpu.make_async_remote_copy(
                src_ref=src.at[s], dst_ref=dst.at[me_head], send_sem=out, recv_sem=rs.at[i],
                device_id=device, device_id_type=MESH,
            ).start()

    weights = {
        "q": (w_q, s_in.at[1, pl.ds(0, 1)], g_q, c_q, p_q, q_q, z_q, o_in.at[1, pl.ds(0, 1)]),
    }

    for i in range(2):
        one = pl.ds(i, 1)
        refs = (w_out, s_out, g_out, c_out, p_out, q_out, z_out, o_out)
        weights["out" + str(i)] = tuple(
            ref.at[:, one] if ref is p_out or ref is q_out or ref is z_out else ref.at[one] for ref in refs
        )
        refs = (w_up, s_up, g_up, c_up, p_up, q_up, z_up, o_up)
        cols = pl.ds(i * 1024, 1024)
        weights["up" + str(i)] = tuple(
            ref.at[:, one] if ref is p_up or ref is q_up or ref is z_up
            else ref.at[:, :, cols] if ref is s_up or ref is o_up else ref.at[one]
            for ref in refs
        )
        refs = (w_dn, s_dn, g_dn, c_dn, p_dn, q_dn, z_dn, o_dn)
        cols = pl.ds(i * 256, 256)
        weights["dn" + str(i)] = tuple(
            ref.at[:, one] if ref is p_dn or ref is q_dn or ref is z_dn
            else ref.at[:, :, cols] if ref is s_dn or ref is o_dn else ref.at[one]
            for ref in refs
        )

    def halves(ref):
        cols = ref.shape[-1] // 2
        return pl.ds(0, cols), pl.ds(cols, cols)

    x_next, y_next, core_next = (c, at(z, y, 1 - x)), (c, at(z, 1 - y, x)), (1 - c, seq)

    def gather_z(g):
        full, shard = weights[g][:2]
        keep(g + "z", shard, full.at[:, c, z, y, x])
        along_z(g, shard, lambda zz: full.at[:, c, zz, y, x])

    def gather_f(g):
        full = weights[g][0]
        pass_on(g, lambda zz: full.at[:, c, zz, y, x])

    def gather_1(g):
        full = weights[g][0]
        first, second = halves(full)
        line_landed(g, lambda n: full.at[:, c, pl.ds(0, n), y, x], 1)
        part = full.at[:, c, :, y, x, :, first]
        send(g + "1a", part, part, x_next)
        sent_later(g + "1a", part)
        part = full.at[:, c, :, y, x, :, second]
        send(g + "1b", part, part, y_next)
        sent_later(g + "1b", part)

    def gather_2(g):
        full = weights[g][0]
        first, second = halves(full)
        landed(g + "1a", full.at[:, c, :, y, 1 - x, :, first])
        part = full.at[:, c, :, y, :, :, first]
        send(g + "2a", part, part, y_next)
        sent_later(g + "2a", part)
        landed(g + "1b", full.at[:, c, :, 1 - y, x, :, second])
        part = full.at[:, c, :, :, x, :, second]
        send(g + "2b", part, part, x_next)
        sent_later(g + "2b", part)

    def gather_3(g):
        full = weights[g][0]
        first, second = halves(full)
        landed(g + "2a", full.at[:, c, :, 1 - y, :, :, first])
        landed(g + "2b", full.at[:, c, :, :, 1 - x, :, second])
        send(g + "3", full.at[:, c], full.at[:, c], core_next)
        sent_later(g + "3", full.at[:, c])

    def gathered(g):
        landed(g + "3", weights[g][0].at[:, 1 - c])

    def add(target, other):
        target[...] = (target[...].astype(F32) + other[...].astype(F32)).astype(BF16)

    def scatter_0(g):
        grad, across = weights[g][2:4]
        send(g + "r0", grad.at[:, 1 - c], across, core_next)
        sent_later(g + "r0", across)

    def scatter_1(g):
        grad, across, part = weights[g][2:5]
        first, second = halves(grad)
        landed(g + "r0", across)
        for lead in range(grad.shape[0]):

            @pl.loop(0, PLANES)
            def _(zz):
                add(grad.at[lead, c, zz], across.at[lead, zz])

        send(g + "r1a", grad.at[:, c, :, 1 - y, :, :, first], part.at[0], y_next)
        sent_later(g + "r1a", part.at[0])
        send(g + "r1b", grad.at[:, c, :, :, 1 - x, :, second], part.at[1], x_next)
        sent_later(g + "r1b", part.at[1])

    def scatter_2(g):
        grad, _, part, piece = weights[g][2:6]
        first, second = halves(grad)
        landed(g + "r1a", part.at[0])
        landed(g + "r1b", part.at[1])
        for lead in range(grad.shape[0]):

            @pl.loop(0, PLANES)
            def _(zz):
                add(grad.at[lead, c, zz, y, :, :, first], part.at[0, lead, zz])
                add(grad.at[lead, c, zz, :, x, :, second], part.at[1, lead, zz])

        send(g + "r2a", grad.at[:, c, :, y, 1 - x, :, first], piece.at[0], x_next)
        sent_later(g + "r2a", piece.at[0])
        send(g + "r2b", grad.at[:, c, :, 1 - y, x, :, second], piece.at[1], y_next)
        sent_later(g + "r2b", piece.at[1])

    def scatter_3(g):
        grad, _, _, piece, line = weights[g][2:7]
        first, second = halves(grad)
        landed(g + "r2a", piece.at[0])
        landed(g + "r2b", piece.at[1])
        for lead in range(grad.shape[0]):

            @pl.loop(0, PLANES)
            def _(zz):
                add(grad.at[lead, c, zz, y, x, :, first], piece.at[0, lead, zz])
                add(grad.at[lead, c, zz, y, x, :, second], piece.at[1, lead, zz])

        for k in range(3):
            send(g + "r3", grad.at[:, c, z_peers[k], y, x], line.at[2 - k], (c, at(z_peers[k], y, x)))
        sent_later(g + "r3", line)

    def scattered(g):
        grad, _, _, _, line, result = weights[g][2:8]
        landed(g + "r3", line)
        total = grad[:, c, z, y, x].astype(F32)
        for k in range(3):
            total = total + line[k].astype(F32)
        result[...] = total

    left, right = pl.ds(0, 256), pl.ds(256, 256)
    y_slot, x_slot, far_slot = slot(c, 1 - y, x), slot(c, y, 1 - x), slot(c, 1 - y, 1 - x)

    def spread_1(name, full, half):
        own = full.at[me_slot, half]
        landed(name + "h" + str(half), own)
        for which, device in (("y", y_next), ("x", x_next), ("c", core_next)):
            which = which if which == "c" else which + str(half)
            send(name + which, own, own, device)
            sent_later(name + which, own)

    def spread_2(name, full, half):
        for which, place, cols, device in (("y", y_slot, right, x_next), ("x", x_slot, left, y_next)):
            part = full.at[place, half]
            landed(name + which + str(half), part)
            half_of = full.at[place, half, :, cols]
            send(name + "q" + which + str(half), half_of, half_of, device)
            sent_later(name + "q" + which + str(half), half_of)
            send(name + "d", part, part, core_next)
            sent_later(name + "d", part)

    def spread_4(name, full, half):
        part = full.at[far_slot, half]
        landed(name + "qy" + str(half), full.at[far_slot, half, :, right])
        landed(name + "qx" + str(half), full.at[far_slot, half, :, left])
        send(name + "d", part, part, core_next)
        sent_later(name + "d", part)

    def spread_3(name, full):
        landed(name + "c", full.at[0])
        landed(name + "d", full.at[pl.ds(0, 3)])

    def merge_0(name, full, across):
        send(name + "c", full.at[pl.ds((1 - c) * 4, 4)], across, core_next)
        sent_later(name + "c", across)

    def merge_1(name, full, across, parts):
        landed(name + "c", across)
        add(full.at[far_slot], across.at[(1 - y) * 2 + 1 - x])
        send(name + "qx", full.at[far_slot, :, :, left], parts.at[2, :, :, left], y_next)
        send(name + "qy", full.at[far_slot, :, :, right], parts.at[2, :, :, right], x_next)
        sent_later(name + "q", parts.at[2])
        add(full.at[x_slot], across.at[y * 2 + 1 - x])
        add(full.at[y_slot], across.at[(1 - y) * 2 + x])
        add(full.at[me_slot], across.at[yx])

    def merge_3(name, full, parts):
        landed(name + "qx", parts.at[2, :, :, left])
        add(full.at[x_slot, :, :, left], parts.at[2, :, :, left])
        send(name + "px", full.at[x_slot], parts.at[0], x_next)
        sent_later(name + "px", parts.at[0])
        landed(name + "qy", parts.at[2, :, :, right])
        add(full.at[y_slot, :, :, right], parts.at[2, :, :, right])
        send(name + "py", full.at[y_slot], parts.at[1], y_next)
        sent_later(name + "py", parts.at[1])

    def merge_2(name, full, parts):
        landed(name + "px", parts.at[0])
        landed(name + "py", parts.at[1])
        total = full[me_slot].astype(F32)
        for k in range(2):
            total = total + parts[k].astype(F32)
        return total.reshape(here, width)

    def tile(index):
        return pl.ds(pl.multiple_of(index * 128, 128), 128)

    def slice_1(name, shard, full):
        keep(name + "p", shard.at[:, :, tile(yx)], full.at[:, c, z, yx])
        for yy, xx in trio:
            send(name + "p", shard.at[:, :, tile(yy * 2 + xx)], full.at[:, c, z, yx], (c, at(z, yy, xx)))
        sent_later(name + "p", full.at[:, c, z, pl.ds(0, 3)])

    def slice_2(name, full):
        landed(name + "p", full.at[:, c, z])
        along_z(name, full.at[:, c, z], lambda zz: full.at[:, c, zz])

    def slice_f(name, full):
        pass_on(name, lambda zz: full.at[:, c, zz])

    def slice_3(name, full):
        line_landed(name, lambda n: full.at[:, c, pl.ds(0, n)], 0)
        send(name + "c", full.at[:, c], full.at[:, c], core_next)
        sent_later(name + "c", full.at[:, c])

    def slice_4(name, full):
        landed(name + "c", full.at[:, 1 - c])

    def unslice_0(name, grad, across):
        send(name + "c", grad.at[:, 1 - c], across, core_next)
        sent_later(name + "c", across)

    def unslice_1(name, grad, across, line):
        landed(name + "c", across)
        for lead in range(grad.shape[0]):
            add(grad.at[lead, c], across.at[lead])
        for k in range(3):
            send(name + "z", grad.at[:, c, z_peers[k]], line.at[2 - k], (c, at(z_peers[k], y, x)))
        sent_later(name + "z", line)

    def unslice_2(name, grad, line, total, result):
        landed(name + "z", line)
        value = grad[:, c, z].astype(F32)
        for k in range(3):
            value = value + line[k].astype(F32)
        total[...] = value
        for yy, xx in trio:
            send(name + "p", total.at[:, yy * 2 + xx], result.at[:, :, tile(yx)], (c, at(z, yy, xx)))
        sent_later(name + "p", total.at[:, pl.ds(0, 3)])
        result[:, :, tile(yx)] = total[:, yx]

    def unslice_3(name, result):
        landed(name + "p", result.at[:, :, pl.ds(0, 384)])

    def matrix(ref):
        return ref[...].reshape(-1, ref.shape[-1])

    def put(ref, value):
        ref[...] = value.astype(BF16).reshape(ref.shape)

    def norm(r, i, kept):
        centered = r - jnp.mean(r, axis=1, keepdims=True)
        scale = lax.rsqrt(jnp.mean(centered * centered, axis=1, keepdims=True) + 1e-05)
        xhat = centered * scale
        kept[...] = xhat
        return xhat * gain[i : i + 1, :] + shift[i : i + 1, :], scale

    def column(row, value):
        sg0[row : row + 1, :] = jnp.sum(value, axis=0, keepdims=True)

    def norm_back(grad, i, kept, scale, skip):
        xhat = kept[...]
        column(11 + i, grad * xhat)
        column(14 + i, grad)
        dxhat = grad * gain[i : i + 1, :]
        dr = dxhat - jnp.mean(dxhat, axis=1, keepdims=True)
        dr = (dr - xhat * jnp.mean(dxhat * xhat, axis=1, keepdims=True)) * scale
        column(17 + i, dr * skip)
        return dr, dr * omega[i : i + 1, :]

    BLOCK = 256

    def attend(b, queries, keys, values_t, weights_t, sums, outputs, causal, name, target, arrives):
        extent = 512 if causal and b < 2 else 1024
        cols = slice(b * BLOCK, (b + 1) * BLOCK)
        scores = nn(keys[:extent, :], queries[:, cols])
        seg = rows_f[0:1, cols]
        code = (code_self if causal else code_cross)[:extent, :]
        permit = jnp.concatenate([code, code], axis=1) == seg
        if causal:
            pos = key_pos[:extent, :]
            pos = jnp.concatenate([pos, pos], axis=1)
            mine = rows_f[1:2, cols]
            permit = (permit & (pos <= mine)) | (pos == mine)
        weight = jnp.where(permit, jnp.exp(scores), 0.0)
        total = jnp.sum(weight, axis=0, keepdims=True)
        low = weight.astype(BF16)
        weights_t[:extent, cols] = low
        out = nn(values_t[:, :extent], low) / total
        sums[0:1, cols] = total
        outputs[:, cols] = out
        for k in range(2):
            target[2 * b + k] = out[:, k * here : (k + 1) * here].astype(BF16)
            to_slot(name, target, arrives, 2 * b + k)
        if b == 3:
            sent_later(name, target.at[pl.ds(0, GROUP - 1)])

    def attend_start(buffer, sums, outputs):
        acc_k[...] = jnp.zeros_like(acc_k)
        acc_v[...] = jnp.zeros_like(acc_v)
        for s in range(GROUP):
            cols = slice(s * here, (s + 1) * here)
            grad = buffer[s].astype(F32)
            inverse = 1.0 / sums[0:1, cols]
            dnt[:, cols] = (grad * inverse).astype(BF16)
            rows_f[2:3, cols] = -jnp.sum(grad * outputs[:, cols], axis=0, keepdims=True) * inverse

    def attend_back(b, queries, keys_t, values, weights_t, causal, name, target, arrives):
        extent = 512 if causal and b < 2 else 1024
        cols = slice(b * BLOCK, (b + 1) * BLOCK)
        low = weights_t[:extent, cols]
        dn = dnt[:, cols]
        spread = nn(values[:extent, :], dn)
        slopes = (low.astype(F32) * (spread + rows_f[2:3, cols])).astype(BF16)
        block = (nn(keys_t[:, :extent], slopes) * 0.125).astype(BF16)
        if name is None:
            dt0[0:64, cols] = block
        else:
            for k in range(2):
                target[2 * b + k] = block[:, k * here : (k + 1) * here]
                to_slot(name, target, arrives, 2 * b + k)
            if b == 3:
                sent_later(name, target.at[pl.ds(0, GROUP - 1)])
        acc_k[:, :extent] += nt(queries[:, cols], slopes)
        acc_v[:, :extent] += nt(dn, low)

    def by_head(target, value):
        target[...] = flip(value).astype(BF16).reshape(GROUP, 64, here)

    def heads_weights(first, full):
        for j in range(full.shape[0]):
            wt[first + j] = flip(matrix(full.at[j])).astype(BF16)

    own_rows = pl.ds(pl.multiple_of(c * 64, 64), 64)
    own_head = pl.ds(pl.multiple_of(me_head * 64, 64), 64)

    def own_weights(first, count):
        return jnp.concatenate([wt[first + j, own_rows, :] for j in range(count)], axis=0)

    def wide_bias(i):
        col = bias_cols[i, own_head, :]
        return jnp.concatenate([col, col], axis=1)

    def project_heads(rows, first, queries, keys, keys_t, values, values_t):
        count = 2 if queries is None else 3
        own = own_weights(first, count)
        for b in range(4):
            cols = slice(b * 256, (b + 1) * 256)
            out = nt(own, rows[2 * b : 2 * b + 2].reshape(256, width))
            if queries is not None:
                queries[:, cols] = ((out[0:64] + wide_bias(0)).astype(BF16).astype(F32) * 0.125).astype(BF16)
            at_k = 64 * (count - 2)
            block = out[at_k : at_k + 64].astype(BF16)
            keys_t[:, cols] = block
            keys[cols, :] = flip(block).astype(BF16)
            block = (out[at_k + 64 : at_k + 128] + wide_bias(1 if count == 3 else 2)).astype(BF16)
            values_t[:, cols] = block
            values[cols, :] = flip(block).astype(BF16)

    def rows_back(grads_t, first, target, core):
        count = grads_t.shape[0] // 64
        own = own_weights(first, count)
        for b in range(2):
            cols = pl.ds(pl.multiple_of(core * 512 + b * 256, 256), 256)
            out = tn(grads_t[:, cols], own)
            target[pl.ds(core * 4 + b * 2, 2)] = out.astype(BF16).reshape(2, 2, 64, width)

    def slices_back(grads_t, rows, grad):
        count = grads_t.shape[0] // 64
        out = nn(grads_t[...], rows[...].reshape(1024, width))
        wz[...] = jnp.zeros_like(wz)
        for j in range(count):
            wz[j, own_rows, :] = out[j * 64 : (j + 1) * 64]
            put(grad.at[j], jnp.transpose(wz[j]))

    def bias(i):
        return biases[i : i + 1, :]

    def make_masks():
        landed("marks", all_meta.at[pl.ds(0, 7)])
        order = lax.broadcasted_iota(jnp.int32, (1, 1024), 1)
        place = (order // 512) * 512 + lax.rem(order // 64, 2) * 256 + lax.rem(order // 128, 4) * 64 + lax.rem(order, 64)
        place = place.astype(F32)
        marks = [all_meta[s].astype(F32) for s in range(GROUP)]
        tgt_real = jnp.concatenate([mark[0:1, :] for mark in marks], axis=1)
        src_real = jnp.concatenate([mark[1:2, :] for mark in marks], axis=1)
        lower = lax.broadcasted_iota(jnp.int32, (32, 128), 1)
        later = lax.broadcasted_iota(jnp.int32, (32, 128), 0)

        def ends_of(row):
            lengths = jnp.broadcast_to(row, (32, 128))
            ends = jnp.sum(jnp.where(lower <= later, lengths, 0.0), axis=1, keepdims=True)
            starts = jnp.sum(jnp.where(lower < later, lengths, 0.0), axis=1, keepdims=True)
            return ends, starts

        def count(flags):
            return jnp.sum(jnp.where(flags, 1.0, 0.0), axis=0, keepdims=True)

        tgt_ends, _ = ends_of(marks[0][2:3, :])
        src_ends, src_starts = ends_of(marks[0][3:4, :])
        tgt_seg = count(tgt_ends <= place)
        src_seg = count(src_ends <= place)
        src_first = count(src_starts == place)
        self_row = jnp.where(tgt_real > 0.5, tgt_seg, -1.0)
        cross_row = jnp.where((src_real > 0.5) | (src_first > 0.5), src_seg, -1.0)
        rows_f[0:1, :] = tgt_seg
        rows_f[1:2, :] = place
        code_self[...] = jnp.transpose(jnp.broadcast_to(self_row, (128, 1024)))
        code_cross[...] = jnp.transpose(jnp.broadcast_to(cross_row, (128, 1024)))
        key_pos[...] = jnp.transpose(jnp.broadcast_to(place, (128, 1024)))

    def feed_up(rows, i):
        for k in (2 * i, 2 * i + 1):
            cols = slice(k * width, (k + 1) * width)
            inner = slice((k % 2) * width, (k % 2 + 1) * width)
            u = nn(rows, matrix(w_up.at[i, :, :, :, :, :, inner])) + up_bias[0:1, cols]
            square = u * u
            t = jnp.tanh(u * (0.7978845608028654 + 0.035677408136300125 * square))
            act[:, cols] = (0.5 * u * (1.0 + t)).astype(BF16)
            inner = 0.7978845608028654 + 0.10703222440890037 * square
            slope[:, cols] = 0.5 * (1.0 + t) + 0.5 * u * (1.0 - t * t) * inner

    def feed_back(gf, back):
        for k in range(4):
            cols = slice(k * width, (k + 1) * width)
            inner = slice((k % 2) * width, (k % 2 + 1) * width)
            rows = pl.ds(2 * (k % 2), 2)
            gu = nt(gf[:, 0:256], matrix(w_dn.at[0, k // 2, rows]))
            gu = gu + nt(gf[:, 256:512], matrix(w_dn.at[1, k // 2, rows]))
            gu = (gu * slope[:, cols]).astype(BF16)
            gul[:, cols] = gu
            column(7 + k, gu.astype(F32))
            back = back + nt(gu, matrix(w_up.at[k // 2, :, :, :, :, :, inner]))
        return back

    def value_sums(grads_t):
        total = jnp.sum(grads_t[64:128, :].astype(F32), axis=1, keepdims=True)
        bias_cols[0] = jnp.zeros((width, 128), F32)
        bias_cols[0, own_head, :] = jnp.broadcast_to(total, (64, 128))
        sg0[4:5, :] = jnp.transpose(bias_cols[0])[0:1, :]

    def head_sums(grads_t):
        lanes = lax.broadcasted_iota(jnp.int32, (64, 128), 1)
        dq_sum = jnp.sum(grads_t[0:64, :].astype(F32), axis=1, keepdims=True)
        dv_sum = jnp.sum(grads_t[128:192, :].astype(F32), axis=1, keepdims=True)
        bias_cols[0] = jnp.zeros((width, 128), F32)
        bias_cols[0, own_head, :] = jnp.where(lanes == 0, dq_sum, dv_sum)
        tg0[...] = jnp.transpose(bias_cols[0])[0:8, :]

    def small(name, src, dst, device):
        send(name, src, dst, device)
        sent_later(name, dst)

    def small_add(name, arrived, mine, total):
        landed(name, arrived)
        total[...] = mine[...] + arrived[...]

    def small_z(name, src, dst):
        for k in range(3):
            send(name, src, dst.at[2 - k], (c, at(z_peers[k], y, x)))
        sent_later(name, dst)

    def small_out():
        landed("s3", sr3)
        sg4[...] = sg3[...] + sr3[0] + sr3[1] + sr3[2]
        landed("t3", tr3)
        sg4[0:2, :] = (tg3[...] + tr3[0] + tr3[1] + tr3[2])[0:2, :]
        block = c * 16 + seq
        tile_of = sg4[:, pl.ds(pl.multiple_of((block // 8) * 128, 128), 128)]
        turned = pltpu.roll(tile_of, lax.rem(128 - lax.rem(block, 8) * 16, 128), 1)
        o_bias[...] = turned[0:7, 0:16]
        o_gain[...] = turned[11:14, 0:16]
        o_shift[...] = turned[14:17, 0:16]
        o_omega[...] = turned[17:20, 0:16]
        tile_of = sg4[:, pl.ds(pl.multiple_of((lax.rem(block, 8) // 2) * 128, 128), 128)]
        turned = pltpu.roll(tile_of, lax.rem(block, 2) * 64, 1)
        wanted = block // 8
        row = jnp.zeros((1, 64), F32)
        for k in range(4):
            row = row + turned[7 + k : 8 + k, 0:64] * (wanted == k).astype(F32)
        o_upb[...] = row
        ends = ((o_bias, h_bias), (o_upb, h_upb), (o_gain, h_gain_o), (o_shift, h_shift_o), (o_omega, h_omega_o))
        for i, (src, dst) in enumerate(ends):
            keep("e" + str(4 + i), src, dst)

    raw = ((raw_tm, tgt_msk), (raw_sm, src_msk), (raw_tl, tgt_len), (raw_sl, src_len))
    for i, (ref, given) in enumerate(raw):
        keep("raw" + str(i), given, ref)
    given = ((h_biases, biases), (h_up_bias, up_bias), (h_gain, gain), (h_shift, shift), (h_omega, omega))
    for i, (src, ref) in enumerate(given):
        keep("given" + str(i), src, ref)
    barrier = pltpu.get_barrier_semaphore()
    greet = [(cc, at(z, yy, xx)) for cc, yy, xx in plane_peers]
    greet += [(cc, at(zz, y, x)) for zz in z_peers for cc in (c, 1 - c)]
    for device in greet:
        pl.semaphore_signal(barrier, inc=1, device_id=device, device_id_type=MESH)
    pl.semaphore_wait(barrier, len(greet))
    gather_z("q")
    to_plane("m", mem, all_mem, True)
    for i, (ref, _) in enumerate(raw):
        landed("raw" + str(i), ref)
        span = ref.shape[2]
        for m in range(2):
            for start in (0, 64):
                meta[m, i : i + 1, start : start + span] = ref[m]
    gather_f("q")
    slice_1("w0", s_in.at[0], ws0)
    to_plane("meta", meta, in_meta)
    gather_z("out0")
    slice_1("w1", s_in.at[1, pl.ds(1, 2)], ws1)
    to_plane("x", tok, all_tok, True)
    gather_1("q")
    gather_z("up0")
    spread_1("m", all_mem, 0)
    spread_1("m", all_mem, 1)
    gather_z("out1")
    gather_f("out0")
    gather_z("dn1")
    landed("meta", in_meta)
    lane = lax.broadcasted_iota(jnp.int32, (8, 128), 1)
    slice_2("w0", ws0)
    gather_2("q")
    all_meta[me_slot] = jnp.where(lane < 64, in_meta[0], in_meta[1])
    spread_2("m", all_mem, 0)
    spread_1("x", all_tok, 0)
    spread_1("x", all_tok, 1)
    spread_2("m", all_mem, 1)
    gather_f("up0")
    gather_f("out1")
    gather_z("up1")
    gather_3("q")
    for i, (_, ref) in enumerate(given):
        landed("given" + str(i), ref)
    gather_1("out0")
    spread_2("x", all_tok, 0)
    slice_2("w1", ws1)
    gather_1("up0")
    spread_4("m", all_mem, 0)
    spread_2("x", all_tok, 1)
    gather_2("out0")
    gather_f("dn1")
    for cc, yy, xx in plane_peers:
        send("marks", all_meta.at[me_slot], all_meta.at[me_slot], (cc, at(z, yy, xx)))
    slice_f("w0", ws0)
    gather_z("dn0")
    for i, row in enumerate((0, 1, 4)):
        bias_cols[i] = jnp.transpose(jnp.broadcast_to(bias(row), (128, width)))
    gather_1("out1")
    gather_2("up0")
    gather_f("up1")
    spread_4("x", all_tok, 0)
    slice_f("w1", ws1)
    spread_4("x", all_tok, 1)
    sent_later("marks", all_meta.at[pl.ds(0, 7)])
    gather_1("dn1")
    slice_3("w0", ws0)
    gather_2("out1")
    make_masks()
    gather_1("up1")
    slice_4("w0", ws0)
    gather_3("out0")
    heads_weights(0, ws0)
    gather_3("up0")
    spread_4("m", all_mem, 1)
    gather_2("dn1")
    spread_3("x", all_tok)
    project_heads(all_tok, 0, qt0, k0, kt0, v0, vt0)
    attend(0, qt0, k0, vt0, pt0, l0, ot0, True, "x3", a3, b3)
    slice_3("w1", ws1)
    gather_f("dn0")
    attend(1, qt0, k0, vt0, pt0, l0, ot0, True, "x3", a3, b3)
    attend(2, qt0, k0, vt0, pt0, l0, ot0, True, "x3", a3, b3)
    spread_3("m", all_mem)
    attend(3, qt0, k0, vt0, pt0, l0, ot0, True, "x3", a3, b3)
    gather_1("dn0")
    slice_4("w1", ws1)
    to_plane("cot", cot, in_cot)
    gather_2("up1")
    gathered("out0")
    gathered("q")
    heads_weights(3, ws1)
    project_heads(all_mem, 3, None, k1, kt1, v1, vt1)
    landed("x3", b3)
    words_f = all_tok[me_slot].reshape(here, width).astype(F32)
    branch = tn(b3[...].reshape(width, here), matrix(w_out.at[0])) + bias(2)
    h1, scale0 = norm(words_f * omega[0:1, :] + branch, 0, xh0)
    h1_f[...] = h1
    h1_low = h1.astype(BF16)
    by_head(a4, nn(h1_low, matrix(w_q.at[0])) + bias(3))
    to_heads("x4", a4, b4)
    gather_3("dn1")
    gather_2("dn0")
    gathered("up0")
    gather_3("out1")
    gather_3("up1")
    gathered("out1")
    landed("x4", b4)
    for s in range(GROUP):
        qt1[:, s * here : (s + 1) * here] = (b4[s].astype(F32) * 0.125).astype(BF16)
    attend(0, qt1, k1, vt1, pt1, l1, ot1, False, "x5", a5, b5)
    attend(1, qt1, k1, vt1, pt1, l1, ot1, False, "x5", a5, b5)
    attend(2, qt1, k1, vt1, pt1, l1, ot1, False, "x5", a5, b5)
    attend(3, qt1, k1, vt1, pt1, l1, ot1, False, "x5", a5, b5)
    gather_3("dn0")
    gathered("dn0")
    gathered("up1")
    gathered("dn1")
    landed("x5", b5)
    branch = tn(b5[...].reshape(width, here), matrix(w_out.at[1])) + bias(5)
    h2, scale1 = norm(h1_f[...] * omega[1:2, :] + branch, 1, xh1)
    h2_f[...] = h2
    h2_low = h2.astype(BF16)
    feed_up(h2_low, 0)
    feed_up(h2_low, 1)
    first = nn(act[...], matrix(w_dn.at[0]))
    second = nn(act[...], matrix(w_dn.at[1]))
    h3, scale2 = norm(h2_f[...] * omega[2:3, :] + jnp.concatenate([first, second], axis=1) + bias(6), 2, xh2)
    out_res[...] = h3.astype(BF16).reshape(2, 64, width)
    landed("cot", in_cot)
    grad = in_cot[...].reshape(here, width).astype(F32)
    dr, skip = norm_back(grad, 2, xh2, scale2, h2_f[...])
    gf = dr.astype(BF16)
    column(6, gf.astype(F32))
    back = feed_back(gf, skip)
    put(g_up.at[0], tn(h2_low, gul[:, 0:1024]))
    scatter_0("up0")
    dr, skip = norm_back(back, 1, xh1, scale1, h1_f[...])
    gc = dr.astype(BF16)
    column(5, gc.astype(F32))
    by_head(a6, nt(gc, matrix(w_out.at[1])))
    to_heads("x6", a6, b6)
    put(g_up.at[1], tn(h2_low, gul[:, 1024:2048]))
    scatter_1("up0")
    scatter_0("up1")
    from_plane("res", out_res, o_res)
    put(g_dn.at[0], tn(act[...], gf[:, 0:256]))
    put(g_dn.at[1], tn(act[...], gf[:, 256:512]))
    scatter_1("up1")
    back = skip
    landed("x6", b6)
    attend_start(b6, l1, ot1)
    attend_back(0, qt1, kt1, v1, pt1, False, "x7", a7, b7)
    scatter_0("dn1")
    attend_back(1, qt1, kt1, v1, pt1, False, "x7", a7, b7)
    attend_back(2, qt1, kt1, v1, pt1, False, "x7", a7, b7)
    attend_back(3, qt1, kt1, v1, pt1, False, "x7", a7, b7)
    scatter_2("up0")
    dt1[0:64, :] = acc_k[...].astype(BF16)
    dt1[64:128, :] = acc_v[...].astype(BF16)
    scatter_2("up1")
    put(g_out.at[1], nn(b5[...].reshape(width, here), gc))
    rows_back(dt1, 3, dx1, 1 - c)
    merge_0("dm", dx1, dc1)
    rows_back(dt1, 3, dx1, c)
    slices_back(dt1, all_mem, gs1)
    unslice_0("u1", gs1, cs1)
    scatter_1("dn1")
    value_sums(dt1)
    landed("x7", b7)
    dq = b7[...].reshape(width, here)
    dq_row = flip(dq)
    column(3, dq_row)
    scatter_3("up0")
    back = back + nt(dq_row.astype(BF16), matrix(w_q.at[0]))
    dr, skip = norm_back(back, 0, xh0, scale0, words_f)
    ga = dr.astype(BF16)
    column(2, ga.astype(F32))
    scatter_0("out1")
    by_head(a8, nt(ga, matrix(w_out.at[0])))
    put(g_q.at[0], nt(flip(h1_low).astype(BF16), dq))
    to_heads("x8", a8, b8)
    scatter_0("q")
    merge_1("dm", dx1, dc1, dp1)
    put(g_out.at[0], nn(b3[...].reshape(width, here), ga))
    scatter_3("up1")
    small("s0", sg0, sr0, core_next)
    scatter_0("out0")
    scatter_0("dn0")
    scatter_2("dn1")
    unslice_1("u1", gs1, cs1, zs1)
    small_add("s0", sr0, sg0, sg1)
    scatter_1("out0")
    small("s1", sg1, sr1, y_next)
    last = skip
    landed("x8", b8)
    attend_start(b8, l0, ot0)
    attend_back(0, qt0, kt0, v0, pt0, True, None, None, None)
    attend_back(1, qt0, kt0, v0, pt0, True, None, None, None)
    merge_3("dm", dx1, dp1)
    attend_back(2, qt0, kt0, v0, pt0, True, None, None, None)
    scatter_3("dn1")
    attend_back(3, qt0, kt0, v0, pt0, True, None, None, None)
    dt0[64:128, :] = acc_k[...].astype(BF16)
    dt0[128:192, :] = acc_v[...].astype(BF16)
    slices_back(dt0, all_tok, gs0)
    unslice_0("u0", gs0, cs0)
    scattered("up0")
    rows_back(dt0, 0, dx0, 1 - c)
    small_add("s1", sr1, sg1, sg2)
    small("s2", sg2, sr2, x_next)
    head_sums(dt0)
    scatter_1("q")
    unslice_1("u0", gs0, cs0, zs0)
    merge_0("dx", dx0, dc0)
    scatter_1("dn0")
    scatter_1("out1")
    rows_back(dt0, 0, dx0, c)
    small("t0", tg0, tr0, core_next)
    small_add("t0", tr0, tg0, tg1)
    scatter_2("out0")
    small("t1", tg1, tr1, y_next)
    merge_1("dx", dx0, dc0, dp0)
    small_add("s2", sr2, sg2, sg3)
    small_z("s3", sg3, sr3)
    scatter_2("q")
    out_mem[...] = merge_2("dm", dx1, dp1).astype(BF16).reshape(2, 64, width)
    from_plane("gmem", out_mem, o_mem)
    scatter_2("dn0")
    small_add("t1", tr1, tg1, tg2)
    scatter_2("out1")
    unslice_2("u1", gs1, zs1, fs1, o_in.at[1, pl.ds(1, 2)])
    scatter_3("out0")
    small("t2", tg2, tr2, x_next)
    merge_3("dx", dx0, dp0)
    scatter_3("dn0")
    scatter_3("q")
    scatter_3("out1")
    unslice_3("u1", o_in.at[1, pl.ds(1, 2)])
    scattered("out0")
    out_tok[...] = (merge_2("dx", dx0, dp0) + last).astype(BF16).reshape(2, 64, width)
    unslice_2("u0", gs0, zs0, fs0, o_in.at[0])
    small_add("t2", tr2, tg2, tg3)
    scattered("up1")
    small_z("t3", tg3, tr3)
    landed("res", o_res)
    from_plane("gtok", out_tok, o_tok)
    scattered("dn1")
    scattered("dn0")
    unslice_3("u0", o_in.at[0])
    landed("gmem", o_mem)
    scattered("out1")
    keep("e3", o_dn, h_dn)
    small_out()
    keep("e2", o_up, h_up)
    keep("e1", o_out, h_out)
    scattered("q")
    keep("e0", o_in, h_in)
    landed("gtok", o_tok)
    for i, ref in enumerate((h_in, h_out, h_up, h_dn, h_bias, h_upb, h_gain_o, h_shift_o, h_omega_o)):
        landed("e" + str(i), ref)
    for semaphore, ref, when in pending:
        if when is None:
            wait(semaphore, ref)
        else:

            @pl.when(when)
            def _():
                wait(semaphore, ref)

    for i, total in enumerate(bins):
        if total:
            wait(ss.at[i], gauge.at[pl.ds(0, total // 1024)])
    units = line_bytes[0] // UNIT
    assert line_bytes[0] % UNIT == 0

    @pl.when(edge)
    def _():
        wait(ss.at[BINS], gauge.at[pl.ds(0, 2 * units * 16)])

    @pl.when(jnp.logical_not(edge))
    def _():
        wait(ss.at[BINS], gauge.at[pl.ds(0, 4 * units * 16)])

    assert len(names) <= NAMES and len(bins) <= BINS and BINS + 1 + len(odd) <= ss.shape[0]


def copy_kernel(*refs):
    count = len(refs) // 2
    for i in range(count):
        refs[count + i][...] = refs[i][...]


def fused_local(
    tokens, memory, cotangent, tgt_lengths, src_lengths, tgt_mask, src_mask, attn_in, attn_out, w_up, w_down,
    biases, up_bias, norm_gain, norm_shift, omega,
):
    any_space = pl.BlockSpec(memory_space=pl.ANY)
    vmem = pl.BlockSpec(memory_space=pltpu.VMEM)
    lines = (CORES, PLANES, YS, XS)
    leads = {"q": 1, "out": 2, "up": 2, "dn": 2}
    shards = {"q": (16, 512), "out": (16, 512), "up": (16, 1024), "dn": (64, 256)}
    kinds = tuple(leads)

    def low(*shape):
        return pltpu.VMEM(shape, BF16)

    def full(*shape):
        return pltpu.VMEM(shape, F32)

    def whole(k):
        return low(leads[k], *lines, *shards[k])

    def halved(k, *middle):
        return low(2, leads[k], *middle, shards[k][0], shards[k][1] // 2)

    params = [full(7, 512), full(1, 2048), full(3, 512), full(3, 512), full(3, 512)]
    results = [(2, 3, 16, 512), (2, 16, 512), (1, 16, 2048), (1, 64, 512), (7, 16), (1, 64), (3, 16), (3, 16), (3, 16)]
    scratch = params + [full(*shape) for shape in results]
    scratch += [whole(k) for k in kinds] * 2
    scratch += [low(leads[k], *lines[1:], *shards[k]) for k in kinds]
    scratch += [halved(k, PLANES, 2) for k in kinds] + [halved(k, PLANES) for k in kinds]
    scratch += [low(3, leads[k], *shards[k]) for k in kinds]
    scratch += [low(n, CORES, PLANES, 4, 16, 128) for n in (3, 2)] * 2
    scratch += [low(n, PLANES, 4, 16, 128) for n in (3, 2)] + [low(3, n, 4, 16, 128) for n in (3, 2)]
    scratch += [full(n, 4, 16, 128) for n in (3, 2)]
    local_rows = low(2, 64, 512)
    marks = [pltpu.VMEM((2, 1, n), jnp.int32) for n in (32, 32, 64, 64)] + [pltpu.VMEM((2, 8, 128), jnp.int32)] * 2
    scratch += [low(GROUP, 2, 64, 512)] * 2 + [local_rows] + marks + [pltpu.VMEM((GROUP, 8, 128), jnp.int32)]
    scratch += [low(GROUP, 2, 64, 512)] * 2 + [low(4, 2, 64, 512)] * 2 + [low(3, 2, 64, 512)] * 2
    scratch += [low(GROUP, 64, 128)] * 12 + [local_rows] * 3
    scratch += [full(24, 512)] * 8 + [full(3, 24, 512)]
    scratch += [full(8, 512)] * 7 + [full(3, 8, 512)]
    scratch += [full(1024, 128)] * 3 + [full(8, 1024)]
    scratch += ([low(64, 1024)] * 3 + [low(1024, 64)] * 2 + [low(1024, 1024), full(1, 1024), full(64, 1024)]) * 2
    scratch += [low(64, 1024)] + [full(64, 1024)] * 2
    scratch += [low(128, 2048), full(128, 2048), low(128, 2048)] + [full(128, 512)] * 5
    scratch += [low(5, 128, 512), full(3, 512, 128), full(3, 128, 512), low(192, 1024), low(128, 1024), low(2048, 512)]
    scratch += [pltpu.SemaphoreType.DMA((40,)), pltpu.SemaphoreType.DMA((NAMES,))]
    rows = jax.ShapeDtypeStruct((2, 64, 512), BF16)

    def wide_out(*shape):
        return jax.ShapeDtypeStruct(shape, F32)

    outs = pl.pallas_call(
        fused_kernel,
        name="layer",
        out_shape=(rows, rows, rows, *(wide_out(*shape) for shape in results)),
        in_specs=[any_space] * 16,
        out_specs=(any_space,) * 12,
        scratch_shapes=scratch,
        compiler_params=pltpu.CompilerParams(collective_id=0, has_side_effects=True, vmem_limit_bytes=60 * 1024 * 1024),
    )(
        tokens.reshape(2, 64, 512), memory.reshape(2, 64, 512), cotangent.reshape(2, 64, 512),
        tgt_lengths, src_lengths, jnp.transpose(tgt_mask, (0, 2, 1)), jnp.transpose(src_mask, (0, 2, 1)),
        attn_in, attn_out, w_up.reshape(1, 16, 2048), w_down.reshape(1, 64, 512),
        biases, up_bias.reshape(1, 2048), norm_gain, norm_shift, omega,
    )
    outs = pl.pallas_call(
        copy_kernel,
        name="hand_over",
        out_shape=tuple(jax.ShapeDtypeStruct(out.shape, out.dtype) for out in outs),
        in_specs=[vmem] * len(outs),
        out_specs=(vmem,) * len(outs),
    )(*outs)
    shaped = [out.reshape(2, 64, 1, 512) for out in outs[:3]]
    return (
        *shaped, outs[3], outs[4], outs[5].reshape(16, 2048), outs[6].reshape(64, 512), outs[7], outs[8].reshape(64),
        outs[9], outs[10], outs[11],
    )


def solution(mesh):
    if mesh.shape["seq"] != PLANES * YS * XS or mesh.shape["rows"] != CORES:
        return general(mesh)
    return over(mesh, fused_local)
```

```python
import functools
import math

import jax
import jax.numpy as jnp
from jax import lax
from jax.experimental import pallas as pl
from jax.experimental.pallas import tpu as pltpu
from jax.sharding import PartitionSpec as P

HEADS = 8


def norm_block(branch, skip, scale, gain, shift):
    mixed = skip * scale + branch
    centered = mixed - jnp.mean(mixed, axis=-1, keepdims=True)
    variance = jnp.mean(centered * centered, axis=-1, keepdims=True)
    return centered * lax.rsqrt(variance + 1e-05) * gain + shift


def project(values, matrix):
    return jnp.einsum("trd,de->tre", values, matrix, preferred_element_type=jnp.float32)


def project_back(grads, matrix):
    return jnp.einsum("tre,de->trd", grads, matrix, preferred_element_type=jnp.float32)


def matrix_grad(values, grads):
    return jnp.einsum("trd,tre->de", values, grads, preferred_element_type=jnp.float32)


def column_sum(grads):
    return jnp.sum(grads.astype(jnp.float32), axis=(0, 1))


def segment_of(positions, ends):
    return jnp.sum((ends[None, :, :] <= positions[:, None, None]).astype(jnp.int32), axis=-1)


def segment_bounds(first, last, ends):
    lowest = jnp.sum((ends <= first).astype(jnp.int32), axis=-1)
    highest = jnp.sum((ends <= last).astype(jnp.int32), axis=-1)
    return (lowest, highest)


def ranges_share(query_bounds, key_bounds):
    return jnp.any((key_bounds[0] <= query_bounds[1]) & (key_bounds[1] >= query_bounds[0]))


def key_status(positions, real_marks, ends, starts, causal):
    segments = segment_of(positions, ends)
    usable = real_marks > 0.5
    if not causal:
        usable = usable | jnp.any(starts[None, :, :] == positions[:, None, None], axis=-1)
    return (segments, usable)


def permitted(query_pos, query_seg, key_pos, key_seg, usable, causal):
    same = jnp.transpose(query_seg)[:, :, None] == jnp.transpose(key_seg)[:, None, :]
    usable_keys = jnp.transpose(usable)[:, None, :]
    if causal:
        before = (key_pos[None, :] <= query_pos[:, None])[None]
        itself = (key_pos[None, :] == query_pos[:, None])[None]
        return same & before & (usable_keys | itself)
    return same & usable_keys


def block_grads(query_heads, grad_heads, lambdas, key_heads, value_heads, permit):
    scores = (
        jnp.einsum("arhd,brhd->rhab", query_heads, key_heads, preferred_element_type=jnp.float32)
        * 0.125
    )
    weights = jnp.where(permit[:, None], jnp.exp(scores), 0.0)
    spread = jnp.einsum(
        "arhd,brhd->rhab", grad_heads, value_heads, preferred_element_type=jnp.float32
    )
    slopes = weights * (spread + jnp.transpose(lambdas, (1, 2, 0))[..., None])
    return (weights.astype(jnp.bfloat16), slopes.astype(jnp.bfloat16))


def local(
    tokens,
    memory,
    cotangent,
    tgt_lengths,
    src_lengths,
    tgt_mask,
    src_mask,
    attn_in,
    attn_out,
    w_up,
    w_down,
    biases,
    up_bias,
    norm_gain,
    norm_shift,
    omega,
):
    micro_count, tokens_here, rows_here, width = tokens.shape
    head_size = width // HEADS
    my_pos = lax.axis_index("seq") * tokens_here + jnp.arange(tokens_here, dtype=jnp.int32)
    my_first = my_pos[0]
    my_last = my_pos[tokens_here - 1]

    def split_heads(values):
        return values.reshape(values.shape[0], rows_here, HEADS, head_size)

    def zero_heads():
        return jnp.zeros((tokens_here, rows_here, HEADS, head_size), jnp.float32)

    results = []
    grads_words = []
    grads_sources = []
    shares_all = None
    for micro_index in range(micro_count):
        in_weights = lax.all_gather(attn_in, ("rows", "seq"), axis=2, tiled=True)
        out_weights = lax.all_gather(attn_out, ("rows", "seq"), axis=1, tiled=True)
        up_weights = lax.all_gather(w_up, ("rows", "seq"), axis=0, tiled=True)
        down_weights = lax.all_gather(w_down, ("rows", "seq"), axis=0, tiled=True)
        words = tokens[micro_index]
        sources = memory[micro_index]
        words_full = words.astype(jnp.float32)
        tgt_len = tgt_lengths[micro_index]
        src_len = src_lengths[micro_index]
        tgt_ends = jnp.cumsum(tgt_len, axis=-1)
        src_ends = jnp.cumsum(src_len, axis=-1)
        src_starts = src_ends - src_len
        query_seg = segment_of(my_pos, tgt_ends)
        query_bounds = segment_bounds(my_first, my_last, tgt_ends)
        tgt_real = tgt_mask[micro_index].astype(jnp.bfloat16)
        src_real = src_mask[micro_index].astype(jnp.bfloat16)

        def attend(queries, keys, values, real_marks, ends, starts, causal):
            full_keys, full_values, full_real = (
                lax.all_gather(keys, "seq", axis=0, tiled=True),
                lax.all_gather(values, "seq", axis=0, tiled=True),
                lax.all_gather(real_marks, "seq", axis=0, tiled=True),
            )
            length = full_keys.shape[0]
            block = math.gcd(length, 512)
            query_heads = split_heads(queries)

            def step(carry, block_index):
                begin = block_index * block
                shares = ranges_share(query_bounds, segment_bounds(begin, begin + block - 1, ends))

                def step_compute(state):
                    totals, accum = state
                    key_heads = split_heads(lax.dynamic_slice_in_dim(full_keys, begin, block, 0))
                    value_heads = split_heads(
                        lax.dynamic_slice_in_dim(full_values, begin, block, 0)
                    )
                    key_pos = begin + jnp.arange(block, dtype=jnp.int32)
                    key_seg, usable = key_status(
                        key_pos,
                        lax.dynamic_slice_in_dim(full_real, begin, block, 0),
                        ends,
                        starts,
                        causal,
                    )
                    permit = permitted(my_pos, query_seg, key_pos, key_seg, usable, causal)
                    scores = (
                        jnp.einsum(
                            "trhd,krhd->rhtk",
                            query_heads,
                            key_heads,
                            preferred_element_type=jnp.float32,
                        )
                        * 0.125
                    )
                    weights = jnp.where(permit[:, None], jnp.exp(scores), 0.0)
                    totals = totals + jnp.sum(weights, axis=-1)
                    accum = accum + jnp.einsum(
                        "rhtk,krhd->trhd",
                        weights.astype(jnp.bfloat16),
                        value_heads,
                        preferred_element_type=jnp.float32,
                    )
                    return (totals, accum)

                return (lax.cond(shares, step_compute, lambda unchanged: unchanged, carry), None)

            start_carry = (jnp.zeros((rows_here, HEADS, tokens_here), jnp.float32), zero_heads())
            (totals, accum), unused = lax.scan(
                step, start_carry, jnp.arange(length // block, dtype=jnp.int32)
            )
            sums = jnp.transpose(totals, (2, 0, 1))
            output = (accum / sums[..., None]).reshape(tokens_here, rows_here, width)
            return (output, sums, (full_keys, full_values, full_real))

        def attention_back(
            grad_out,
            output,
            sums,
            queries,
            keys,
            values,
            real_marks,
            gathered_set,
            ends,
            starts,
            causal,
        ):
            full_keys, full_values, full_real = gathered_set
            grad_heads = split_heads(grad_out)
            lambdas = -jnp.sum(grad_heads * split_heads(output), axis=-1) / sums
            scaled = (grad_heads / sums[..., None]).astype(jnp.bfloat16)
            query_heads = split_heads(queries)
            length = full_keys.shape[0]
            block = math.gcd(length, 512)

            def query_step(accum, block_index):
                begin = block_index * block
                shares = ranges_share(query_bounds, segment_bounds(begin, begin + block - 1, ends))

                def query_compute(state):
                    key_heads = split_heads(lax.dynamic_slice_in_dim(full_keys, begin, block, 0))
                    value_heads = split_heads(
                        lax.dynamic_slice_in_dim(full_values, begin, block, 0)
                    )
                    key_pos = begin + jnp.arange(block, dtype=jnp.int32)
                    key_seg, usable = key_status(
                        key_pos,
                        lax.dynamic_slice_in_dim(full_real, begin, block, 0),
                        ends,
                        starts,
                        causal,
                    )
                    permit = permitted(my_pos, query_seg, key_pos, key_seg, usable, causal)
                    weights, slopes = block_grads(
                        query_heads, scaled, lambdas, key_heads, value_heads, permit
                    )
                    return (
                        state
                        + jnp.einsum(
                            "rhab,brhd->arhd", slopes, key_heads, preferred_element_type=jnp.float32
                        )
                        * 0.125
                    )

                return (lax.cond(shares, query_compute, lambda unchanged: unchanged, accum), None)

            grad_query, unused = lax.scan(
                query_step, zero_heads(), jnp.arange(length // block, dtype=jnp.int32)
            )
            all_lambdas = lax.all_gather(lambdas, "seq", axis=0, tiled=True)
            local_seg, local_usable = key_status(my_pos, real_marks, ends, starts, causal)
            local_bounds = segment_bounds(my_first, my_last, ends)
            local_keys = split_heads(keys)
            local_values = split_heads(values)
            query_piece = lax.all_gather(queries, "seq", axis=0, tiled=True)
            scaled_piece = lax.all_gather(
                scaled.reshape(tokens_here, rows_here, width), "seq", axis=0, tiled=True
            )
            size = query_piece.shape[0]
            inner = math.gcd(size, 512)

            def inner_step(inner_carry, inner_index):
                offset = inner_index * inner
                piece_first = offset
                shares = ranges_share(
                    segment_bounds(piece_first, piece_first + inner - 1, tgt_ends), local_bounds
                )

                def inner_compute(state):
                    acc_key, acc_value = state
                    query_blk = split_heads(lax.dynamic_slice_in_dim(query_piece, offset, inner, 0))
                    scaled_blk = split_heads(
                        lax.dynamic_slice_in_dim(scaled_piece, offset, inner, 0)
                    )
                    lambda_blk = lax.dynamic_slice_in_dim(all_lambdas, piece_first, inner, 0)
                    query_pos = piece_first + jnp.arange(inner, dtype=jnp.int32)
                    permit = permitted(
                        query_pos,
                        segment_of(query_pos, tgt_ends),
                        my_pos,
                        local_seg,
                        local_usable,
                        causal,
                    )
                    weights, slopes = block_grads(
                        query_blk, scaled_blk, lambda_blk, local_keys, local_values, permit
                    )
                    acc_key = (
                        acc_key
                        + jnp.einsum(
                            "rhab,arhd->brhd", slopes, query_blk, preferred_element_type=jnp.float32
                        )
                        * 0.125
                    )
                    acc_value = acc_value + jnp.einsum(
                        "rhab,arhd->brhd", weights, scaled_blk, preferred_element_type=jnp.float32
                    )
                    return (acc_key, acc_value)

                return (
                    lax.cond(shares, inner_compute, lambda unchanged: unchanged, inner_carry),
                    None,
                )

            folded, unused_inner = lax.scan(
                inner_step, (zero_heads(), zero_heads()), jnp.arange(size // inner, dtype=jnp.int32)
            )
            grad_key, grad_value = folded
            grad_key = grad_key.reshape(tokens_here, rows_here, width)
            grad_value = grad_value.reshape(tokens_here, rows_here, width)
            return (grad_query.reshape(tokens_here, rows_here, width), grad_key, grad_value)

        self_query = (project(words, in_weights[0, 0]) + biases[0]).astype(jnp.bfloat16)
        self_key = project(words, in_weights[0, 1]).astype(jnp.bfloat16)
        self_value = (project(words, in_weights[0, 2]) + biases[1]).astype(jnp.bfloat16)
        heard, heard_sums, self_set = attend(
            self_query, self_key, self_value, tgt_real, tgt_ends, None, True
        )
        heard_low = heard.astype(jnp.bfloat16)
        branch_self = project(heard_low, out_weights[0]) + biases[2]
        hidden_one, pull_one = jax.vjp(
            norm_block, branch_self, words_full, omega[0], norm_gain[0], norm_shift[0]
        )
        hidden_one_low = hidden_one.astype(jnp.bfloat16)
        cross_query = (project(hidden_one_low, in_weights[1, 0]) + biases[3]).astype(jnp.bfloat16)
        cross_key = project(sources, in_weights[1, 1]).astype(jnp.bfloat16)
        cross_value = (project(sources, in_weights[1, 2]) + biases[4]).astype(jnp.bfloat16)
        recalled, recalled_sums, cross_set = attend(
            cross_query, cross_key, cross_value, src_real, src_ends, src_starts, False
        )
        recalled_low = recalled.astype(jnp.bfloat16)
        branch_cross = project(recalled_low, out_weights[1]) + biases[5]
        hidden_two, pull_two = jax.vjp(
            norm_block, branch_cross, hidden_one, omega[1], norm_gain[1], norm_shift[1]
        )
        hidden_two_low = hidden_two.astype(jnp.bfloat16)
        up_pre = project(hidden_two_low, up_weights) + up_bias
        active, pull_active = jax.vjp(jax.nn.gelu, up_pre)
        active_low = active.astype(jnp.bfloat16)
        branch_ffn = project(active_low, down_weights) + biases[6]
        outcome, pull_three = jax.vjp(
            norm_block, branch_ffn, hidden_two, omega[2], norm_gain[2], norm_shift[2]
        )
        grad_result = cotangent[micro_index].astype(jnp.float32)
        grad_ffn, grad_two, omega_three, gain_three, shift_three = pull_three(grad_result)
        grad_ffn_low = grad_ffn.astype(jnp.bfloat16)
        grad_down = matrix_grad(active_low, grad_ffn_low)
        bias_ffn = column_sum(grad_ffn_low)
        grad_up_pre = pull_active(project_back(grad_ffn_low, down_weights))[0].astype(jnp.bfloat16)
        grad_up = matrix_grad(hidden_two_low, grad_up_pre)
        bias_up = column_sum(grad_up_pre)
        grad_two = grad_two + project_back(grad_up_pre, up_weights)
        grad_cross, grad_one, omega_two, gain_two, shift_two = pull_two(grad_two)
        grad_cross_low = grad_cross.astype(jnp.bfloat16)
        grad_out_cross = matrix_grad(recalled_low, grad_cross_low)
        bias_out_cross = column_sum(grad_cross_low)
        grad_recalled = project_back(grad_cross_low, out_weights[1])
        cross_gq, cross_gk, cross_gv = attention_back(
            grad_recalled,
            recalled,
            recalled_sums,
            cross_query,
            cross_key,
            cross_value,
            src_real,
            cross_set,
            src_ends,
            src_starts,
            False,
        )
        cross_gq = cross_gq.astype(jnp.bfloat16)
        cross_gk = cross_gk.astype(jnp.bfloat16)
        cross_gv = cross_gv.astype(jnp.bfloat16)
        grad_cross_query = matrix_grad(hidden_one_low, cross_gq)
        grad_cross_key = matrix_grad(sources, cross_gk)
        grad_cross_value = matrix_grad(sources, cross_gv)
        grad_one = grad_one + project_back(cross_gq, in_weights[1, 0])
        grad_sources = project_back(cross_gk, in_weights[1, 1]) + project_back(
            cross_gv, in_weights[1, 2]
        )
        grad_self, grad_words, omega_one, gain_one, shift_one = pull_one(grad_one)
        grad_self_low = grad_self.astype(jnp.bfloat16)
        grad_out_self = matrix_grad(heard_low, grad_self_low)
        bias_out_self = column_sum(grad_self_low)
        grad_heard = project_back(grad_self_low, out_weights[0])
        self_gq, self_gk, self_gv = attention_back(
            grad_heard,
            heard,
            heard_sums,
            self_query,
            self_key,
            self_value,
            tgt_real,
            self_set,
            tgt_ends,
            None,
            True,
        )
        self_gq = self_gq.astype(jnp.bfloat16)
        self_gk = self_gk.astype(jnp.bfloat16)
        self_gv = self_gv.astype(jnp.bfloat16)
        grad_words = (
            grad_words
            + project_back(self_gq, in_weights[0, 0])
            + project_back(self_gk, in_weights[0, 1])
            + project_back(self_gv, in_weights[0, 2])
        )
        grad_in = jnp.stack(
            [
                jnp.stack(
                    [
                        matrix_grad(words, self_gq),
                        matrix_grad(words, self_gk),
                        matrix_grad(words, self_gv),
                    ]
                ),
                jnp.stack([grad_cross_query, grad_cross_key, grad_cross_value]),
            ]
        )
        grad_out = jnp.stack([grad_out_self, grad_out_cross])
        grad_bias = jnp.stack(
            [
                column_sum(self_gq),
                column_sum(self_gv),
                bias_out_self,
                column_sum(cross_gq),
                column_sum(cross_gv),
                bias_out_cross,
                bias_ffn,
            ]
        )
        grad_gain = jnp.stack([gain_one, gain_two, gain_three])
        grad_shift = jnp.stack([shift_one, shift_two, shift_three])
        grad_omega = jnp.stack([omega_one, omega_two, omega_three])
        grads = (
            grad_in,
            grad_out,
            grad_up,
            grad_down,
            grad_bias,
            bias_up,
            grad_gain,
            grad_shift,
            grad_omega,
        )
        outcome, grad_words, grad_sources, grads = (
            outcome.astype(jnp.bfloat16),
            grad_words.astype(jnp.bfloat16),
            grad_sources.astype(jnp.bfloat16),
            grads,
        )
        results.append(outcome)
        grads_words.append(grad_words)
        grads_sources.append(grad_sources)
        part_shares = (
            lax.psum_scatter(grads[0], ("rows", "seq"), scatter_dimension=2, tiled=True),
            lax.psum_scatter(grads[1], ("rows", "seq"), scatter_dimension=1, tiled=True),
            lax.psum_scatter(grads[2], ("rows", "seq"), scatter_dimension=0, tiled=True),
            lax.psum_scatter(grads[3], ("rows", "seq"), scatter_dimension=0, tiled=True),
            lax.psum_scatter(grads[4], ("rows", "seq"), scatter_dimension=1, tiled=True),
            lax.psum_scatter(grads[5], ("rows", "seq"), scatter_dimension=0, tiled=True),
            lax.psum_scatter(grads[6], ("rows", "seq"), scatter_dimension=1, tiled=True),
            lax.psum_scatter(grads[7], ("rows", "seq"), scatter_dimension=1, tiled=True),
            lax.psum_scatter(grads[8], ("rows", "seq"), scatter_dimension=1, tiled=True),
        )
        shares_all = (
            part_shares if shares_all is None else jax.tree.map(jnp.add, shares_all, part_shares)
        )
    return (jnp.stack(results), jnp.stack(grads_words), jnp.stack(grads_sources)) + tuple(
        shares_all
    )


def over(mesh, function):
    return jax.shard_map(
        function,
        mesh=mesh,
        in_specs=(
            P(None, "seq", "rows", None),
            P(None, "seq", "rows", None),
            P(None, "seq", "rows", None),
            P(None, "rows", None),
            P(None, "rows", None),
            P(None, "seq", "rows"),
            P(None, "seq", "rows"),
            P(None, None, ("rows", "seq"), None),
            P(None, ("rows", "seq"), None),
            P(("rows", "seq"), None),
            P(("rows", "seq"), None),
            P(),
            P(),
            P(),
            P(),
            P(),
        ),
        out_specs=(
            P(None, "seq", "rows", None),
            P(None, "seq", "rows", None),
            P(None, "seq", "rows", None),
            P(None, None, ("rows", "seq"), None),
            P(None, ("rows", "seq"), None),
            P(("rows", "seq"), None),
            P(("rows", "seq"), None),
            P(None, ("rows", "seq")),
            P(("rows", "seq")),
            P(None, ("rows", "seq")),
            P(None, ("rows", "seq")),
            P(None, ("rows", "seq")),
        ),
        check_vma=False,
    )


def general(mesh):
    return over(mesh, local)


MESH = pl.DeviceIdType.MESH
UNIT = 16 * 1024
BINS = 16
NAMES = 192
ODD = ("marks", "w0p", "w1p", "u0p", "x3", "x5", "x7", "sa", "sb", "ta")
F32 = jnp.float32
BF16 = jnp.bfloat16
PLANES, YS, XS, CORES = 4, 2, 2, 2
GROUP = YS * XS * CORES


def nn(left, right):
    return lax.dot_general(left, right, (((1,), (0,)), ((), ())), preferred_element_type=F32)


def nt(left, right):
    return lax.dot_general(left, right, (((1,), (1,)), ((), ())), preferred_element_type=F32)


def tn(left, right):
    return lax.dot_general(left, right, (((0,), (0,)), ((), ())), preferred_element_type=F32)


def flip(value):
    return jnp.transpose(value.astype(F32))


def fused_kernel(
    tok, mem, cot, tgt_len, src_len, tgt_msk, src_msk, s_in, s_out, s_up, s_dn, h_biases, h_up_bias, h_gain, h_shift, h_omega,
    o_res, o_tok, o_mem, h_in, h_out, h_up, h_dn, h_bias, h_upb, h_gain_o, h_shift_o, h_omega_o,
    biases, up_bias, gain, shift, omega, o_in, o_out, o_up, o_dn, o_bias, o_upb, o_gain, o_shift, o_omega,
    w_q, w_out, w_up, w_dn, g_q, g_out, g_up, g_dn,
    c_q, c_out, c_up, c_dn,
    p_q, p_out, p_up, p_dn,
    q_q, q_out, q_up, q_dn,
    z_q, z_out, z_up, z_dn,
    ws0, ws1, gs0, gs1, cs0, cs1, zs0, zs1, fs0, fs1,
    all_tok, all_mem, in_cot, raw_tl, raw_sl, raw_tm, raw_sm, meta, in_meta, all_meta,
    dx0, dx1, dc0, dc1, dp0, dp1,
    a3, b3, a4, b4, a5, b5, a6, b6, a7, b7, a8, b8,
    out_res, out_tok, out_mem,
    sg0, sg1, sg2, sg3, sr0, sr1, sr2, sra, srb,
    tg0, tg1, tg2, tg3, tr0, tr1, tr2, tra,
    code_self, code_cross, key_pos, rows_f,
    qt0, kt0, vt0, k0, v0, pt0, l0, ot0,
    qt1, kt1, vt1, k1, v1, pt1, l1, ot1,
    dnt, acc_k, acc_v,
    act, slope, gul, xh0, xh1, xh2, h1_f, h2_f,
    wt, bias_cols, wz, dt0, dt1, gauge,
    f_q, f_out, f_up, f_dn, f_u0, f_u1,
    ss, rs,
):
    c = lax.axis_index("rows")
    seq = lax.axis_index("seq")
    z = seq // (YS * XS)
    yx = lax.rem(seq, YS * XS)
    y = yx // XS
    x = lax.rem(yx, XS)
    width = 512
    here = 2 * 64

    def at(zz, yy, xx):
        return zz * (YS * XS) + yy * XS + xx

    def slot(cc, yy, xx):
        return cc * 4 + yy * 2 + xx

    def head(cc, yy, xx):
        return (yy * 2 + xx) * 2 + cc

    me_slot, me_head = slot(c, y, x), head(c, y, x)
    plane_peers = []
    for k in range(1, GROUP):
        cc = 1 - c if k & 4 else c
        yy = 1 - y if k & 2 else y
        xx = 1 - x if k & 1 else x
        plane_peers.append((cc, yy, xx))
    trio = [(1 - y, x), (y, 1 - x), (1 - y, 1 - x)]
    z_peers = [lax.rem(z + k, PLANES) for k in (1, 2, 3)]

    names, expected_bytes = {}, {}
    pending = []
    edge = (z == 0) | (z == PLANES - 1)

    def sem(name):
        return names.setdefault(name, len(names))

    def wait(semaphore, ref):
        pltpu.make_async_copy(ref, ref, semaphore).wait()

    def size(ref):
        return math.prod(ref.shape) * jnp.dtype(ref.dtype).itemsize

    bins = [0]
    odd = {}

    def out_sem(name):
        return ss.at[odd.setdefault(name, BINS + 1 + len(odd))] if name in ODD else ss.at[len(bins) - 1]

    def send(name, src, dst, device, recv=None):
        pltpu.make_async_remote_copy(
            src_ref=src, dst_ref=dst, send_sem=out_sem(name), recv_sem=rs.at[sem(name)] if recv is None else recv,
            device_id=device, device_id_type=MESH,
        ).start()

    def keep(name, src, dst):
        pltpu.make_async_copy(src, dst, rs.at[sem(name)]).start()

    def landed(name, ref):
        wait(rs.at[sem(name)], ref)

    def sent_later(name, ref):
        if name in ODD:
            pending.append((ss.at[odd[name]], ref, None))
            return
        bins[-1] += size(ref)
        assert size(ref) % UNIT == 0, (name, size(ref))
        if bins[-1] > 1024 * UNIT // 16:
            bins.append(0)

    line_bytes = [0]

    def along_z(name, src, block):
        i, j = sem(name + "z"), sem(name + "f")
        for step in (1, -1, 2, -2):
            to = z + step
            far = (z == 0) if step == 2 else (z == PLANES - 1) if step == -2 else None

            @pl.when((to >= 0) & (to < PLANES))
            def _():
                pltpu.make_async_remote_copy(
                    src_ref=src, dst_ref=block(z), send_sem=ss.at[BINS],
                    recv_sem=rs.at[i] if far is None else rs.at[jnp.where(far, j, i)],
                    device_id=(c, at(to, y, x)), device_id_type=MESH,
                ).start()

        line_bytes[0] += size(src)

    def pass_on(name, block):
        for mine, origin, to in ((1, 3, 0), (2, 0, 3)):

            @pl.when(z == mine)
            def _():
                landed(name + "f", block(origin))
                pltpu.make_async_remote_copy(
                    src_ref=block(origin), dst_ref=block(origin), send_sem=ss.at[BINS], recv_sem=rs.at[sem(name + "z")],
                    device_id=(c, at(to, y, x)), device_id_type=MESH,
                ).start()

    fold_bytes = [0]

    def fold_send(name, block, target, to):
        pltpu.make_async_remote_copy(
            src_ref=block, dst_ref=target, send_sem=ss.at[BINS], recv_sem=rs.at[sem(name)],
            device_id=(c, at(to, y, x)), device_id_type=MESH,
        ).start()

    def fold_z(name, block, far, line):
        inner = jnp.where(edge, 0, 1)
        for origin, step, hops in ((0, 3, 1), (3, -3, -1)):

            @pl.when(z == origin)
            def _():
                fold_send(name + "a", block(origin + step), far, origin + hops)
                fold_send(name + "l", block(origin + 2 * hops), line.at[2], origin + 2 * hops)

        for step in (1, -1):
            to = z + step

            @pl.when((to >= 0) & (to < PLANES))
            def _():
                between = jnp.where((to == 0) | (to == PLANES - 1), 0, inner)
                fold_send(name + "l", block(to), line.at[between], to)

        fold_bytes[0] += size(far)

    def fold_f(name, block, far, line):
        for mine, to in ((1, 3), (2, 0)):

            @pl.when(z == mine)
            def _():
                landed(name + "a", far)
                add(block(to), far)
                fold_send(name + "l", block(to), line.at[1], to)

    def fold_sum(name, own, line, result):
        @pl.when(edge)
        def _():
            landed(name + "l", line.at[pl.ds(0, 2)])

        @pl.when(jnp.logical_not(edge))
        def _():
            landed(name + "l", line)

        result[...] = own.astype(F32) + line[0].astype(F32) + line[1].astype(F32)

        @pl.when(jnp.logical_not(edge))
        def _():
            result[...] += line[2].astype(F32)

    def line_landed(name, blocks, own):
        @pl.when(edge)
        def _():
            landed(name + "z", blocks(3 + own))

        @pl.when(jnp.logical_not(edge))
        def _():
            landed(name + "z", blocks(2 + own))

    def to_plane(name, src, dst, slotted=False):
        half = lax.rem(z, 2)
        core = z // 2
        if slotted:
            recv = rs.at[jnp.where(half == 0, sem(name + "h0"), sem(name + "h1"))]
            part = dst.at[slot(core, y, x), half]
        else:
            recv = rs.at[sem(name)]
            part = dst.at[half]
        for m in range(2):
            plane = 2 * m + c
            own = (plane == z) & (core == c)
            out = ss.at[odd.setdefault(name + str(m), BINS + 1 + len(odd))]

            @pl.when(own)
            def _():
                pltpu.make_async_copy(src.at[m], part, recv).start()

            @pl.when(jnp.logical_not(own))
            def _():
                pltpu.make_async_remote_copy(
                    src_ref=src.at[m], dst_ref=part, send_sem=out, recv_sem=recv,
                    device_id=(core, at(plane, y, x)), device_id_type=MESH,
                ).start()

            pending.append((out, src.at[m], jnp.logical_not(own)))

    def from_plane(name, src, dst):
        micro, core = z // 2, lax.rem(z, 2)
        recv = rs.at[sem(name)]
        for half in range(2):
            zz = 2 * c + half
            own = (core == c) & (zz == z)
            part = dst.at[micro]
            out = ss.at[odd.setdefault(name + str(half), BINS + 1 + len(odd))]

            @pl.when(own)
            def _():
                pltpu.make_async_copy(src.at[half], part, recv).start()

            @pl.when(jnp.logical_not(own))
            def _():
                pltpu.make_async_remote_copy(
                    src_ref=src.at[half], dst_ref=part, send_sem=out, recv_sem=recv,
                    device_id=(core, at(zz, y, x)), device_id_type=MESH,
                ).start()

            pending.append((out, src.at[half], jnp.logical_not(own)))

    def to_heads(name, src, dst):
        keep(name, src.at[me_head], dst.at[me_slot])
        for cc, yy, xx in plane_peers:
            send(name, src.at[head(cc, yy, xx)], dst.at[me_slot], (cc, at(z, yy, xx)))
        sent_later(name, src.at[pl.ds(0, GROUP - 1)])

    def to_slot(name, src, dst, s):
        device = (s // 4, at(z, (s % 4) // 2, s % 2))
        i = sem(name)
        out = out_sem(name)

        @pl.when(me_slot == s)
        def _():
            pltpu.make_async_copy(src.at[s], dst.at[me_head], rs.at[i]).start()

        @pl.when(me_slot != s)
        def _():
            pltpu.make_async_remote_copy(
                src_ref=src.at[s], dst_ref=dst.at[me_head], send_sem=out, recv_sem=rs.at[i],
                device_id=device, device_id_type=MESH,
            ).start()

    weights = {
        "q": (w_q, s_in.at[1, pl.ds(0, 1)], g_q, c_q, p_q, q_q, z_q, o_in.at[1, pl.ds(0, 1)]),
    }

    for i in range(2):
        one = pl.ds(i, 1)
        refs = (w_out, s_out, g_out, c_out, p_out, q_out, z_out, o_out)
        weights["out" + str(i)] = tuple(
            ref.at[:, one] if ref is p_out or ref is q_out or ref is z_out else ref.at[one] for ref in refs
        )
        refs = (w_up, s_up, g_up, c_up, p_up, q_up, z_up, o_up)
        cols = pl.ds(i * 1024, 1024)
        weights["up" + str(i)] = tuple(
            ref.at[:, one] if ref is p_up or ref is q_up or ref is z_up
            else ref.at[:, :, cols] if ref is s_up or ref is o_up else ref.at[one]
            for ref in refs
        )
        refs = (w_dn, s_dn, g_dn, c_dn, p_dn, q_dn, z_dn, o_dn)
        cols = pl.ds(i * 256, 256)
        weights["dn" + str(i)] = tuple(
            ref.at[:, one] if ref is p_dn or ref is q_dn or ref is z_dn
            else ref.at[:, :, cols] if ref is s_dn or ref is o_dn else ref.at[one]
            for ref in refs
        )

    fars = {"q": f_q, "u0": f_u0, "u1": f_u1}
    for i in range(2):
        one = pl.ds(i, 1)
        fars["out" + str(i)], fars["up" + str(i)], fars["dn" + str(i)] = f_out.at[one], f_up.at[one], f_dn.at[one]

    def halves(ref):
        cols = ref.shape[-1] // 2
        return pl.ds(0, cols), pl.ds(cols, cols)

    x_next, y_next, core_next = (c, at(z, y, 1 - x)), (c, at(z, 1 - y, x)), (1 - c, seq)

    def gather_z(g):
        full, shard = weights[g][:2]
        keep(g + "z", shard, full.at[:, c, z, y, x])
        along_z(g, shard, lambda zz: full.at[:, c, zz, y, x])

    def gather_f(g):
        full = weights[g][0]
        pass_on(g, lambda zz: full.at[:, c, zz, y, x])

    def gather_1(g):
        full = weights[g][0]
        first, second = halves(full)
        line_landed(g, lambda n: full.at[:, c, pl.ds(0, n), y, x], 1)
        part = full.at[:, c, :, y, x, :, first]
        send(g + "1a", part, part, x_next)
        sent_later(g + "1a", part)
        part = full.at[:, c, :, y, x, :, second]
        send(g + "1b", part, part, y_next)
        sent_later(g + "1b", part)

    def gather_2(g):
        full = weights[g][0]
        first, second = halves(full)
        landed(g + "1a", full.at[:, c, :, y, 1 - x, :, first])
        part = full.at[:, c, :, y, :, :, first]
        send(g + "2a", part, part, y_next)
        sent_later(g + "2a", part)
        landed(g + "1b", full.at[:, c, :, 1 - y, x, :, second])
        part = full.at[:, c, :, :, x, :, second]
        send(g + "2b", part, part, x_next)
        sent_later(g + "2b", part)

    def gather_3(g):
        full = weights[g][0]
        first, second = halves(full)
        landed(g + "2a", full.at[:, c, :, 1 - y, :, :, first])
        landed(g + "2b", full.at[:, c, :, :, 1 - x, :, second])
        send(g + "3", full.at[:, c], full.at[:, c], core_next)
        sent_later(g + "3", full.at[:, c])

    def gathered(g):
        landed(g + "3", weights[g][0].at[:, 1 - c])

    def add(target, other):
        target[...] = (target[...].astype(F32) + other[...].astype(F32)).astype(BF16)

    def scatter_0(g):
        grad, across = weights[g][2:4]
        send(g + "r0", grad.at[:, 1 - c], across, core_next)
        sent_later(g + "r0", across)

    def scatter_1(g):
        grad, across, part = weights[g][2:5]
        first, second = halves(grad)
        landed(g + "r0", across)
        for lead in range(grad.shape[0]):

            @pl.loop(0, PLANES)
            def _(zz):
                add(grad.at[lead, c, zz], across.at[lead, zz])

        send(g + "r1a", grad.at[:, c, :, 1 - y, :, :, first], part.at[0], y_next)
        sent_later(g + "r1a", part.at[0])
        send(g + "r1b", grad.at[:, c, :, :, 1 - x, :, second], part.at[1], x_next)
        sent_later(g + "r1b", part.at[1])

    def scatter_2(g):
        grad, _, part, piece = weights[g][2:6]
        first, second = halves(grad)
        landed(g + "r1a", part.at[0])
        landed(g + "r1b", part.at[1])
        for lead in range(grad.shape[0]):

            @pl.loop(0, PLANES)
            def _(zz):
                add(grad.at[lead, c, zz, y, :, :, first], part.at[0, lead, zz])
                add(grad.at[lead, c, zz, :, x, :, second], part.at[1, lead, zz])

        send(g + "r2a", grad.at[:, c, :, y, 1 - x, :, first], piece.at[0], x_next)
        sent_later(g + "r2a", piece.at[0])
        send(g + "r2b", grad.at[:, c, :, 1 - y, x, :, second], piece.at[1], y_next)
        sent_later(g + "r2b", piece.at[1])

    def scatter_3(g):
        grad, _, _, piece, line = weights[g][2:7]
        first, second = halves(grad)
        landed(g + "r2a", piece.at[0])
        landed(g + "r2b", piece.at[1])
        for lead in range(grad.shape[0]):

            @pl.loop(0, PLANES)
            def _(zz):
                add(grad.at[lead, c, zz, y, x, :, first], piece.at[0, lead, zz])
                add(grad.at[lead, c, zz, y, x, :, second], piece.at[1, lead, zz])

        fold_z(g, lambda zz: grad.at[:, c, zz, y, x], fars[g], line)

    def scatter_f(g):
        grad, line = weights[g][2], weights[g][6]
        fold_f(g, lambda zz: grad.at[:, c, zz, y, x], fars[g], line)

    def scattered(g):
        grad, _, _, _, line, result = weights[g][2:8]
        fold_sum(g, grad[:, c, z, y, x], line, result)

    left, right = pl.ds(0, 256), pl.ds(256, 256)
    y_slot, x_slot, far_slot = slot(c, 1 - y, x), slot(c, y, 1 - x), slot(c, 1 - y, 1 - x)

    def spread_1(name, full, half):
        own = full.at[me_slot, half]
        landed(name + "h" + str(half), own)
        for which, device in (("y", y_next), ("x", x_next), ("c", core_next)):
            which = which if which == "c" else which + str(half)
            send(name + which, own, own, device)
            sent_later(name + which, own)

    def spread_2(name, full, half):
        for which, place, cols, device in (("y", y_slot, right, x_next), ("x", x_slot, left, y_next)):
            part = full.at[place, half]
            landed(name + which + str(half), part)
            half_of = full.at[place, half, :, cols]
            send(name + "q" + which + str(half), half_of, half_of, device)
            sent_later(name + "q" + which + str(half), half_of)
            send(name + "d", part, part, core_next)
            sent_later(name + "d", part)

    def spread_4(name, full, half):
        part = full.at[far_slot, half]
        landed(name + "qy" + str(half), full.at[far_slot, half, :, right])
        landed(name + "qx" + str(half), full.at[far_slot, half, :, left])
        send(name + "d", part, part, core_next)
        sent_later(name + "d", part)

    def spread_3(name, full):
        landed(name + "c", full.at[0])
        landed(name + "d", full.at[pl.ds(0, 3)])

    def merge_0(name, full, across):
        send(name + "c", full.at[pl.ds((1 - c) * 4, 4)], across, core_next)
        sent_later(name + "c", across)

    def merge_1(name, full, across, parts):
        landed(name + "c", across)
        add(full.at[far_slot], across.at[(1 - y) * 2 + 1 - x])
        send(name + "qx", full.at[far_slot, :, :, left], parts.at[2, :, :, left], y_next)
        send(name + "qy", full.at[far_slot, :, :, right], parts.at[2, :, :, right], x_next)
        sent_later(name + "q", parts.at[2])
        add(full.at[x_slot], across.at[y * 2 + 1 - x])
        add(full.at[y_slot], across.at[(1 - y) * 2 + x])
        add(full.at[me_slot], across.at[yx])

    def merge_3(name, full, parts):
        landed(name + "qx", parts.at[2, :, :, left])
        add(full.at[x_slot, :, :, left], parts.at[2, :, :, left])
        send(name + "px", full.at[x_slot], parts.at[0], x_next)
        sent_later(name + "px", parts.at[0])
        landed(name + "qy", parts.at[2, :, :, right])
        add(full.at[y_slot, :, :, right], parts.at[2, :, :, right])
        send(name + "py", full.at[y_slot], parts.at[1], y_next)
        sent_later(name + "py", parts.at[1])

    def merge_2(name, full, parts):
        landed(name + "px", parts.at[0])
        landed(name + "py", parts.at[1])
        total = full[me_slot].astype(F32)
        for k in range(2):
            total = total + parts[k].astype(F32)
        return total.reshape(here, width)

    def tile(index):
        return pl.ds(pl.multiple_of(index * 128, 128), 128)

    def slice_1(name, shard, full):
        keep(name + "p", shard.at[:, :, tile(yx)], full.at[:, c, z, yx])
        for yy, xx in trio:
            send(name + "p", shard.at[:, :, tile(yy * 2 + xx)], full.at[:, c, z, yx], (c, at(z, yy, xx)))
        sent_later(name + "p", full.at[:, c, z, pl.ds(0, 3)])

    def slice_2(name, full):
        landed(name + "p", full.at[:, c, z])
        along_z(name, full.at[:, c, z], lambda zz: full.at[:, c, zz])

    def slice_f(name, full):
        pass_on(name, lambda zz: full.at[:, c, zz])

    def slice_3(name, full):
        line_landed(name, lambda n: full.at[:, c, pl.ds(0, n)], 0)
        send(name + "c", full.at[:, c], full.at[:, c], core_next)
        sent_later(name + "c", full.at[:, c])

    def slice_4(name, full):
        landed(name + "c", full.at[:, 1 - c])

    def unslice_0(name, grad, across):
        send(name + "c", grad.at[:, 1 - c], across, core_next)
        sent_later(name + "c", across)

    def unslice_1(name, grad, across, line):
        landed(name + "c", across)
        for lead in range(grad.shape[0]):
            add(grad.at[lead, c], across.at[lead])
        fold_z(name, lambda zz: grad.at[:, c, zz], fars[name], line)

    def unslice_f(name, grad, line):
        fold_f(name, lambda zz: grad.at[:, c, zz], fars[name], line)

    def unslice_2(name, grad, line, total, result):
        fold_sum(name, grad[:, c, z], line, total)
        for yy, xx in trio:
            send(name + "p", total.at[:, yy * 2 + xx], result.at[:, :, tile(yx)], (c, at(z, yy, xx)))
        sent_later(name + "p", total.at[:, pl.ds(0, 3)])
        result[:, :, tile(yx)] = total[:, yx]

    def unslice_3(name, result):
        landed(name + "p", result.at[:, :, pl.ds(0, 384)])

    def matrix(ref):
        return ref[...].reshape(-1, ref.shape[-1])

    def put(ref, value):
        ref[...] = value.astype(BF16).reshape(ref.shape)

    def norm(r, i, kept):
        centered = r - jnp.mean(r, axis=1, keepdims=True)
        scale = lax.rsqrt(jnp.mean(centered * centered, axis=1, keepdims=True) + 1e-05)
        xhat = centered * scale
        kept[...] = xhat
        return xhat * gain[i : i + 1, :] + shift[i : i + 1, :], scale

    def column(row, value):
        sg0[row : row + 1, :] = jnp.sum(value, axis=0, keepdims=True)

    def norm_back(grad, i, kept, scale, skip):
        xhat = kept[...]
        column(12 + i, grad * xhat)
        column(15 + i, grad)
        dxhat = grad * gain[i : i + 1, :]
        dr = dxhat - jnp.mean(dxhat, axis=1, keepdims=True)
        dr = (dr - xhat * jnp.mean(dxhat * xhat, axis=1, keepdims=True)) * scale
        column(18 + i, dr * skip)
        return dr, dr * omega[i : i + 1, :]

    BLOCK = 256

    def attend(b, queries, keys, values_t, weights_t, sums, outputs, causal, name, target, arrives):
        extent = 512 if causal and b < 2 else 1024
        cols = slice(b * BLOCK, (b + 1) * BLOCK)
        scores = nn(keys[:extent, :], queries[:, cols])
        seg = rows_f[0:1, cols]
        code = (code_self if causal else code_cross)[:extent, :]
        permit = jnp.concatenate([code, code], axis=1) == seg
        if causal:
            pos = key_pos[:extent, :]
            pos = jnp.concatenate([pos, pos], axis=1)
            mine = rows_f[1:2, cols]
            permit = (permit & (pos <= mine)) | (pos == mine)
        weight = jnp.where(permit, jnp.exp(scores), 0.0)
        total = jnp.sum(weight, axis=0, keepdims=True)
        low = weight.astype(BF16)
        weights_t[:extent, cols] = low
        out = nn(values_t[:, :extent], low) / total
        sums[0:1, cols] = total
        outputs[:, cols] = out
        for k in range(2):
            target[2 * b + k] = out[:, k * here : (k + 1) * here].astype(BF16)
            to_slot(name, target, arrives, 2 * b + k)
        if b == 3:
            sent_later(name, target.at[pl.ds(0, GROUP - 1)])

    def attend_start(buffer, sums, outputs):
        acc_k[...] = jnp.zeros_like(acc_k)
        acc_v[...] = jnp.zeros_like(acc_v)
        for s in range(GROUP):
            cols = slice(s * here, (s + 1) * here)
            grad = buffer[s].astype(F32)
            inverse = 1.0 / sums[0:1, cols]
            dnt[:, cols] = (grad * inverse).astype(BF16)
            rows_f[2:3, cols] = -jnp.sum(grad * outputs[:, cols], axis=0, keepdims=True) * inverse

    def attend_back(b, queries, keys_t, values, weights_t, causal, name, target, arrives):
        extent = 512 if causal and b < 2 else 1024
        cols = slice(b * BLOCK, (b + 1) * BLOCK)
        low = weights_t[:extent, cols]
        dn = dnt[:, cols]
        spread = nn(values[:extent, :], dn)
        slopes = (low.astype(F32) * (spread + rows_f[2:3, cols])).astype(BF16)
        block = (nn(keys_t[:, :extent], slopes) * 0.125).astype(BF16)
        if name is None:
            dt0[0:64, cols] = block
        else:
            for k in range(2):
                target[2 * b + k] = block[:, k * here : (k + 1) * here]
                to_slot(name, target, arrives, 2 * b + k)
            if b == 3:
                sent_later(name, target.at[pl.ds(0, GROUP - 1)])
        acc_k[:, :extent] += nt(queries[:, cols], slopes)
        acc_v[:, :extent] += nt(dn, low)

    def by_head(target, value):
        target[...] = flip(value).astype(BF16).reshape(GROUP, 64, here)

    def heads_weights(first, full):
        for j in range(full.shape[0]):
            wt[first + j] = flip(matrix(full.at[j])).astype(BF16)

    own_rows = pl.ds(pl.multiple_of(c * 64, 64), 64)
    own_head = pl.ds(pl.multiple_of(me_head * 64, 64), 64)

    def own_weights(first, count):
        return jnp.concatenate([wt[first + j, own_rows, :] for j in range(count)], axis=0)

    def wide_bias(i):
        col = bias_cols[i, own_head, :]
        return jnp.concatenate([col, col], axis=1)

    def project_heads(rows, first, queries, keys, keys_t, values, values_t):
        count = 2 if queries is None else 3
        own = own_weights(first, count)
        for b in range(4):
            cols = slice(b * 256, (b + 1) * 256)
            out = nt(own, rows[2 * b : 2 * b + 2].reshape(256, width))
            if queries is not None:
                queries[:, cols] = ((out[0:64] + wide_bias(0)).astype(BF16).astype(F32) * 0.125).astype(BF16)
            at_k = 64 * (count - 2)
            block = out[at_k : at_k + 64].astype(BF16)
            keys_t[:, cols] = block
            keys[cols, :] = flip(block).astype(BF16)
            block = (out[at_k + 64 : at_k + 128] + wide_bias(1 if count == 3 else 2)).astype(BF16)
            values_t[:, cols] = block
            values[cols, :] = flip(block).astype(BF16)

    def rows_back(grads_t, first, target, core):
        count = grads_t.shape[0] // 64
        own = own_weights(first, count)
        for b in range(2):
            cols = pl.ds(pl.multiple_of(core * 512 + b * 256, 256), 256)
            out = tn(grads_t[:, cols], own)
            target[pl.ds(core * 4 + b * 2, 2)] = out.astype(BF16).reshape(2, 2, 64, width)

    def slices_back(grads_t, rows, grad):
        count = grads_t.shape[0] // 64
        out = nn(grads_t[...], rows[...].reshape(1024, width))
        wz[...] = jnp.zeros_like(wz)
        for j in range(count):
            wz[j, own_rows, :] = out[j * 64 : (j + 1) * 64]
            put(grad.at[j], jnp.transpose(wz[j]))

    def bias(i):
        return biases[i : i + 1, :]

    def make_masks():
        landed("marks", all_meta.at[pl.ds(0, 7)])
        order = lax.broadcasted_iota(jnp.int32, (1, 1024), 1)
        place = (order // 512) * 512 + lax.rem(order // 64, 2) * 256 + lax.rem(order // 128, 4) * 64 + lax.rem(order, 64)
        place = place.astype(F32)
        marks = [all_meta[s].astype(F32) for s in range(GROUP)]
        tgt_real = jnp.concatenate([mark[0:1, :] for mark in marks], axis=1)
        src_real = jnp.concatenate([mark[1:2, :] for mark in marks], axis=1)
        lower = lax.broadcasted_iota(jnp.int32, (32, 128), 1)
        later = lax.broadcasted_iota(jnp.int32, (32, 128), 0)

        def ends_of(row):
            lengths = jnp.broadcast_to(row, (32, 128))
            ends = jnp.sum(jnp.where(lower <= later, lengths, 0.0), axis=1, keepdims=True)
            starts = jnp.sum(jnp.where(lower < later, lengths, 0.0), axis=1, keepdims=True)
            return ends, starts

        def count(flags):
            return jnp.sum(jnp.where(flags, 1.0, 0.0), axis=0, keepdims=True)

        tgt_ends, _ = ends_of(marks[0][2:3, :])
        src_ends, src_starts = ends_of(marks[0][3:4, :])
        tgt_seg = count(tgt_ends <= place)
        src_seg = count(src_ends <= place)
        src_first = count(src_starts == place)
        self_row = jnp.where(tgt_real > 0.5, tgt_seg, -1.0)
        cross_row = jnp.where((src_real > 0.5) | (src_first > 0.5), src_seg, -1.0)
        rows_f[0:1, :] = tgt_seg
        rows_f[1:2, :] = place
        code_self[...] = jnp.transpose(jnp.broadcast_to(self_row, (128, 1024)))
        code_cross[...] = jnp.transpose(jnp.broadcast_to(cross_row, (128, 1024)))
        key_pos[...] = jnp.transpose(jnp.broadcast_to(place, (128, 1024)))

    def feed_up(rows, i):
        for k in (2 * i, 2 * i + 1):
            cols = slice(k * width, (k + 1) * width)
            inner = slice((k % 2) * width, (k % 2 + 1) * width)
            u = nn(rows, matrix(w_up.at[i, :, :, :, :, :, inner])) + up_bias[0:1, cols]
            square = u * u
            t = jnp.tanh(u * (0.7978845608028654 + 0.035677408136300125 * square))
            act[:, cols] = (0.5 * u * (1.0 + t)).astype(BF16)
            inner = 0.7978845608028654 + 0.10703222440890037 * square
            slope[:, cols] = 0.5 * (1.0 + t) + 0.5 * u * (1.0 - t * t) * inner

    def feed_back(gf, back):
        for k in range(4):
            cols = slice(k * width, (k + 1) * width)
            inner = slice((k % 2) * width, (k % 2 + 1) * width)
            rows = pl.ds(2 * (k % 2), 2)
            gu = nt(gf[:, 0:256], matrix(w_dn.at[0, k // 2, rows]))
            gu = gu + nt(gf[:, 256:512], matrix(w_dn.at[1, k // 2, rows]))
            gu = (gu * slope[:, cols]).astype(BF16)
            gul[:, cols] = gu
            column(8 + k, gu.astype(F32))
            back = back + nt(gu, matrix(w_up.at[k // 2, :, :, :, :, :, inner]))
        return back

    def value_sums(grads_t):
        total = jnp.sum(grads_t[64:128, :].astype(F32), axis=1, keepdims=True)
        bias_cols[0] = jnp.zeros((width, 128), F32)
        bias_cols[0, own_head, :] = jnp.broadcast_to(total, (64, 128))
        sg0[4:5, :] = jnp.transpose(bias_cols[0])[0:1, :]

    def head_sums(grads_t):
        lanes = lax.broadcasted_iota(jnp.int32, (64, 128), 1)
        dq_sum = jnp.sum(grads_t[0:64, :].astype(F32), axis=1, keepdims=True)
        dv_sum = jnp.sum(grads_t[128:192, :].astype(F32), axis=1, keepdims=True)
        bias_cols[0] = jnp.zeros((width, 128), F32)
        bias_cols[0, own_head, :] = jnp.where(lanes == 0, dq_sum, dv_sum)
        tg0[...] = jnp.transpose(bias_cols[0])[0:8, :]

    def small(name, src, dst, device):
        send(name, src, dst, device)
        sent_later(name, dst)

    def small_add(name, arrived, mine, total):
        landed(name, arrived)
        total[...] = mine[...] + arrived[...]

    def small_z(name, src, rows, tile_at, dst):
        for k, zz in enumerate(z_peers):
            send(name, src.at[rows, tile(tile_at(zz))], dst.at[2 - k], (c, at(zz, y, x)))
        sent_later(name, dst)

    def tile_own(zz):
        return c * 2 + zz // 2

    def tile_up(zz):
        return lax.rem(zz, 2) * 2 + y

    def small_sum(name, src, rows, tile_at, dst):
        landed(name, dst)
        return src[rows, tile(tile_at(z))] + dst[0] + dst[1] + dst[2]

    def small_out():
        block = c * 16 + seq
        shift_by = lax.rem(128 - lax.rem(block, 8) * 16, 128)
        turned = pltpu.roll(small_sum("sa", sg3, slice(None), tile_own, sra), shift_by, 1)
        o_bias[...] = turned[0:7, 0:16]
        o_gain[...] = turned[12:15, 0:16]
        o_shift[...] = turned[15:18, 0:16]
        o_omega[...] = turned[18:21, 0:16]
        turned = pltpu.roll(small_sum("ta", tg3, slice(None), tile_own, tra), shift_by, 1)
        o_bias[0:2, :] = turned[0:2, 0:16]
        turned = pltpu.roll(small_sum("sb", sg3, pl.ds(8, 8), tile_up, srb), lax.rem(block, 2) * 64, 1)
        wanted = block // 8
        row = jnp.zeros((1, 64), F32)
        for k in range(4):
            row = row + turned[k : k + 1, 0:64] * (wanted == k).astype(F32)
        o_upb[...] = row
        ends = ((o_bias, h_bias), (o_upb, h_upb), (o_gain, h_gain_o), (o_shift, h_shift_o), (o_omega, h_omega_o))
        for i, (src, dst) in enumerate(ends):
            keep("e" + str(4 + i), src, dst)

    raw = ((raw_tm, tgt_msk), (raw_sm, src_msk), (raw_tl, tgt_len), (raw_sl, src_len))
    for i, (ref, given) in enumerate(raw):
        keep("raw" + str(i), given, ref)
    given = ((h_biases, biases), (h_up_bias, up_bias), (h_gain, gain), (h_shift, shift), (h_omega, omega))
    for i, (src, ref) in enumerate(given):
        keep("given" + str(i), src, ref)
    barrier = pltpu.get_barrier_semaphore()
    greet = [(cc, at(z, yy, xx)) for cc, yy, xx in plane_peers]
    greet += [(cc, at(zz, y, x)) for zz in z_peers for cc in (c, 1 - c)]
    for device in greet:
        pl.semaphore_signal(barrier, inc=1, device_id=device, device_id_type=MESH)
    pl.semaphore_wait(barrier, len(greet))
    to_plane("x", tok, all_tok, True)
    slice_1("w1", s_in.at[1, pl.ds(1, 2)], ws1)
    slice_1("w0", s_in.at[0], ws0)
    for i, (_, ref) in enumerate(given):
        landed("given" + str(i), ref)
    to_plane("m", mem, all_mem, True)
    for i, (ref, _) in enumerate(raw):
        landed("raw" + str(i), ref)
        span = ref.shape[2]
        for m in range(2):
            for start in (0, 64):
                meta[m, i : i + 1, start : start + span] = ref[m]
    gather_z("q")
    spread_1("x", all_tok, 0)
    spread_1("x", all_tok, 1)
    gather_z("out0")
    to_plane("meta", meta, in_meta)
    gather_z("dn0")
    spread_1("m", all_mem, 0)
    gather_z("out1")
    spread_1("m", all_mem, 1)
    spread_2("x", all_tok, 0)
    slice_2("w0", ws0)
    landed("meta", in_meta)
    lane = lax.broadcasted_iota(jnp.int32, (8, 128), 1)
    gather_f("q")
    all_meta[me_slot] = jnp.where(lane < 64, in_meta[0], in_meta[1])
    gather_f("out0")
    for cc, yy, xx in plane_peers:
        send("marks", all_meta.at[me_slot], all_meta.at[me_slot], (cc, at(z, yy, xx)))
    sent_later("marks", all_meta.at[pl.ds(0, 7)])
    spread_2("m", all_mem, 0)
    spread_2("m", all_mem, 1)
    gather_f("dn0")
    gather_z("up1")
    spread_2("x", all_tok, 1)
    for i, row in enumerate((0, 1, 4)):
        bias_cols[i] = jnp.transpose(jnp.broadcast_to(bias(row), (128, width)))
    gather_z("dn1")
    gather_1("q")
    gather_1("out0")
    gather_1("dn0")
    gather_2("q")
    spread_4("x", all_tok, 0)
    spread_4("m", all_mem, 0)
    gather_2("out0")
    slice_f("w0", ws0)
    make_masks()
    gather_f("out1")
    gather_2("dn0")
    gather_f("up1")
    slice_3("w0", ws0)
    spread_4("x", all_tok, 1)
    gather_z("up0")
    gather_f("dn1")
    spread_4("m", all_mem, 1)
    to_plane("cot", cot, in_cot)
    gather_3("q")
    gather_1("up1")
    spread_3("x", all_tok)
    slice_4("w0", ws0)
    slice_2("w1", ws1)
    gather_3("out0")
    gather_1("out1")
    heads_weights(0, ws0)
    project_heads(all_tok, 0, qt0, k0, kt0, v0, vt0)
    gather_1("dn1")
    gather_f("up0")
    gathered("out0")
    attend(0, qt0, k0, vt0, pt0, l0, ot0, True, "x3", a3, b3)
    gather_2("up1")
    attend(1, qt0, k0, vt0, pt0, l0, ot0, True, "x3", a3, b3)
    attend(2, qt0, k0, vt0, pt0, l0, ot0, True, "x3", a3, b3)
    attend(3, qt0, k0, vt0, pt0, l0, ot0, True, "x3", a3, b3)
    slice_f("w1", ws1)
    gather_2("dn1")
    gather_1("up0")
    landed("x3", b3)
    gathered("q")
    words_f = all_tok[me_slot].reshape(here, width).astype(F32)
    spread_3("m", all_mem)
    gather_3("dn0")
    branch = tn(b3[...].reshape(width, here), matrix(w_out.at[0])) + bias(2)
    h1, scale0 = norm(words_f * omega[0:1, :] + branch, 0, xh0)
    h1_f[...] = h1
    h1_low = h1.astype(BF16)
    by_head(a4, nn(h1_low, matrix(w_q.at[0])) + bias(3))
    slice_3("w1", ws1)
    to_heads("x4", a4, b4)
    gather_2("out1")
    slice_4("w1", ws1)
    gather_3("up1")
    gather_2("up0")
    heads_weights(3, ws1)
    project_heads(all_mem, 3, None, k1, kt1, v1, vt1)
    gathered("up1")
    landed("x4", b4)
    for s in range(GROUP):
        qt1[:, s * here : (s + 1) * here] = (b4[s].astype(F32) * 0.125).astype(BF16)
    attend(0, qt1, k1, vt1, pt1, l1, ot1, False, "x5", a5, b5)
    gather_3("dn1")
    gather_3("out1")
    attend(1, qt1, k1, vt1, pt1, l1, ot1, False, "x5", a5, b5)
    attend(2, qt1, k1, vt1, pt1, l1, ot1, False, "x5", a5, b5)
    attend(3, qt1, k1, vt1, pt1, l1, ot1, False, "x5", a5, b5)
    gather_3("up0")
    gathered("dn1")
    gathered("up0")
    gathered("dn0")
    gathered("out1")
    landed("x5", b5)
    branch = tn(b5[...].reshape(width, here), matrix(w_out.at[1])) + bias(5)
    h2, scale1 = norm(h1_f[...] * omega[1:2, :] + branch, 1, xh1)
    h2_f[...] = h2
    h2_low = h2.astype(BF16)
    feed_up(h2_low, 0)
    feed_up(h2_low, 1)
    first = nn(act[...], matrix(w_dn.at[0]))
    second = nn(act[...], matrix(w_dn.at[1]))
    h3, scale2 = norm(h2_f[...] * omega[2:3, :] + jnp.concatenate([first, second], axis=1) + bias(6), 2, xh2)
    out_res[...] = h3.astype(BF16).reshape(2, 64, width)
    landed("cot", in_cot)
    grad = in_cot[...].reshape(here, width).astype(F32)
    dr, skip = norm_back(grad, 2, xh2, scale2, h2_f[...])
    gf = dr.astype(BF16)
    put(g_dn.at[0], tn(act[...], gf[:, 0:256]))
    scatter_0("dn0")
    column(6, gf.astype(F32))
    back = feed_back(gf, skip)
    dr, skip = norm_back(back, 1, xh1, scale1, h1_f[...])
    gc = dr.astype(BF16)
    column(5, gc.astype(F32))
    by_head(a6, nt(gc, matrix(w_out.at[1])))
    to_heads("x6", a6, b6)
    scatter_1("dn0")
    put(g_up.at[0], tn(h2_low, gul[:, 0:1024]))
    scatter_0("up0")
    put(g_up.at[1], tn(h2_low, gul[:, 1024:2048]))
    scatter_1("up0")
    scatter_0("up1")
    back = skip
    landed("x6", b6)
    attend_start(b6, l1, ot1)
    attend_back(0, qt1, kt1, v1, pt1, False, "x7", a7, b7)
    attend_back(1, qt1, kt1, v1, pt1, False, "x7", a7, b7)
    attend_back(2, qt1, kt1, v1, pt1, False, "x7", a7, b7)
    attend_back(3, qt1, kt1, v1, pt1, False, "x7", a7, b7)
    put(g_dn.at[1], tn(act[...], gf[:, 256:512]))
    scatter_2("dn0")
    scatter_1("up1")
    dt1[0:64, :] = acc_k[...].astype(BF16)
    dt1[64:128, :] = acc_v[...].astype(BF16)
    rows_back(dt1, 3, dx1, 1 - c)
    scatter_2("up0")
    merge_0("dm", dx1, dc1)
    rows_back(dt1, 3, dx1, c)
    slices_back(dt1, all_mem, gs1)
    landed("x7", b7)
    put(g_out.at[1], nn(b5[...].reshape(width, here), gc))
    scatter_0("dn1")
    scatter_3("dn0")
    from_plane("res", out_res, o_res)
    dq = b7[...].reshape(width, here)
    dq_row = flip(dq)
    column(3, dq_row)
    back = back + nt(dq_row.astype(BF16), matrix(w_q.at[0]))
    dr, skip = norm_back(back, 0, xh0, scale0, words_f)
    value_sums(dt1)
    ga = dr.astype(BF16)
    unslice_0("u1", gs1, cs1)
    column(2, ga.astype(F32))
    small("s0", sg0, sr0, core_next)
    by_head(a8, nt(ga, matrix(w_out.at[0])))
    put(g_q.at[0], nt(flip(h1_low).astype(BF16), dq))
    to_heads("x8", a8, b8)
    small_add("s0", sr0, sg0, sg1)
    small("s1", sg1, sr1, y_next)
    scatter_0("q")
    scatter_0("out1")
    put(g_out.at[0], nn(b3[...].reshape(width, here), ga))
    scatter_2("up1")
    last = skip
    scatter_1("dn1")
    scatter_f("dn0")
    scatter_3("up0")
    landed("x8", b8)
    attend_start(b8, l0, ot0)
    scatter_0("out0")
    attend_back(0, qt0, kt0, v0, pt0, True, None, None, None)
    unslice_1("u1", gs1, cs1, zs1)
    merge_1("dm", dx1, dc1, dp1)
    attend_back(1, qt0, kt0, v0, pt0, True, None, None, None)
    small_add("s1", sr1, sg1, sg2)
    scatter_f("up0")
    small("s2", sg2, sr2, x_next)
    attend_back(2, qt0, kt0, v0, pt0, True, None, None, None)
    attend_back(3, qt0, kt0, v0, pt0, True, None, None, None)
    scatter_1("out1")
    scatter_3("up1")
    scattered("dn0")
    unslice_f("u1", gs1, zs1)
    dt0[64:128, :] = acc_k[...].astype(BF16)
    scatter_1("q")
    dt0[128:192, :] = acc_v[...].astype(BF16)
    slices_back(dt0, all_tok, gs0)
    rows_back(dt0, 0, dx0, 1 - c)
    unslice_0("u0", gs0, cs0)
    head_sums(dt0)
    scatter_2("dn1")
    merge_3("dm", dx1, dp1)
    small("t0", tg0, tr0, core_next)
    unslice_1("u0", gs0, cs0, zs0)
    small_add("s2", sr2, sg2, sg3)
    scatter_f("up1")
    merge_0("dx", dx0, dc0)
    scatter_2("out1")
    small_z("sa", sg3, slice(None), tile_own, sra)
    small_z("sb", sg3, pl.ds(8, 8), tile_up, srb)
    small_add("t0", tr0, tg0, tg1)
    scatter_3("dn1")
    small("t1", tg1, tr1, y_next)
    rows_back(dt0, 0, dx0, c)
    scattered("up0")
    scatter_1("out0")
    merge_1("dx", dx0, dc0, dp0)
    scatter_2("q")
    out_mem[...] = merge_2("dm", dx1, dp1).astype(BF16).reshape(2, 64, width)
    from_plane("gmem", out_mem, o_mem)
    small_add("t1", tr1, tg1, tg2)
    small("t2", tg2, tr2, x_next)
    scatter_f("dn1")
    scatter_3("out1")
    scatter_2("out0")
    merge_3("dx", dx0, dp0)
    unslice_f("u0", gs0, zs0)
    scatter_3("q")
    small_add("t2", tr2, tg2, tg3)
    scatter_3("out0")
    scattered("dn1")
    landed("res", o_res)
    unslice_2("u1", gs1, zs1, fs1, o_in.at[1, pl.ds(1, 2)])
    scatter_f("q")
    scatter_f("out1")
    small_z("ta", tg3, slice(None), tile_own, tra)
    unslice_2("u0", gs0, zs0, fs0, o_in.at[0])
    keep("e3", o_dn, h_dn)
    scatter_f("out0")
    out_tok[...] = (merge_2("dx", dx0, dp0) + last).astype(BF16).reshape(2, 64, width)
    from_plane("gtok", out_tok, o_tok)
    landed("gmem", o_mem)
    small_out()
    scattered("up1")
    unslice_3("u1", o_in.at[1, pl.ds(1, 2)])
    scattered("out1")
    scattered("q")
    keep("e2", o_up, h_up)
    scattered("out0")
    keep("e1", o_out, h_out)
    unslice_3("u0", o_in.at[0])
    keep("e0", o_in, h_in)
    landed("gtok", o_tok)
    for i, ref in enumerate((h_in, h_out, h_up, h_dn, h_bias, h_upb, h_gain_o, h_shift_o, h_omega_o)):
        landed("e" + str(i), ref)
    for semaphore, ref, when in pending:
        if when is None:
            wait(semaphore, ref)
        else:

            @pl.when(when)
            def _():
                wait(semaphore, ref)

    for i, total in enumerate(bins):
        if total:
            wait(ss.at[i], gauge.at[pl.ds(0, total // 1024)])
    spans = [2 * line_bytes[0] + 3 * fold_bytes[0], 4 * line_bytes[0] + 3 * fold_bytes[0]]
    assert spans[0] % UNIT == 0 and spans[1] % UNIT == 0

    @pl.when(edge)
    def _():
        wait(ss.at[BINS], gauge.at[pl.ds(0, spans[0] // 1024)])

    @pl.when(jnp.logical_not(edge))
    def _():
        wait(ss.at[BINS], gauge.at[pl.ds(0, spans[1] // 1024)])

    assert len(names) <= NAMES and len(bins) <= BINS and BINS + 1 + len(odd) <= ss.shape[0]


def copy_kernel(*refs):
    count = len(refs) // 2
    for i in range(count):
        refs[count + i][...] = refs[i][...]


def fused_local(
    tokens, memory, cotangent, tgt_lengths, src_lengths, tgt_mask, src_mask, attn_in, attn_out, w_up, w_down,
    biases, up_bias, norm_gain, norm_shift, omega,
):
    any_space = pl.BlockSpec(memory_space=pl.ANY)
    vmem = pl.BlockSpec(memory_space=pltpu.VMEM)
    lines = (CORES, PLANES, YS, XS)
    leads = {"q": 1, "out": 2, "up": 2, "dn": 2}
    shards = {"q": (16, 512), "out": (16, 512), "up": (16, 1024), "dn": (64, 256)}
    kinds = tuple(leads)

    def low(*shape):
        return pltpu.VMEM(shape, BF16)

    def full(*shape):
        return pltpu.VMEM(shape, F32)

    def whole(k):
        return low(leads[k], *lines, *shards[k])

    def halved(k, *middle):
        return low(2, leads[k], *middle, shards[k][0], shards[k][1] // 2)

    params = [full(7, 512), full(1, 2048), full(3, 512), full(3, 512), full(3, 512)]
    results = [(2, 3, 16, 512), (2, 16, 512), (1, 16, 2048), (1, 64, 512), (7, 16), (1, 64), (3, 16), (3, 16), (3, 16)]
    scratch = params + [full(*shape) for shape in results]
    scratch += [whole(k) for k in kinds] * 2
    scratch += [low(leads[k], *lines[1:], *shards[k]) for k in kinds]
    scratch += [halved(k, PLANES, 2) for k in kinds] + [halved(k, PLANES) for k in kinds]
    scratch += [low(3, leads[k], *shards[k]) for k in kinds]
    scratch += [low(n, CORES, PLANES, 4, 16, 128) for n in (3, 2)] * 2
    scratch += [low(n, PLANES, 4, 16, 128) for n in (3, 2)] + [low(3, n, 4, 16, 128) for n in (3, 2)]
    scratch += [full(n, 4, 16, 128) for n in (3, 2)]
    local_rows = low(2, 64, 512)
    marks = [pltpu.VMEM((2, 1, n), jnp.int32) for n in (32, 32, 64, 64)] + [pltpu.VMEM((2, 8, 128), jnp.int32)] * 2
    scratch += [low(GROUP, 2, 64, 512)] * 2 + [local_rows] + marks + [pltpu.VMEM((GROUP, 8, 128), jnp.int32)]
    scratch += [low(GROUP, 2, 64, 512)] * 2 + [low(4, 2, 64, 512)] * 2 + [low(3, 2, 64, 512)] * 2
    scratch += [low(GROUP, 64, 128)] * 12 + [local_rows] * 3
    scratch += [full(24, 512)] * 7 + [full(3, 24, 128), full(3, 8, 128)]
    scratch += [full(8, 512)] * 7 + [full(3, 8, 128)]
    scratch += [full(1024, 128)] * 3 + [full(8, 1024)]
    scratch += ([low(64, 1024)] * 3 + [low(1024, 64)] * 2 + [low(1024, 1024), full(1, 1024), full(64, 1024)]) * 2
    scratch += [low(64, 1024)] + [full(64, 1024)] * 2
    scratch += [low(128, 2048), full(128, 2048), low(128, 2048)] + [full(128, 512)] * 5
    scratch += [low(5, 128, 512), full(3, 512, 128), full(3, 128, 512), low(192, 1024), low(128, 1024), low(2048, 512)]
    scratch += [low(leads[k], *shards[k]) for k in kinds] + [low(n, 4, 16, 128) for n in (3, 2)]
    scratch += [pltpu.SemaphoreType.DMA((44,)), pltpu.SemaphoreType.DMA((NAMES,))]
    rows = jax.ShapeDtypeStruct((2, 64, 512), BF16)

    def wide_out(*shape):
        return jax.ShapeDtypeStruct(shape, F32)

    outs = pl.pallas_call(
        fused_kernel,
        name="layer",
        out_shape=(rows, rows, rows, *(wide_out(*shape) for shape in results)),
        in_specs=[any_space] * 16,
        out_specs=(any_space,) * 12,
        scratch_shapes=scratch,
        compiler_params=pltpu.CompilerParams(collective_id=0, has_side_effects=True, vmem_limit_bytes=60 * 1024 * 1024),
    )(
        tokens.reshape(2, 64, 512), memory.reshape(2, 64, 512), cotangent.reshape(2, 64, 512),
        tgt_lengths, src_lengths, jnp.transpose(tgt_mask, (0, 2, 1)), jnp.transpose(src_mask, (0, 2, 1)),
        attn_in, attn_out, w_up.reshape(1, 16, 2048), w_down.reshape(1, 64, 512),
        biases, up_bias.reshape(1, 2048), norm_gain, norm_shift, omega,
    )
    outs = pl.pallas_call(
        copy_kernel,
        name="hand_over",
        out_shape=tuple(jax.ShapeDtypeStruct(out.shape, out.dtype) for out in outs),
        in_specs=[vmem] * len(outs),
        out_specs=(vmem,) * len(outs),
    )(*outs)
    shaped = [out.reshape(2, 64, 1, 512) for out in outs[:3]]
    return (
        *shaped, outs[3], outs[4], outs[5].reshape(16, 2048), outs[6].reshape(64, 512), outs[7], outs[8].reshape(64),
        outs[9], outs[10], outs[11],
    )


def solution(mesh):
    if mesh.shape["seq"] != PLANES * YS * XS or mesh.shape["rows"] != CORES:
        return general(mesh)
    return over(mesh, fused_local)
```

```python
import functools
import math

import jax
import jax.numpy as jnp
from jax import lax
from jax.experimental import pallas as pl
from jax.experimental.pallas import tpu as pltpu
from jax.sharding import PartitionSpec as P

HEADS = 8


def norm_block(branch, skip, scale, gain, shift):
    mixed = skip * scale + branch
    centered = mixed - jnp.mean(mixed, axis=-1, keepdims=True)
    variance = jnp.mean(centered * centered, axis=-1, keepdims=True)
    return centered * lax.rsqrt(variance + 1e-05) * gain + shift


def project(values, matrix):
    return jnp.einsum("trd,de->tre", values, matrix, preferred_element_type=jnp.float32)


def project_back(grads, matrix):
    return jnp.einsum("tre,de->trd", grads, matrix, preferred_element_type=jnp.float32)


def matrix_grad(values, grads):
    return jnp.einsum("trd,tre->de", values, grads, preferred_element_type=jnp.float32)


def column_sum(grads):
    return jnp.sum(grads.astype(jnp.float32), axis=(0, 1))


def segment_of(positions, ends):
    return jnp.sum((ends[None, :, :] <= positions[:, None, None]).astype(jnp.int32), axis=-1)


def segment_bounds(first, last, ends):
    lowest = jnp.sum((ends <= first).astype(jnp.int32), axis=-1)
    highest = jnp.sum((ends <= last).astype(jnp.int32), axis=-1)
    return (lowest, highest)


def ranges_share(query_bounds, key_bounds):
    return jnp.any((key_bounds[0] <= query_bounds[1]) & (key_bounds[1] >= query_bounds[0]))


def key_status(positions, real_marks, ends, starts, causal):
    segments = segment_of(positions, ends)
    usable = real_marks > 0.5
    if not causal:
        usable = usable | jnp.any(starts[None, :, :] == positions[:, None, None], axis=-1)
    return (segments, usable)


def permitted(query_pos, query_seg, key_pos, key_seg, usable, causal):
    same = jnp.transpose(query_seg)[:, :, None] == jnp.transpose(key_seg)[:, None, :]
    usable_keys = jnp.transpose(usable)[:, None, :]
    if causal:
        before = (key_pos[None, :] <= query_pos[:, None])[None]
        itself = (key_pos[None, :] == query_pos[:, None])[None]
        return same & before & (usable_keys | itself)
    return same & usable_keys


def block_grads(query_heads, grad_heads, lambdas, key_heads, value_heads, permit):
    scores = (
        jnp.einsum("arhd,brhd->rhab", query_heads, key_heads, preferred_element_type=jnp.float32)
        * 0.125
    )
    weights = jnp.where(permit[:, None], jnp.exp(scores), 0.0)
    spread = jnp.einsum(
        "arhd,brhd->rhab", grad_heads, value_heads, preferred_element_type=jnp.float32
    )
    slopes = weights * (spread + jnp.transpose(lambdas, (1, 2, 0))[..., None])
    return (weights.astype(jnp.bfloat16), slopes.astype(jnp.bfloat16))


def local(
    tokens,
    memory,
    cotangent,
    tgt_lengths,
    src_lengths,
    tgt_mask,
    src_mask,
    attn_in,
    attn_out,
    w_up,
    w_down,
    biases,
    up_bias,
    norm_gain,
    norm_shift,
    omega,
):
    micro_count, tokens_here, rows_here, width = tokens.shape
    head_size = width // HEADS
    my_pos = lax.axis_index("seq") * tokens_here + jnp.arange(tokens_here, dtype=jnp.int32)
    my_first = my_pos[0]
    my_last = my_pos[tokens_here - 1]

    def split_heads(values):
        return values.reshape(values.shape[0], rows_here, HEADS, head_size)

    def zero_heads():
        return jnp.zeros((tokens_here, rows_here, HEADS, head_size), jnp.float32)

    results = []
    grads_words = []
    grads_sources = []
    shares_all = None
    for micro_index in range(micro_count):
        in_weights = lax.all_gather(attn_in, ("rows", "seq"), axis=2, tiled=True)
        out_weights = lax.all_gather(attn_out, ("rows", "seq"), axis=1, tiled=True)
        up_weights = lax.all_gather(w_up, ("rows", "seq"), axis=0, tiled=True)
        down_weights = lax.all_gather(w_down, ("rows", "seq"), axis=0, tiled=True)
        words = tokens[micro_index]
        sources = memory[micro_index]
        words_full = words.astype(jnp.float32)
        tgt_len = tgt_lengths[micro_index]
        src_len = src_lengths[micro_index]
        tgt_ends = jnp.cumsum(tgt_len, axis=-1)
        src_ends = jnp.cumsum(src_len, axis=-1)
        src_starts = src_ends - src_len
        query_seg = segment_of(my_pos, tgt_ends)
        query_bounds = segment_bounds(my_first, my_last, tgt_ends)
        tgt_real = tgt_mask[micro_index].astype(jnp.bfloat16)
        src_real = src_mask[micro_index].astype(jnp.bfloat16)

        def attend(queries, keys, values, real_marks, ends, starts, causal):
            full_keys, full_values, full_real = (
                lax.all_gather(keys, "seq", axis=0, tiled=True),
                lax.all_gather(values, "seq", axis=0, tiled=True),
                lax.all_gather(real_marks, "seq", axis=0, tiled=True),
            )
            length = full_keys.shape[0]
            block = math.gcd(length, 512)
            query_heads = split_heads(queries)

            def step(carry, block_index):
                begin = block_index * block
                shares = ranges_share(query_bounds, segment_bounds(begin, begin + block - 1, ends))

                def step_compute(state):
                    totals, accum = state
                    key_heads = split_heads(lax.dynamic_slice_in_dim(full_keys, begin, block, 0))
                    value_heads = split_heads(
                        lax.dynamic_slice_in_dim(full_values, begin, block, 0)
                    )
                    key_pos = begin + jnp.arange(block, dtype=jnp.int32)
                    key_seg, usable = key_status(
                        key_pos,
                        lax.dynamic_slice_in_dim(full_real, begin, block, 0),
                        ends,
                        starts,
                        causal,
                    )
                    permit = permitted(my_pos, query_seg, key_pos, key_seg, usable, causal)
                    scores = (
                        jnp.einsum(
                            "trhd,krhd->rhtk",
                            query_heads,
                            key_heads,
                            preferred_element_type=jnp.float32,
                        )
                        * 0.125
                    )
                    weights = jnp.where(permit[:, None], jnp.exp(scores), 0.0)
                    totals = totals + jnp.sum(weights, axis=-1)
                    accum = accum + jnp.einsum(
                        "rhtk,krhd->trhd",
                        weights.astype(jnp.bfloat16),
                        value_heads,
                        preferred_element_type=jnp.float32,
                    )
                    return (totals, accum)

                return (lax.cond(shares, step_compute, lambda unchanged: unchanged, carry), None)

            start_carry = (jnp.zeros((rows_here, HEADS, tokens_here), jnp.float32), zero_heads())
            (totals, accum), unused = lax.scan(
                step, start_carry, jnp.arange(length // block, dtype=jnp.int32)
            )
            sums = jnp.transpose(totals, (2, 0, 1))
            output = (accum / sums[..., None]).reshape(tokens_here, rows_here, width)
            return (output, sums, (full_keys, full_values, full_real))

        def attention_back(
            grad_out,
            output,
            sums,
            queries,
            keys,
            values,
            real_marks,
            gathered_set,
            ends,
            starts,
            causal,
        ):
            full_keys, full_values, full_real = gathered_set
            grad_heads = split_heads(grad_out)
            lambdas = -jnp.sum(grad_heads * split_heads(output), axis=-1) / sums
            scaled = (grad_heads / sums[..., None]).astype(jnp.bfloat16)
            query_heads = split_heads(queries)
            length = full_keys.shape[0]
            block = math.gcd(length, 512)

            def query_step(accum, block_index):
                begin = block_index * block
                shares = ranges_share(query_bounds, segment_bounds(begin, begin + block - 1, ends))

                def query_compute(state):
                    key_heads = split_heads(lax.dynamic_slice_in_dim(full_keys, begin, block, 0))
                    value_heads = split_heads(
                        lax.dynamic_slice_in_dim(full_values, begin, block, 0)
                    )
                    key_pos = begin + jnp.arange(block, dtype=jnp.int32)
                    key_seg, usable = key_status(
                        key_pos,
                        lax.dynamic_slice_in_dim(full_real, begin, block, 0),
                        ends,
                        starts,
                        causal,
                    )
                    permit = permitted(my_pos, query_seg, key_pos, key_seg, usable, causal)
                    weights, slopes = block_grads(
                        query_heads, scaled, lambdas, key_heads, value_heads, permit
                    )
                    return (
                        state
                        + jnp.einsum(
                            "rhab,brhd->arhd", slopes, key_heads, preferred_element_type=jnp.float32
                        )
                        * 0.125
                    )

                return (lax.cond(shares, query_compute, lambda unchanged: unchanged, accum), None)

            grad_query, unused = lax.scan(
                query_step, zero_heads(), jnp.arange(length // block, dtype=jnp.int32)
            )
            all_lambdas = lax.all_gather(lambdas, "seq", axis=0, tiled=True)
            local_seg, local_usable = key_status(my_pos, real_marks, ends, starts, causal)
            local_bounds = segment_bounds(my_first, my_last, ends)
            local_keys = split_heads(keys)
            local_values = split_heads(values)
            query_piece = lax.all_gather(queries, "seq", axis=0, tiled=True)
            scaled_piece = lax.all_gather(
                scaled.reshape(tokens_here, rows_here, width), "seq", axis=0, tiled=True
            )
            size = query_piece.shape[0]
            inner = math.gcd(size, 512)

            def inner_step(inner_carry, inner_index):
                offset = inner_index * inner
                piece_first = offset
                shares = ranges_share(
                    segment_bounds(piece_first, piece_first + inner - 1, tgt_ends), local_bounds
                )

                def inner_compute(state):
                    acc_key, acc_value = state
                    query_blk = split_heads(lax.dynamic_slice_in_dim(query_piece, offset, inner, 0))
                    scaled_blk = split_heads(
                        lax.dynamic_slice_in_dim(scaled_piece, offset, inner, 0)
                    )
                    lambda_blk = lax.dynamic_slice_in_dim(all_lambdas, piece_first, inner, 0)
                    query_pos = piece_first + jnp.arange(inner, dtype=jnp.int32)
                    permit = permitted(
                        query_pos,
                        segment_of(query_pos, tgt_ends),
                        my_pos,
                        local_seg,
                        local_usable,
                        causal,
                    )
                    weights, slopes = block_grads(
                        query_blk, scaled_blk, lambda_blk, local_keys, local_values, permit
                    )
                    acc_key = (
                        acc_key
                        + jnp.einsum(
                            "rhab,arhd->brhd", slopes, query_blk, preferred_element_type=jnp.float32
                        )
                        * 0.125
                    )
                    acc_value = acc_value + jnp.einsum(
                        "rhab,arhd->brhd", weights, scaled_blk, preferred_element_type=jnp.float32
                    )
                    return (acc_key, acc_value)

                return (
                    lax.cond(shares, inner_compute, lambda unchanged: unchanged, inner_carry),
                    None,
                )

            folded, unused_inner = lax.scan(
                inner_step, (zero_heads(), zero_heads()), jnp.arange(size // inner, dtype=jnp.int32)
            )
            grad_key, grad_value = folded
            grad_key = grad_key.reshape(tokens_here, rows_here, width)
            grad_value = grad_value.reshape(tokens_here, rows_here, width)
            return (grad_query.reshape(tokens_here, rows_here, width), grad_key, grad_value)

        self_query = (project(words, in_weights[0, 0]) + biases[0]).astype(jnp.bfloat16)
        self_key = project(words, in_weights[0, 1]).astype(jnp.bfloat16)
        self_value = (project(words, in_weights[0, 2]) + biases[1]).astype(jnp.bfloat16)
        heard, heard_sums, self_set = attend(
            self_query, self_key, self_value, tgt_real, tgt_ends, None, True
        )
        heard_low = heard.astype(jnp.bfloat16)
        branch_self = project(heard_low, out_weights[0]) + biases[2]
        hidden_one, pull_one = jax.vjp(
            norm_block, branch_self, words_full, omega[0], norm_gain[0], norm_shift[0]
        )
        hidden_one_low = hidden_one.astype(jnp.bfloat16)
        cross_query = (project(hidden_one_low, in_weights[1, 0]) + biases[3]).astype(jnp.bfloat16)
        cross_key = project(sources, in_weights[1, 1]).astype(jnp.bfloat16)
        cross_value = (project(sources, in_weights[1, 2]) + biases[4]).astype(jnp.bfloat16)
        recalled, recalled_sums, cross_set = attend(
            cross_query, cross_key, cross_value, src_real, src_ends, src_starts, False
        )
        recalled_low = recalled.astype(jnp.bfloat16)
        branch_cross = project(recalled_low, out_weights[1]) + biases[5]
        hidden_two, pull_two = jax.vjp(
            norm_block, branch_cross, hidden_one, omega[1], norm_gain[1], norm_shift[1]
        )
        hidden_two_low = hidden_two.astype(jnp.bfloat16)
        up_pre = project(hidden_two_low, up_weights) + up_bias
        active, pull_active = jax.vjp(jax.nn.gelu, up_pre)
        active_low = active.astype(jnp.bfloat16)
        branch_ffn = project(active_low, down_weights) + biases[6]
        outcome, pull_three = jax.vjp(
            norm_block, branch_ffn, hidden_two, omega[2], norm_gain[2], norm_shift[2]
        )
        grad_result = cotangent[micro_index].astype(jnp.float32)
        grad_ffn, grad_two, omega_three, gain_three, shift_three = pull_three(grad_result)
        grad_ffn_low = grad_ffn.astype(jnp.bfloat16)
        grad_down = matrix_grad(active_low, grad_ffn_low)
        bias_ffn = column_sum(grad_ffn_low)
        grad_up_pre = pull_active(project_back(grad_ffn_low, down_weights))[0].astype(jnp.bfloat16)
        grad_up = matrix_grad(hidden_two_low, grad_up_pre)
        bias_up = column_sum(grad_up_pre)
        grad_two = grad_two + project_back(grad_up_pre, up_weights)
        grad_cross, grad_one, omega_two, gain_two, shift_two = pull_two(grad_two)
        grad_cross_low = grad_cross.astype(jnp.bfloat16)
        grad_out_cross = matrix_grad(recalled_low, grad_cross_low)
        bias_out_cross = column_sum(grad_cross_low)
        grad_recalled = project_back(grad_cross_low, out_weights[1])
        cross_gq, cross_gk, cross_gv = attention_back(
            grad_recalled,
            recalled,
            recalled_sums,
            cross_query,
            cross_key,
            cross_value,
            src_real,
            cross_set,
            src_ends,
            src_starts,
            False,
        )
        cross_gq = cross_gq.astype(jnp.bfloat16)
        cross_gk = cross_gk.astype(jnp.bfloat16)
        cross_gv = cross_gv.astype(jnp.bfloat16)
        grad_cross_query = matrix_grad(hidden_one_low, cross_gq)
        grad_cross_key = matrix_grad(sources, cross_gk)
        grad_cross_value = matrix_grad(sources, cross_gv)
        grad_one = grad_one + project_back(cross_gq, in_weights[1, 0])
        grad_sources = project_back(cross_gk, in_weights[1, 1]) + project_back(
            cross_gv, in_weights[1, 2]
        )
        grad_self, grad_words, omega_one, gain_one, shift_one = pull_one(grad_one)
        grad_self_low = grad_self.astype(jnp.bfloat16)
        grad_out_self = matrix_grad(heard_low, grad_self_low)
        bias_out_self = column_sum(grad_self_low)
        grad_heard = project_back(grad_self_low, out_weights[0])
        self_gq, self_gk, self_gv = attention_back(
            grad_heard,
            heard,
            heard_sums,
            self_query,
            self_key,
            self_value,
            tgt_real,
            self_set,
            tgt_ends,
            None,
            True,
        )
        self_gq = self_gq.astype(jnp.bfloat16)
        self_gk = self_gk.astype(jnp.bfloat16)
        self_gv = self_gv.astype(jnp.bfloat16)
        grad_words = (
            grad_words
            + project_back(self_gq, in_weights[0, 0])
            + project_back(self_gk, in_weights[0, 1])
            + project_back(self_gv, in_weights[0, 2])
        )
        grad_in = jnp.stack(
            [
                jnp.stack(
                    [
                        matrix_grad(words, self_gq),
                        matrix_grad(words, self_gk),
                        matrix_grad(words, self_gv),
                    ]
                ),
                jnp.stack([grad_cross_query, grad_cross_key, grad_cross_value]),
            ]
        )
        grad_out = jnp.stack([grad_out_self, grad_out_cross])
        grad_bias = jnp.stack(
            [
                column_sum(self_gq),
                column_sum(self_gv),
                bias_out_self,
                column_sum(cross_gq),
                column_sum(cross_gv),
                bias_out_cross,
                bias_ffn,
            ]
        )
        grad_gain = jnp.stack([gain_one, gain_two, gain_three])
        grad_shift = jnp.stack([shift_one, shift_two, shift_three])
        grad_omega = jnp.stack([omega_one, omega_two, omega_three])
        grads = (
            grad_in,
            grad_out,
            grad_up,
            grad_down,
            grad_bias,
            bias_up,
            grad_gain,
            grad_shift,
            grad_omega,
        )
        outcome, grad_words, grad_sources, grads = (
            outcome.astype(jnp.bfloat16),
            grad_words.astype(jnp.bfloat16),
            grad_sources.astype(jnp.bfloat16),
            grads,
        )
        results.append(outcome)
        grads_words.append(grad_words)
        grads_sources.append(grad_sources)
        part_shares = (
            lax.psum_scatter(grads[0], ("rows", "seq"), scatter_dimension=2, tiled=True),
            lax.psum_scatter(grads[1], ("rows", "seq"), scatter_dimension=1, tiled=True),
            lax.psum_scatter(grads[2], ("rows", "seq"), scatter_dimension=0, tiled=True),
            lax.psum_scatter(grads[3], ("rows", "seq"), scatter_dimension=0, tiled=True),
            lax.psum_scatter(grads[4], ("rows", "seq"), scatter_dimension=1, tiled=True),
            lax.psum_scatter(grads[5], ("rows", "seq"), scatter_dimension=0, tiled=True),
            lax.psum_scatter(grads[6], ("rows", "seq"), scatter_dimension=1, tiled=True),
            lax.psum_scatter(grads[7], ("rows", "seq"), scatter_dimension=1, tiled=True),
            lax.psum_scatter(grads[8], ("rows", "seq"), scatter_dimension=1, tiled=True),
        )
        shares_all = (
            part_shares if shares_all is None else jax.tree.map(jnp.add, shares_all, part_shares)
        )
    return (jnp.stack(results), jnp.stack(grads_words), jnp.stack(grads_sources)) + tuple(
        shares_all
    )


def over(mesh, function):
    return jax.shard_map(
        function,
        mesh=mesh,
        in_specs=(
            P(None, "seq", "rows", None),
            P(None, "seq", "rows", None),
            P(None, "seq", "rows", None),
            P(None, "rows", None),
            P(None, "rows", None),
            P(None, "seq", "rows"),
            P(None, "seq", "rows"),
            P(None, None, ("rows", "seq"), None),
            P(None, ("rows", "seq"), None),
            P(("rows", "seq"), None),
            P(("rows", "seq"), None),
            P(),
            P(),
            P(),
            P(),
            P(),
        ),
        out_specs=(
            P(None, "seq", "rows", None),
            P(None, "seq", "rows", None),
            P(None, "seq", "rows", None),
            P(None, None, ("rows", "seq"), None),
            P(None, ("rows", "seq"), None),
            P(("rows", "seq"), None),
            P(("rows", "seq"), None),
            P(None, ("rows", "seq")),
            P(("rows", "seq")),
            P(None, ("rows", "seq")),
            P(None, ("rows", "seq")),
            P(None, ("rows", "seq")),
        ),
        check_vma=False,
    )


def general(mesh):
    return over(mesh, local)


MESH = pl.DeviceIdType.MESH
UNIT = 16 * 1024
BINS = 16
NAMES = 200
BETWEEN = ("dn0", "dn1")
ODD = ("marks", "w0p", "w1p", "u0p", "x3", "x5", "x7", "sa", "sb", "ta")
F32 = jnp.float32
BF16 = jnp.bfloat16
PLANES, YS, XS, CORES = 4, 2, 2, 2
GROUP = YS * XS * CORES


def nn(left, right):
    return lax.dot_general(left, right, (((1,), (0,)), ((), ())), preferred_element_type=F32)


def nt(left, right):
    return lax.dot_general(left, right, (((1,), (1,)), ((), ())), preferred_element_type=F32)


def tn(left, right):
    return lax.dot_general(left, right, (((0,), (0,)), ((), ())), preferred_element_type=F32)


def flip(value):
    return jnp.transpose(value.astype(F32))


def fused_kernel(
    tok, mem, cot, tgt_len, src_len, tgt_msk, src_msk, s_in, s_out, s_up, s_dn, h_biases, h_up_bias, h_gain, h_shift, h_omega,
    o_res, o_tok, o_mem, h_in, h_out, h_up, h_dn, h_bias, h_upb, h_gain_o, h_shift_o, h_omega_o,
    biases, up_bias, gain, shift, omega, o_in, o_out, o_up, o_dn, o_bias, o_upb, o_gain, o_shift, o_omega,
    w_q, w_out, w_up, w_dn, g_q, g_out, g_up, g_dn,
    c_q, c_out, c_up, c_dn,
    p_q, p_out, p_up, p_dn,
    q_q, q_out, q_up, q_dn,
    z_q, z_out, z_up, z_dn,
    ws0, ws1, gs0, gs1, cs0, cs1, zs0, zs1, fs0, fs1,
    all_tok, all_mem, in_cot, raw_tl, raw_sl, raw_tm, raw_sm, meta, in_meta, all_meta,
    dx0, dx1, dc0, dc1, dp0, dp1,
    a3, b3, a4, b4, a5, b5, a6, b6, a7, b7, a8, b8,
    out_res, out_tok, out_mem,
    sg0, sg1, sg2, sg3, sr0, sr1, sr2, sra, srb,
    tg0, tg1, tg2, tg3, tr0, tr1, tr2, tra,
    code_self, code_cross, key_pos, rows_f,
    qt0, kt0, vt0, k0, v0, pt0, l0, ot0,
    qt1, kt1, vt1, k1, v1, pt1, l1, ot1,
    dnt, acc_k, acc_v,
    act, slope, gul, xh0, xh1, xh2, h1_f, h2_f,
    wt, bias_cols, wz, dt0, dt1, gauge,
    f_q, f_out, f_up, f_dn, f_u0, f_u1, mid_far, mid_line,
    ss, rs,
):
    c = lax.axis_index("rows")
    seq = lax.axis_index("seq")
    z = seq // (YS * XS)
    yx = lax.rem(seq, YS * XS)
    y = yx // XS
    x = lax.rem(yx, XS)
    width = 512
    here = 2 * 64

    def at(zz, yy, xx):
        return zz * (YS * XS) + yy * XS + xx

    def slot(cc, yy, xx):
        return cc * 4 + yy * 2 + xx

    def head(cc, yy, xx):
        return (yy * 2 + xx) * 2 + cc

    me_slot, me_head = slot(c, y, x), head(c, y, x)
    plane_peers = []
    for k in range(1, GROUP):
        cc = 1 - c if k & 4 else c
        yy = 1 - y if k & 2 else y
        xx = 1 - x if k & 1 else x
        plane_peers.append((cc, yy, xx))
    trio = [(1 - y, x), (y, 1 - x), (1 - y, 1 - x)]
    z_peers = [lax.rem(z + k, PLANES) for k in (1, 2, 3)]

    names, expected_bytes = {}, {}
    pending = []
    edge = (z == 0) | (z == PLANES - 1)

    def sem(name):
        return names.setdefault(name, len(names))

    def wait(semaphore, ref):
        pltpu.make_async_copy(ref, ref, semaphore).wait()

    def size(ref):
        return math.prod(ref.shape) * jnp.dtype(ref.dtype).itemsize

    bins = [0]
    odd = {}

    def out_sem(name):
        return ss.at[odd.setdefault(name, BINS + 1 + len(odd))] if name in ODD else ss.at[len(bins) - 1]

    def send(name, src, dst, device, recv=None):
        pltpu.make_async_remote_copy(
            src_ref=src, dst_ref=dst, send_sem=out_sem(name), recv_sem=rs.at[sem(name)] if recv is None else recv,
            device_id=device, device_id_type=MESH,
        ).start()

    def keep(name, src, dst):
        pltpu.make_async_copy(src, dst, rs.at[sem(name)]).start()

    def landed(name, ref):
        wait(rs.at[sem(name)], ref)

    def sent_later(name, ref):
        if name in ODD:
            pending.append((ss.at[odd[name]], ref, None))
            return
        bins[-1] += size(ref)
        assert size(ref) % UNIT == 0, (name, size(ref))
        if bins[-1] > 1024 * UNIT // 16:
            bins.append(0)

    line_bytes = [0]

    def along_z(name, src, block):
        i, j = sem(name + "z"), sem(name + "f")
        for step in (1, -1, 2, -2):
            to = z + step
            far = (z == 0) if step == 2 else (z == PLANES - 1) if step == -2 else None

            @pl.when((to >= 0) & (to < PLANES))
            def _():
                pltpu.make_async_remote_copy(
                    src_ref=src, dst_ref=block(z), send_sem=ss.at[BINS],
                    recv_sem=rs.at[i] if far is None else rs.at[jnp.where(far, j, i)],
                    device_id=(c, at(to, y, x)), device_id_type=MESH,
                ).start()

        line_bytes[0] += size(src)

    def pass_on(name, block):
        for mine, origin, to in ((1, 3, 0), (2, 0, 3)):

            @pl.when(z == mine)
            def _():
                landed(name + "f", block(origin))
                pltpu.make_async_remote_copy(
                    src_ref=block(origin), dst_ref=block(origin), send_sem=ss.at[BINS], recv_sem=rs.at[sem(name + "z")],
                    device_id=(c, at(to, y, x)), device_id_type=MESH,
                ).start()

    fold_bytes = [0]

    def fold_send(name, block, target, to):
        pltpu.make_async_remote_copy(
            src_ref=block, dst_ref=target, send_sem=ss.at[BINS], recv_sem=rs.at[sem(name)],
            device_id=(c, at(to, y, x)), device_id_type=MESH,
        ).start()

    def fold_z(name, block, far, line):
        inner = jnp.where(edge, 0, 1)
        for origin, step, hops in ((0, 3, 1), (3, -3, -1)):

            @pl.when(z == origin)
            def _():
                fold_send(name + "a", block(origin + step), far, origin + hops)
                fold_send(name + "l", block(origin + 2 * hops), line.at[2], origin + 2 * hops)

        for step in (1, -1):
            to = z + step

            @pl.when((to >= 0) & (to < PLANES))
            def _():
                between = jnp.where((to == 0) | (to == PLANES - 1), 0, inner)
                fold_send(name + "l", block(to), line.at[between], to)

        fold_bytes[0] += size(far)

    def fold_f(name, block, far, line):
        for mine, to in ((1, 3), (2, 0)):

            @pl.when(z == mine)
            def _():
                landed(name + "a", far)
                add(block(to), far)
                fold_send(name + "l", block(to), line.at[1], to)

    def fold_sum(name, own, line, result):
        @pl.when(edge)
        def _():
            landed(name + "l", line.at[pl.ds(0, 2)])

        @pl.when(jnp.logical_not(edge))
        def _():
            landed(name + "l", line)

        total = own.astype(F32) + line[0].astype(F32) + line[1].astype(F32)

        @pl.when(edge)
        def _():
            result[...] = total.astype(result.dtype)

        @pl.when(jnp.logical_not(edge))
        def _():
            result[...] = (total + line[2].astype(F32)).astype(result.dtype)

    def line_landed(name, blocks, own):
        @pl.when(edge)
        def _():
            landed(name + "z", blocks(3 + own))

        @pl.when(jnp.logical_not(edge))
        def _():
            landed(name + "z", blocks(2 + own))

    def to_plane(name, src, dst, slotted=False):
        half = lax.rem(z, 2)
        core = z // 2
        if slotted:
            recv = rs.at[jnp.where(half == 0, sem(name + "h0"), sem(name + "h1"))]
            part = dst.at[slot(core, y, x), half]
        else:
            recv = rs.at[sem(name)]
            part = dst.at[half]
        for m in range(2):
            plane = 2 * m + c
            own = (plane == z) & (core == c)
            out = ss.at[odd.setdefault(name + str(m), BINS + 1 + len(odd))]

            @pl.when(own)
            def _():
                pltpu.make_async_copy(src.at[m], part, recv).start()

            @pl.when(jnp.logical_not(own))
            def _():
                pltpu.make_async_remote_copy(
                    src_ref=src.at[m], dst_ref=part, send_sem=out, recv_sem=recv,
                    device_id=(core, at(plane, y, x)), device_id_type=MESH,
                ).start()

            pending.append((out, src.at[m], jnp.logical_not(own)))

    def from_plane(name, src, dst):
        micro, core = z // 2, lax.rem(z, 2)
        recv = rs.at[sem(name)]
        for half in range(2):
            zz = 2 * c + half
            own = (core == c) & (zz == z)
            part = dst.at[micro]
            out = ss.at[odd.setdefault(name + str(half), BINS + 1 + len(odd))]

            @pl.when(own)
            def _():
                pltpu.make_async_copy(src.at[half], part, recv).start()

            @pl.when(jnp.logical_not(own))
            def _():
                pltpu.make_async_remote_copy(
                    src_ref=src.at[half], dst_ref=part, send_sem=out, recv_sem=recv,
                    device_id=(core, at(zz, y, x)), device_id_type=MESH,
                ).start()

            pending.append((out, src.at[half], jnp.logical_not(own)))

    def to_heads(name, src, dst):
        keep(name, src.at[me_head], dst.at[me_slot])
        for cc, yy, xx in plane_peers:
            send(name, src.at[head(cc, yy, xx)], dst.at[me_slot], (cc, at(z, yy, xx)))
        sent_later(name, src.at[pl.ds(0, GROUP - 1)])

    def to_slot(name, src, dst, s):
        device = (s // 4, at(z, (s % 4) // 2, s % 2))
        i = sem(name)
        out = out_sem(name)

        @pl.when(me_slot == s)
        def _():
            pltpu.make_async_copy(src.at[s], dst.at[me_head], rs.at[i]).start()

        @pl.when(me_slot != s)
        def _():
            pltpu.make_async_remote_copy(
                src_ref=src.at[s], dst_ref=dst.at[me_head], send_sem=out, recv_sem=rs.at[i],
                device_id=device, device_id_type=MESH,
            ).start()

    weights = {
        "q": (w_q, s_in.at[1, pl.ds(0, 1)], g_q, c_q, p_q, q_q, z_q, o_in.at[1, pl.ds(0, 1)]),
    }

    for i in range(2):
        one = pl.ds(i, 1)
        refs = (w_out, s_out, g_out, c_out, p_out, q_out, z_out, o_out)
        weights["out" + str(i)] = tuple(
            ref.at[:, one] if ref is p_out or ref is q_out or ref is z_out else ref.at[one] for ref in refs
        )
        refs = (w_up, s_up, g_up, c_up, p_up, q_up, z_up, o_up)
        cols = pl.ds(i * 1024, 1024)
        weights["up" + str(i)] = tuple(
            ref.at[:, one] if ref is p_up or ref is q_up or ref is z_up
            else ref.at[:, :, cols] if ref is s_up or ref is o_up else ref.at[one]
            for ref in refs
        )
        refs = (w_dn, s_dn, g_dn, c_dn, p_dn, q_dn, z_dn, o_dn)
        cols = pl.ds(i * 256, 256)
        weights["dn" + str(i)] = tuple(
            ref.at[:, one] if ref is p_dn or ref is q_dn or ref is z_dn
            else ref.at[:, :, cols] if ref is s_dn or ref is o_dn else ref.at[one]
            for ref in refs
        )

    mids = {g: (mid_far.at[i], mid_line.at[i]) for i, g in enumerate(BETWEEN)}
    fars = {"q": f_q, "u0": f_u0, "u1": f_u1}
    for i in range(2):
        one = pl.ds(i, 1)
        fars["out" + str(i)], fars["up" + str(i)], fars["dn" + str(i)] = f_out.at[one], f_up.at[one], f_dn.at[one]

    def halves(ref):
        cols = ref.shape[-1] // 2
        return pl.ds(0, cols), pl.ds(cols, cols)

    x_next, y_next, core_next = (c, at(z, y, 1 - x)), (c, at(z, 1 - y, x)), (1 - c, seq)

    def gather_z(g):
        full, shard = weights[g][:2]
        if g in BETWEEN:
            first, second = halves(full)
            whole = s_dn if g[:2] == "dn" else s_up
            keep(g + "o", shard, full.at[:, c, z, y, x])
            for which, cols, device in (("1a", first, x_next), ("1b", second, y_next)):
                part = full.at[:, c, z, y, x, :, cols]
                send(g + which, whole.at[:, :, shard_cols(g, cols)], part, device)
                sent_later(g + which, part)
            return
        keep(g + "z", shard, full.at[:, c, z, y, x])
        along_z(g, shard, lambda zz: full.at[:, c, zz, y, x])

    def gather_f(g):
        full = weights[g][0]
        if g in BETWEEN:
            first, second = halves(full)
            pass_on(g + "A", lambda zz: full.at[:, c, zz, y, :, :, first])
            pass_on(g + "B", lambda zz: full.at[:, c, zz, :, x, :, second])
            return
        pass_on(g, lambda zz: full.at[:, c, zz, y, x])

    def gather_1(g):
        full = weights[g][0]
        first, second = halves(full)
        if g in BETWEEN:
            landed(g + "o", full.at[:, c, z, y, x])
            landed(g + "1a", full.at[:, c, z, y, 1 - x, :, first])
            along_z(g + "A", full.at[:, c, z, y, :, :, first], lambda zz: full.at[:, c, zz, y, :, :, first])
            landed(g + "1b", full.at[:, c, z, 1 - y, x, :, second])
            along_z(g + "B", full.at[:, c, z, :, x, :, second], lambda zz: full.at[:, c, zz, :, x, :, second])
            return
        line_landed(g, lambda n: full.at[:, c, pl.ds(0, n), y, x], 1)
        part = full.at[:, c, :, y, x, :, first]
        send(g + "1a", part, part, x_next)
        sent_later(g + "1a", part)
        part = full.at[:, c, :, y, x, :, second]
        send(g + "1b", part, part, y_next)
        sent_later(g + "1b", part)

    def gather_2(g):
        full = weights[g][0]
        first, second = halves(full)
        if g in BETWEEN:
            line_landed(g + "A", lambda n: full.at[:, c, pl.ds(0, n), y, :, :, first], 0)
        else:
            landed(g + "1a", full.at[:, c, :, y, 1 - x, :, first])
        part = full.at[:, c, :, y, :, :, first]
        send(g + "2a", part, part, y_next)
        sent_later(g + "2a", part)
        if g in BETWEEN:
            line_landed(g + "B", lambda n: full.at[:, c, pl.ds(0, n), :, x, :, second], 0)
        else:
            landed(g + "1b", full.at[:, c, :, 1 - y, x, :, second])
        part = full.at[:, c, :, :, x, :, second]
        send(g + "2b", part, part, x_next)
        sent_later(g + "2b", part)

    def shard_cols(g, cols):
        start = 256 * int(g[-1]) if g[:2] == "dn" else 1024 * int(g[-1])
        return pl.ds(start + cols.start, cols.size)

    def gather_3(g):
        full = weights[g][0]
        first, second = halves(full)
        landed(g + "2a", full.at[:, c, :, 1 - y, :, :, first])
        landed(g + "2b", full.at[:, c, :, :, 1 - x, :, second])
        send(g + "3", full.at[:, c], full.at[:, c], core_next)
        sent_later(g + "3", full.at[:, c])

    def gathered(g):
        landed(g + "3", weights[g][0].at[:, 1 - c])

    def add(target, other):
        target[...] = (target[...].astype(F32) + other[...].astype(F32)).astype(BF16)

    def scatter_0(g):
        grad, across = weights[g][2:4]
        send(g + "r0", grad.at[:, 1 - c], across, core_next)
        sent_later(g + "r0", across)

    def scatter_1(g):
        grad, across, part = weights[g][2:5]
        first, second = halves(grad)
        landed(g + "r0", across)
        for lead in range(grad.shape[0]):

            @pl.loop(0, PLANES)
            def _(zz):
                add(grad.at[lead, c, zz], across.at[lead, zz])

        send(g + "r1a", grad.at[:, c, :, 1 - y, :, :, first], part.at[0], y_next)
        sent_later(g + "r1a", part.at[0])
        send(g + "r1b", grad.at[:, c, :, :, 1 - x, :, second], part.at[1], x_next)
        sent_later(g + "r1b", part.at[1])

    def scatter_2(g):
        grad, _, part, piece = weights[g][2:6]
        first, second = halves(grad)
        landed(g + "r1a", part.at[0])
        landed(g + "r1b", part.at[1])
        for lead in range(grad.shape[0]):

            @pl.loop(0, PLANES)
            def _(zz):
                add(grad.at[lead, c, zz, y, :, :, first], part.at[0, lead, zz])
                add(grad.at[lead, c, zz, :, x, :, second], part.at[1, lead, zz])

        if g in BETWEEN:
            fold_z(g + "A", lambda zz: grad.at[:, c, zz, y, :, :, first], mids[g][0].at[0, 0], mids[g][1].at[:, 0])
            fold_z(g + "B", lambda zz: grad.at[:, c, zz, :, x, :, second], mids[g][0].at[1, 0], mids[g][1].at[:, 1])
            return
        send(g + "r2a", grad.at[:, c, :, y, 1 - x, :, first], piece.at[0], x_next)
        sent_later(g + "r2a", piece.at[0])
        send(g + "r2b", grad.at[:, c, :, 1 - y, x, :, second], piece.at[1], y_next)
        sent_later(g + "r2b", piece.at[1])

    def scatter_3(g):
        grad, _, _, piece, line = weights[g][2:7]
        first, second = halves(grad)
        if g in BETWEEN:
            fold_sum(g + "A", grad[:, c, z, y, :, :, first], mids[g][1].at[:, 0], grad.at[:, c, z, y, :, :, first])
            send(g + "r2a", grad.at[:, c, z, y, 1 - x, :, first], piece.at[0, :, 0], x_next)
            sent_later(g + "r2a", piece.at[0, :, 0])
            fold_sum(g + "B", grad[:, c, z, :, x, :, second], mids[g][1].at[:, 1], grad.at[:, c, z, :, x, :, second])
            send(g + "r2b", grad.at[:, c, z, 1 - y, x, :, second], piece.at[1, :, 0], y_next)
            sent_later(g + "r2b", piece.at[1, :, 0])
            return
        landed(g + "r2a", piece.at[0])
        landed(g + "r2b", piece.at[1])
        for lead in range(grad.shape[0]):

            @pl.loop(0, PLANES)
            def _(zz):
                add(grad.at[lead, c, zz, y, x, :, first], piece.at[0, lead, zz])
                add(grad.at[lead, c, zz, y, x, :, second], piece.at[1, lead, zz])

        fold_z(g, lambda zz: grad.at[:, c, zz, y, x], fars[g], line)

    def scatter_f(g):
        grad, line = weights[g][2], weights[g][6]
        if g in BETWEEN:
            first, second = halves(grad)
            fold_f(g + "A", lambda zz: grad.at[:, c, zz, y, :, :, first], mids[g][0].at[0, 0], mids[g][1].at[:, 0])
            fold_f(g + "B", lambda zz: grad.at[:, c, zz, :, x, :, second], mids[g][0].at[1, 0], mids[g][1].at[:, 1])
            return
        fold_f(g, lambda zz: grad.at[:, c, zz, y, x], fars[g], line)

    def scattered(g):
        grad, _, _, piece, line, result = weights[g][2:8]
        if g in BETWEEN:
            landed(g + "r2a", piece.at[0, :, 0])
            landed(g + "r2b", piece.at[1, :, 0])
            across = jnp.concatenate([piece[0, :, 0], piece[1, :, 0]], axis=-1)
            result[...] = grad[:, c, z, y, x].astype(F32) + across.astype(F32)
            return
        fold_sum(g, grad[:, c, z, y, x], line, result)

    left, right = pl.ds(0, 256), pl.ds(256, 256)
    y_slot, x_slot, far_slot = slot(c, 1 - y, x), slot(c, y, 1 - x), slot(c, 1 - y, 1 - x)

    def spread_1(name, full, half):
        own = full.at[me_slot, half]
        landed(name + "h" + str(half), own)
        for which, device in (("y", y_next), ("x", x_next), ("c", core_next)):
            which = which if which == "c" else which + str(half)
            send(name + which, own, own, device)
            sent_later(name + which, own)

    def spread_2(name, full, half):
        for which, place, cols, device in (("y", y_slot, right, x_next), ("x", x_slot, left, y_next)):
            part = full.at[place, half]
            landed(name + which + str(half), part)
            half_of = full.at[place, half, :, cols]
            send(name + "q" + which + str(half), half_of, half_of, device)
            sent_later(name + "q" + which + str(half), half_of)
            send(name + "d", part, part, core_next)
            sent_later(name + "d", part)

    def spread_4(name, full, half):
        part = full.at[far_slot, half]
        landed(name + "qy" + str(half), full.at[far_slot, half, :, right])
        landed(name + "qx" + str(half), full.at[far_slot, half, :, left])
        send(name + "d", part, part, core_next)
        sent_later(name + "d", part)

    def spread_3(name, full):
        landed(name + "c", full.at[0])
        landed(name + "d", full.at[pl.ds(0, 3)])

    def merge_0(name, full, across):
        send(name + "c", full.at[pl.ds((1 - c) * 4, 4)], across, core_next)
        sent_later(name + "c", across)

    def merge_1(name, full, across, parts):
        landed(name + "c", across)
        add(full.at[far_slot], across.at[(1 - y) * 2 + 1 - x])
        send(name + "qx", full.at[far_slot, :, :, left], parts.at[2, :, :, left], y_next)
        send(name + "qy", full.at[far_slot, :, :, right], parts.at[2, :, :, right], x_next)
        sent_later(name + "q", parts.at[2])
        add(full.at[x_slot], across.at[y * 2 + 1 - x])
        add(full.at[y_slot], across.at[(1 - y) * 2 + x])
        add(full.at[me_slot], across.at[yx])

    def merge_3(name, full, parts):
        landed(name + "qx", parts.at[2, :, :, left])
        add(full.at[x_slot, :, :, left], parts.at[2, :, :, left])
        send(name + "px", full.at[x_slot], parts.at[0], x_next)
        sent_later(name + "px", parts.at[0])
        landed(name + "qy", parts.at[2, :, :, right])
        add(full.at[y_slot, :, :, right], parts.at[2, :, :, right])
        send(name + "py", full.at[y_slot], parts.at[1], y_next)
        sent_later(name + "py", parts.at[1])

    def merge_2(name, full, parts):
        landed(name + "px", parts.at[0])
        landed(name + "py", parts.at[1])
        total = full[me_slot].astype(F32)
        for k in range(2):
            total = total + parts[k].astype(F32)
        return total.reshape(here, width)

    def tile(index):
        return pl.ds(pl.multiple_of(index * 128, 128), 128)

    def slice_1(name, shard, full):
        keep(name + "p", shard.at[:, :, tile(yx)], full.at[:, c, z, yx])
        for yy, xx in trio:
            send(name + "p", shard.at[:, :, tile(yy * 2 + xx)], full.at[:, c, z, yx], (c, at(z, yy, xx)))
        sent_later(name + "p", full.at[:, c, z, pl.ds(0, 3)])

    def slice_2(name, full):
        landed(name + "p", full.at[:, c, z])
        along_z(name, full.at[:, c, z], lambda zz: full.at[:, c, zz])

    def slice_f(name, full):
        pass_on(name, lambda zz: full.at[:, c, zz])

    def slice_3(name, full):
        line_landed(name, lambda n: full.at[:, c, pl.ds(0, n)], 0)
        send(name + "c", full.at[:, c], full.at[:, c], core_next)
        sent_later(name + "c", full.at[:, c])

    def slice_4(name, full):
        landed(name + "c", full.at[:, 1 - c])

    def unslice_0(name, grad, across):
        send(name + "c", grad.at[:, 1 - c], across, core_next)
        sent_later(name + "c", across)

    def unslice_1(name, grad, across, line):
        landed(name + "c", across)
        for lead in range(grad.shape[0]):
            add(grad.at[lead, c], across.at[lead])
        fold_z(name, lambda zz: grad.at[:, c, zz], fars[name], line)

    def unslice_f(name, grad, line):
        fold_f(name, lambda zz: grad.at[:, c, zz], fars[name], line)

    def unslice_2(name, grad, line, total, result):
        fold_sum(name, grad[:, c, z], line, total)
        for yy, xx in trio:
            send(name + "p", total.at[:, yy * 2 + xx], result.at[:, :, tile(yx)], (c, at(z, yy, xx)))
        sent_later(name + "p", total.at[:, pl.ds(0, 3)])
        result[:, :, tile(yx)] = total[:, yx]

    def unslice_3(name, result):
        landed(name + "p", result.at[:, :, pl.ds(0, 384)])

    def matrix(ref):
        return ref[...].reshape(-1, ref.shape[-1])

    def put(ref, value):
        ref[...] = value.astype(BF16).reshape(ref.shape)

    def norm(r, i, kept):
        centered = r - jnp.mean(r, axis=1, keepdims=True)
        scale = lax.rsqrt(jnp.mean(centered * centered, axis=1, keepdims=True) + 1e-05)
        xhat = centered * scale
        kept[...] = xhat
        return xhat * gain[i : i + 1, :] + shift[i : i + 1, :], scale

    def column(row, value):
        sg0[row : row + 1, :] = jnp.sum(value, axis=0, keepdims=True)

    def norm_back(grad, i, kept, scale, skip):
        xhat = kept[...]
        column(12 + i, grad * xhat)
        column(15 + i, grad)
        dxhat = grad * gain[i : i + 1, :]
        dr = dxhat - jnp.mean(dxhat, axis=1, keepdims=True)
        dr = (dr - xhat * jnp.mean(dxhat * xhat, axis=1, keepdims=True)) * scale
        column(18 + i, dr * skip)
        return dr, dr * omega[i : i + 1, :]

    BLOCK = 256

    def attend(b, queries, keys, values_t, weights_t, sums, outputs, causal, name, target, arrives):
        extent = 512 if causal and b < 2 else 1024
        cols = slice(b * BLOCK, (b + 1) * BLOCK)
        scores = nn(keys[:extent, :], queries[:, cols])
        seg = rows_f[0:1, cols]
        code = (code_self if causal else code_cross)[:extent, :]
        permit = jnp.concatenate([code, code], axis=1) == seg
        if causal:
            pos = key_pos[:extent, :]
            pos = jnp.concatenate([pos, pos], axis=1)
            mine = rows_f[1:2, cols]
            permit = (permit & (pos <= mine)) | (pos == mine)
        weight = jnp.where(permit, jnp.exp(scores), 0.0)
        total = jnp.sum(weight, axis=0, keepdims=True)
        low = weight.astype(BF16)
        weights_t[:extent, cols] = low
        out = nn(values_t[:, :extent], low) / total
        sums[0:1, cols] = total
        outputs[:, cols] = out
        for k in range(2):
            target[2 * b + k] = out[:, k * here : (k + 1) * here].astype(BF16)
            to_slot(name, target, arrives, 2 * b + k)
        if b == 3:
            sent_later(name, target.at[pl.ds(0, GROUP - 1)])

    def attend_start(buffer, sums, outputs):
        acc_k[...] = jnp.zeros_like(acc_k)
        acc_v[...] = jnp.zeros_like(acc_v)
        for s in range(GROUP):
            cols = slice(s * here, (s + 1) * here)
            grad = buffer[s].astype(F32)
            inverse = 1.0 / sums[0:1, cols]
            dnt[:, cols] = (grad * inverse).astype(BF16)
            rows_f[2:3, cols] = -jnp.sum(grad * outputs[:, cols], axis=0, keepdims=True) * inverse

    def attend_back(b, queries, keys_t, values, weights_t, causal, name, target, arrives):
        extent = 512 if causal and b < 2 else 1024
        cols = slice(b * BLOCK, (b + 1) * BLOCK)
        low = weights_t[:extent, cols]
        dn = dnt[:, cols]
        spread = nn(values[:extent, :], dn)
        slopes = (low.astype(F32) * (spread + rows_f[2:3, cols])).astype(BF16)
        block = (nn(keys_t[:, :extent], slopes) * 0.125).astype(BF16)
        if name is None:
            dt0[0:64, cols] = block
        else:
            for k in range(2):
                target[2 * b + k] = block[:, k * here : (k + 1) * here]
                to_slot(name, target, arrives, 2 * b + k)
            if b == 3:
                sent_later(name, target.at[pl.ds(0, GROUP - 1)])
        acc_k[:, :extent] += nt(queries[:, cols], slopes)
        acc_v[:, :extent] += nt(dn, low)

    def by_head(target, value):
        target[...] = flip(value).astype(BF16).reshape(GROUP, 64, here)

    def heads_weights(first, full):
        for j in range(full.shape[0]):
            wt[first + j] = flip(matrix(full.at[j])).astype(BF16)

    own_rows = pl.ds(pl.multiple_of(c * 64, 64), 64)
    own_head = pl.ds(pl.multiple_of(me_head * 64, 64), 64)

    def own_weights(first, count):
        return jnp.concatenate([wt[first + j, own_rows, :] for j in range(count)], axis=0)

    def wide_bias(i):
        col = bias_cols[i, own_head, :]
        return jnp.concatenate([col, col], axis=1)

    def project_heads(rows, first, queries, keys, keys_t, values, values_t):
        count = 2 if queries is None else 3
        own = own_weights(first, count)
        for b in range(4):
            cols = slice(b * 256, (b + 1) * 256)
            out = nt(own, rows[2 * b : 2 * b + 2].reshape(256, width))
            if queries is not None:
                queries[:, cols] = ((out[0:64] + wide_bias(0)).astype(BF16).astype(F32) * 0.125).astype(BF16)
            at_k = 64 * (count - 2)
            block = out[at_k : at_k + 64].astype(BF16)
            keys_t[:, cols] = block
            keys[cols, :] = flip(block).astype(BF16)
            block = (out[at_k + 64 : at_k + 128] + wide_bias(1 if count == 3 else 2)).astype(BF16)
            values_t[:, cols] = block
            values[cols, :] = flip(block).astype(BF16)

    def rows_back(grads_t, first, target, core):
        count = grads_t.shape[0] // 64
        own = own_weights(first, count)
        for b in range(2):
            cols = pl.ds(pl.multiple_of(core * 512 + b * 256, 256), 256)
            out = tn(grads_t[:, cols], own)
            target[pl.ds(core * 4 + b * 2, 2)] = out.astype(BF16).reshape(2, 2, 64, width)

    def slices_back(grads_t, rows, grad):
        count = grads_t.shape[0] // 64
        out = nn(grads_t[...], rows[...].reshape(1024, width))
        wz[...] = jnp.zeros_like(wz)
        for j in range(count):
            wz[j, own_rows, :] = out[j * 64 : (j + 1) * 64]
            put(grad.at[j], jnp.transpose(wz[j]))

    def bias(i):
        return biases[i : i + 1, :]

    def make_masks():
        landed("marks", all_meta.at[pl.ds(0, 7)])
        order = lax.broadcasted_iota(jnp.int32, (1, 1024), 1)
        place = (order // 512) * 512 + lax.rem(order // 64, 2) * 256 + lax.rem(order // 128, 4) * 64 + lax.rem(order, 64)
        place = place.astype(F32)
        marks = [all_meta[s].astype(F32) for s in range(GROUP)]
        tgt_real = jnp.concatenate([mark[0:1, :] for mark in marks], axis=1)
        src_real = jnp.concatenate([mark[1:2, :] for mark in marks], axis=1)
        lower = lax.broadcasted_iota(jnp.int32, (32, 128), 1)
        later = lax.broadcasted_iota(jnp.int32, (32, 128), 0)

        def ends_of(row):
            lengths = jnp.broadcast_to(row, (32, 128))
            ends = jnp.sum(jnp.where(lower <= later, lengths, 0.0), axis=1, keepdims=True)
            starts = jnp.sum(jnp.where(lower < later, lengths, 0.0), axis=1, keepdims=True)
            return ends, starts

        def count(flags):
            return jnp.sum(jnp.where(flags, 1.0, 0.0), axis=0, keepdims=True)

        tgt_ends, _ = ends_of(marks[0][2:3, :])
        src_ends, src_starts = ends_of(marks[0][3:4, :])
        tgt_seg = count(tgt_ends <= place)
        src_seg = count(src_ends <= place)
        src_first = count(src_starts == place)
        self_row = jnp.where(tgt_real > 0.5, tgt_seg, -1.0)
        cross_row = jnp.where((src_real > 0.5) | (src_first > 0.5), src_seg, -1.0)
        rows_f[0:1, :] = tgt_seg
        rows_f[1:2, :] = place
        code_self[...] = jnp.transpose(jnp.broadcast_to(self_row, (128, 1024)))
        code_cross[...] = jnp.transpose(jnp.broadcast_to(cross_row, (128, 1024)))
        key_pos[...] = jnp.transpose(jnp.broadcast_to(place, (128, 1024)))

    def feed_up(rows, i):
        for k in (2 * i, 2 * i + 1):
            cols = slice(k * width, (k + 1) * width)
            inner = slice((k % 2) * width, (k % 2 + 1) * width)
            u = nn(rows, matrix(w_up.at[i, :, :, :, :, :, inner])) + up_bias[0:1, cols]
            square = u * u
            t = jnp.tanh(u * (0.7978845608028654 + 0.035677408136300125 * square))
            act[:, cols] = (0.5 * u * (1.0 + t)).astype(BF16)
            inner = 0.7978845608028654 + 0.10703222440890037 * square
            slope[:, cols] = 0.5 * (1.0 + t) + 0.5 * u * (1.0 - t * t) * inner

    def feed_back(gf, back):
        for k in range(4):
            cols = slice(k * width, (k + 1) * width)
            inner = slice((k % 2) * width, (k % 2 + 1) * width)
            rows = pl.ds(2 * (k % 2), 2)
            gu = nt(gf[:, 0:256], matrix(w_dn.at[0, k // 2, rows]))
            gu = gu + nt(gf[:, 256:512], matrix(w_dn.at[1, k // 2, rows]))
            gu = (gu * slope[:, cols]).astype(BF16)
            gul[:, cols] = gu
            column(8 + k, gu.astype(F32))
            back = back + nt(gu, matrix(w_up.at[k // 2, :, :, :, :, :, inner]))
        return back

    def value_sums(grads_t):
        total = jnp.sum(grads_t[64:128, :].astype(F32), axis=1, keepdims=True)
        bias_cols[0] = jnp.zeros((width, 128), F32)
        bias_cols[0, own_head, :] = jnp.broadcast_to(total, (64, 128))
        sg0[4:5, :] = jnp.transpose(bias_cols[0])[0:1, :]

    def head_sums(grads_t):
        lanes = lax.broadcasted_iota(jnp.int32, (64, 128), 1)
        dq_sum = jnp.sum(grads_t[0:64, :].astype(F32), axis=1, keepdims=True)
        dv_sum = jnp.sum(grads_t[128:192, :].astype(F32), axis=1, keepdims=True)
        bias_cols[0] = jnp.zeros((width, 128), F32)
        bias_cols[0, own_head, :] = jnp.where(lanes == 0, dq_sum, dv_sum)
        tg0[...] = jnp.transpose(bias_cols[0])[0:8, :]

    def small(name, src, dst, device):
        send(name, src, dst, device)
        sent_later(name, dst)

    def small_add(name, arrived, mine, total):
        landed(name, arrived)
        total[...] = mine[...] + arrived[...]

    def small_z(name, src, rows, tile_at, dst):
        for k, zz in enumerate(z_peers):
            send(name, src.at[rows, tile(tile_at(zz))], dst.at[2 - k], (c, at(zz, y, x)))
        sent_later(name, dst)

    def tile_own(zz):
        return c * 2 + zz // 2

    def tile_up(zz):
        return lax.rem(zz, 2) * 2 + y

    def small_sum(name, src, rows, tile_at, dst):
        landed(name, dst)
        return src[rows, tile(tile_at(z))] + dst[0] + dst[1] + dst[2]

    def small_out():
        block = c * 16 + seq
        shift_by = lax.rem(128 - lax.rem(block, 8) * 16, 128)
        turned = pltpu.roll(small_sum("sa", sg3, slice(None), tile_own, sra), shift_by, 1)
        o_bias[...] = turned[0:7, 0:16]
        o_gain[...] = turned[12:15, 0:16]
        o_shift[...] = turned[15:18, 0:16]
        o_omega[...] = turned[18:21, 0:16]
        turned = pltpu.roll(small_sum("ta", tg3, slice(None), tile_own, tra), shift_by, 1)
        o_bias[0:2, :] = turned[0:2, 0:16]
        turned = pltpu.roll(small_sum("sb", sg3, pl.ds(8, 8), tile_up, srb), lax.rem(block, 2) * 64, 1)
        wanted = block // 8
        row = jnp.zeros((1, 64), F32)
        for k in range(4):
            row = row + turned[k : k + 1, 0:64] * (wanted == k).astype(F32)
        o_upb[...] = row
        ends = ((o_bias, h_bias), (o_upb, h_upb), (o_gain, h_gain_o), (o_shift, h_shift_o), (o_omega, h_omega_o))
        for i, (src, dst) in enumerate(ends):
            keep("e" + str(4 + i), src, dst)

    raw = ((raw_tm, tgt_msk), (raw_sm, src_msk), (raw_tl, tgt_len), (raw_sl, src_len))
    for i, (ref, given) in enumerate(raw):
        keep("raw" + str(i), given, ref)
    given = ((h_biases, biases), (h_up_bias, up_bias), (h_gain, gain), (h_shift, shift), (h_omega, omega))
    for i, (src, ref) in enumerate(given):
        keep("given" + str(i), src, ref)
    barrier = pltpu.get_barrier_semaphore()
    greet = [(cc, at(z, yy, xx)) for cc, yy, xx in plane_peers]
    greet += [(cc, at(zz, y, x)) for zz in z_peers for cc in (c, 1 - c)]
    for device in greet:
        pl.semaphore_signal(barrier, inc=1, device_id=device, device_id_type=MESH)
    pl.semaphore_wait(barrier, len(greet))
    to_plane("x", tok, all_tok, True)
    gather_z("out0")
    gather_z("dn0")
    gather_z("dn1")
    for i, (_, ref) in enumerate(given):
        landed("given" + str(i), ref)
    for i, (ref, _) in enumerate(raw):
        landed("raw" + str(i), ref)
        span = ref.shape[2]
        for m in range(2):
            for start in (0, 64):
                meta[m, i : i + 1, start : start + span] = ref[m]
    gather_z("up0")
    to_plane("meta", meta, in_meta)
    slice_1("w0", s_in.at[0], ws0)
    spread_1("x", all_tok, 0)
    spread_1("x", all_tok, 1)
    slice_1("w1", s_in.at[1, pl.ds(1, 2)], ws1)
    to_plane("m", mem, all_mem, True)
    gather_f("out0")
    spread_2("x", all_tok, 0)
    gather_f("up0")
    gather_z("up1")
    spread_2("x", all_tok, 1)
    slice_2("w0", ws0)
    gather_z("q")
    gather_1("out0")
    spread_4("x", all_tok, 0)
    landed("meta", in_meta)
    lane = lax.broadcasted_iota(jnp.int32, (8, 128), 1)
    all_meta[me_slot] = jnp.where(lane < 64, in_meta[0], in_meta[1])
    for cc, yy, xx in plane_peers:
        send("marks", all_meta.at[me_slot], all_meta.at[me_slot], (cc, at(z, yy, xx)))
    gather_1("up0")
    sent_later("marks", all_meta.at[pl.ds(0, 7)])
    spread_1("m", all_mem, 0)
    slice_2("w1", ws1)
    gather_2("out0")
    gather_2("up0")
    gather_f("up1")
    spread_4("x", all_tok, 1)
    slice_f("w0", ws0)
    gather_z("out1")
    gather_1("up1")
    gather_3("out0")
    spread_1("m", all_mem, 1)
    make_masks()
    gather_f("q")
    for i, row in enumerate((0, 1, 4)):
        bias_cols[i] = jnp.transpose(jnp.broadcast_to(bias(row), (128, width)))
    spread_2("m", all_mem, 0)
    slice_3("w0", ws0)
    gather_1("dn1")
    spread_3("x", all_tok)
    slice_4("w0", ws0)
    gather_3("up0")
    gather_1("q")
    gather_2("up1")
    heads_weights(0, ws0)
    project_heads(all_tok, 0, qt0, k0, kt0, v0, vt0)
    attend(0, qt0, k0, vt0, pt0, l0, ot0, True, "x3", a3, b3)
    spread_2("m", all_mem, 1)
    gather_2("q")
    attend(1, qt0, k0, vt0, pt0, l0, ot0, True, "x3", a3, b3)
    gather_f("out1")
    gather_f("dn1")
    spread_4("m", all_mem, 0)
    gather_1("dn0")
    slice_f("w1", ws1)
    gather_1("out1")
    attend(2, qt0, k0, vt0, pt0, l0, ot0, True, "x3", a3, b3)
    gathered("out0")
    attend(3, qt0, k0, vt0, pt0, l0, ot0, True, "x3", a3, b3)
    spread_4("m", all_mem, 1)
    gather_2("dn1")
    gather_3("q")
    gather_2("out1")
    slice_3("w1", ws1)
    gathered("q")
    landed("x3", b3)
    words_f = all_tok[me_slot].reshape(here, width).astype(F32)
    gather_3("up1")
    gather_f("dn0")
    branch = tn(b3[...].reshape(width, here), matrix(w_out.at[0])) + bias(2)
    h1, scale0 = norm(words_f * omega[0:1, :] + branch, 0, xh0)
    h1_f[...] = h1
    h1_low = h1.astype(BF16)
    spread_3("m", all_mem)
    by_head(a4, nn(h1_low, matrix(w_q.at[0])) + bias(3))
    to_heads("x4", a4, b4)
    slice_4("w1", ws1)
    gather_2("dn0")
    gather_3("out1")
    heads_weights(3, ws1)
    to_plane("cot", cot, in_cot)
    gather_3("dn1")
    project_heads(all_mem, 3, None, k1, kt1, v1, vt1)
    landed("x4", b4)
    for s in range(GROUP):
        qt1[:, s * here : (s + 1) * here] = (b4[s].astype(F32) * 0.125).astype(BF16)
    attend(0, qt1, k1, vt1, pt1, l1, ot1, False, "x5", a5, b5)
    attend(1, qt1, k1, vt1, pt1, l1, ot1, False, "x5", a5, b5)
    attend(2, qt1, k1, vt1, pt1, l1, ot1, False, "x5", a5, b5)
    attend(3, qt1, k1, vt1, pt1, l1, ot1, False, "x5", a5, b5)
    gathered("out1")
    gathered("up1")
    gathered("dn1")
    gathered("up0")
    gather_3("dn0")
    gathered("dn0")
    landed("x5", b5)
    branch = tn(b5[...].reshape(width, here), matrix(w_out.at[1])) + bias(5)
    h2, scale1 = norm(h1_f[...] * omega[1:2, :] + branch, 1, xh1)
    h2_f[...] = h2
    h2_low = h2.astype(BF16)
    feed_up(h2_low, 0)
    feed_up(h2_low, 1)
    first = nn(act[...], matrix(w_dn.at[0]))
    second = nn(act[...], matrix(w_dn.at[1]))
    h3, scale2 = norm(h2_f[...] * omega[2:3, :] + jnp.concatenate([first, second], axis=1) + bias(6), 2, xh2)
    out_res[...] = h3.astype(BF16).reshape(2, 64, width)
    landed("cot", in_cot)
    grad = in_cot[...].reshape(here, width).astype(F32)
    dr, skip = norm_back(grad, 2, xh2, scale2, h2_f[...])
    gf = dr.astype(BF16)
    column(6, gf.astype(F32))
    put(g_dn.at[0], tn(act[...], gf[:, 0:256]))
    back = feed_back(gf, skip)
    scatter_0("dn0")
    dr, skip = norm_back(back, 1, xh1, scale1, h1_f[...])
    gc = dr.astype(BF16)
    column(5, gc.astype(F32))
    by_head(a6, nt(gc, matrix(w_out.at[1])))
    to_heads("x6", a6, b6)
    put(g_up.at[0], tn(h2_low, gul[:, 0:1024]))
    scatter_1("dn0")
    scatter_0("up0")
    put(g_up.at[1], tn(h2_low, gul[:, 1024:2048]))
    scatter_1("up0")
    back = skip
    scatter_0("up1")
    landed("x6", b6)
    attend_start(b6, l1, ot1)
    attend_back(0, qt1, kt1, v1, pt1, False, "x7", a7, b7)
    from_plane("res", out_res, o_res)
    put(g_out.at[1], nn(b5[...].reshape(width, here), gc))
    attend_back(1, qt1, kt1, v1, pt1, False, "x7", a7, b7)
    attend_back(2, qt1, kt1, v1, pt1, False, "x7", a7, b7)
    attend_back(3, qt1, kt1, v1, pt1, False, "x7", a7, b7)
    dt1[0:64, :] = acc_k[...].astype(BF16)
    dt1[64:128, :] = acc_v[...].astype(BF16)
    scatter_1("up1")
    put(g_dn.at[1], tn(act[...], gf[:, 256:512]))
    scatter_0("dn1")
    scatter_2("dn0")
    rows_back(dt1, 3, dx1, 1 - c)
    scatter_2("up0")
    merge_0("dm", dx1, dc1)
    rows_back(dt1, 3, dx1, c)
    slices_back(dt1, all_mem, gs1)
    value_sums(dt1)
    landed("x7", b7)
    dq = b7[...].reshape(width, here)
    unslice_0("u1", gs1, cs1)
    dq_row = flip(dq)
    column(3, dq_row)
    back = back + nt(dq_row.astype(BF16), matrix(w_q.at[0]))
    dr, skip = norm_back(back, 0, xh0, scale0, words_f)
    ga = dr.astype(BF16)
    column(2, ga.astype(F32))
    by_head(a8, nt(ga, matrix(w_out.at[0])))
    to_heads("x8", a8, b8)
    put(g_out.at[0], nn(b3[...].reshape(width, here), ga))
    scatter_1("dn1")
    put(g_q.at[0], nt(flip(h1_low).astype(BF16), dq))
    last = skip
    unslice_1("u1", gs1, cs1, zs1)
    scatter_0("out1")
    scatter_1("out1")
    scatter_3("up0")
    scatter_2("up1")
    scatter_0("q")
    small("s0", sg0, sr0, core_next)
    scatter_0("out0")
    landed("x8", b8)
    attend_start(b8, l0, ot0)
    attend_back(0, qt0, kt0, v0, pt0, True, None, None, None)
    scatter_f("dn0")
    attend_back(1, qt0, kt0, v0, pt0, True, None, None, None)
    small_add("s0", sr0, sg0, sg1)
    scatter_2("dn1")
    scatter_1("q")
    attend_back(2, qt0, kt0, v0, pt0, True, None, None, None)
    attend_back(3, qt0, kt0, v0, pt0, True, None, None, None)
    scatter_2("out1")
    merge_1("dm", dx1, dc1, dp1)
    scatter_3("up1")
    dt0[64:128, :] = acc_k[...].astype(BF16)
    dt0[128:192, :] = acc_v[...].astype(BF16)
    scatter_f("up0")
    slices_back(dt0, all_tok, gs0)
    scatter_1("out0")
    unslice_0("u0", gs0, cs0)
    head_sums(dt0)
    scatter_3("out1")
    scatter_2("q")
    unslice_1("u0", gs0, cs0, zs0)
    small("t0", tg0, tr0, core_next)
    small("s1", sg1, sr1, y_next)
    rows_back(dt0, 0, dx0, 1 - c)
    small_add("t0", tr0, tg0, tg1)
    small("t1", tg1, tr1, y_next)
    merge_0("dx", dx0, dc0)
    rows_back(dt0, 0, dx0, c)
    merge_3("dm", dx1, dp1)
    scatter_f("dn1")
    unslice_f("u1", gs1, zs1)
    merge_1("dx", dx0, dc0, dp0)
    scatter_f("out1")
    small_add("t1", tr1, tg1, tg2)
    small("t2", tg2, tr2, x_next)
    scatter_3("q")
    scatter_f("up1")
    small_add("s1", sr1, sg1, sg2)
    small("s2", sg2, sr2, x_next)
    landed("res", o_res)
    unslice_f("u0", gs0, zs0)
    scatter_2("out0")
    scatter_3("dn1")
    scatter_f("q")
    out_mem[...] = merge_2("dm", dx1, dp1).astype(BF16).reshape(2, 64, width)
    from_plane("gmem", out_mem, o_mem)
    small_add("t2", tr2, tg2, tg3)
    merge_3("dx", dx0, dp0)
    small_add("s2", sr2, sg2, sg3)
    scattered("up0")
    scatter_3("out0")
    small_z("sa", sg3, slice(None), tile_own, sra)
    small_z("sb", sg3, pl.ds(8, 8), tile_up, srb)
    unslice_2("u0", gs0, zs0, fs0, o_in.at[0])
    unslice_2("u1", gs1, zs1, fs1, o_in.at[1, pl.ds(1, 2)])
    small_z("ta", tg3, slice(None), tile_own, tra)
    scattered("up1")
    scattered("out1")
    scattered("dn1")
    scatter_3("dn0")
    scatter_f("out0")
    out_tok[...] = (merge_2("dx", dx0, dp0) + last).astype(BF16).reshape(2, 64, width)
    from_plane("gtok", out_tok, o_tok)
    unslice_3("u1", o_in.at[1, pl.ds(1, 2)])
    unslice_3("u0", o_in.at[0])
    scattered("q")
    landed("gmem", o_mem)
    scattered("dn0")
    keep("e3", o_dn, h_dn)
    small_out()
    keep("e2", o_up, h_up)
    scattered("out0")
    keep("e1", o_out, h_out)
    keep("e0", o_in, h_in)
    landed("gtok", o_tok)
    for i, ref in enumerate((h_in, h_out, h_up, h_dn, h_bias, h_upb, h_gain_o, h_shift_o, h_omega_o)):
        landed("e" + str(i), ref)
    for semaphore, ref, when in pending:
        if when is None:
            wait(semaphore, ref)
        else:

            @pl.when(when)
            def _():
                wait(semaphore, ref)

    for i, total in enumerate(bins):
        if total:
            wait(ss.at[i], gauge.at[pl.ds(0, total // 1024)])
    spans = [2 * line_bytes[0] + 3 * fold_bytes[0], 4 * line_bytes[0] + 3 * fold_bytes[0]]
    assert spans[0] % UNIT == 0 and spans[1] % UNIT == 0

    @pl.when(edge)
    def _():
        wait(ss.at[BINS], gauge.at[pl.ds(0, spans[0] // 1024)])

    @pl.when(jnp.logical_not(edge))
    def _():
        wait(ss.at[BINS], gauge.at[pl.ds(0, spans[1] // 1024)])

    assert len(names) <= NAMES and len(bins) <= BINS and BINS + 1 + len(odd) <= ss.shape[0]


def copy_kernel(*refs):
    count = len(refs) // 2
    for i in range(count):
        refs[count + i][...] = refs[i][...]


def fused_local(
    tokens, memory, cotangent, tgt_lengths, src_lengths, tgt_mask, src_mask, attn_in, attn_out, w_up, w_down,
    biases, up_bias, norm_gain, norm_shift, omega,
):
    any_space = pl.BlockSpec(memory_space=pl.ANY)
    vmem = pl.BlockSpec(memory_space=pltpu.VMEM)
    lines = (CORES, PLANES, YS, XS)
    leads = {"q": 1, "out": 2, "up": 2, "dn": 2}
    shards = {"q": (16, 512), "out": (16, 512), "up": (16, 1024), "dn": (64, 256)}
    kinds = tuple(leads)

    def low(*shape):
        return pltpu.VMEM(shape, BF16)

    def full(*shape):
        return pltpu.VMEM(shape, F32)

    def whole(k):
        return low(leads[k], *lines, *shards[k])

    def halved(k, *middle):
        return low(2, leads[k], *middle, shards[k][0], shards[k][1] // 2)

    params = [full(7, 512), full(1, 2048), full(3, 512), full(3, 512), full(3, 512)]
    results = [(2, 3, 16, 512), (2, 16, 512), (1, 16, 2048), (1, 64, 512), (7, 16), (1, 64), (3, 16), (3, 16), (3, 16)]
    scratch = params + [full(*shape) for shape in results]
    scratch += [whole(k) for k in kinds] * 2
    scratch += [low(leads[k], *lines[1:], *shards[k]) for k in kinds]
    scratch += [halved(k, PLANES, 2) for k in kinds] + [halved(k, PLANES) for k in kinds]
    scratch += [low(3, leads[k], *shards[k]) for k in kinds]
    scratch += [low(n, CORES, PLANES, 4, 16, 128) for n in (3, 2)] * 2
    scratch += [low(n, PLANES, 4, 16, 128) for n in (3, 2)] + [low(3, n, 4, 16, 128) for n in (3, 2)]
    scratch += [full(n, 4, 16, 128) for n in (3, 2)]
    local_rows = low(2, 64, 512)
    marks = [pltpu.VMEM((2, 1, n), jnp.int32) for n in (32, 32, 64, 64)] + [pltpu.VMEM((2, 8, 128), jnp.int32)] * 2
    scratch += [low(GROUP, 2, 64, 512)] * 2 + [local_rows] + marks + [pltpu.VMEM((GROUP, 8, 128), jnp.int32)]
    scratch += [low(GROUP, 2, 64, 512)] * 2 + [low(4, 2, 64, 512)] * 2 + [low(3, 2, 64, 512)] * 2
    scratch += [low(GROUP, 64, 128)] * 12 + [local_rows] * 3
    scratch += [full(24, 512)] * 7 + [full(3, 24, 128), full(3, 8, 128)]
    scratch += [full(8, 512)] * 7 + [full(3, 8, 128)]
    scratch += [full(1024, 128)] * 3 + [full(8, 1024)]
    scratch += ([low(64, 1024)] * 3 + [low(1024, 64)] * 2 + [low(1024, 1024), full(1, 1024), full(64, 1024)]) * 2
    scratch += [low(64, 1024)] + [full(64, 1024)] * 2
    scratch += [low(128, 2048), full(128, 2048), low(128, 2048)] + [full(128, 512)] * 5
    scratch += [low(5, 128, 512), full(3, 512, 128), full(3, 128, 512), low(192, 1024), low(128, 1024), low(2304, 512)]
    scratch += [low(leads[k], *shards[k]) for k in kinds] + [low(n, 4, 16, 128) for n in (3, 2)]
    scratch += [low(2, 2, 1, 1, 2, 64, 128), low(2, 3, 2, 1, 2, 64, 128)]
    scratch += [pltpu.SemaphoreType.DMA((44,)), pltpu.SemaphoreType.DMA((NAMES,))]
    rows = jax.ShapeDtypeStruct((2, 64, 512), BF16)

    def wide_out(*shape):
        return jax.ShapeDtypeStruct(shape, F32)

    outs = pl.pallas_call(
        fused_kernel,
        name="layer",
        out_shape=(rows, rows, rows, *(wide_out(*shape) for shape in results)),
        in_specs=[any_space] * 16,
        out_specs=(any_space,) * 12,
        scratch_shapes=scratch,
        compiler_params=pltpu.CompilerParams(collective_id=0, has_side_effects=True, vmem_limit_bytes=60 * 1024 * 1024),
    )(
        tokens.reshape(2, 64, 512), memory.reshape(2, 64, 512), cotangent.reshape(2, 64, 512),
        tgt_lengths, src_lengths, jnp.transpose(tgt_mask, (0, 2, 1)), jnp.transpose(src_mask, (0, 2, 1)),
        attn_in, attn_out, w_up.reshape(1, 16, 2048), w_down.reshape(1, 64, 512),
        biases, up_bias.reshape(1, 2048), norm_gain, norm_shift, omega,
    )
    outs = pl.pallas_call(
        copy_kernel,
        name="hand_over",
        out_shape=tuple(jax.ShapeDtypeStruct(out.shape, out.dtype) for out in outs),
        in_specs=[vmem] * len(outs),
        out_specs=(vmem,) * len(outs),
    )(*outs)
    shaped = [out.reshape(2, 64, 1, 512) for out in outs[:3]]
    return (
        *shaped, outs[3], outs[4], outs[5].reshape(16, 2048), outs[6].reshape(64, 512), outs[7], outs[8].reshape(64),
        outs[9], outs[10], outs[11],
    )


def solution(mesh):
    if mesh.shape["seq"] != PLANES * YS * XS or mesh.shape["rows"] != CORES:
        return general(mesh)
    return over(mesh, fused_local)
```

```python
import functools
import math

import jax
import jax.numpy as jnp
from jax import lax
from jax.experimental import pallas as pl
from jax.experimental.pallas import tpu as pltpu
from jax.sharding import PartitionSpec as P

HEADS = 8


def norm_block(branch, skip, scale, gain, shift):
    mixed = skip * scale + branch
    centered = mixed - jnp.mean(mixed, axis=-1, keepdims=True)
    variance = jnp.mean(centered * centered, axis=-1, keepdims=True)
    return centered * lax.rsqrt(variance + 1e-05) * gain + shift


def project(values, matrix):
    return jnp.einsum("trd,de->tre", values, matrix, preferred_element_type=jnp.float32)


def project_back(grads, matrix):
    return jnp.einsum("tre,de->trd", grads, matrix, preferred_element_type=jnp.float32)


def matrix_grad(values, grads):
    return jnp.einsum("trd,tre->de", values, grads, preferred_element_type=jnp.float32)


def column_sum(grads):
    return jnp.sum(grads.astype(jnp.float32), axis=(0, 1))


def segment_of(positions, ends):
    return jnp.sum((ends[None, :, :] <= positions[:, None, None]).astype(jnp.int32), axis=-1)


def segment_bounds(first, last, ends):
    lowest = jnp.sum((ends <= first).astype(jnp.int32), axis=-1)
    highest = jnp.sum((ends <= last).astype(jnp.int32), axis=-1)
    return (lowest, highest)


def ranges_share(query_bounds, key_bounds):
    return jnp.any((key_bounds[0] <= query_bounds[1]) & (key_bounds[1] >= query_bounds[0]))


def key_status(positions, real_marks, ends, starts, causal):
    segments = segment_of(positions, ends)
    usable = real_marks > 0.5
    if not causal:
        usable = usable | jnp.any(starts[None, :, :] == positions[:, None, None], axis=-1)
    return (segments, usable)


def permitted(query_pos, query_seg, key_pos, key_seg, usable, causal):
    same = jnp.transpose(query_seg)[:, :, None] == jnp.transpose(key_seg)[:, None, :]
    usable_keys = jnp.transpose(usable)[:, None, :]
    if causal:
        before = (key_pos[None, :] <= query_pos[:, None])[None]
        itself = (key_pos[None, :] == query_pos[:, None])[None]
        return same & before & (usable_keys | itself)
    return same & usable_keys


def block_grads(query_heads, grad_heads, lambdas, key_heads, value_heads, permit):
    scores = (
        jnp.einsum("arhd,brhd->rhab", query_heads, key_heads, preferred_element_type=jnp.float32)
        * 0.125
    )
    weights = jnp.where(permit[:, None], jnp.exp(scores), 0.0)
    spread = jnp.einsum(
        "arhd,brhd->rhab", grad_heads, value_heads, preferred_element_type=jnp.float32
    )
    slopes = weights * (spread + jnp.transpose(lambdas, (1, 2, 0))[..., None])
    return (weights.astype(jnp.bfloat16), slopes.astype(jnp.bfloat16))


def local(
    tokens,
    memory,
    cotangent,
    tgt_lengths,
    src_lengths,
    tgt_mask,
    src_mask,
    attn_in,
    attn_out,
    w_up,
    w_down,
    biases,
    up_bias,
    norm_gain,
    norm_shift,
    omega,
):
    micro_count, tokens_here, rows_here, width = tokens.shape
    head_size = width // HEADS
    my_pos = lax.axis_index("seq") * tokens_here + jnp.arange(tokens_here, dtype=jnp.int32)
    my_first = my_pos[0]
    my_last = my_pos[tokens_here - 1]

    def split_heads(values):
        return values.reshape(values.shape[0], rows_here, HEADS, head_size)

    def zero_heads():
        return jnp.zeros((tokens_here, rows_here, HEADS, head_size), jnp.float32)

    results = []
    grads_words = []
    grads_sources = []
    shares_all = None
    for micro_index in range(micro_count):
        in_weights = lax.all_gather(attn_in, ("rows", "seq"), axis=2, tiled=True)
        out_weights = lax.all_gather(attn_out, ("rows", "seq"), axis=1, tiled=True)
        up_weights = lax.all_gather(w_up, ("rows", "seq"), axis=0, tiled=True)
        down_weights = lax.all_gather(w_down, ("rows", "seq"), axis=0, tiled=True)
        words = tokens[micro_index]
        sources = memory[micro_index]
        words_full = words.astype(jnp.float32)
        tgt_len = tgt_lengths[micro_index]
        src_len = src_lengths[micro_index]
        tgt_ends = jnp.cumsum(tgt_len, axis=-1)
        src_ends = jnp.cumsum(src_len, axis=-1)
        src_starts = src_ends - src_len
        query_seg = segment_of(my_pos, tgt_ends)
        query_bounds = segment_bounds(my_first, my_last, tgt_ends)
        tgt_real = tgt_mask[micro_index].astype(jnp.bfloat16)
        src_real = src_mask[micro_index].astype(jnp.bfloat16)

        def attend(queries, keys, values, real_marks, ends, starts, causal):
            full_keys, full_values, full_real = (
                lax.all_gather(keys, "seq", axis=0, tiled=True),
                lax.all_gather(values, "seq", axis=0, tiled=True),
                lax.all_gather(real_marks, "seq", axis=0, tiled=True),
            )
            length = full_keys.shape[0]
            block = math.gcd(length, 512)
            query_heads = split_heads(queries)

            def step(carry, block_index):
                begin = block_index * block
                shares = ranges_share(query_bounds, segment_bounds(begin, begin + block - 1, ends))

                def step_compute(state):
                    totals, accum = state
                    key_heads = split_heads(lax.dynamic_slice_in_dim(full_keys, begin, block, 0))
                    value_heads = split_heads(
                        lax.dynamic_slice_in_dim(full_values, begin, block, 0)
                    )
                    key_pos = begin + jnp.arange(block, dtype=jnp.int32)
                    key_seg, usable = key_status(
                        key_pos,
                        lax.dynamic_slice_in_dim(full_real, begin, block, 0),
                        ends,
                        starts,
                        causal,
                    )
                    permit = permitted(my_pos, query_seg, key_pos, key_seg, usable, causal)
                    scores = (
                        jnp.einsum(
                            "trhd,krhd->rhtk",
                            query_heads,
                            key_heads,
                            preferred_element_type=jnp.float32,
                        )
                        * 0.125
                    )
                    weights = jnp.where(permit[:, None], jnp.exp(scores), 0.0)
                    totals = totals + jnp.sum(weights, axis=-1)
                    accum = accum + jnp.einsum(
                        "rhtk,krhd->trhd",
                        weights.astype(jnp.bfloat16),
                        value_heads,
                        preferred_element_type=jnp.float32,
                    )
                    return (totals, accum)

                return (lax.cond(shares, step_compute, lambda unchanged: unchanged, carry), None)

            start_carry = (jnp.zeros((rows_here, HEADS, tokens_here), jnp.float32), zero_heads())
            (totals, accum), unused = lax.scan(
                step, start_carry, jnp.arange(length // block, dtype=jnp.int32)
            )
            sums = jnp.transpose(totals, (2, 0, 1))
            output = (accum / sums[..., None]).reshape(tokens_here, rows_here, width)
            return (output, sums, (full_keys, full_values, full_real))

        def attention_back(
            grad_out,
            output,
            sums,
            queries,
            keys,
            values,
            real_marks,
            gathered_set,
            ends,
            starts,
            causal,
        ):
            full_keys, full_values, full_real = gathered_set
            grad_heads = split_heads(grad_out)
            lambdas = -jnp.sum(grad_heads * split_heads(output), axis=-1) / sums
            scaled = (grad_heads / sums[..., None]).astype(jnp.bfloat16)
            query_heads = split_heads(queries)
            length = full_keys.shape[0]
            block = math.gcd(length, 512)

            def query_step(accum, block_index):
                begin = block_index * block
                shares = ranges_share(query_bounds, segment_bounds(begin, begin + block - 1, ends))

                def query_compute(state):
                    key_heads = split_heads(lax.dynamic_slice_in_dim(full_keys, begin, block, 0))
                    value_heads = split_heads(
                        lax.dynamic_slice_in_dim(full_values, begin, block, 0)
                    )
                    key_pos = begin + jnp.arange(block, dtype=jnp.int32)
                    key_seg, usable = key_status(
                        key_pos,
                        lax.dynamic_slice_in_dim(full_real, begin, block, 0),
                        ends,
                        starts,
                        causal,
                    )
                    permit = permitted(my_pos, query_seg, key_pos, key_seg, usable, causal)
                    weights, slopes = block_grads(
                        query_heads, scaled, lambdas, key_heads, value_heads, permit
                    )
                    return (
                        state
                        + jnp.einsum(
                            "rhab,brhd->arhd", slopes, key_heads, preferred_element_type=jnp.float32
                        )
                        * 0.125
                    )

                return (lax.cond(shares, query_compute, lambda unchanged: unchanged, accum), None)

            grad_query, unused = lax.scan(
                query_step, zero_heads(), jnp.arange(length // block, dtype=jnp.int32)
            )
            all_lambdas = lax.all_gather(lambdas, "seq", axis=0, tiled=True)
            local_seg, local_usable = key_status(my_pos, real_marks, ends, starts, causal)
            local_bounds = segment_bounds(my_first, my_last, ends)
            local_keys = split_heads(keys)
            local_values = split_heads(values)
            query_piece = lax.all_gather(queries, "seq", axis=0, tiled=True)
            scaled_piece = lax.all_gather(
                scaled.reshape(tokens_here, rows_here, width), "seq", axis=0, tiled=True
            )
            size = query_piece.shape[0]
            inner = math.gcd(size, 512)

            def inner_step(inner_carry, inner_index):
                offset = inner_index * inner
                piece_first = offset
                shares = ranges_share(
                    segment_bounds(piece_first, piece_first + inner - 1, tgt_ends), local_bounds
                )

                def inner_compute(state):
                    acc_key, acc_value = state
                    query_blk = split_heads(lax.dynamic_slice_in_dim(query_piece, offset, inner, 0))
                    scaled_blk = split_heads(
                        lax.dynamic_slice_in_dim(scaled_piece, offset, inner, 0)
                    )
                    lambda_blk = lax.dynamic_slice_in_dim(all_lambdas, piece_first, inner, 0)
                    query_pos = piece_first + jnp.arange(inner, dtype=jnp.int32)
                    permit = permitted(
                        query_pos,
                        segment_of(query_pos, tgt_ends),
                        my_pos,
                        local_seg,
                        local_usable,
                        causal,
                    )
                    weights, slopes = block_grads(
                        query_blk, scaled_blk, lambda_blk, local_keys, local_values, permit
                    )
                    acc_key = (
                        acc_key
                        + jnp.einsum(
                            "rhab,arhd->brhd", slopes, query_blk, preferred_element_type=jnp.float32
                        )
                        * 0.125
                    )
                    acc_value = acc_value + jnp.einsum(
                        "rhab,arhd->brhd", weights, scaled_blk, preferred_element_type=jnp.float32
                    )
                    return (acc_key, acc_value)

                return (
                    lax.cond(shares, inner_compute, lambda unchanged: unchanged, inner_carry),
                    None,
                )

            folded, unused_inner = lax.scan(
                inner_step, (zero_heads(), zero_heads()), jnp.arange(size // inner, dtype=jnp.int32)
            )
            grad_key, grad_value = folded
            grad_key = grad_key.reshape(tokens_here, rows_here, width)
            grad_value = grad_value.reshape(tokens_here, rows_here, width)
            return (grad_query.reshape(tokens_here, rows_here, width), grad_key, grad_value)

        self_query = (project(words, in_weights[0, 0]) + biases[0]).astype(jnp.bfloat16)
        self_key = project(words, in_weights[0, 1]).astype(jnp.bfloat16)
        self_value = (project(words, in_weights[0, 2]) + biases[1]).astype(jnp.bfloat16)
        heard, heard_sums, self_set = attend(
            self_query, self_key, self_value, tgt_real, tgt_ends, None, True
        )
        heard_low = heard.astype(jnp.bfloat16)
        branch_self = project(heard_low, out_weights[0]) + biases[2]
        hidden_one, pull_one = jax.vjp(
            norm_block, branch_self, words_full, omega[0], norm_gain[0], norm_shift[0]
        )
        hidden_one_low = hidden_one.astype(jnp.bfloat16)
        cross_query = (project(hidden_one_low, in_weights[1, 0]) + biases[3]).astype(jnp.bfloat16)
        cross_key = project(sources, in_weights[1, 1]).astype(jnp.bfloat16)
        cross_value = (project(sources, in_weights[1, 2]) + biases[4]).astype(jnp.bfloat16)
        recalled, recalled_sums, cross_set = attend(
            cross_query, cross_key, cross_value, src_real, src_ends, src_starts, False
        )
        recalled_low = recalled.astype(jnp.bfloat16)
        branch_cross = project(recalled_low, out_weights[1]) + biases[5]
        hidden_two, pull_two = jax.vjp(
            norm_block, branch_cross, hidden_one, omega[1], norm_gain[1], norm_shift[1]
        )
        hidden_two_low = hidden_two.astype(jnp.bfloat16)
        up_pre = project(hidden_two_low, up_weights) + up_bias
        active, pull_active = jax.vjp(jax.nn.gelu, up_pre)
        active_low = active.astype(jnp.bfloat16)
        branch_ffn = project(active_low, down_weights) + biases[6]
        outcome, pull_three = jax.vjp(
            norm_block, branch_ffn, hidden_two, omega[2], norm_gain[2], norm_shift[2]
        )
        grad_result = cotangent[micro_index].astype(jnp.float32)
        grad_ffn, grad_two, omega_three, gain_three, shift_three = pull_three(grad_result)
        grad_ffn_low = grad_ffn.astype(jnp.bfloat16)
        grad_down = matrix_grad(active_low, grad_ffn_low)
        bias_ffn = column_sum(grad_ffn_low)
        grad_up_pre = pull_active(project_back(grad_ffn_low, down_weights))[0].astype(jnp.bfloat16)
        grad_up = matrix_grad(hidden_two_low, grad_up_pre)
        bias_up = column_sum(grad_up_pre)
        grad_two = grad_two + project_back(grad_up_pre, up_weights)
        grad_cross, grad_one, omega_two, gain_two, shift_two = pull_two(grad_two)
        grad_cross_low = grad_cross.astype(jnp.bfloat16)
        grad_out_cross = matrix_grad(recalled_low, grad_cross_low)
        bias_out_cross = column_sum(grad_cross_low)
        grad_recalled = project_back(grad_cross_low, out_weights[1])
        cross_gq, cross_gk, cross_gv = attention_back(
            grad_recalled,
            recalled,
            recalled_sums,
            cross_query,
            cross_key,
            cross_value,
            src_real,
            cross_set,
            src_ends,
            src_starts,
            False,
        )
        cross_gq = cross_gq.astype(jnp.bfloat16)
        cross_gk = cross_gk.astype(jnp.bfloat16)
        cross_gv = cross_gv.astype(jnp.bfloat16)
        grad_cross_query = matrix_grad(hidden_one_low, cross_gq)
        grad_cross_key = matrix_grad(sources, cross_gk)
        grad_cross_value = matrix_grad(sources, cross_gv)
        grad_one = grad_one + project_back(cross_gq, in_weights[1, 0])
        grad_sources = project_back(cross_gk, in_weights[1, 1]) + project_back(
            cross_gv, in_weights[1, 2]
        )
        grad_self, grad_words, omega_one, gain_one, shift_one = pull_one(grad_one)
        grad_self_low = grad_self.astype(jnp.bfloat16)
        grad_out_self = matrix_grad(heard_low, grad_self_low)
        bias_out_self = column_sum(grad_self_low)
        grad_heard = project_back(grad_self_low, out_weights[0])
        self_gq, self_gk, self_gv = attention_back(
            grad_heard,
            heard,
            heard_sums,
            self_query,
            self_key,
            self_value,
            tgt_real,
            self_set,
            tgt_ends,
            None,
            True,
        )
        self_gq = self_gq.astype(jnp.bfloat16)
        self_gk = self_gk.astype(jnp.bfloat16)
        self_gv = self_gv.astype(jnp.bfloat16)
        grad_words = (
            grad_words
            + project_back(self_gq, in_weights[0, 0])
            + project_back(self_gk, in_weights[0, 1])
            + project_back(self_gv, in_weights[0, 2])
        )
        grad_in = jnp.stack(
            [
                jnp.stack(
                    [
                        matrix_grad(words, self_gq),
                        matrix_grad(words, self_gk),
                        matrix_grad(words, self_gv),
                    ]
                ),
                jnp.stack([grad_cross_query, grad_cross_key, grad_cross_value]),
            ]
        )
        grad_out = jnp.stack([grad_out_self, grad_out_cross])
        grad_bias = jnp.stack(
            [
                column_sum(self_gq),
                column_sum(self_gv),
                bias_out_self,
                column_sum(cross_gq),
                column_sum(cross_gv),
                bias_out_cross,
                bias_ffn,
            ]
        )
        grad_gain = jnp.stack([gain_one, gain_two, gain_three])
        grad_shift = jnp.stack([shift_one, shift_two, shift_three])
        grad_omega = jnp.stack([omega_one, omega_two, omega_three])
        grads = (
            grad_in,
            grad_out,
            grad_up,
            grad_down,
            grad_bias,
            bias_up,
            grad_gain,
            grad_shift,
            grad_omega,
        )
        outcome, grad_words, grad_sources, grads = (
            outcome.astype(jnp.bfloat16),
            grad_words.astype(jnp.bfloat16),
            grad_sources.astype(jnp.bfloat16),
            grads,
        )
        results.append(outcome)
        grads_words.append(grad_words)
        grads_sources.append(grad_sources)
        part_shares = (
            lax.psum_scatter(grads[0], ("rows", "seq"), scatter_dimension=2, tiled=True),
            lax.psum_scatter(grads[1], ("rows", "seq"), scatter_dimension=1, tiled=True),
            lax.psum_scatter(grads[2], ("rows", "seq"), scatter_dimension=0, tiled=True),
            lax.psum_scatter(grads[3], ("rows", "seq"), scatter_dimension=0, tiled=True),
            lax.psum_scatter(grads[4], ("rows", "seq"), scatter_dimension=1, tiled=True),
            lax.psum_scatter(grads[5], ("rows", "seq"), scatter_dimension=0, tiled=True),
            lax.psum_scatter(grads[6], ("rows", "seq"), scatter_dimension=1, tiled=True),
            lax.psum_scatter(grads[7], ("rows", "seq"), scatter_dimension=1, tiled=True),
            lax.psum_scatter(grads[8], ("rows", "seq"), scatter_dimension=1, tiled=True),
        )
        shares_all = (
            part_shares if shares_all is None else jax.tree.map(jnp.add, shares_all, part_shares)
        )
    return (jnp.stack(results), jnp.stack(grads_words), jnp.stack(grads_sources)) + tuple(
        shares_all
    )


def over(mesh, function):
    return jax.shard_map(
        function,
        mesh=mesh,
        in_specs=(
            P(None, "seq", "rows", None),
            P(None, "seq", "rows", None),
            P(None, "seq", "rows", None),
            P(None, "rows", None),
            P(None, "rows", None),
            P(None, "seq", "rows"),
            P(None, "seq", "rows"),
            P(None, None, ("rows", "seq"), None),
            P(None, ("rows", "seq"), None),
            P(("rows", "seq"), None),
            P(("rows", "seq"), None),
            P(),
            P(),
            P(),
            P(),
            P(),
        ),
        out_specs=(
            P(None, "seq", "rows", None),
            P(None, "seq", "rows", None),
            P(None, "seq", "rows", None),
            P(None, None, ("rows", "seq"), None),
            P(None, ("rows", "seq"), None),
            P(("rows", "seq"), None),
            P(("rows", "seq"), None),
            P(None, ("rows", "seq")),
            P(("rows", "seq")),
            P(None, ("rows", "seq")),
            P(None, ("rows", "seq")),
            P(None, ("rows", "seq")),
        ),
        check_vma=False,
    )


def general(mesh):
    return over(mesh, local)


MESH = pl.DeviceIdType.MESH
UNIT = 16 * 1024
BINS = 16
NAMES = 208
BETWEEN = ("dn0", "dn1")
BETWEEN_OUT = BETWEEN + ("up1", "out1")
ODD = ("marks", "w0p", "w1p", "u0p", "x3", "x5", "x7", "sa", "sb", "ta", "out11a", "out11b")
F32 = jnp.float32
BF16 = jnp.bfloat16
PLANES, YS, XS, CORES = 4, 2, 2, 2
GROUP = YS * XS * CORES


def nn(left, right):
    return lax.dot_general(left, right, (((1,), (0,)), ((), ())), preferred_element_type=F32)


def nt(left, right):
    return lax.dot_general(left, right, (((1,), (1,)), ((), ())), preferred_element_type=F32)


def tn(left, right):
    return lax.dot_general(left, right, (((0,), (0,)), ((), ())), preferred_element_type=F32)


def flip(value):
    return jnp.transpose(value.astype(F32))


def fused_kernel(
    tok, mem, cot, tgt_len, src_len, tgt_msk, src_msk, s_in, s_out, s_up, s_dn, h_biases, h_up_bias, h_gain, h_shift, h_omega,
    o_res, o_tok, o_mem, h_in, h_out, h_up, h_dn, h_bias, h_upb, h_gain_o, h_shift_o, h_omega_o,
    biases, up_bias, gain, shift, omega, o_in, o_out, o_up, o_dn, o_bias, o_upb, o_gain, o_shift, o_omega,
    w_q, w_out, w_up, w_dn, g_q, g_out, g_up, g_dn,
    c_q, c_out, c_up, c_dn,
    p_q, p_out, p_up, p_dn,
    q_q, q_out, q_up, q_dn,
    z_q, z_out, z_up, z_dn,
    ws0, ws1, gs0, gs1, cs0, cs1, zs0, zs1, fs0, fs1,
    all_tok, all_mem, in_cot, raw_tl, raw_sl, raw_tm, raw_sm, meta, in_meta, all_meta,
    dx0, dx1, dc0, dc1, dp0, dp1,
    a3, b3, a4, b4, a5, b5, a6, b6, a7, b7, a8, b8,
    out_res, out_tok, out_mem,
    sg0, sg1, sg2, sg3, sr0, sr1, sr2, sra, srb,
    tg0, tg1, tg2, tg3, tr0, tr1, tr2, tra,
    code_self, code_cross, key_pos, rows_f,
    qt0, kt0, vt0, k0, v0, pt0, l0, ot0,
    qt1, kt1, vt1, k1, v1, pt1, l1, ot1,
    dnt, acc_k, acc_v,
    act, slope, gul, xh0, xh1, xh2, h1_f, h2_f,
    wt, bias_cols, wz, dt0, dt1, gauge,
    f_q, f_out, f_up, f_dn, f_u0, f_u1, mid_far, mid_line,
    ss, rs,
):
    c = lax.axis_index("rows")
    seq = lax.axis_index("seq")
    z = seq // (YS * XS)
    yx = lax.rem(seq, YS * XS)
    y = yx // XS
    x = lax.rem(yx, XS)
    width = 512
    here = 2 * 64

    def at(zz, yy, xx):
        return zz * (YS * XS) + yy * XS + xx

    def slot(cc, yy, xx):
        return cc * 4 + yy * 2 + xx

    def head(cc, yy, xx):
        return (yy * 2 + xx) * 2 + cc

    me_slot, me_head = slot(c, y, x), head(c, y, x)
    plane_peers = []
    for k in range(1, GROUP):
        cc = 1 - c if k & 4 else c
        yy = 1 - y if k & 2 else y
        xx = 1 - x if k & 1 else x
        plane_peers.append((cc, yy, xx))
    trio = [(1 - y, x), (y, 1 - x), (1 - y, 1 - x)]
    z_peers = [lax.rem(z + k, PLANES) for k in (1, 2, 3)]

    names, expected_bytes = {}, {}
    pending = []
    edge = (z == 0) | (z == PLANES - 1)

    def sem(name):
        return names.setdefault(name, len(names))

    def wait(semaphore, ref):
        pltpu.make_async_copy(ref, ref, semaphore).wait()

    def size(ref):
        return math.prod(ref.shape) * jnp.dtype(ref.dtype).itemsize

    bins = [0]
    odd = {}

    def out_sem(name):
        return ss.at[odd.setdefault(name, BINS + 1 + len(odd))] if name in ODD else ss.at[len(bins) - 1]

    def send(name, src, dst, device, recv=None):
        pltpu.make_async_remote_copy(
            src_ref=src, dst_ref=dst, send_sem=out_sem(name), recv_sem=rs.at[sem(name)] if recv is None else recv,
            device_id=device, device_id_type=MESH,
        ).start()

    def keep(name, src, dst):
        pltpu.make_async_copy(src, dst, rs.at[sem(name)]).start()

    def landed(name, ref):
        wait(rs.at[sem(name)], ref)

    def sent_later(name, ref):
        if name in ODD:
            pending.append((ss.at[odd[name]], ref, None))
            return
        bins[-1] += size(ref)
        assert size(ref) % UNIT == 0, (name, size(ref))
        if bins[-1] > 1024 * UNIT // 16:
            bins.append(0)

    line_bytes = [0]

    def along_z(name, src, block):
        i, j = sem(name + "z"), sem(name + "f")
        for step in (1, -1, 2, -2):
            to = z + step
            far = (z == 0) if step == 2 else (z == PLANES - 1) if step == -2 else None

            @pl.when((to >= 0) & (to < PLANES))
            def _():
                pltpu.make_async_remote_copy(
                    src_ref=src, dst_ref=block(z), send_sem=ss.at[BINS],
                    recv_sem=rs.at[i] if far is None else rs.at[jnp.where(far, j, i)],
                    device_id=(c, at(to, y, x)), device_id_type=MESH,
                ).start()

        line_bytes[0] += size(src)

    def pass_on(name, block):
        for mine, origin, to in ((1, 3, 0), (2, 0, 3)):

            @pl.when(z == mine)
            def _():
                landed(name + "f", block(origin))
                pltpu.make_async_remote_copy(
                    src_ref=block(origin), dst_ref=block(origin), send_sem=ss.at[BINS], recv_sem=rs.at[sem(name + "z")],
                    device_id=(c, at(to, y, x)), device_id_type=MESH,
                ).start()

    fold_bytes = [0]

    def fold_send(name, block, target, to):
        pltpu.make_async_remote_copy(
            src_ref=block, dst_ref=target, send_sem=ss.at[BINS], recv_sem=rs.at[sem(name)],
            device_id=(c, at(to, y, x)), device_id_type=MESH,
        ).start()

    def fold_z(name, block, far, line):
        inner = jnp.where(edge, 0, 1)
        for origin, step, hops in ((0, 3, 1), (3, -3, -1)):

            @pl.when(z == origin)
            def _():
                fold_send(name + "a", block(origin + step), far, origin + hops)
                fold_send(name + "l", block(origin + 2 * hops), line.at[2], origin + 2 * hops)

        for step in (1, -1):
            to = z + step

            @pl.when((to >= 0) & (to < PLANES))
            def _():
                between = jnp.where((to == 0) | (to == PLANES - 1), 0, inner)
                fold_send(name + "l", block(to), line.at[between], to)

        fold_bytes[0] += size(far)

    def fold_f(name, block, far, line):
        for mine, to in ((1, 3), (2, 0)):

            @pl.when(z == mine)
            def _():
                landed(name + "a", far)
                add(block(to), far)
                fold_send(name + "l", block(to), line.at[1], to)

    def fold_sum(name, own, line, result):
        @pl.when(edge)
        def _():
            landed(name + "l", line.at[pl.ds(0, 2)])

        @pl.when(jnp.logical_not(edge))
        def _():
            landed(name + "l", line)

        total = own.astype(F32) + line[0].astype(F32) + line[1].astype(F32)

        @pl.when(edge)
        def _():
            result[...] = total.astype(result.dtype)

        @pl.when(jnp.logical_not(edge))
        def _():
            result[...] = (total + line[2].astype(F32)).astype(result.dtype)

    def line_landed(name, blocks, own):
        @pl.when(edge)
        def _():
            landed(name + "z", blocks(3 + own))

        @pl.when(jnp.logical_not(edge))
        def _():
            landed(name + "z", blocks(2 + own))

    def to_plane(name, src, dst, slotted=False):
        half = lax.rem(z, 2)
        core = z // 2
        if slotted:
            recv = rs.at[jnp.where(half == 0, sem(name + "h0"), sem(name + "h1"))]
            part = dst.at[slot(core, y, x), half]
        else:
            recv = rs.at[sem(name)]
            part = dst.at[half]
        for m in range(2):
            plane = 2 * m + c
            own = (plane == z) & (core == c)
            out = ss.at[odd.setdefault(name + str(m), BINS + 1 + len(odd))]

            @pl.when(own)
            def _():
                pltpu.make_async_copy(src.at[m], part, recv).start()

            @pl.when(jnp.logical_not(own))
            def _():
                pltpu.make_async_remote_copy(
                    src_ref=src.at[m], dst_ref=part, send_sem=out, recv_sem=recv,
                    device_id=(core, at(plane, y, x)), device_id_type=MESH,
                ).start()

            pending.append((out, src.at[m], jnp.logical_not(own)))

    def from_plane(name, src, dst):
        micro, core = z // 2, lax.rem(z, 2)
        recv = rs.at[sem(name)]
        for half in range(2):
            zz = 2 * c + half
            own = (core == c) & (zz == z)
            part = dst.at[micro]
            out = ss.at[odd.setdefault(name + str(half), BINS + 1 + len(odd))]

            @pl.when(own)
            def _():
                pltpu.make_async_copy(src.at[half], part, recv).start()

            @pl.when(jnp.logical_not(own))
            def _():
                pltpu.make_async_remote_copy(
                    src_ref=src.at[half], dst_ref=part, send_sem=out, recv_sem=recv,
                    device_id=(core, at(zz, y, x)), device_id_type=MESH,
                ).start()

            pending.append((out, src.at[half], jnp.logical_not(own)))

    def to_heads(name, src, dst):
        keep(name, src.at[me_head], dst.at[me_slot])
        for cc, yy, xx in plane_peers:
            send(name, src.at[head(cc, yy, xx)], dst.at[me_slot], (cc, at(z, yy, xx)))
        sent_later(name, src.at[pl.ds(0, GROUP - 1)])

    def to_slot(name, src, dst, s):
        device = (s // 4, at(z, (s % 4) // 2, s % 2))
        i = sem(name)
        out = out_sem(name)

        @pl.when(me_slot == s)
        def _():
            pltpu.make_async_copy(src.at[s], dst.at[me_head], rs.at[i]).start()

        @pl.when(me_slot != s)
        def _():
            pltpu.make_async_remote_copy(
                src_ref=src.at[s], dst_ref=dst.at[me_head], send_sem=out, recv_sem=rs.at[i],
                device_id=device, device_id_type=MESH,
            ).start()

    weights = {
        "q": (w_q, s_in.at[1, pl.ds(0, 1)], g_q, c_q, p_q, q_q, z_q, o_in.at[1, pl.ds(0, 1)]),
    }

    for i in range(2):
        one = pl.ds(i, 1)
        refs = (w_out, s_out, g_out, c_out, p_out, q_out, z_out, o_out)
        weights["out" + str(i)] = tuple(
            ref.at[:, one] if ref is p_out or ref is q_out or ref is z_out else ref.at[one] for ref in refs
        )
        refs = (w_up, s_up, g_up, c_up, p_up, q_up, z_up, o_up)
        cols = pl.ds(i * 1024, 1024)
        weights["up" + str(i)] = tuple(
            ref.at[:, one] if ref is p_up or ref is q_up or ref is z_up
            else ref.at[:, :, cols] if ref is s_up or ref is o_up else ref.at[one]
            for ref in refs
        )
        refs = (w_dn, s_dn, g_dn, c_dn, p_dn, q_dn, z_dn, o_dn)
        cols = pl.ds(i * 256, 256)
        weights["dn" + str(i)] = tuple(
            ref.at[:, one] if ref is p_dn or ref is q_dn or ref is z_dn
            else ref.at[:, :, cols] if ref is s_dn or ref is o_dn else ref.at[one]
            for ref in refs
        )

    mids = {g: (mid_far.at[i], mid_line.at[i]) for i, g in enumerate(BETWEEN)}
    fars = {"q": f_q, "u0": f_u0, "u1": f_u1}
    for i in range(2):
        one = pl.ds(i, 1)
        fars["out" + str(i)], fars["up" + str(i)], fars["dn" + str(i)] = f_out.at[one], f_up.at[one], f_dn.at[one]

    def halves(ref):
        cols = ref.shape[-1] // 2
        return pl.ds(0, cols), pl.ds(cols, cols)

    x_next, y_next, core_next = (c, at(z, y, 1 - x)), (c, at(z, 1 - y, x)), (1 - c, seq)

    def gather_z(g):
        full, shard = weights[g][:2]
        if g in BETWEEN_OUT:
            first, second = halves(full)
            whole = s_dn if g[:2] == "dn" else s_up if g[:2] == "up" else shard
            keep(g + "o", shard, full.at[:, c, z, y, x])
            for which, cols, device in (("1a", first, x_next), ("1b", second, y_next)):
                part = full.at[:, c, z, y, x, :, cols]
                send(g + which, whole.at[:, :, shard_cols(g, cols)], part, device)
                sent_later(g + which, part)
            return
        keep(g + "z", shard, full.at[:, c, z, y, x])
        along_z(g, shard, lambda zz: full.at[:, c, zz, y, x])

    def gather_f(g):
        full = weights[g][0]
        if g in BETWEEN_OUT:
            first, second = halves(full)
            pass_on(g + "A", lambda zz: full.at[:, c, zz, y, :, :, first])
            pass_on(g + "B", lambda zz: full.at[:, c, zz, :, x, :, second])
            return
        pass_on(g, lambda zz: full.at[:, c, zz, y, x])

    def gather_1(g):
        full = weights[g][0]
        first, second = halves(full)
        if g in BETWEEN_OUT:
            landed(g + "o", full.at[:, c, z, y, x])
            landed(g + "1a", full.at[:, c, z, y, 1 - x, :, first])
            along_z(g + "A", full.at[:, c, z, y, :, :, first], lambda zz: full.at[:, c, zz, y, :, :, first])
            landed(g + "1b", full.at[:, c, z, 1 - y, x, :, second])
            along_z(g + "B", full.at[:, c, z, :, x, :, second], lambda zz: full.at[:, c, zz, :, x, :, second])
            return
        line_landed(g, lambda n: full.at[:, c, pl.ds(0, n), y, x], 1)
        part = full.at[:, c, :, y, x, :, first]
        send(g + "1a", part, part, x_next)
        sent_later(g + "1a", part)
        part = full.at[:, c, :, y, x, :, second]
        send(g + "1b", part, part, y_next)
        sent_later(g + "1b", part)

    def gather_2(g):
        full = weights[g][0]
        first, second = halves(full)
        if g in BETWEEN_OUT:
            line_landed(g + "A", lambda n: full.at[:, c, pl.ds(0, n), y, :, :, first], 0)
        else:
            landed(g + "1a", full.at[:, c, :, y, 1 - x, :, first])
        part = full.at[:, c, :, y, :, :, first]
        send(g + "2a", part, part, y_next)
        sent_later(g + "2a", part)
        if g in BETWEEN_OUT:
            line_landed(g + "B", lambda n: full.at[:, c, pl.ds(0, n), :, x, :, second], 0)
        else:
            landed(g + "1b", full.at[:, c, :, 1 - y, x, :, second])
        part = full.at[:, c, :, :, x, :, second]
        send(g + "2b", part, part, x_next)
        sent_later(g + "2b", part)

    def shard_cols(g, cols):
        start = int(g[-1]) * {"dn": 256, "up": 1024, "ou": 0}[g[:2]]
        return pl.ds(start + cols.start, cols.size)

    def gather_3(g):
        full = weights[g][0]
        first, second = halves(full)
        landed(g + "2a", full.at[:, c, :, 1 - y, :, :, first])
        landed(g + "2b", full.at[:, c, :, :, 1 - x, :, second])
        send(g + "3", full.at[:, c], full.at[:, c], core_next)
        sent_later(g + "3", full.at[:, c])

    def gathered(g):
        landed(g + "3", weights[g][0].at[:, 1 - c])

    def add(target, other):
        target[...] = (target[...].astype(F32) + other[...].astype(F32)).astype(BF16)

    def scatter_0(g):
        grad, across = weights[g][2:4]
        send(g + "r0", grad.at[:, 1 - c], across, core_next)
        sent_later(g + "r0", across)

    def scatter_1(g):
        grad, across, part = weights[g][2:5]
        first, second = halves(grad)
        landed(g + "r0", across)
        for lead in range(grad.shape[0]):

            @pl.loop(0, PLANES)
            def _(zz):
                add(grad.at[lead, c, zz], across.at[lead, zz])

        send(g + "r1a", grad.at[:, c, :, 1 - y, :, :, first], part.at[0], y_next)
        sent_later(g + "r1a", part.at[0])
        send(g + "r1b", grad.at[:, c, :, :, 1 - x, :, second], part.at[1], x_next)
        sent_later(g + "r1b", part.at[1])

    def scatter_2(g):
        grad, _, part, piece = weights[g][2:6]
        first, second = halves(grad)
        landed(g + "r1a", part.at[0])
        landed(g + "r1b", part.at[1])
        for lead in range(grad.shape[0]):

            @pl.loop(0, PLANES)
            def _(zz):
                add(grad.at[lead, c, zz, y, :, :, first], part.at[0, lead, zz])
                add(grad.at[lead, c, zz, :, x, :, second], part.at[1, lead, zz])

        if g in BETWEEN:
            fold_z(g + "A", lambda zz: grad.at[:, c, zz, y, :, :, first], mids[g][0].at[0, 0], mids[g][1].at[:, 0])
            fold_z(g + "B", lambda zz: grad.at[:, c, zz, :, x, :, second], mids[g][0].at[1, 0], mids[g][1].at[:, 1])
            return
        send(g + "r2a", grad.at[:, c, :, y, 1 - x, :, first], piece.at[0], x_next)
        sent_later(g + "r2a", piece.at[0])
        send(g + "r2b", grad.at[:, c, :, 1 - y, x, :, second], piece.at[1], y_next)
        sent_later(g + "r2b", piece.at[1])

    def scatter_3(g):
        grad, _, _, piece, line = weights[g][2:7]
        first, second = halves(grad)
        if g in BETWEEN:
            fold_sum(g + "A", grad[:, c, z, y, :, :, first], mids[g][1].at[:, 0], grad.at[:, c, z, y, :, :, first])
            send(g + "r2a", grad.at[:, c, z, y, 1 - x, :, first], piece.at[0, :, 0], x_next)
            sent_later(g + "r2a", piece.at[0, :, 0])
            fold_sum(g + "B", grad[:, c, z, :, x, :, second], mids[g][1].at[:, 1], grad.at[:, c, z, :, x, :, second])
            send(g + "r2b", grad.at[:, c, z, 1 - y, x, :, second], piece.at[1, :, 0], y_next)
            sent_later(g + "r2b", piece.at[1, :, 0])
            return
        landed(g + "r2a", piece.at[0])
        landed(g + "r2b", piece.at[1])
        for lead in range(grad.shape[0]):

            @pl.loop(0, PLANES)
            def _(zz):
                add(grad.at[lead, c, zz, y, x, :, first], piece.at[0, lead, zz])
                add(grad.at[lead, c, zz, y, x, :, second], piece.at[1, lead, zz])

        fold_z(g, lambda zz: grad.at[:, c, zz, y, x], fars[g], line)

    def scatter_f(g):
        grad, line = weights[g][2], weights[g][6]
        if g in BETWEEN:
            first, second = halves(grad)
            fold_f(g + "A", lambda zz: grad.at[:, c, zz, y, :, :, first], mids[g][0].at[0, 0], mids[g][1].at[:, 0])
            fold_f(g + "B", lambda zz: grad.at[:, c, zz, :, x, :, second], mids[g][0].at[1, 0], mids[g][1].at[:, 1])
            return
        fold_f(g, lambda zz: grad.at[:, c, zz, y, x], fars[g], line)

    def scattered(g):
        grad, _, _, piece, line, result = weights[g][2:8]
        if g in BETWEEN:
            landed(g + "r2a", piece.at[0, :, 0])
            landed(g + "r2b", piece.at[1, :, 0])
            across = jnp.concatenate([piece[0, :, 0], piece[1, :, 0]], axis=-1)
            result[...] = grad[:, c, z, y, x].astype(F32) + across.astype(F32)
            return
        fold_sum(g, grad[:, c, z, y, x], line, result)

    left, right = pl.ds(0, 256), pl.ds(256, 256)
    y_slot, x_slot, far_slot = slot(c, 1 - y, x), slot(c, y, 1 - x), slot(c, 1 - y, 1 - x)

    def spread_1(name, full, half):
        own = full.at[me_slot, half]
        landed(name + "h" + str(half), own)
        for which, device in (("y", y_next), ("x", x_next), ("c", core_next)):
            which = which if which == "c" else which + str(half)
            send(name + which, own, own, device)
            sent_later(name + which, own)

    def spread_2(name, full, half):
        for which, place, cols, device in (("y", y_slot, right, x_next), ("x", x_slot, left, y_next)):
            part = full.at[place, half]
            landed(name + which + str(half), part)
            half_of = full.at[place, half, :, cols]
            send(name + "q" + which + str(half), half_of, half_of, device)
            sent_later(name + "q" + which + str(half), half_of)
            send(name + "d", part, part, core_next)
            sent_later(name + "d", part)

    def spread_4(name, full, half):
        part = full.at[far_slot, half]
        landed(name + "qy" + str(half), full.at[far_slot, half, :, right])
        landed(name + "qx" + str(half), full.at[far_slot, half, :, left])
        send(name + "d", part, part, core_next)
        sent_later(name + "d", part)

    def spread_3(name, full):
        landed(name + "c", full.at[0])
        landed(name + "d", full.at[pl.ds(0, 3)])

    def merge_0(name, full, across):
        send(name + "c", full.at[pl.ds((1 - c) * 4, 4)], across, core_next)
        sent_later(name + "c", across)

    def merge_1(name, full, across, parts):
        landed(name + "c", across)
        add(full.at[far_slot], across.at[(1 - y) * 2 + 1 - x])
        send(name + "qx", full.at[far_slot, :, :, left], parts.at[2, :, :, left], y_next)
        send(name + "qy", full.at[far_slot, :, :, right], parts.at[2, :, :, right], x_next)
        sent_later(name + "q", parts.at[2])
        add(full.at[x_slot], across.at[y * 2 + 1 - x])
        add(full.at[y_slot], across.at[(1 - y) * 2 + x])
        add(full.at[me_slot], across.at[yx])

    def merge_3(name, full, parts):
        landed(name + "qx", parts.at[2, :, :, left])
        add(full.at[x_slot, :, :, left], parts.at[2, :, :, left])
        send(name + "px", full.at[x_slot], parts.at[0], x_next)
        sent_later(name + "px", parts.at[0])
        landed(name + "qy", parts.at[2, :, :, right])
        add(full.at[y_slot, :, :, right], parts.at[2, :, :, right])
        send(name + "py", full.at[y_slot], parts.at[1], y_next)
        sent_later(name + "py", parts.at[1])

    def merge_2(name, full, parts):
        landed(name + "px", parts.at[0])
        landed(name + "py", parts.at[1])
        total = full[me_slot].astype(F32)
        for k in range(2):
            total = total + parts[k].astype(F32)
        return total.reshape(here, width)

    def tile(index):
        return pl.ds(pl.multiple_of(index * 128, 128), 128)

    def slice_1(name, shard, full):
        keep(name + "p", shard.at[:, :, tile(yx)], full.at[:, c, z, yx])
        for yy, xx in trio:
            send(name + "p", shard.at[:, :, tile(yy * 2 + xx)], full.at[:, c, z, yx], (c, at(z, yy, xx)))
        sent_later(name + "p", full.at[:, c, z, pl.ds(0, 3)])

    def slice_2(name, full):
        landed(name + "p", full.at[:, c, z])
        along_z(name, full.at[:, c, z], lambda zz: full.at[:, c, zz])

    def slice_f(name, full):
        pass_on(name, lambda zz: full.at[:, c, zz])

    def slice_3(name, full):
        line_landed(name, lambda n: full.at[:, c, pl.ds(0, n)], 0)
        send(name + "c", full.at[:, c], full.at[:, c], core_next)
        sent_later(name + "c", full.at[:, c])

    def slice_4(name, full):
        landed(name + "c", full.at[:, 1 - c])

    def unslice_0(name, grad, across):
        send(name + "c", grad.at[:, 1 - c], across, core_next)
        sent_later(name + "c", across)

    def unslice_1(name, grad, across, line):
        landed(name + "c", across)
        for lead in range(grad.shape[0]):
            add(grad.at[lead, c], across.at[lead])
        fold_z(name, lambda zz: grad.at[:, c, zz], fars[name], line)

    def unslice_f(name, grad, line):
        fold_f(name, lambda zz: grad.at[:, c, zz], fars[name], line)

    def unslice_2(name, grad, line, total, result):
        fold_sum(name, grad[:, c, z], line, total)
        for yy, xx in trio:
            send(name + "p", total.at[:, yy * 2 + xx], result.at[:, :, tile(yx)], (c, at(z, yy, xx)))
        sent_later(name + "p", total.at[:, pl.ds(0, 3)])
        result[:, :, tile(yx)] = total[:, yx]

    def unslice_3(name, result):
        landed(name + "p", result.at[:, :, pl.ds(0, 384)])

    def matrix(ref):
        return ref[...].reshape(-1, ref.shape[-1])

    def put(ref, value):
        ref[...] = value.astype(BF16).reshape(ref.shape)

    def norm(r, i, kept):
        centered = r - jnp.mean(r, axis=1, keepdims=True)
        scale = lax.rsqrt(jnp.mean(centered * centered, axis=1, keepdims=True) + 1e-05)
        xhat = centered * scale
        kept[...] = xhat
        return xhat * gain[i : i + 1, :] + shift[i : i + 1, :], scale

    def column(row, value):
        sg0[row : row + 1, :] = jnp.sum(value, axis=0, keepdims=True)

    def norm_back(grad, i, kept, scale, skip):
        xhat = kept[...]
        column(12 + i, grad * xhat)
        column(15 + i, grad)
        dxhat = grad * gain[i : i + 1, :]
        dr = dxhat - jnp.mean(dxhat, axis=1, keepdims=True)
        dr = (dr - xhat * jnp.mean(dxhat * xhat, axis=1, keepdims=True)) * scale
        column(18 + i, dr * skip)
        return dr, dr * omega[i : i + 1, :]

    BLOCK = 256

    def attend(b, queries, keys, values_t, weights_t, sums, outputs, causal, name, target, arrives):
        extent = 512 if causal and b < 2 else 1024
        cols = slice(b * BLOCK, (b + 1) * BLOCK)
        scores = nn(keys[:extent, :], queries[:, cols])
        seg = rows_f[0:1, cols]
        code = (code_self if causal else code_cross)[:extent, :]
        permit = jnp.concatenate([code, code], axis=1) == seg
        if causal:
            pos = key_pos[:extent, :]
            pos = jnp.concatenate([pos, pos], axis=1)
            mine = rows_f[1:2, cols]
            permit = (permit & (pos <= mine)) | (pos == mine)
        weight = jnp.where(permit, jnp.exp(scores), 0.0)
        total = jnp.sum(weight, axis=0, keepdims=True)
        low = weight.astype(BF16)
        weights_t[:extent, cols] = low
        out = nn(values_t[:, :extent], low) / total
        sums[0:1, cols] = total
        outputs[:, cols] = out
        for k in range(2):
            target[2 * b + k] = out[:, k * here : (k + 1) * here].astype(BF16)
            to_slot(name, target, arrives, 2 * b + k)
        if b == 3:
            sent_later(name, target.at[pl.ds(0, GROUP - 1)])

    def attend_start(buffer, sums, outputs):
        acc_k[...] = jnp.zeros_like(acc_k)
        acc_v[...] = jnp.zeros_like(acc_v)
        for s in range(GROUP):
            cols = slice(s * here, (s + 1) * here)
            grad = buffer[s].astype(F32)
            inverse = 1.0 / sums[0:1, cols]
            dnt[:, cols] = (grad * inverse).astype(BF16)
            rows_f[2:3, cols] = -jnp.sum(grad * outputs[:, cols], axis=0, keepdims=True) * inverse

    def attend_back(b, queries, keys_t, values, weights_t, causal, name, target, arrives):
        extent = 512 if causal and b < 2 else 1024
        cols = slice(b * BLOCK, (b + 1) * BLOCK)
        low = weights_t[:extent, cols]
        dn = dnt[:, cols]
        spread = nn(values[:extent, :], dn)
        slopes = (low.astype(F32) * (spread + rows_f[2:3, cols])).astype(BF16)
        block = (nn(keys_t[:, :extent], slopes) * 0.125).astype(BF16)
        if name is None:
            dt0[0:64, cols] = block
        else:
            for k in range(2):
                target[2 * b + k] = block[:, k * here : (k + 1) * here]
                to_slot(name, target, arrives, 2 * b + k)
            if b == 3:
                sent_later(name, target.at[pl.ds(0, GROUP - 1)])
        acc_k[:, :extent] += nt(queries[:, cols], slopes)
        acc_v[:, :extent] += nt(dn, low)

    def by_head(target, value):
        target[...] = flip(value).astype(BF16).reshape(GROUP, 64, here)

    def heads_weights(first, full):
        for j in range(full.shape[0]):
            wt[first + j] = flip(matrix(full.at[j])).astype(BF16)

    own_rows = pl.ds(pl.multiple_of(c * 64, 64), 64)
    own_head = pl.ds(pl.multiple_of(me_head * 64, 64), 64)

    def own_weights(first, count):
        return jnp.concatenate([wt[first + j, own_rows, :] for j in range(count)], axis=0)

    def wide_bias(i):
        col = bias_cols[i, own_head, :]
        return jnp.concatenate([col, col], axis=1)

    def project_heads(rows, first, queries, keys, keys_t, values, values_t):
        count = 2 if queries is None else 3
        own = own_weights(first, count)
        for b in range(4):
            cols = slice(b * 256, (b + 1) * 256)
            out = nt(own, rows[2 * b : 2 * b + 2].reshape(256, width))
            if queries is not None:
                queries[:, cols] = ((out[0:64] + wide_bias(0)).astype(BF16).astype(F32) * 0.125).astype(BF16)
            at_k = 64 * (count - 2)
            block = out[at_k : at_k + 64].astype(BF16)
            keys_t[:, cols] = block
            keys[cols, :] = flip(block).astype(BF16)
            block = (out[at_k + 64 : at_k + 128] + wide_bias(1 if count == 3 else 2)).astype(BF16)
            values_t[:, cols] = block
            values[cols, :] = flip(block).astype(BF16)

    def rows_back(grads_t, first, target, core):
        count = grads_t.shape[0] // 64
        own = own_weights(first, count)
        for b in range(2):
            cols = pl.ds(pl.multiple_of(core * 512 + b * 256, 256), 256)
            out = tn(grads_t[:, cols], own)
            target[pl.ds(core * 4 + b * 2, 2)] = out.astype(BF16).reshape(2, 2, 64, width)

    def slices_back(grads_t, rows, grad):
        count = grads_t.shape[0] // 64
        out = nn(grads_t[...], rows[...].reshape(1024, width))
        wz[...] = jnp.zeros_like(wz)
        for j in range(count):
            wz[j, own_rows, :] = out[j * 64 : (j + 1) * 64]
            put(grad.at[j], jnp.transpose(wz[j]))

    def bias(i):
        return biases[i : i + 1, :]

    def make_masks():
        landed("marks", all_meta.at[pl.ds(0, 7)])
        order = lax.broadcasted_iota(jnp.int32, (1, 1024), 1)
        place = (order // 512) * 512 + lax.rem(order // 64, 2) * 256 + lax.rem(order // 128, 4) * 64 + lax.rem(order, 64)
        place = place.astype(F32)
        marks = [all_meta[s].astype(F32) for s in range(GROUP)]
        tgt_real = jnp.concatenate([mark[0:1, :] for mark in marks], axis=1)
        src_real = jnp.concatenate([mark[1:2, :] for mark in marks], axis=1)
        lower = lax.broadcasted_iota(jnp.int32, (32, 128), 1)
        later = lax.broadcasted_iota(jnp.int32, (32, 128), 0)

        def ends_of(row):
            lengths = jnp.broadcast_to(row, (32, 128))
            ends = jnp.sum(jnp.where(lower <= later, lengths, 0.0), axis=1, keepdims=True)
            starts = jnp.sum(jnp.where(lower < later, lengths, 0.0), axis=1, keepdims=True)
            return ends, starts

        def count(flags):
            return jnp.sum(jnp.where(flags, 1.0, 0.0), axis=0, keepdims=True)

        tgt_ends, _ = ends_of(marks[0][2:3, :])
        src_ends, src_starts = ends_of(marks[0][3:4, :])
        tgt_seg = count(tgt_ends <= place)
        src_seg = count(src_ends <= place)
        src_first = count(src_starts == place)
        self_row = jnp.where(tgt_real > 0.5, tgt_seg, -1.0)
        cross_row = jnp.where((src_real > 0.5) | (src_first > 0.5), src_seg, -1.0)
        rows_f[0:1, :] = tgt_seg
        rows_f[1:2, :] = place
        code_self[...] = jnp.transpose(jnp.broadcast_to(self_row, (128, 1024)))
        code_cross[...] = jnp.transpose(jnp.broadcast_to(cross_row, (128, 1024)))
        key_pos[...] = jnp.transpose(jnp.broadcast_to(place, (128, 1024)))

    def feed_up(rows, i):
        for k in (2 * i, 2 * i + 1):
            cols = slice(k * width, (k + 1) * width)
            inner = slice((k % 2) * width, (k % 2 + 1) * width)
            u = nn(rows, matrix(w_up.at[i, :, :, :, :, :, inner])) + up_bias[0:1, cols]
            square = u * u
            t = jnp.tanh(u * (0.7978845608028654 + 0.035677408136300125 * square))
            act[:, cols] = (0.5 * u * (1.0 + t)).astype(BF16)
            inner = 0.7978845608028654 + 0.10703222440890037 * square
            slope[:, cols] = 0.5 * (1.0 + t) + 0.5 * u * (1.0 - t * t) * inner

    def feed_back(gf, back):
        for k in range(4):
            cols = slice(k * width, (k + 1) * width)
            inner = slice((k % 2) * width, (k % 2 + 1) * width)
            rows = pl.ds(2 * (k % 2), 2)
            gu = nt(gf[:, 0:256], matrix(w_dn.at[0, k // 2, rows]))
            gu = gu + nt(gf[:, 256:512], matrix(w_dn.at[1, k // 2, rows]))
            gu = (gu * slope[:, cols]).astype(BF16)
            gul[:, cols] = gu
            column(8 + k, gu.astype(F32))
            back = back + nt(gu, matrix(w_up.at[k // 2, :, :, :, :, :, inner]))
        return back

    def value_sums(grads_t):
        total = jnp.sum(grads_t[64:128, :].astype(F32), axis=1, keepdims=True)
        bias_cols[0] = jnp.zeros((width, 128), F32)
        bias_cols[0, own_head, :] = jnp.broadcast_to(total, (64, 128))
        sg0[4:5, :] = jnp.transpose(bias_cols[0])[0:1, :]

    def head_sums(grads_t):
        lanes = lax.broadcasted_iota(jnp.int32, (64, 128), 1)
        dq_sum = jnp.sum(grads_t[0:64, :].astype(F32), axis=1, keepdims=True)
        dv_sum = jnp.sum(grads_t[128:192, :].astype(F32), axis=1, keepdims=True)
        bias_cols[0] = jnp.zeros((width, 128), F32)
        bias_cols[0, own_head, :] = jnp.where(lanes == 0, dq_sum, dv_sum)
        tg0[...] = jnp.transpose(bias_cols[0])[0:8, :]

    def small(name, src, dst, device):
        send(name, src, dst, device)
        sent_later(name, dst)

    def small_add(name, arrived, mine, total):
        landed(name, arrived)
        total[...] = mine[...] + arrived[...]

    def small_z(name, src, rows, tile_at, dst):
        for k, zz in enumerate(z_peers):
            send(name, src.at[rows, tile(tile_at(zz))], dst.at[2 - k], (c, at(zz, y, x)))
        sent_later(name, dst)

    def tile_own(zz):
        return c * 2 + zz // 2

    def tile_up(zz):
        return lax.rem(zz, 2) * 2 + y

    def small_sum(name, src, rows, tile_at, dst):
        landed(name, dst)
        return src[rows, tile(tile_at(z))] + dst[0] + dst[1] + dst[2]

    def small_out():
        block = c * 16 + seq
        shift_by = lax.rem(128 - lax.rem(block, 8) * 16, 128)
        turned = pltpu.roll(small_sum("sa", sg3, slice(None), tile_own, sra), shift_by, 1)
        o_bias[...] = turned[0:7, 0:16]
        o_gain[...] = turned[12:15, 0:16]
        o_shift[...] = turned[15:18, 0:16]
        o_omega[...] = turned[18:21, 0:16]
        turned = pltpu.roll(small_sum("ta", tg3, slice(None), tile_own, tra), shift_by, 1)
        o_bias[0:2, :] = turned[0:2, 0:16]
        turned = pltpu.roll(small_sum("sb", sg3, pl.ds(8, 8), tile_up, srb), lax.rem(block, 2) * 64, 1)
        wanted = block // 8
        row = jnp.zeros((1, 64), F32)
        for k in range(4):
            row = row + turned[k : k + 1, 0:64] * (wanted == k).astype(F32)
        o_upb[...] = row
        ends = ((o_bias, h_bias), (o_upb, h_upb), (o_gain, h_gain_o), (o_shift, h_shift_o), (o_omega, h_omega_o))
        for i, (src, dst) in enumerate(ends):
            keep("e" + str(4 + i), src, dst)

    raw = ((raw_tm, tgt_msk), (raw_sm, src_msk), (raw_tl, tgt_len), (raw_sl, src_len))
    for i, (ref, given) in enumerate(raw):
        keep("raw" + str(i), given, ref)
    given = ((h_biases, biases), (h_up_bias, up_bias), (h_gain, gain), (h_shift, shift), (h_omega, omega))
    for i, (src, ref) in enumerate(given):
        keep("given" + str(i), src, ref)
    barrier = pltpu.get_barrier_semaphore()
    greet = [(cc, at(z, yy, xx)) for cc, yy, xx in plane_peers]
    greet += [(cc, at(zz, y, x)) for zz in z_peers for cc in (c, 1 - c)]
    for device in greet:
        pl.semaphore_signal(barrier, inc=1, device_id=device, device_id_type=MESH)
    pl.semaphore_wait(barrier, len(greet))
    gather_z("out0")
    gather_z("dn1")
    gather_z("up1")
    to_plane("x", tok, all_tok, True)
    slice_1("w0", s_in.at[0], ws0)
    gather_z("dn0")
    gather_z("out1")
    gather_z("q")
    gather_z("up0")
    for i, (ref, _) in enumerate(raw):
        landed("raw" + str(i), ref)
        span = ref.shape[2]
        for m in range(2):
            for start in (0, 64):
                meta[m, i : i + 1, start : start + span] = ref[m]
    slice_1("w1", s_in.at[1, pl.ds(1, 2)], ws1)
    gather_f("out0")
    spread_1("x", all_tok, 0)
    slice_2("w0", ws0)
    gather_1("out0")
    gather_f("q")
    to_plane("meta", meta, in_meta)
    spread_1("x", all_tok, 1)
    spread_2("x", all_tok, 0)
    gather_f("up0")
    gather_2("out0")
    gather_1("q")
    gather_1("out1")
    slice_f("w0", ws0)
    gather_1("up0")
    to_plane("m", mem, all_mem, True)
    for i, (_, ref) in enumerate(given):
        landed("given" + str(i), ref)
    spread_2("x", all_tok, 1)
    landed("meta", in_meta)
    lane = lax.broadcasted_iota(jnp.int32, (8, 128), 1)
    gather_2("q")
    slice_3("w0", ws0)
    gather_1("dn0")
    all_meta[me_slot] = jnp.where(lane < 64, in_meta[0], in_meta[1])
    for cc, yy, xx in plane_peers:
        send("marks", all_meta.at[me_slot], all_meta.at[me_slot], (cc, at(z, yy, xx)))
    gather_3("out0")
    gather_2("up0")
    spread_4("x", all_tok, 0)
    spread_4("x", all_tok, 1)
    slice_2("w1", ws1)
    slice_4("w0", ws0)
    spread_3("x", all_tok)
    gather_3("q")
    spread_1("m", all_mem, 0)
    gathered("out0")
    spread_1("m", all_mem, 1)
    gather_f("out1")
    heads_weights(0, ws0)
    sent_later("marks", all_meta.at[pl.ds(0, 7)])
    gather_1("up1")
    make_masks()
    for i, row in enumerate((0, 1, 4)):
        bias_cols[i] = jnp.transpose(jnp.broadcast_to(bias(row), (128, width)))
    project_heads(all_tok, 0, qt0, k0, kt0, v0, vt0)
    attend(0, qt0, k0, vt0, pt0, l0, ot0, True, "x3", a3, b3)
    gather_f("dn0")
    gather_2("out1")
    attend(1, qt0, k0, vt0, pt0, l0, ot0, True, "x3", a3, b3)
    spread_2("m", all_mem, 0)
    slice_f("w1", ws1)
    spread_2("m", all_mem, 1)
    attend(2, qt0, k0, vt0, pt0, l0, ot0, True, "x3", a3, b3)
    gather_1("dn1")
    attend(3, qt0, k0, vt0, pt0, l0, ot0, True, "x3", a3, b3)
    slice_3("w1", ws1)
    gather_3("up0")
    gather_2("dn0")
    gathered("q")
    gather_f("up1")
    landed("x3", b3)
    words_f = all_tok[me_slot].reshape(here, width).astype(F32)
    branch = tn(b3[...].reshape(width, here), matrix(w_out.at[0])) + bias(2)
    h1, scale0 = norm(words_f * omega[0:1, :] + branch, 0, xh0)
    h1_f[...] = h1
    gather_3("out1")
    h1_low = h1.astype(BF16)
    slice_4("w1", ws1)
    by_head(a4, nn(h1_low, matrix(w_q.at[0])) + bias(3))
    to_heads("x4", a4, b4)
    gather_2("up1")
    gather_f("dn1")
    spread_4("m", all_mem, 0)
    spread_4("m", all_mem, 1)
    landed("x4", b4)
    spread_3("m", all_mem)
    gathered("out1")
    heads_weights(3, ws1)
    gather_2("dn1")
    project_heads(all_mem, 3, None, k1, kt1, v1, vt1)
    for s in range(GROUP):
        qt1[:, s * here : (s + 1) * here] = (b4[s].astype(F32) * 0.125).astype(BF16)
    gather_3("dn0")
    gathered("up0")
    gather_3("up1")
    attend(0, qt1, k1, vt1, pt1, l1, ot1, False, "x5", a5, b5)
    attend(1, qt1, k1, vt1, pt1, l1, ot1, False, "x5", a5, b5)
    attend(2, qt1, k1, vt1, pt1, l1, ot1, False, "x5", a5, b5)
    attend(3, qt1, k1, vt1, pt1, l1, ot1, False, "x5", a5, b5)
    gathered("dn0")
    gather_3("dn1")
    to_plane("cot", cot, in_cot)
    gathered("dn1")
    gathered("up1")
    landed("x5", b5)
    branch = tn(b5[...].reshape(width, here), matrix(w_out.at[1])) + bias(5)
    h2, scale1 = norm(h1_f[...] * omega[1:2, :] + branch, 1, xh1)
    h2_f[...] = h2
    h2_low = h2.astype(BF16)
    feed_up(h2_low, 0)
    feed_up(h2_low, 1)
    first = nn(act[...], matrix(w_dn.at[0]))
    second = nn(act[...], matrix(w_dn.at[1]))
    h3, scale2 = norm(h2_f[...] * omega[2:3, :] + jnp.concatenate([first, second], axis=1) + bias(6), 2, xh2)
    out_res[...] = h3.astype(BF16).reshape(2, 64, width)
    landed("cot", in_cot)
    grad = in_cot[...].reshape(here, width).astype(F32)
    dr, skip = norm_back(grad, 2, xh2, scale2, h2_f[...])
    gf = dr.astype(BF16)
    column(6, gf.astype(F32))
    put(g_dn.at[0], tn(act[...], gf[:, 0:256]))
    back = feed_back(gf, skip)
    scatter_0("dn0")
    dr, skip = norm_back(back, 1, xh1, scale1, h1_f[...])
    gc = dr.astype(BF16)
    column(5, gc.astype(F32))
    by_head(a6, nt(gc, matrix(w_out.at[1])))
    to_heads("x6", a6, b6)
    put(g_out.at[1], nn(b5[...].reshape(width, here), gc))
    scatter_1("dn0")
    put(g_dn.at[1], tn(act[...], gf[:, 256:512]))
    scatter_0("dn1")
    from_plane("res", out_res, o_res)
    put(g_up.at[0], tn(h2_low, gul[:, 0:1024]))
    put(g_up.at[1], tn(h2_low, gul[:, 1024:2048]))
    back = skip
    landed("x6", b6)
    attend_start(b6, l1, ot1)
    scatter_0("up0")
    scatter_1("dn1")
    attend_back(0, qt1, kt1, v1, pt1, False, "x7", a7, b7)
    attend_back(1, qt1, kt1, v1, pt1, False, "x7", a7, b7)
    attend_back(2, qt1, kt1, v1, pt1, False, "x7", a7, b7)
    scatter_2("dn0")
    attend_back(3, qt1, kt1, v1, pt1, False, "x7", a7, b7)
    dt1[0:64, :] = acc_k[...].astype(BF16)
    dt1[64:128, :] = acc_v[...].astype(BF16)
    scatter_1("up0")
    scatter_0("out1")
    scatter_0("up1")
    rows_back(dt1, 3, dx1, 1 - c)
    scatter_1("up1")
    landed("x7", b7)
    merge_0("dm", dx1, dc1)
    rows_back(dt1, 3, dx1, c)
    dq = b7[...].reshape(width, here)
    dq_row = flip(dq)
    scatter_2("dn1")
    column(3, dq_row)
    back = back + nt(dq_row.astype(BF16), matrix(w_q.at[0]))
    slices_back(dt1, all_mem, gs1)
    dr, skip = norm_back(back, 0, xh0, scale0, words_f)
    ga = dr.astype(BF16)
    value_sums(dt1)
    column(2, ga.astype(F32))
    small("s0", sg0, sr0, core_next)
    by_head(a8, nt(ga, matrix(w_out.at[0])))
    to_heads("x8", a8, b8)
    last = skip
    scatter_f("dn0")
    merge_1("dm", dx1, dc1, dp1)
    unslice_0("u1", gs1, cs1)
    put(g_out.at[0], nn(b3[...].reshape(width, here), ga))
    scatter_2("up1")
    scatter_2("up0")
    scatter_1("out1")
    put(g_q.at[0], nt(flip(h1_low).astype(BF16), dq))
    unslice_1("u1", gs1, cs1, zs1)
    scatter_0("out0")
    scatter_f("dn1")
    landed("x8", b8)
    small_add("s0", sr0, sg0, sg1)
    small("s1", sg1, sr1, y_next)
    attend_start(b8, l0, ot0)
    attend_back(0, qt0, kt0, v0, pt0, True, None, None, None)
    attend_back(1, qt0, kt0, v0, pt0, True, None, None, None)
    attend_back(2, qt0, kt0, v0, pt0, True, None, None, None)
    merge_3("dm", dx1, dp1)
    scatter_0("q")
    scatter_3("up1")
    attend_back(3, qt0, kt0, v0, pt0, True, None, None, None)
    dt0[64:128, :] = acc_k[...].astype(BF16)
    dt0[128:192, :] = acc_v[...].astype(BF16)
    rows_back(dt0, 0, dx0, 1 - c)
    unslice_f("u1", gs1, zs1)
    scatter_3("up0")
    scatter_1("q")
    head_sums(dt0)
    scatter_1("out0")
    slices_back(dt0, all_tok, gs0)
    unslice_0("u0", gs0, cs0)
    scatter_f("up1")
    scatter_2("out1")
    small_add("s1", sr1, sg1, sg2)
    merge_0("dx", dx0, dc0)
    small("s2", sg2, sr2, x_next)
    unslice_1("u0", gs0, cs0, zs0)
    small("t0", tg0, tr0, core_next)
    landed("res", o_res)
    small_add("t0", tr0, tg0, tg1)
    out_mem[...] = merge_2("dm", dx1, dp1).astype(BF16).reshape(2, 64, width)
    from_plane("gmem", out_mem, o_mem)
    rows_back(dt0, 0, dx0, c)
    merge_1("dx", dx0, dc0, dp0)
    scatter_2("out0")
    unslice_f("u0", gs0, zs0)
    small_add("s2", sr2, sg2, sg3)
    scatter_f("up0")
    scatter_2("q")
    scatter_3("out1")
    small("t1", tg1, tr1, y_next)
    merge_3("dx", dx0, dp0)
    scatter_3("out0")
    scatter_3("q")
    small_add("t1", tr1, tg1, tg2)
    small_z("sa", sg3, slice(None), tile_own, sra)
    small("t2", tg2, tr2, x_next)
    unslice_2("u1", gs1, zs1, fs1, o_in.at[1, pl.ds(1, 2)])
    scatter_f("out0")
    unslice_2("u0", gs0, zs0, fs0, o_in.at[0])
    scattered("up0")
    small_z("sb", sg3, pl.ds(8, 8), tile_up, srb)
    scatter_f("out1")
    scatter_3("dn1")
    scatter_f("q")
    small_add("t2", tr2, tg2, tg3)
    small_z("ta", tg3, slice(None), tile_own, tra)
    out_tok[...] = (merge_2("dx", dx0, dp0) + last).astype(BF16).reshape(2, 64, width)
    from_plane("gtok", out_tok, o_tok)
    unslice_3("u1", o_in.at[1, pl.ds(1, 2)])
    scattered("up1")
    scatter_3("dn0")
    scattered("q")
    scattered("out0")
    landed("gmem", o_mem)
    scattered("dn1")
    scattered("out1")
    scattered("dn0")
    keep("e3", o_dn, h_dn)
    small_out()
    keep("e2", o_up, h_up)
    unslice_3("u0", o_in.at[0])
    keep("e1", o_out, h_out)
    keep("e0", o_in, h_in)
    landed("gtok", o_tok)
    for i, ref in enumerate((h_in, h_out, h_up, h_dn, h_bias, h_upb, h_gain_o, h_shift_o, h_omega_o)):
        landed("e" + str(i), ref)
    for semaphore, ref, when in pending:
        if when is None:
            wait(semaphore, ref)
        else:

            @pl.when(when)
            def _():
                wait(semaphore, ref)

    for i, total in enumerate(bins):
        if total:
            wait(ss.at[i], gauge.at[pl.ds(0, total // 1024)])
    spans = [2 * line_bytes[0] + 3 * fold_bytes[0], 4 * line_bytes[0] + 3 * fold_bytes[0]]
    assert spans[0] % UNIT == 0 and spans[1] % UNIT == 0

    @pl.when(edge)
    def _():
        wait(ss.at[BINS], gauge.at[pl.ds(0, spans[0] // 1024)])

    @pl.when(jnp.logical_not(edge))
    def _():
        wait(ss.at[BINS], gauge.at[pl.ds(0, spans[1] // 1024)])

    assert len(names) <= NAMES and len(bins) <= BINS and BINS + 1 + len(odd) <= ss.shape[0]


def copy_kernel(*refs):
    count = len(refs) // 2
    for i in range(count):
        refs[count + i][...] = refs[i][...]


def fused_local(
    tokens, memory, cotangent, tgt_lengths, src_lengths, tgt_mask, src_mask, attn_in, attn_out, w_up, w_down,
    biases, up_bias, norm_gain, norm_shift, omega,
):
    any_space = pl.BlockSpec(memory_space=pl.ANY)
    vmem = pl.BlockSpec(memory_space=pltpu.VMEM)
    lines = (CORES, PLANES, YS, XS)
    leads = {"q": 1, "out": 2, "up": 2, "dn": 2}
    shards = {"q": (16, 512), "out": (16, 512), "up": (16, 1024), "dn": (64, 256)}
    kinds = tuple(leads)

    def low(*shape):
        return pltpu.VMEM(shape, BF16)

    def full(*shape):
        return pltpu.VMEM(shape, F32)

    def whole(k):
        return low(leads[k], *lines, *shards[k])

    def halved(k, *middle):
        return low(2, leads[k], *middle, shards[k][0], shards[k][1] // 2)

    params = [full(7, 512), full(1, 2048), full(3, 512), full(3, 512), full(3, 512)]
    results = [(2, 3, 16, 512), (2, 16, 512), (1, 16, 2048), (1, 64, 512), (7, 16), (1, 64), (3, 16), (3, 16), (3, 16)]
    scratch = params + [full(*shape) for shape in results]
    scratch += [whole(k) for k in kinds] * 2
    scratch += [low(leads[k], *lines[1:], *shards[k]) for k in kinds]
    scratch += [halved(k, PLANES, 2) for k in kinds] + [halved(k, PLANES) for k in kinds]
    scratch += [low(3, leads[k], *shards[k]) for k in kinds]
    scratch += [low(n, CORES, PLANES, 4, 16, 128) for n in (3, 2)] * 2
    scratch += [low(n, PLANES, 4, 16, 128) for n in (3, 2)] + [low(3, n, 4, 16, 128) for n in (3, 2)]
    scratch += [full(n, 4, 16, 128) for n in (3, 2)]
    local_rows = low(2, 64, 512)
    marks = [pltpu.VMEM((2, 1, n), jnp.int32) for n in (32, 32, 64, 64)] + [pltpu.VMEM((2, 8, 128), jnp.int32)] * 2
    scratch += [low(GROUP, 2, 64, 512)] * 2 + [local_rows] + marks + [pltpu.VMEM((GROUP, 8, 128), jnp.int32)]
    scratch += [low(GROUP, 2, 64, 512)] * 2 + [low(4, 2, 64, 512)] * 2 + [low(3, 2, 64, 512)] * 2
    scratch += [low(GROUP, 64, 128)] * 12 + [local_rows] * 3
    scratch += [full(24, 512)] * 7 + [full(3, 24, 128), full(3, 8, 128)]
    scratch += [full(8, 512)] * 7 + [full(3, 8, 128)]
    scratch += [full(1024, 128)] * 3 + [full(8, 1024)]
    scratch += ([low(64, 1024)] * 3 + [low(1024, 64)] * 2 + [low(1024, 1024), full(1, 1024), full(64, 1024)]) * 2
    scratch += [low(64, 1024)] + [full(64, 1024)] * 2
    scratch += [low(128, 2048), full(128, 2048), low(128, 2048)] + [full(128, 512)] * 5
    scratch += [low(5, 128, 512), full(3, 512, 128), full(3, 128, 512), low(192, 1024), low(128, 1024), low(2560, 512)]
    scratch += [low(leads[k], *shards[k]) for k in kinds] + [low(n, 4, 16, 128) for n in (3, 2)]
    scratch += [low(2, 2, 1, 1, 2, 64, 128), low(2, 3, 2, 1, 2, 64, 128)]
    scratch += [pltpu.SemaphoreType.DMA((46,)), pltpu.SemaphoreType.DMA((NAMES,))]
    rows = jax.ShapeDtypeStruct((2, 64, 512), BF16)

    def wide_out(*shape):
        return jax.ShapeDtypeStruct(shape, F32)

    outs = pl.pallas_call(
        fused_kernel,
        name="layer",
        out_shape=(rows, rows, rows, *(wide_out(*shape) for shape in results)),
        in_specs=[any_space] * 16,
        out_specs=(any_space,) * 12,
        scratch_shapes=scratch,
        compiler_params=pltpu.CompilerParams(collective_id=0, has_side_effects=True, vmem_limit_bytes=60 * 1024 * 1024),
    )(
        tokens.reshape(2, 64, 512), memory.reshape(2, 64, 512), cotangent.reshape(2, 64, 512),
        tgt_lengths, src_lengths, jnp.transpose(tgt_mask, (0, 2, 1)), jnp.transpose(src_mask, (0, 2, 1)),
        attn_in, attn_out, w_up.reshape(1, 16, 2048), w_down.reshape(1, 64, 512),
        biases, up_bias.reshape(1, 2048), norm_gain, norm_shift, omega,
    )
    outs = pl.pallas_call(
        copy_kernel,
        name="hand_over",
        out_shape=tuple(jax.ShapeDtypeStruct(out.shape, out.dtype) for out in outs),
        in_specs=[vmem] * len(outs),
        out_specs=(vmem,) * len(outs),
    )(*outs)
    shaped = [out.reshape(2, 64, 1, 512) for out in outs[:3]]
    return (
        *shaped, outs[3], outs[4], outs[5].reshape(16, 2048), outs[6].reshape(64, 512), outs[7], outs[8].reshape(64),
        outs[9], outs[10], outs[11],
    )


def solution(mesh):
    if mesh.shape["seq"] != PLANES * YS * XS or mesh.shape["rows"] != CORES:
        return general(mesh)
    return over(mesh, fused_local)
```

```python
import functools
import math

import jax
import jax.numpy as jnp
from jax import lax
from jax.experimental import pallas as pl
from jax.experimental.pallas import tpu as pltpu
from jax.sharding import PartitionSpec as P

HEADS = 8


def norm_block(branch, skip, scale, gain, shift):
    mixed = skip * scale + branch
    centered = mixed - jnp.mean(mixed, axis=-1, keepdims=True)
    variance = jnp.mean(centered * centered, axis=-1, keepdims=True)
    return centered * lax.rsqrt(variance + 1e-05) * gain + shift


def project(values, matrix):
    return jnp.einsum("trd,de->tre", values, matrix, preferred_element_type=jnp.float32)


def project_back(grads, matrix):
    return jnp.einsum("tre,de->trd", grads, matrix, preferred_element_type=jnp.float32)


def matrix_grad(values, grads):
    return jnp.einsum("trd,tre->de", values, grads, preferred_element_type=jnp.float32)


def column_sum(grads):
    return jnp.sum(grads.astype(jnp.float32), axis=(0, 1))


def segment_of(positions, ends):
    return jnp.sum((ends[None, :, :] <= positions[:, None, None]).astype(jnp.int32), axis=-1)


def segment_bounds(first, last, ends):
    lowest = jnp.sum((ends <= first).astype(jnp.int32), axis=-1)
    highest = jnp.sum((ends <= last).astype(jnp.int32), axis=-1)
    return (lowest, highest)


def ranges_share(query_bounds, key_bounds):
    return jnp.any((key_bounds[0] <= query_bounds[1]) & (key_bounds[1] >= query_bounds[0]))


def key_status(positions, real_marks, ends, starts, causal):
    segments = segment_of(positions, ends)
    usable = real_marks > 0.5
    if not causal:
        usable = usable | jnp.any(starts[None, :, :] == positions[:, None, None], axis=-1)
    return (segments, usable)


def permitted(query_pos, query_seg, key_pos, key_seg, usable, causal):
    same = jnp.transpose(query_seg)[:, :, None] == jnp.transpose(key_seg)[:, None, :]
    usable_keys = jnp.transpose(usable)[:, None, :]
    if causal:
        before = (key_pos[None, :] <= query_pos[:, None])[None]
        itself = (key_pos[None, :] == query_pos[:, None])[None]
        return same & before & (usable_keys | itself)
    return same & usable_keys


def block_grads(query_heads, grad_heads, lambdas, key_heads, value_heads, permit):
    scores = (
        jnp.einsum("arhd,brhd->rhab", query_heads, key_heads, preferred_element_type=jnp.float32)
        * 0.125
    )
    weights = jnp.where(permit[:, None], jnp.exp(scores), 0.0)
    spread = jnp.einsum(
        "arhd,brhd->rhab", grad_heads, value_heads, preferred_element_type=jnp.float32
    )
    slopes = weights * (spread + jnp.transpose(lambdas, (1, 2, 0))[..., None])
    return (weights.astype(jnp.bfloat16), slopes.astype(jnp.bfloat16))


def local(
    tokens,
    memory,
    cotangent,
    tgt_lengths,
    src_lengths,
    tgt_mask,
    src_mask,
    attn_in,
    attn_out,
    w_up,
    w_down,
    biases,
    up_bias,
    norm_gain,
    norm_shift,
    omega,
):
    micro_count, tokens_here, rows_here, width = tokens.shape
    head_size = width // HEADS
    my_pos = lax.axis_index("seq") * tokens_here + jnp.arange(tokens_here, dtype=jnp.int32)
    my_first = my_pos[0]
    my_last = my_pos[tokens_here - 1]

    def split_heads(values):
        return values.reshape(values.shape[0], rows_here, HEADS, head_size)

    def zero_heads():
        return jnp.zeros((tokens_here, rows_here, HEADS, head_size), jnp.float32)

    results = []
    grads_words = []
    grads_sources = []
    shares_all = None
    for micro_index in range(micro_count):
        in_weights = lax.all_gather(attn_in, ("rows", "seq"), axis=2, tiled=True)
        out_weights = lax.all_gather(attn_out, ("rows", "seq"), axis=1, tiled=True)
        up_weights = lax.all_gather(w_up, ("rows", "seq"), axis=0, tiled=True)
        down_weights = lax.all_gather(w_down, ("rows", "seq"), axis=0, tiled=True)
        words = tokens[micro_index]
        sources = memory[micro_index]
        words_full = words.astype(jnp.float32)
        tgt_len = tgt_lengths[micro_index]
        src_len = src_lengths[micro_index]
        tgt_ends = jnp.cumsum(tgt_len, axis=-1)
        src_ends = jnp.cumsum(src_len, axis=-1)
        src_starts = src_ends - src_len
        query_seg = segment_of(my_pos, tgt_ends)
        query_bounds = segment_bounds(my_first, my_last, tgt_ends)
        tgt_real = tgt_mask[micro_index].astype(jnp.bfloat16)
        src_real = src_mask[micro_index].astype(jnp.bfloat16)

        def attend(queries, keys, values, real_marks, ends, starts, causal):
            full_keys, full_values, full_real = (
                lax.all_gather(keys, "seq", axis=0, tiled=True),
                lax.all_gather(values, "seq", axis=0, tiled=True),
                lax.all_gather(real_marks, "seq", axis=0, tiled=True),
            )
            length = full_keys.shape[0]
            block = math.gcd(length, 512)
            query_heads = split_heads(queries)

            def step(carry, block_index):
                begin = block_index * block
                shares = ranges_share(query_bounds, segment_bounds(begin, begin + block - 1, ends))

                def step_compute(state):
                    totals, accum = state
                    key_heads = split_heads(lax.dynamic_slice_in_dim(full_keys, begin, block, 0))
                    value_heads = split_heads(
                        lax.dynamic_slice_in_dim(full_values, begin, block, 0)
                    )
                    key_pos = begin + jnp.arange(block, dtype=jnp.int32)
                    key_seg, usable = key_status(
                        key_pos,
                        lax.dynamic_slice_in_dim(full_real, begin, block, 0),
                        ends,
                        starts,
                        causal,
                    )
                    permit = permitted(my_pos, query_seg, key_pos, key_seg, usable, causal)
                    scores = (
                        jnp.einsum(
                            "trhd,krhd->rhtk",
                            query_heads,
                            key_heads,
                            preferred_element_type=jnp.float32,
                        )
                        * 0.125
                    )
                    weights = jnp.where(permit[:, None], jnp.exp(scores), 0.0)
                    totals = totals + jnp.sum(weights, axis=-1)
                    accum = accum + jnp.einsum(
                        "rhtk,krhd->trhd",
                        weights.astype(jnp.bfloat16),
                        value_heads,
                        preferred_element_type=jnp.float32,
                    )
                    return (totals, accum)

                return (lax.cond(shares, step_compute, lambda unchanged: unchanged, carry), None)

            start_carry = (jnp.zeros((rows_here, HEADS, tokens_here), jnp.float32), zero_heads())
            (totals, accum), unused = lax.scan(
                step, start_carry, jnp.arange(length // block, dtype=jnp.int32)
            )
            sums = jnp.transpose(totals, (2, 0, 1))
            output = (accum / sums[..., None]).reshape(tokens_here, rows_here, width)
            return (output, sums, (full_keys, full_values, full_real))

        def attention_back(
            grad_out,
            output,
            sums,
            queries,
            keys,
            values,
            real_marks,
            gathered_set,
            ends,
            starts,
            causal,
        ):
            full_keys, full_values, full_real = gathered_set
            grad_heads = split_heads(grad_out)
            lambdas = -jnp.sum(grad_heads * split_heads(output), axis=-1) / sums
            scaled = (grad_heads / sums[..., None]).astype(jnp.bfloat16)
            query_heads = split_heads(queries)
            length = full_keys.shape[0]
            block = math.gcd(length, 512)

            def query_step(accum, block_index):
                begin = block_index * block
                shares = ranges_share(query_bounds, segment_bounds(begin, begin + block - 1, ends))

                def query_compute(state):
                    key_heads = split_heads(lax.dynamic_slice_in_dim(full_keys, begin, block, 0))
                    value_heads = split_heads(
                        lax.dynamic_slice_in_dim(full_values, begin, block, 0)
                    )
                    key_pos = begin + jnp.arange(block, dtype=jnp.int32)
                    key_seg, usable = key_status(
                        key_pos,
                        lax.dynamic_slice_in_dim(full_real, begin, block, 0),
                        ends,
                        starts,
                        causal,
                    )
                    permit = permitted(my_pos, query_seg, key_pos, key_seg, usable, causal)
                    weights, slopes = block_grads(
                        query_heads, scaled, lambdas, key_heads, value_heads, permit
                    )
                    return (
                        state
                        + jnp.einsum(
                            "rhab,brhd->arhd", slopes, key_heads, preferred_element_type=jnp.float32
                        )
                        * 0.125
                    )

                return (lax.cond(shares, query_compute, lambda unchanged: unchanged, accum), None)

            grad_query, unused = lax.scan(
                query_step, zero_heads(), jnp.arange(length // block, dtype=jnp.int32)
            )
            all_lambdas = lax.all_gather(lambdas, "seq", axis=0, tiled=True)
            local_seg, local_usable = key_status(my_pos, real_marks, ends, starts, causal)
            local_bounds = segment_bounds(my_first, my_last, ends)
            local_keys = split_heads(keys)
            local_values = split_heads(values)
            query_piece = lax.all_gather(queries, "seq", axis=0, tiled=True)
            scaled_piece = lax.all_gather(
                scaled.reshape(tokens_here, rows_here, width), "seq", axis=0, tiled=True
            )
            size = query_piece.shape[0]
            inner = math.gcd(size, 512)

            def inner_step(inner_carry, inner_index):
                offset = inner_index * inner
                piece_first = offset
                shares = ranges_share(
                    segment_bounds(piece_first, piece_first + inner - 1, tgt_ends), local_bounds
                )

                def inner_compute(state):
                    acc_key, acc_value = state
                    query_blk = split_heads(lax.dynamic_slice_in_dim(query_piece, offset, inner, 0))
                    scaled_blk = split_heads(
                        lax.dynamic_slice_in_dim(scaled_piece, offset, inner, 0)
                    )
                    lambda_blk = lax.dynamic_slice_in_dim(all_lambdas, piece_first, inner, 0)
                    query_pos = piece_first + jnp.arange(inner, dtype=jnp.int32)
                    permit = permitted(
                        query_pos,
                        segment_of(query_pos, tgt_ends),
                        my_pos,
                        local_seg,
                        local_usable,
                        causal,
                    )
                    weights, slopes = block_grads(
                        query_blk, scaled_blk, lambda_blk, local_keys, local_values, permit
                    )
                    acc_key = (
                        acc_key
                        + jnp.einsum(
                            "rhab,arhd->brhd", slopes, query_blk, preferred_element_type=jnp.float32
                        )
                        * 0.125
                    )
                    acc_value = acc_value + jnp.einsum(
                        "rhab,arhd->brhd", weights, scaled_blk, preferred_element_type=jnp.float32
                    )
                    return (acc_key, acc_value)

                return (
                    lax.cond(shares, inner_compute, lambda unchanged: unchanged, inner_carry),
                    None,
                )

            folded, unused_inner = lax.scan(
                inner_step, (zero_heads(), zero_heads()), jnp.arange(size // inner, dtype=jnp.int32)
            )
            grad_key, grad_value = folded
            grad_key = grad_key.reshape(tokens_here, rows_here, width)
            grad_value = grad_value.reshape(tokens_here, rows_here, width)
            return (grad_query.reshape(tokens_here, rows_here, width), grad_key, grad_value)

        self_query = (project(words, in_weights[0, 0]) + biases[0]).astype(jnp.bfloat16)
        self_key = project(words, in_weights[0, 1]).astype(jnp.bfloat16)
        self_value = (project(words, in_weights[0, 2]) + biases[1]).astype(jnp.bfloat16)
        heard, heard_sums, self_set = attend(
            self_query, self_key, self_value, tgt_real, tgt_ends, None, True
        )
        heard_low = heard.astype(jnp.bfloat16)
        branch_self = project(heard_low, out_weights[0]) + biases[2]
        hidden_one, pull_one = jax.vjp(
            norm_block, branch_self, words_full, omega[0], norm_gain[0], norm_shift[0]
        )
        hidden_one_low = hidden_one.astype(jnp.bfloat16)
        cross_query = (project(hidden_one_low, in_weights[1, 0]) + biases[3]).astype(jnp.bfloat16)
        cross_key = project(sources, in_weights[1, 1]).astype(jnp.bfloat16)
        cross_value = (project(sources, in_weights[1, 2]) + biases[4]).astype(jnp.bfloat16)
        recalled, recalled_sums, cross_set = attend(
            cross_query, cross_key, cross_value, src_real, src_ends, src_starts, False
        )
        recalled_low = recalled.astype(jnp.bfloat16)
        branch_cross = project(recalled_low, out_weights[1]) + biases[5]
        hidden_two, pull_two = jax.vjp(
            norm_block, branch_cross, hidden_one, omega[1], norm_gain[1], norm_shift[1]
        )
        hidden_two_low = hidden_two.astype(jnp.bfloat16)
        up_pre = project(hidden_two_low, up_weights) + up_bias
        active, pull_active = jax.vjp(jax.nn.gelu, up_pre)
        active_low = active.astype(jnp.bfloat16)
        branch_ffn = project(active_low, down_weights) + biases[6]
        outcome, pull_three = jax.vjp(
            norm_block, branch_ffn, hidden_two, omega[2], norm_gain[2], norm_shift[2]
        )
        grad_result = cotangent[micro_index].astype(jnp.float32)
        grad_ffn, grad_two, omega_three, gain_three, shift_three = pull_three(grad_result)
        grad_ffn_low = grad_ffn.astype(jnp.bfloat16)
        grad_down = matrix_grad(active_low, grad_ffn_low)
        bias_ffn = column_sum(grad_ffn_low)
        grad_up_pre = pull_active(project_back(grad_ffn_low, down_weights))[0].astype(jnp.bfloat16)
        grad_up = matrix_grad(hidden_two_low, grad_up_pre)
        bias_up = column_sum(grad_up_pre)
        grad_two = grad_two + project_back(grad_up_pre, up_weights)
        grad_cross, grad_one, omega_two, gain_two, shift_two = pull_two(grad_two)
        grad_cross_low = grad_cross.astype(jnp.bfloat16)
        grad_out_cross = matrix_grad(recalled_low, grad_cross_low)
        bias_out_cross = column_sum(grad_cross_low)
        grad_recalled = project_back(grad_cross_low, out_weights[1])
        cross_gq, cross_gk, cross_gv = attention_back(
            grad_recalled,
            recalled,
            recalled_sums,
            cross_query,
            cross_key,
            cross_value,
            src_real,
            cross_set,
            src_ends,
            src_starts,
            False,
        )
        cross_gq = cross_gq.astype(jnp.bfloat16)
        cross_gk = cross_gk.astype(jnp.bfloat16)
        cross_gv = cross_gv.astype(jnp.bfloat16)
        grad_cross_query = matrix_grad(hidden_one_low, cross_gq)
        grad_cross_key = matrix_grad(sources, cross_gk)
        grad_cross_value = matrix_grad(sources, cross_gv)
        grad_one = grad_one + project_back(cross_gq, in_weights[1, 0])
        grad_sources = project_back(cross_gk, in_weights[1, 1]) + project_back(
            cross_gv, in_weights[1, 2]
        )
        grad_self, grad_words, omega_one, gain_one, shift_one = pull_one(grad_one)
        grad_self_low = grad_self.astype(jnp.bfloat16)
        grad_out_self = matrix_grad(heard_low, grad_self_low)
        bias_out_self = column_sum(grad_self_low)
        grad_heard = project_back(grad_self_low, out_weights[0])
        self_gq, self_gk, self_gv = attention_back(
            grad_heard,
            heard,
            heard_sums,
            self_query,
            self_key,
            self_value,
            tgt_real,
            self_set,
            tgt_ends,
            None,
            True,
        )
        self_gq = self_gq.astype(jnp.bfloat16)
        self_gk = self_gk.astype(jnp.bfloat16)
        self_gv = self_gv.astype(jnp.bfloat16)
        grad_words = (
            grad_words
            + project_back(self_gq, in_weights[0, 0])
            + project_back(self_gk, in_weights[0, 1])
            + project_back(self_gv, in_weights[0, 2])
        )
        grad_in = jnp.stack(
            [
                jnp.stack(
                    [
                        matrix_grad(words, self_gq),
                        matrix_grad(words, self_gk),
                        matrix_grad(words, self_gv),
                    ]
                ),
                jnp.stack([grad_cross_query, grad_cross_key, grad_cross_value]),
            ]
        )
        grad_out = jnp.stack([grad_out_self, grad_out_cross])
        grad_bias = jnp.stack(
            [
                column_sum(self_gq),
                column_sum(self_gv),
                bias_out_self,
                column_sum(cross_gq),
                column_sum(cross_gv),
                bias_out_cross,
                bias_ffn,
            ]
        )
        grad_gain = jnp.stack([gain_one, gain_two, gain_three])
        grad_shift = jnp.stack([shift_one, shift_two, shift_three])
        grad_omega = jnp.stack([omega_one, omega_two, omega_three])
        grads = (
            grad_in,
            grad_out,
            grad_up,
            grad_down,
            grad_bias,
            bias_up,
            grad_gain,
            grad_shift,
            grad_omega,
        )
        outcome, grad_words, grad_sources, grads = (
            outcome.astype(jnp.bfloat16),
            grad_words.astype(jnp.bfloat16),
            grad_sources.astype(jnp.bfloat16),
            grads,
        )
        results.append(outcome)
        grads_words.append(grad_words)
        grads_sources.append(grad_sources)
        part_shares = (
            lax.psum_scatter(grads[0], ("rows", "seq"), scatter_dimension=2, tiled=True),
            lax.psum_scatter(grads[1], ("rows", "seq"), scatter_dimension=1, tiled=True),
            lax.psum_scatter(grads[2], ("rows", "seq"), scatter_dimension=0, tiled=True),
            lax.psum_scatter(grads[3], ("rows", "seq"), scatter_dimension=0, tiled=True),
            lax.psum_scatter(grads[4], ("rows", "seq"), scatter_dimension=1, tiled=True),
            lax.psum_scatter(grads[5], ("rows", "seq"), scatter_dimension=0, tiled=True),
            lax.psum_scatter(grads[6], ("rows", "seq"), scatter_dimension=1, tiled=True),
            lax.psum_scatter(grads[7], ("rows", "seq"), scatter_dimension=1, tiled=True),
            lax.psum_scatter(grads[8], ("rows", "seq"), scatter_dimension=1, tiled=True),
        )
        shares_all = (
            part_shares if shares_all is None else jax.tree.map(jnp.add, shares_all, part_shares)
        )
    return (jnp.stack(results), jnp.stack(grads_words), jnp.stack(grads_sources)) + tuple(
        shares_all
    )


def over(mesh, function):
    return jax.shard_map(
        function,
        mesh=mesh,
        in_specs=(
            P(None, "seq", "rows", None),
            P(None, "seq", "rows", None),
            P(None, "seq", "rows", None),
            P(None, "rows", None),
            P(None, "rows", None),
            P(None, "seq", "rows"),
            P(None, "seq", "rows"),
            P(None, None, ("rows", "seq"), None),
            P(None, ("rows", "seq"), None),
            P(("rows", "seq"), None),
            P(("rows", "seq"), None),
            P(),
            P(),
            P(),
            P(),
            P(),
        ),
        out_specs=(
            P(None, "seq", "rows", None),
            P(None, "seq", "rows", None),
            P(None, "seq", "rows", None),
            P(None, None, ("rows", "seq"), None),
            P(None, ("rows", "seq"), None),
            P(("rows", "seq"), None),
            P(("rows", "seq"), None),
            P(None, ("rows", "seq")),
            P(("rows", "seq")),
            P(None, ("rows", "seq")),
            P(None, ("rows", "seq")),
            P(None, ("rows", "seq")),
        ),
        check_vma=False,
    )


def general(mesh):
    return over(mesh, local)


MESH = pl.DeviceIdType.MESH
UNIT = 16 * 1024
BINS = 16
NAMES = 208
BETWEEN = ("dn0", "dn1")
BETWEEN_OUT = BETWEEN + ("up1", "out1")
ODD = ("marks", "w0p", "w1p", "u0p", "x3", "x5", "x7", "sa", "sb", "ta", "out11a", "out11b")
F32 = jnp.float32
BF16 = jnp.bfloat16
PLANES, YS, XS, CORES = 4, 2, 2, 2
GROUP = YS * XS * CORES


def nn(left, right):
    return lax.dot_general(left, right, (((1,), (0,)), ((), ())), preferred_element_type=F32)


def nt(left, right):
    return lax.dot_general(left, right, (((1,), (1,)), ((), ())), preferred_element_type=F32)


def tn(left, right):
    return lax.dot_general(left, right, (((0,), (0,)), ((), ())), preferred_element_type=F32)


def flip(value):
    return jnp.transpose(value.astype(F32))


def fused_kernel(
    tok, mem, cot, tgt_len, src_len, tgt_msk, src_msk, s_in, s_out, s_up, s_dn, h_biases, h_up_bias, h_gain, h_shift, h_omega,
    o_res, o_tok, o_mem, h_in, h_out, h_up, h_dn, h_bias, h_upb, h_gain_o, h_shift_o, h_omega_o,
    biases, up_bias, gain, shift, omega, o_in, o_out, o_up, o_dn, o_bias, o_upb, o_gain, o_shift, o_omega,
    w_q, w_out, w_up, w_dn, g_q, g_out, g_up, g_dn,
    c_q, c_out, c_up, c_dn,
    p_q, p_out, p_up, p_dn,
    q_q, q_out, q_up, q_dn,
    z_q, z_out, z_up, z_dn,
    ws0, ws1, gs0, gs1, cs0, cs1, zs0, zs1, fs0, fs1,
    all_tok, all_mem, in_cot, raw_tl, raw_sl, raw_tm, raw_sm, meta, in_meta, all_meta,
    dx0, dx1, dc0, dc1, dp0, dp1,
    a3, b3, a4, b4, a5, b5, a6, b6, a7, b7, a8, b8,
    out_res, out_tok, out_mem,
    sg0, sg1, sg2, sg3, sr0, sr1, sr2, sra, srb,
    tg0, tg1, tg2, tg3, tr0, tr1, tr2, tra,
    code_self, code_cross, key_pos, rows_f,
    qt0, kt0, vt0, k0, v0, pt0, l0, ot0,
    qt1, kt1, vt1, k1, v1, pt1, l1, ot1,
    dnt, acc_k, acc_v,
    act, slope, gul, xh0, xh1, xh2, h1_f, h2_f,
    wt, bias_cols, wz, dt0, dt1, gauge,
    f_q, f_out, f_up, f_dn, f_u0, f_u1, mid_far, mid_line,
    ss, rs,
):
    c = lax.axis_index("rows")
    seq = lax.axis_index("seq")
    z = seq // (YS * XS)
    yx = lax.rem(seq, YS * XS)
    y = yx // XS
    x = lax.rem(yx, XS)
    width = 512
    here = 2 * 64

    def at(zz, yy, xx):
        return zz * (YS * XS) + yy * XS + xx

    def slot(cc, yy, xx):
        return cc * 4 + yy * 2 + xx

    def head(cc, yy, xx):
        return (yy * 2 + xx) * 2 + cc

    me_slot, me_head = slot(c, y, x), head(c, y, x)
    plane_peers = []
    for k in range(1, GROUP):
        cc = 1 - c if k & 4 else c
        yy = 1 - y if k & 2 else y
        xx = 1 - x if k & 1 else x
        plane_peers.append((cc, yy, xx))
    trio = [(1 - y, x), (y, 1 - x), (1 - y, 1 - x)]
    z_peers = [lax.rem(z + k, PLANES) for k in (1, 2, 3)]

    names, expected_bytes = {}, {}
    pending = []
    edge = (z == 0) | (z == PLANES - 1)

    def sem(name):
        return names.setdefault(name, len(names))

    def wait(semaphore, ref):
        pltpu.make_async_copy(ref, ref, semaphore).wait()

    def size(ref):
        return math.prod(ref.shape) * jnp.dtype(ref.dtype).itemsize

    bins = [0]
    odd = {}

    def out_sem(name):
        return ss.at[odd.setdefault(name, BINS + 1 + len(odd))] if name in ODD else ss.at[len(bins) - 1]

    def send(name, src, dst, device, recv=None):
        pltpu.make_async_remote_copy(
            src_ref=src, dst_ref=dst, send_sem=out_sem(name), recv_sem=rs.at[sem(name)] if recv is None else recv,
            device_id=device, device_id_type=MESH,
        ).start()

    def keep(name, src, dst):
        pltpu.make_async_copy(src, dst, rs.at[sem(name)]).start()

    def landed(name, ref):
        wait(rs.at[sem(name)], ref)

    def sent_later(name, ref):
        if name in ODD:
            pending.append((ss.at[odd[name]], ref, None))
            return
        bins[-1] += size(ref)
        assert size(ref) % UNIT == 0, (name, size(ref))
        if bins[-1] > 1024 * UNIT // 16:
            bins.append(0)

    line_bytes = [0]

    def along_z(name, src, block):
        i, j = sem(name + "z"), sem(name + "f")
        for step in (1, -1, 2, -2):
            to = z + step
            far = (z == 0) if step == 2 else (z == PLANES - 1) if step == -2 else None

            @pl.when((to >= 0) & (to < PLANES))
            def _():
                pltpu.make_async_remote_copy(
                    src_ref=src, dst_ref=block(z), send_sem=ss.at[BINS],
                    recv_sem=rs.at[i] if far is None else rs.at[jnp.where(far, j, i)],
                    device_id=(c, at(to, y, x)), device_id_type=MESH,
                ).start()

        line_bytes[0] += size(src)

    def pass_on(name, block):
        for mine, origin, to in ((1, 3, 0), (2, 0, 3)):

            @pl.when(z == mine)
            def _():
                landed(name + "f", block(origin))
                pltpu.make_async_remote_copy(
                    src_ref=block(origin), dst_ref=block(origin), send_sem=ss.at[BINS], recv_sem=rs.at[sem(name + "z")],
                    device_id=(c, at(to, y, x)), device_id_type=MESH,
                ).start()

    fold_bytes = [0]

    def fold_send(name, block, target, to):
        pltpu.make_async_remote_copy(
            src_ref=block, dst_ref=target, send_sem=ss.at[BINS], recv_sem=rs.at[sem(name)],
            device_id=(c, at(to, y, x)), device_id_type=MESH,
        ).start()

    def fold_z(name, block, far, line):
        inner = jnp.where(edge, 0, 1)
        for origin, step, hops in ((0, 3, 1), (3, -3, -1)):

            @pl.when(z == origin)
            def _():
                fold_send(name + "a", block(origin + step), far, origin + hops)
                fold_send(name + "l", block(origin + 2 * hops), line.at[2], origin + 2 * hops)

        for step in (1, -1):
            to = z + step

            @pl.when((to >= 0) & (to < PLANES))
            def _():
                between = jnp.where((to == 0) | (to == PLANES - 1), 0, inner)
                fold_send(name + "l", block(to), line.at[between], to)

        fold_bytes[0] += size(far)

    def fold_f(name, block, far, line):
        for mine, to in ((1, 3), (2, 0)):

            @pl.when(z == mine)
            def _():
                landed(name + "a", far)
                add(block(to), far)
                fold_send(name + "l", block(to), line.at[1], to)

    def fold_sum(name, own, line, result):
        @pl.when(edge)
        def _():
            landed(name + "l", line.at[pl.ds(0, 2)])

        @pl.when(jnp.logical_not(edge))
        def _():
            landed(name + "l", line)

        total = own.astype(F32) + line[0].astype(F32) + line[1].astype(F32)

        @pl.when(edge)
        def _():
            result[...] = total.astype(result.dtype)

        @pl.when(jnp.logical_not(edge))
        def _():
            result[...] = (total + line[2].astype(F32)).astype(result.dtype)

    def line_landed(name, blocks, own):
        @pl.when(edge)
        def _():
            landed(name + "z", blocks(3 + own))

        @pl.when(jnp.logical_not(edge))
        def _():
            landed(name + "z", blocks(2 + own))

    def to_plane(name, src, dst, slotted=False):
        half = lax.rem(z, 2)
        core = z // 2
        if slotted:
            recv = rs.at[jnp.where(half == 0, sem(name + "h0"), sem(name + "h1"))]
            part = dst.at[slot(core, y, x), half]
        else:
            recv = rs.at[sem(name)]
            part = dst.at[half]
        for m in range(2):
            plane = 2 * m + c
            own = (plane == z) & (core == c)
            out = ss.at[odd.setdefault(name + str(m), BINS + 1 + len(odd))]

            @pl.when(own)
            def _():
                pltpu.make_async_copy(src.at[m], part, recv).start()

            @pl.when(jnp.logical_not(own))
            def _():
                pltpu.make_async_remote_copy(
                    src_ref=src.at[m], dst_ref=part, send_sem=out, recv_sem=recv,
                    device_id=(core, at(plane, y, x)), device_id_type=MESH,
                ).start()

            pending.append((out, src.at[m], jnp.logical_not(own)))

    def from_plane(name, src, dst):
        micro, core = z // 2, lax.rem(z, 2)
        recv = rs.at[sem(name)]
        for half in range(2):
            zz = 2 * c + half
            own = (core == c) & (zz == z)
            part = dst.at[micro]
            out = ss.at[odd.setdefault(name + str(half), BINS + 1 + len(odd))]

            @pl.when(own)
            def _():
                pltpu.make_async_copy(src.at[half], part, recv).start()

            @pl.when(jnp.logical_not(own))
            def _():
                pltpu.make_async_remote_copy(
                    src_ref=src.at[half], dst_ref=part, send_sem=out, recv_sem=recv,
                    device_id=(core, at(zz, y, x)), device_id_type=MESH,
                ).start()

            pending.append((out, src.at[half], jnp.logical_not(own)))

    def to_heads(name, src, dst):
        keep(name, src.at[me_head], dst.at[me_slot])
        for cc, yy, xx in plane_peers:
            send(name, src.at[head(cc, yy, xx)], dst.at[me_slot], (cc, at(z, yy, xx)))
        sent_later(name, src.at[pl.ds(0, GROUP - 1)])

    def to_slot(name, src, dst, s):
        device = (s // 4, at(z, (s % 4) // 2, s % 2))
        i = sem(name)
        out = out_sem(name)

        @pl.when(me_slot == s)
        def _():
            pltpu.make_async_copy(src.at[s], dst.at[me_head], rs.at[i]).start()

        @pl.when(me_slot != s)
        def _():
            pltpu.make_async_remote_copy(
                src_ref=src.at[s], dst_ref=dst.at[me_head], send_sem=out, recv_sem=rs.at[i],
                device_id=device, device_id_type=MESH,
            ).start()

    weights = {
        "q": (w_q, s_in.at[1, pl.ds(0, 1)], g_q, c_q, p_q, q_q, z_q, o_in.at[1, pl.ds(0, 1)]),
    }

    for i in range(2):
        one = pl.ds(i, 1)
        refs = (w_out, s_out, g_out, c_out, p_out, q_out, z_out, o_out)
        weights["out" + str(i)] = tuple(
            ref.at[:, one] if ref is p_out or ref is q_out or ref is z_out else ref.at[one] for ref in refs
        )
        refs = (w_up, s_up, g_up, c_up, p_up, q_up, z_up, o_up)
        cols = pl.ds(i * 1024, 1024)
        weights["up" + str(i)] = tuple(
            ref.at[:, one] if ref is p_up or ref is q_up or ref is z_up
            else ref.at[:, :, cols] if ref is s_up or ref is o_up else ref.at[one]
            for ref in refs
        )
        refs = (w_dn, s_dn, g_dn, c_dn, p_dn, q_dn, z_dn, o_dn)
        cols = pl.ds(i * 256, 256)
        weights["dn" + str(i)] = tuple(
            ref.at[:, one] if ref is p_dn or ref is q_dn or ref is z_dn
            else ref.at[:, :, cols] if ref is s_dn or ref is o_dn else ref.at[one]
            for ref in refs
        )

    mids = {g: (mid_far.at[i], mid_line.at[i]) for i, g in enumerate(BETWEEN)}
    fars = {"q": f_q, "u0": f_u0, "u1": f_u1}
    for i in range(2):
        one = pl.ds(i, 1)
        fars["out" + str(i)], fars["up" + str(i)], fars["dn" + str(i)] = f_out.at[one], f_up.at[one], f_dn.at[one]

    def halves(ref):
        cols = ref.shape[-1] // 2
        return pl.ds(0, cols), pl.ds(cols, cols)

    x_next, y_next, core_next = (c, at(z, y, 1 - x)), (c, at(z, 1 - y, x)), (1 - c, seq)

    def gather_z(g):
        full, shard = weights[g][:2]
        if g in BETWEEN_OUT:
            first, second = halves(full)
            whole = s_dn if g[:2] == "dn" else s_up if g[:2] == "up" else shard
            keep(g + "o", shard, full.at[:, c, z, y, x])
            for which, cols, device in (("1a", first, x_next), ("1b", second, y_next)):
                part = full.at[:, c, z, y, x, :, cols]
                send(g + which, whole.at[:, :, shard_cols(g, cols)], part, device)
                sent_later(g + which, part)
            return
        keep(g + "z", shard, full.at[:, c, z, y, x])
        along_z(g, shard, lambda zz: full.at[:, c, zz, y, x])

    def gather_f(g):
        full = weights[g][0]
        if g in BETWEEN_OUT:
            first, second = halves(full)
            pass_on(g + "A", lambda zz: full.at[:, c, zz, y, :, :, first])
            pass_on(g + "B", lambda zz: full.at[:, c, zz, :, x, :, second])
            return
        pass_on(g, lambda zz: full.at[:, c, zz, y, x])

    def gather_1(g):
        full = weights[g][0]
        first, second = halves(full)
        if g in BETWEEN_OUT:
            landed(g + "o", full.at[:, c, z, y, x])
            landed(g + "1a", full.at[:, c, z, y, 1 - x, :, first])
            along_z(g + "A", full.at[:, c, z, y, :, :, first], lambda zz: full.at[:, c, zz, y, :, :, first])
            landed(g + "1b", full.at[:, c, z, 1 - y, x, :, second])
            along_z(g + "B", full.at[:, c, z, :, x, :, second], lambda zz: full.at[:, c, zz, :, x, :, second])
            return
        line_landed(g, lambda n: full.at[:, c, pl.ds(0, n), y, x], 1)
        part = full.at[:, c, :, y, x, :, first]
        send(g + "1a", part, part, x_next)
        sent_later(g + "1a", part)
        part = full.at[:, c, :, y, x, :, second]
        send(g + "1b", part, part, y_next)
        sent_later(g + "1b", part)

    def gather_2(g):
        full = weights[g][0]
        first, second = halves(full)
        if g in BETWEEN_OUT:
            line_landed(g + "A", lambda n: full.at[:, c, pl.ds(0, n), y, :, :, first], 0)
        else:
            landed(g + "1a", full.at[:, c, :, y, 1 - x, :, first])
        part = full.at[:, c, :, y, :, :, first]
        send(g + "2a", part, part, y_next)
        sent_later(g + "2a", part)
        if g in BETWEEN_OUT:
            line_landed(g + "B", lambda n: full.at[:, c, pl.ds(0, n), :, x, :, second], 0)
        else:
            landed(g + "1b", full.at[:, c, :, 1 - y, x, :, second])
        part = full.at[:, c, :, :, x, :, second]
        send(g + "2b", part, part, x_next)
        sent_later(g + "2b", part)

    def shard_cols(g, cols):
        start = int(g[-1]) * {"dn": 256, "up": 1024, "ou": 0}[g[:2]]
        return pl.ds(start + cols.start, cols.size)

    def gather_3(g):
        full = weights[g][0]
        first, second = halves(full)
        landed(g + "2a", full.at[:, c, :, 1 - y, :, :, first])
        landed(g + "2b", full.at[:, c, :, :, 1 - x, :, second])
        send(g + "3", full.at[:, c], full.at[:, c], core_next)
        sent_later(g + "3", full.at[:, c])

    def gathered(g):
        landed(g + "3", weights[g][0].at[:, 1 - c])

    def add(target, other):
        target[...] = (target[...].astype(F32) + other[...].astype(F32)).astype(BF16)

    def scatter_0(g):
        grad, across = weights[g][2:4]
        send(g + "r0", grad.at[:, 1 - c], across, core_next)
        sent_later(g + "r0", across)

    def scatter_1(g):
        grad, across, part = weights[g][2:5]
        first, second = halves(grad)
        landed(g + "r0", across)
        for lead in range(grad.shape[0]):

            @pl.loop(0, PLANES)
            def _(zz):
                add(grad.at[lead, c, zz], across.at[lead, zz])

        send(g + "r1a", grad.at[:, c, :, 1 - y, :, :, first], part.at[0], y_next)
        sent_later(g + "r1a", part.at[0])
        send(g + "r1b", grad.at[:, c, :, :, 1 - x, :, second], part.at[1], x_next)
        sent_later(g + "r1b", part.at[1])

    def scatter_2(g):
        grad, _, part, piece = weights[g][2:6]
        first, second = halves(grad)
        landed(g + "r1a", part.at[0])
        landed(g + "r1b", part.at[1])
        for lead in range(grad.shape[0]):

            @pl.loop(0, PLANES)
            def _(zz):
                add(grad.at[lead, c, zz, y, :, :, first], part.at[0, lead, zz])
                add(grad.at[lead, c, zz, :, x, :, second], part.at[1, lead, zz])

        if g in BETWEEN:
            fold_z(g + "A", lambda zz: grad.at[:, c, zz, y, :, :, first], mids[g][0].at[0, 0], mids[g][1].at[:, 0])
            fold_z(g + "B", lambda zz: grad.at[:, c, zz, :, x, :, second], mids[g][0].at[1, 0], mids[g][1].at[:, 1])
            return
        send(g + "r2a", grad.at[:, c, :, y, 1 - x, :, first], piece.at[0], x_next)
        sent_later(g + "r2a", piece.at[0])
        send(g + "r2b", grad.at[:, c, :, 1 - y, x, :, second], piece.at[1], y_next)
        sent_later(g + "r2b", piece.at[1])

    def scatter_3(g):
        grad, _, _, piece, line = weights[g][2:7]
        first, second = halves(grad)
        if g in BETWEEN:
            fold_sum(g + "A", grad[:, c, z, y, :, :, first], mids[g][1].at[:, 0], grad.at[:, c, z, y, :, :, first])
            send(g + "r2a", grad.at[:, c, z, y, 1 - x, :, first], piece.at[0, :, 0], x_next)
            sent_later(g + "r2a", piece.at[0, :, 0])
            fold_sum(g + "B", grad[:, c, z, :, x, :, second], mids[g][1].at[:, 1], grad.at[:, c, z, :, x, :, second])
            send(g + "r2b", grad.at[:, c, z, 1 - y, x, :, second], piece.at[1, :, 0], y_next)
            sent_later(g + "r2b", piece.at[1, :, 0])
            return
        landed(g + "r2a", piece.at[0])
        landed(g + "r2b", piece.at[1])
        for lead in range(grad.shape[0]):

            @pl.loop(0, PLANES)
            def _(zz):
                add(grad.at[lead, c, zz, y, x, :, first], piece.at[0, lead, zz])
                add(grad.at[lead, c, zz, y, x, :, second], piece.at[1, lead, zz])

        fold_z(g, lambda zz: grad.at[:, c, zz, y, x], fars[g], line)

    def scatter_f(g):
        grad, line = weights[g][2], weights[g][6]
        if g in BETWEEN:
            first, second = halves(grad)
            fold_f(g + "A", lambda zz: grad.at[:, c, zz, y, :, :, first], mids[g][0].at[0, 0], mids[g][1].at[:, 0])
            fold_f(g + "B", lambda zz: grad.at[:, c, zz, :, x, :, second], mids[g][0].at[1, 0], mids[g][1].at[:, 1])
            return
        fold_f(g, lambda zz: grad.at[:, c, zz, y, x], fars[g], line)

    def scattered(g):
        grad, _, _, piece, line, result = weights[g][2:8]
        if g in BETWEEN:
            landed(g + "r2a", piece.at[0, :, 0])
            landed(g + "r2b", piece.at[1, :, 0])
            across = jnp.concatenate([piece[0, :, 0], piece[1, :, 0]], axis=-1)
            result[...] = grad[:, c, z, y, x].astype(F32) + across.astype(F32)
            return
        fold_sum(g, grad[:, c, z, y, x], line, result)

    left, right = pl.ds(0, 256), pl.ds(256, 256)
    y_slot, x_slot, far_slot = slot(c, 1 - y, x), slot(c, y, 1 - x), slot(c, 1 - y, 1 - x)

    def spread_1(name, full, half):
        own = full.at[me_slot, half]
        landed(name + "h" + str(half), own)
        for which, device in (("y", y_next), ("x", x_next), ("c", core_next)):
            which = which if which == "c" else which + str(half)
            send(name + which, own, own, device)
            sent_later(name + which, own)

    def spread_2(name, full, half):
        for which, place, cols, device in (("y", y_slot, right, x_next), ("x", x_slot, left, y_next)):
            part = full.at[place, half]
            landed(name + which + str(half), part)
            half_of = full.at[place, half, :, cols]
            send(name + "q" + which + str(half), half_of, half_of, device)
            sent_later(name + "q" + which + str(half), half_of)
            send(name + "d", part, part, core_next)
            sent_later(name + "d", part)

    def spread_4(name, full, half):
        part = full.at[far_slot, half]
        landed(name + "qy" + str(half), full.at[far_slot, half, :, right])
        landed(name + "qx" + str(half), full.at[far_slot, half, :, left])
        send(name + "d", part, part, core_next)
        sent_later(name + "d", part)

    def spread_3(name, full):
        landed(name + "c", full.at[0])
        landed(name + "d", full.at[pl.ds(0, 3)])

    def merge_0(name, full, across):
        send(name + "c", full.at[pl.ds((1 - c) * 4, 4)], across, core_next)
        sent_later(name + "c", across)

    def merge_1(name, full, across, parts):
        landed(name + "c", across)
        add(full.at[far_slot], across.at[(1 - y) * 2 + 1 - x])
        send(name + "qx", full.at[far_slot, :, :, left], parts.at[2, :, :, left], y_next)
        send(name + "qy", full.at[far_slot, :, :, right], parts.at[2, :, :, right], x_next)
        sent_later(name + "q", parts.at[2])
        add(full.at[x_slot], across.at[y * 2 + 1 - x])
        add(full.at[y_slot], across.at[(1 - y) * 2 + x])
        add(full.at[me_slot], across.at[yx])

    def merge_3(name, full, parts):
        landed(name + "qx", parts.at[2, :, :, left])
        add(full.at[x_slot, :, :, left], parts.at[2, :, :, left])
        send(name + "px", full.at[x_slot], parts.at[0], x_next)
        sent_later(name + "px", parts.at[0])
        landed(name + "qy", parts.at[2, :, :, right])
        add(full.at[y_slot, :, :, right], parts.at[2, :, :, right])
        send(name + "py", full.at[y_slot], parts.at[1], y_next)
        sent_later(name + "py", parts.at[1])

    def merge_2(name, full, parts):
        landed(name + "px", parts.at[0])
        landed(name + "py", parts.at[1])
        total = full[me_slot].astype(F32)
        for k in range(2):
            total = total + parts[k].astype(F32)
        return total.reshape(here, width)

    def tile(index):
        return pl.ds(pl.multiple_of(index * 128, 128), 128)

    def slice_1(name, shard, full):
        keep(name + "p", shard.at[:, :, tile(yx)], full.at[:, c, z, yx])
        for yy, xx in trio:
            send(name + "p", shard.at[:, :, tile(yy * 2 + xx)], full.at[:, c, z, yx], (c, at(z, yy, xx)))
        sent_later(name + "p", full.at[:, c, z, pl.ds(0, 3)])

    def slice_2(name, full):
        landed(name + "p", full.at[:, c, z])
        along_z(name, full.at[:, c, z], lambda zz: full.at[:, c, zz])

    def slice_f(name, full):
        pass_on(name, lambda zz: full.at[:, c, zz])

    def slice_3(name, full):
        line_landed(name, lambda n: full.at[:, c, pl.ds(0, n)], 0)
        send(name + "c", full.at[:, c], full.at[:, c], core_next)
        sent_later(name + "c", full.at[:, c])

    def slice_4(name, full):
        landed(name + "c", full.at[:, 1 - c])

    def unslice_0(name, grad, across):
        send(name + "c", grad.at[:, 1 - c], across, core_next)
        sent_later(name + "c", across)

    def unslice_1(name, grad, across, line):
        landed(name + "c", across)
        for lead in range(grad.shape[0]):
            add(grad.at[lead, c], across.at[lead])
        fold_z(name, lambda zz: grad.at[:, c, zz], fars[name], line)

    def unslice_f(name, grad, line):
        fold_f(name, lambda zz: grad.at[:, c, zz], fars[name], line)

    def unslice_2(name, grad, line, total, result):
        fold_sum(name, grad[:, c, z], line, total)
        for yy, xx in trio:
            send(name + "p", total.at[:, yy * 2 + xx], result.at[:, :, tile(yx)], (c, at(z, yy, xx)))
        sent_later(name + "p", total.at[:, pl.ds(0, 3)])
        result[:, :, tile(yx)] = total[:, yx]

    def unslice_3(name, result):
        landed(name + "p", result.at[:, :, pl.ds(0, 384)])

    def matrix(ref):
        return ref[...].reshape(-1, ref.shape[-1])

    def put(ref, value):
        ref[...] = value.astype(BF16).reshape(ref.shape)

    def norm(r, i, kept):
        centered = r - jnp.mean(r, axis=1, keepdims=True)
        scale = lax.rsqrt(jnp.mean(centered * centered, axis=1, keepdims=True) + 1e-05)
        xhat = centered * scale
        kept[...] = xhat
        return xhat * gain[i : i + 1, :] + shift[i : i + 1, :], scale

    def column(row, value):
        sg0[row : row + 1, :] = jnp.sum(value, axis=0, keepdims=True)

    def norm_back(grad, i, kept, scale, skip):
        xhat = kept[...]
        column(12 + i, grad * xhat)
        column(15 + i, grad)
        dxhat = grad * gain[i : i + 1, :]
        dr = dxhat - jnp.mean(dxhat, axis=1, keepdims=True)
        dr = (dr - xhat * jnp.mean(dxhat * xhat, axis=1, keepdims=True)) * scale
        column(18 + i, dr * skip)
        return dr, dr * omega[i : i + 1, :]

    BLOCK = 256

    def attend(b, queries, keys, values_t, weights_t, sums, outputs, causal, name, target, arrives):
        extent = 512 if causal and b < 2 else 1024
        cols = slice(b * BLOCK, (b + 1) * BLOCK)
        scores = nn(keys[:extent, :], queries[:, cols])
        seg = rows_f[0:1, cols]
        code = (code_self if causal else code_cross)[:extent, :]
        permit = jnp.concatenate([code, code], axis=1) == seg
        if causal:
            pos = key_pos[:extent, :]
            pos = jnp.concatenate([pos, pos], axis=1)
            mine = rows_f[1:2, cols]
            permit = (permit & (pos <= mine)) | (pos == mine)
        weight = jnp.where(permit, jnp.exp(scores), 0.0)
        total = jnp.sum(weight, axis=0, keepdims=True)
        low = weight.astype(BF16)
        weights_t[:extent, cols] = low
        out = nn(values_t[:, :extent], low) / total
        sums[0:1, cols] = total
        outputs[:, cols] = out
        for k in range(2):
            target[2 * b + k] = out[:, k * here : (k + 1) * here].astype(BF16)
            to_slot(name, target, arrives, 2 * b + k)
        if b == 3:
            sent_later(name, target.at[pl.ds(0, GROUP - 1)])

    def attend_start(buffer, sums, outputs):
        acc_k[...] = jnp.zeros_like(acc_k)
        acc_v[...] = jnp.zeros_like(acc_v)
        for s in range(GROUP):
            cols = slice(s * here, (s + 1) * here)
            grad = buffer[s].astype(F32)
            inverse = 1.0 / sums[0:1, cols]
            dnt[:, cols] = (grad * inverse).astype(BF16)
            rows_f[2:3, cols] = -jnp.sum(grad * outputs[:, cols], axis=0, keepdims=True) * inverse

    def attend_back(b, queries, keys_t, values, weights_t, causal, name, target, arrives):
        extent = 512 if causal and b < 2 else 1024
        cols = slice(b * BLOCK, (b + 1) * BLOCK)
        low = weights_t[:extent, cols]
        dn = dnt[:, cols]
        spread = nn(values[:extent, :], dn)
        slopes = (low.astype(F32) * (spread + rows_f[2:3, cols])).astype(BF16)
        block = (nn(keys_t[:, :extent], slopes) * 0.125).astype(BF16)
        if name is None:
            dt0[0:64, cols] = block
        else:
            for k in range(2):
                target[2 * b + k] = block[:, k * here : (k + 1) * here]
                to_slot(name, target, arrives, 2 * b + k)
            if b == 3:
                sent_later(name, target.at[pl.ds(0, GROUP - 1)])
        acc_k[:, :extent] += nt(queries[:, cols], slopes)
        acc_v[:, :extent] += nt(dn, low)

    def by_head(target, value):
        target[...] = flip(value).astype(BF16).reshape(GROUP, 64, here)

    def heads_weights(first, full):
        for j in range(full.shape[0]):
            wt[first + j] = flip(matrix(full.at[j])).astype(BF16)

    own_rows = pl.ds(pl.multiple_of(c * 64, 64), 64)
    own_head = pl.ds(pl.multiple_of(me_head * 64, 64), 64)

    def own_weights(first, count):
        return jnp.concatenate([wt[first + j, own_rows, :] for j in range(count)], axis=0)

    def wide_bias(i):
        col = bias_cols[i, own_head, :]
        return jnp.concatenate([col, col], axis=1)

    def project_heads(rows, first, queries, keys, keys_t, values, values_t):
        count = 2 if queries is None else 3
        own = own_weights(first, count)
        for b in range(4):
            cols = slice(b * 256, (b + 1) * 256)
            out = nt(own, rows[2 * b : 2 * b + 2].reshape(256, width))
            if queries is not None:
                queries[:, cols] = ((out[0:64] + wide_bias(0)).astype(BF16).astype(F32) * 0.125).astype(BF16)
            at_k = 64 * (count - 2)
            block = out[at_k : at_k + 64].astype(BF16)
            keys_t[:, cols] = block
            keys[cols, :] = flip(block).astype(BF16)
            block = (out[at_k + 64 : at_k + 128] + wide_bias(1 if count == 3 else 2)).astype(BF16)
            values_t[:, cols] = block
            values[cols, :] = flip(block).astype(BF16)

    def rows_back(grads_t, first, target, core):
        count = grads_t.shape[0] // 64
        own = own_weights(first, count)
        for b in range(2):
            cols = pl.ds(pl.multiple_of(core * 512 + b * 256, 256), 256)
            out = tn(grads_t[:, cols], own)
            target[pl.ds(core * 4 + b * 2, 2)] = out.astype(BF16).reshape(2, 2, 64, width)

    def slices_back(grads_t, rows, grad):
        count = grads_t.shape[0] // 64
        out = nn(grads_t[...], rows[...].reshape(1024, width))
        wz[...] = jnp.zeros_like(wz)
        for j in range(count):
            wz[j, own_rows, :] = out[j * 64 : (j + 1) * 64]
            put(grad.at[j], jnp.transpose(wz[j]))

    def bias(i):
        return biases[i : i + 1, :]

    def make_masks():
        landed("marks", all_meta.at[pl.ds(0, 7)])
        order = lax.broadcasted_iota(jnp.int32, (1, 1024), 1)
        place = (order // 512) * 512 + lax.rem(order // 64, 2) * 256 + lax.rem(order // 128, 4) * 64 + lax.rem(order, 64)
        place = place.astype(F32)
        marks = [all_meta[s].astype(F32) for s in range(GROUP)]
        tgt_real = jnp.concatenate([mark[0:1, :] for mark in marks], axis=1)
        src_real = jnp.concatenate([mark[1:2, :] for mark in marks], axis=1)
        lower = lax.broadcasted_iota(jnp.int32, (32, 128), 1)
        later = lax.broadcasted_iota(jnp.int32, (32, 128), 0)

        def ends_of(row):
            lengths = jnp.broadcast_to(row, (32, 128))
            ends = jnp.sum(jnp.where(lower <= later, lengths, 0.0), axis=1, keepdims=True)
            starts = jnp.sum(jnp.where(lower < later, lengths, 0.0), axis=1, keepdims=True)
            return ends, starts

        def count(flags):
            return jnp.sum(jnp.where(flags, 1.0, 0.0), axis=0, keepdims=True)

        tgt_ends, _ = ends_of(marks[0][2:3, :])
        src_ends, src_starts = ends_of(marks[0][3:4, :])
        tgt_seg = count(tgt_ends <= place)
        src_seg = count(src_ends <= place)
        src_first = count(src_starts == place)
        self_row = jnp.where(tgt_real > 0.5, tgt_seg, -1.0)
        cross_row = jnp.where((src_real > 0.5) | (src_first > 0.5), src_seg, -1.0)
        rows_f[0:1, :] = tgt_seg
        rows_f[1:2, :] = place
        code_self[...] = jnp.transpose(jnp.broadcast_to(self_row, (128, 1024)))
        code_cross[...] = jnp.transpose(jnp.broadcast_to(cross_row, (128, 1024)))
        key_pos[...] = jnp.transpose(jnp.broadcast_to(place, (128, 1024)))

    def feed_up(rows, i):
        for k in (2 * i, 2 * i + 1):
            cols = slice(k * width, (k + 1) * width)
            inner = slice((k % 2) * width, (k % 2 + 1) * width)
            u = nn(rows, matrix(w_up.at[i, :, :, :, :, :, inner])) + up_bias[0:1, cols]
            square = u * u
            t = jnp.tanh(u * (0.7978845608028654 + 0.035677408136300125 * square))
            act[:, cols] = (0.5 * u * (1.0 + t)).astype(BF16)
            inner = 0.7978845608028654 + 0.10703222440890037 * square
            slope[:, cols] = 0.5 * (1.0 + t) + 0.5 * u * (1.0 - t * t) * inner

    def feed_back(gf, back):
        for k in range(4):
            cols = slice(k * width, (k + 1) * width)
            inner = slice((k % 2) * width, (k % 2 + 1) * width)
            rows = pl.ds(2 * (k % 2), 2)
            gu = nt(gf[:, 0:256], matrix(w_dn.at[0, k // 2, rows]))
            gu = gu + nt(gf[:, 256:512], matrix(w_dn.at[1, k // 2, rows]))
            gu = (gu * slope[:, cols]).astype(BF16)
            gul[:, cols] = gu
            column(8 + k, gu.astype(F32))
            back = back + nt(gu, matrix(w_up.at[k // 2, :, :, :, :, :, inner]))
        return back

    def value_sums(grads_t):
        total = jnp.sum(grads_t[64:128, :].astype(F32), axis=1, keepdims=True)
        bias_cols[0] = jnp.zeros((width, 128), F32)
        bias_cols[0, own_head, :] = jnp.broadcast_to(total, (64, 128))
        sg0[4:5, :] = jnp.transpose(bias_cols[0])[0:1, :]

    def head_sums(grads_t):
        lanes = lax.broadcasted_iota(jnp.int32, (64, 128), 1)
        dq_sum = jnp.sum(grads_t[0:64, :].astype(F32), axis=1, keepdims=True)
        dv_sum = jnp.sum(grads_t[128:192, :].astype(F32), axis=1, keepdims=True)
        bias_cols[0] = jnp.zeros((width, 128), F32)
        bias_cols[0, own_head, :] = jnp.where(lanes == 0, dq_sum, dv_sum)
        tg0[...] = jnp.transpose(bias_cols[0])[0:8, :]

    def small(name, src, dst, device):
        send(name, src, dst, device)
        sent_later(name, dst)

    def small_add(name, arrived, mine, total):
        landed(name, arrived)
        total[...] = mine[...] + arrived[...]

    def small_z(name, src, rows, tile_at, dst):
        for k, zz in enumerate(z_peers):
            send(name, src.at[rows, tile(tile_at(zz))], dst.at[2 - k], (c, at(zz, y, x)))
        sent_later(name, dst)

    def tile_own(zz):
        return c * 2 + zz // 2

    def tile_up(zz):
        return lax.rem(zz, 2) * 2 + y

    def small_sum(name, src, rows, tile_at, dst):
        landed(name, dst)
        return src[rows, tile(tile_at(z))] + dst[0] + dst[1] + dst[2]

    def small_out():
        block = c * 16 + seq
        shift_by = lax.rem(128 - lax.rem(block, 8) * 16, 128)
        turned = pltpu.roll(small_sum("sa", sg3, slice(None), tile_own, sra), shift_by, 1)
        o_bias[...] = turned[0:7, 0:16]
        o_gain[...] = turned[12:15, 0:16]
        o_shift[...] = turned[15:18, 0:16]
        o_omega[...] = turned[18:21, 0:16]
        turned = pltpu.roll(small_sum("ta", tg3, slice(None), tile_own, tra), shift_by, 1)
        o_bias[0:2, :] = turned[0:2, 0:16]
        turned = pltpu.roll(small_sum("sb", sg3, pl.ds(8, 8), tile_up, srb), lax.rem(block, 2) * 64, 1)
        wanted = block // 8
        row = jnp.zeros((1, 64), F32)
        for k in range(4):
            row = row + turned[k : k + 1, 0:64] * (wanted == k).astype(F32)
        o_upb[...] = row
        ends = ((o_bias, h_bias), (o_upb, h_upb), (o_gain, h_gain_o), (o_shift, h_shift_o), (o_omega, h_omega_o))
        for i, (src, dst) in enumerate(ends):
            keep("e" + str(4 + i), src, dst)

    raw = ((raw_tm, tgt_msk), (raw_sm, src_msk), (raw_tl, tgt_len), (raw_sl, src_len))
    for i, (ref, given) in enumerate(raw):
        keep("raw" + str(i), given, ref)
    given = ((h_biases, biases), (h_up_bias, up_bias), (h_gain, gain), (h_shift, shift), (h_omega, omega))
    for i, (src, ref) in enumerate(given):
        keep("given" + str(i), src, ref)
    barrier = pltpu.get_barrier_semaphore()
    greet = [(cc, at(z, yy, xx)) for cc, yy, xx in plane_peers]
    greet += [(cc, at(zz, y, x)) for zz in z_peers for cc in (c, 1 - c)]
    for device in greet:
        pl.semaphore_signal(barrier, inc=1, device_id=device, device_id_type=MESH)
    pl.semaphore_wait(barrier, len(greet))
    gather_z("out0")
    gather_z("up1")
    gather_z("dn1")
    to_plane("x", tok, all_tok, True)
    for i, (ref, _) in enumerate(raw):
        landed("raw" + str(i), ref)
        span = ref.shape[2]
        for m in range(2):
            for start in (0, 64):
                meta[m, i : i + 1, start : start + span] = ref[m]
    gather_z("q")
    slice_1("w0", s_in.at[0], ws0)
    gather_f("out0")
    to_plane("meta", meta, in_meta)
    gather_z("dn0")
    to_plane("m", mem, all_mem, True)
    spread_1("x", all_tok, 0)
    gather_z("up0")
    gather_z("out1")
    spread_1("x", all_tok, 1)
    gather_f("q")
    gather_1("out0")
    landed("meta", in_meta)
    slice_2("w0", ws0)
    lane = lax.broadcasted_iota(jnp.int32, (8, 128), 1)
    all_meta[me_slot] = jnp.where(lane < 64, in_meta[0], in_meta[1])
    gather_1("dn0")
    for cc, yy, xx in plane_peers:
        send("marks", all_meta.at[me_slot], all_meta.at[me_slot], (cc, at(z, yy, xx)))
    spread_1("m", all_mem, 0)
    spread_2("x", all_tok, 0)
    spread_2("x", all_tok, 1)
    spread_1("m", all_mem, 1)
    gather_1("out1")
    gather_f("up0")
    gather_2("out0")
    spread_4("x", all_tok, 0)
    spread_4("x", all_tok, 1)
    gather_1("q")
    slice_1("w1", s_in.at[1, pl.ds(1, 2)], ws1)
    spread_2("m", all_mem, 0)
    slice_f("w0", ws0)
    sent_later("marks", all_meta.at[pl.ds(0, 7)])
    for i, (_, ref) in enumerate(given):
        landed("given" + str(i), ref)
    for i, row in enumerate((0, 1, 4)):
        bias_cols[i] = jnp.transpose(jnp.broadcast_to(bias(row), (128, width)))
    gather_1("up1")
    gather_1("up0")
    gather_2("q")
    slice_2("w1", ws1)
    slice_3("w0", ws0)
    spread_2("m", all_mem, 1)
    make_masks()
    spread_3("x", all_tok)
    gather_3("out0")
    gather_f("dn0")
    gather_2("up0")
    slice_4("w0", ws0)
    gather_1("dn1")
    heads_weights(0, ws0)
    project_heads(all_tok, 0, qt0, k0, kt0, v0, vt0)
    attend(0, qt0, k0, vt0, pt0, l0, ot0, True, "x3", a3, b3)
    gather_f("out1")
    attend(1, qt0, k0, vt0, pt0, l0, ot0, True, "x3", a3, b3)
    attend(2, qt0, k0, vt0, pt0, l0, ot0, True, "x3", a3, b3)
    gather_2("dn0")
    attend(3, qt0, k0, vt0, pt0, l0, ot0, True, "x3", a3, b3)
    spread_4("m", all_mem, 0)
    spread_4("m", all_mem, 1)
    gathered("out0")
    gather_3("up0")
    gather_f("up1")
    gather_3("q")
    gather_2("out1")
    gather_2("up1")
    landed("x3", b3)
    words_f = all_tok[me_slot].reshape(here, width).astype(F32)
    gathered("q")
    slice_f("w1", ws1)
    branch = tn(b3[...].reshape(width, here), matrix(w_out.at[0])) + bias(2)
    spread_3("m", all_mem)
    h1, scale0 = norm(words_f * omega[0:1, :] + branch, 0, xh0)
    h1_f[...] = h1
    gather_f("dn1")
    h1_low = h1.astype(BF16)
    by_head(a4, nn(h1_low, matrix(w_q.at[0])) + bias(3))
    to_heads("x4", a4, b4)
    to_plane("cot", cot, in_cot)
    slice_3("w1", ws1)
    gather_3("dn0")
    gather_2("dn1")
    slice_4("w1", ws1)
    heads_weights(3, ws1)
    project_heads(all_mem, 3, None, k1, kt1, v1, vt1)
    gather_3("out1")
    gathered("up0")
    gather_3("up1")
    landed("x4", b4)
    for s in range(GROUP):
        qt1[:, s * here : (s + 1) * here] = (b4[s].astype(F32) * 0.125).astype(BF16)
    attend(0, qt1, k1, vt1, pt1, l1, ot1, False, "x5", a5, b5)
    attend(1, qt1, k1, vt1, pt1, l1, ot1, False, "x5", a5, b5)
    attend(2, qt1, k1, vt1, pt1, l1, ot1, False, "x5", a5, b5)
    attend(3, qt1, k1, vt1, pt1, l1, ot1, False, "x5", a5, b5)
    gathered("dn0")
    gathered("out1")
    gathered("up1")
    gather_3("dn1")
    gathered("dn1")
    landed("x5", b5)
    branch = tn(b5[...].reshape(width, here), matrix(w_out.at[1])) + bias(5)
    h2, scale1 = norm(h1_f[...] * omega[1:2, :] + branch, 1, xh1)
    h2_f[...] = h2
    h2_low = h2.astype(BF16)
    feed_up(h2_low, 0)
    feed_up(h2_low, 1)
    first = nn(act[...], matrix(w_dn.at[0]))
    second = nn(act[...], matrix(w_dn.at[1]))
    h3, scale2 = norm(h2_f[...] * omega[2:3, :] + jnp.concatenate([first, second], axis=1) + bias(6), 2, xh2)
    out_res[...] = h3.astype(BF16).reshape(2, 64, width)
    landed("cot", in_cot)
    grad = in_cot[...].reshape(here, width).astype(F32)
    dr, skip = norm_back(grad, 2, xh2, scale2, h2_f[...])
    gf = dr.astype(BF16)
    column(6, gf.astype(F32))
    back = feed_back(gf, skip)
    put(g_up.at[0], tn(h2_low, gul[:, 0:1024]))
    scatter_0("up0")
    dr, skip = norm_back(back, 1, xh1, scale1, h1_f[...])
    gc = dr.astype(BF16)
    column(5, gc.astype(F32))
    by_head(a6, nt(gc, matrix(w_out.at[1])))
    to_heads("x6", a6, b6)
    put(g_dn.at[0], tn(act[...], gf[:, 0:256]))
    from_plane("res", out_res, o_res)
    scatter_1("up0")
    put(g_dn.at[1], tn(act[...], gf[:, 256:512]))
    scatter_0("dn1")
    put(g_out.at[1], nn(b5[...].reshape(width, here), gc))
    scatter_0("out1")
    put(g_up.at[1], tn(h2_low, gul[:, 1024:2048]))
    scatter_0("up1")
    back = skip
    landed("x6", b6)
    attend_start(b6, l1, ot1)
    scatter_1("dn1")
    attend_back(0, qt1, kt1, v1, pt1, False, "x7", a7, b7)
    attend_back(1, qt1, kt1, v1, pt1, False, "x7", a7, b7)
    scatter_0("dn0")
    attend_back(2, qt1, kt1, v1, pt1, False, "x7", a7, b7)
    attend_back(3, qt1, kt1, v1, pt1, False, "x7", a7, b7)
    scatter_2("up0")
    scatter_1("dn0")
    dt1[0:64, :] = acc_k[...].astype(BF16)
    scatter_2("dn1")
    dt1[64:128, :] = acc_v[...].astype(BF16)
    scatter_1("out1")
    rows_back(dt1, 3, dx1, 1 - c)
    merge_0("dm", dx1, dc1)
    rows_back(dt1, 3, dx1, c)
    landed("x7", b7)
    dq = b7[...].reshape(width, here)
    slices_back(dt1, all_mem, gs1)
    unslice_0("u1", gs1, cs1)
    dq_row = flip(dq)
    column(3, dq_row)
    value_sums(dt1)
    back = back + nt(dq_row.astype(BF16), matrix(w_q.at[0]))
    dr, skip = norm_back(back, 0, xh0, scale0, words_f)
    ga = dr.astype(BF16)
    column(2, ga.astype(F32))
    scatter_3("up0")
    by_head(a8, nt(ga, matrix(w_out.at[0])))
    to_heads("x8", a8, b8)
    last = skip
    scatter_1("up1")
    put(g_q.at[0], nt(flip(h1_low).astype(BF16), dq))
    scatter_2("dn0")
    merge_1("dm", dx1, dc1, dp1)
    scatter_2("out1")
    small("s0", sg0, sr0, core_next)
    scatter_f("up0")
    put(g_out.at[0], nn(b3[...].reshape(width, here), ga))
    landed("x8", b8)
    attend_start(b8, l0, ot0)
    attend_back(0, qt0, kt0, v0, pt0, True, None, None, None)
    scatter_f("dn1")
    attend_back(1, qt0, kt0, v0, pt0, True, None, None, None)
    unslice_1("u1", gs1, cs1, zs1)
    attend_back(2, qt0, kt0, v0, pt0, True, None, None, None)
    scatter_2("up1")
    scatter_0("q")
    small_add("s0", sr0, sg0, sg1)
    scatter_0("out0")
    scatter_f("dn0")
    small("s1", sg1, sr1, y_next)
    merge_3("dm", dx1, dp1)
    attend_back(3, qt0, kt0, v0, pt0, True, None, None, None)
    dt0[64:128, :] = acc_k[...].astype(BF16)
    dt0[128:192, :] = acc_v[...].astype(BF16)
    scatter_3("out1")
    head_sums(dt0)
    small("t0", tg0, tr0, core_next)
    scatter_3("up1")
    slices_back(dt0, all_tok, gs0)
    unslice_0("u0", gs0, cs0)
    scatter_1("q")
    unslice_f("u1", gs1, zs1)
    small_add("t0", tr0, tg0, tg1)
    small_add("s1", sr1, sg1, sg2)
    small("s2", sg2, sr2, x_next)
    rows_back(dt0, 0, dx0, 1 - c)
    unslice_1("u0", gs0, cs0, zs0)
    merge_0("dx", dx0, dc0)
    small("t1", tg1, tr1, y_next)
    rows_back(dt0, 0, dx0, c)
    scatter_1("out0")
    out_mem[...] = merge_2("dm", dx1, dp1).astype(BF16).reshape(2, 64, width)
    scatter_f("out1")
    from_plane("gmem", out_mem, o_mem)
    merge_1("dx", dx0, dc0, dp0)
    scatter_2("q")
    scattered("up0")
    small_add("t1", tr1, tg1, tg2)
    landed("res", o_res)
    scatter_2("out0")
    scatter_f("up1")
    unslice_f("u0", gs0, zs0)
    small("t2", tg2, tr2, x_next)
    merge_3("dx", dx0, dp0)
    scatter_3("q")
    scatter_3("out0")
    small_add("s2", sr2, sg2, sg3)
    landed("gmem", o_mem)
    small_z("sa", sg3, slice(None), tile_own, sra)
    small_z("sb", sg3, pl.ds(8, 8), tile_up, srb)
    scatter_3("dn0")
    scattered("out1")
    unslice_2("u1", gs1, zs1, fs1, o_in.at[1, pl.ds(1, 2)])
    scatter_3("dn1")
    scattered("up1")
    small_add("t2", tr2, tg2, tg3)
    small_z("ta", tg3, slice(None), tile_own, tra)
    scatter_f("q")
    scatter_f("out0")
    out_tok[...] = (merge_2("dx", dx0, dp0) + last).astype(BF16).reshape(2, 64, width)
    from_plane("gtok", out_tok, o_tok)
    unslice_2("u0", gs0, zs0, fs0, o_in.at[0])
    scattered("q")
    scattered("out0")
    scattered("dn1")
    unslice_3("u1", o_in.at[1, pl.ds(1, 2)])
    scattered("dn0")
    keep("e3", o_dn, h_dn)
    small_out()
    unslice_3("u0", o_in.at[0])
    keep("e2", o_up, h_up)
    keep("e1", o_out, h_out)
    keep("e0", o_in, h_in)
    landed("gtok", o_tok)
    for i, ref in enumerate((h_in, h_out, h_up, h_dn, h_bias, h_upb, h_gain_o, h_shift_o, h_omega_o)):
        landed("e" + str(i), ref)
    for semaphore, ref, when in pending:
        if when is None:
            wait(semaphore, ref)
        else:

            @pl.when(when)
            def _():
                wait(semaphore, ref)

    for i, total in enumerate(bins):
        if total:
            wait(ss.at[i], gauge.at[pl.ds(0, total // 1024)])
    spans = [2 * line_bytes[0] + 3 * fold_bytes[0], 4 * line_bytes[0] + 3 * fold_bytes[0]]
    assert spans[0] % UNIT == 0 and spans[1] % UNIT == 0

    @pl.when(edge)
    def _():
        wait(ss.at[BINS], gauge.at[pl.ds(0, spans[0] // 1024)])

    @pl.when(jnp.logical_not(edge))
    def _():
        wait(ss.at[BINS], gauge.at[pl.ds(0, spans[1] // 1024)])

    assert len(names) <= NAMES and len(bins) <= BINS and BINS + 1 + len(odd) <= ss.shape[0]


def copy_kernel(*refs):
    count = len(refs) // 2
    for i in range(count):
        refs[count + i][...] = refs[i][...]


def fused_local(
    tokens, memory, cotangent, tgt_lengths, src_lengths, tgt_mask, src_mask, attn_in, attn_out, w_up, w_down,
    biases, up_bias, norm_gain, norm_shift, omega,
):
    any_space = pl.BlockSpec(memory_space=pl.ANY)
    vmem = pl.BlockSpec(memory_space=pltpu.VMEM)
    lines = (CORES, PLANES, YS, XS)
    leads = {"q": 1, "out": 2, "up": 2, "dn": 2}
    shards = {"q": (16, 512), "out": (16, 512), "up": (16, 1024), "dn": (64, 256)}
    kinds = tuple(leads)

    def low(*shape):
        return pltpu.VMEM(shape, BF16)

    def full(*shape):
        return pltpu.VMEM(shape, F32)

    def whole(k):
        return low(leads[k], *lines, *shards[k])

    def halved(k, *middle):
        return low(2, leads[k], *middle, shards[k][0], shards[k][1] // 2)

    params = [full(7, 512), full(1, 2048), full(3, 512), full(3, 512), full(3, 512)]
    results = [(2, 3, 16, 512), (2, 16, 512), (1, 16, 2048), (1, 64, 512), (7, 16), (1, 64), (3, 16), (3, 16), (3, 16)]
    scratch = params + [full(*shape) for shape in results]
    scratch += [whole(k) for k in kinds] * 2
    scratch += [low(leads[k], *lines[1:], *shards[k]) for k in kinds]
    scratch += [halved(k, PLANES, 2) for k in kinds] + [halved(k, PLANES) for k in kinds]
    scratch += [low(3, leads[k], *shards[k]) for k in kinds]
    scratch += [low(n, CORES, PLANES, 4, 16, 128) for n in (3, 2)] * 2
    scratch += [low(n, PLANES, 4, 16, 128) for n in (3, 2)] + [low(3, n, 4, 16, 128) for n in (3, 2)]
    scratch += [full(n, 4, 16, 128) for n in (3, 2)]
    local_rows = low(2, 64, 512)
    marks = [pltpu.VMEM((2, 1, n), jnp.int32) for n in (32, 32, 64, 64)] + [pltpu.VMEM((2, 8, 128), jnp.int32)] * 2
    scratch += [low(GROUP, 2, 64, 512)] * 2 + [local_rows] + marks + [pltpu.VMEM((GROUP, 8, 128), jnp.int32)]
    scratch += [low(GROUP, 2, 64, 512)] * 2 + [low(4, 2, 64, 512)] * 2 + [low(3, 2, 64, 512)] * 2
    scratch += [low(GROUP, 64, 128)] * 12 + [local_rows] * 3
    scratch += [full(24, 512)] * 7 + [full(3, 24, 128), full(3, 8, 128)]
    scratch += [full(8, 512)] * 7 + [full(3, 8, 128)]
    scratch += [full(1024, 128)] * 3 + [full(8, 1024)]
    scratch += ([low(64, 1024)] * 3 + [low(1024, 64)] * 2 + [low(1024, 1024), full(1, 1024), full(64, 1024)]) * 2
    scratch += [low(64, 1024)] + [full(64, 1024)] * 2
    scratch += [low(128, 2048), full(128, 2048), low(128, 2048)] + [full(128, 512)] * 5
    scratch += [low(5, 128, 512), full(3, 512, 128), full(3, 128, 512), low(192, 1024), low(128, 1024), low(2560, 512)]
    scratch += [low(leads[k], *shards[k]) for k in kinds] + [low(n, 4, 16, 128) for n in (3, 2)]
    scratch += [low(2, 2, 1, 1, 2, 64, 128), low(2, 3, 2, 1, 2, 64, 128)]
    scratch += [pltpu.SemaphoreType.DMA((46,)), pltpu.SemaphoreType.DMA((NAMES,))]
    rows = jax.ShapeDtypeStruct((2, 64, 512), BF16)

    def wide_out(*shape):
        return jax.ShapeDtypeStruct(shape, F32)

    outs = pl.pallas_call(
        fused_kernel,
        name="layer",
        out_shape=(rows, rows, rows, *(wide_out(*shape) for shape in results)),
        in_specs=[any_space] * 16,
        out_specs=(any_space,) * 12,
        scratch_shapes=scratch,
        compiler_params=pltpu.CompilerParams(collective_id=0, has_side_effects=True, vmem_limit_bytes=60 * 1024 * 1024),
    )(
        tokens.reshape(2, 64, 512), memory.reshape(2, 64, 512), cotangent.reshape(2, 64, 512),
        tgt_lengths, src_lengths, jnp.transpose(tgt_mask, (0, 2, 1)), jnp.transpose(src_mask, (0, 2, 1)),
        attn_in, attn_out, w_up.reshape(1, 16, 2048), w_down.reshape(1, 64, 512),
        biases, up_bias.reshape(1, 2048), norm_gain, norm_shift, omega,
    )
    outs = pl.pallas_call(
        copy_kernel,
        name="hand_over",
        out_shape=tuple(jax.ShapeDtypeStruct(out.shape, out.dtype) for out in outs),
        in_specs=[vmem] * len(outs),
        out_specs=(vmem,) * len(outs),
    )(*outs)
    shaped = [out.reshape(2, 64, 1, 512) for out in outs[:3]]
    return (
        *shaped, outs[3], outs[4], outs[5].reshape(16, 2048), outs[6].reshape(64, 512), outs[7], outs[8].reshape(64),
        outs[9], outs[10], outs[11],
    )


def solution(mesh):
    if mesh.shape["seq"] != PLANES * YS * XS or mesh.shape["rows"] != CORES:
        return general(mesh)
    return over(mesh, fused_local)
```

```python
import functools
import math

import jax
import jax.numpy as jnp
from jax import lax
from jax.experimental import pallas as pl
from jax.experimental.pallas import tpu as pltpu
from jax.sharding import PartitionSpec as P

HEADS = 8


def norm_block(branch, skip, scale, gain, shift):
    mixed = skip * scale + branch
    centered = mixed - jnp.mean(mixed, axis=-1, keepdims=True)
    variance = jnp.mean(centered * centered, axis=-1, keepdims=True)
    return centered * lax.rsqrt(variance + 1e-05) * gain + shift


def project(values, matrix):
    return jnp.einsum("trd,de->tre", values, matrix, preferred_element_type=jnp.float32)


def project_back(grads, matrix):
    return jnp.einsum("tre,de->trd", grads, matrix, preferred_element_type=jnp.float32)


def matrix_grad(values, grads):
    return jnp.einsum("trd,tre->de", values, grads, preferred_element_type=jnp.float32)


def column_sum(grads):
    return jnp.sum(grads.astype(jnp.float32), axis=(0, 1))


def segment_of(positions, ends):
    return jnp.sum((ends[None, :, :] <= positions[:, None, None]).astype(jnp.int32), axis=-1)


def segment_bounds(first, last, ends):
    lowest = jnp.sum((ends <= first).astype(jnp.int32), axis=-1)
    highest = jnp.sum((ends <= last).astype(jnp.int32), axis=-1)
    return (lowest, highest)


def ranges_share(query_bounds, key_bounds):
    return jnp.any((key_bounds[0] <= query_bounds[1]) & (key_bounds[1] >= query_bounds[0]))


def key_status(positions, real_marks, ends, starts, causal):
    segments = segment_of(positions, ends)
    usable = real_marks > 0.5
    if not causal:
        usable = usable | jnp.any(starts[None, :, :] == positions[:, None, None], axis=-1)
    return (segments, usable)


def permitted(query_pos, query_seg, key_pos, key_seg, usable, causal):
    same = jnp.transpose(query_seg)[:, :, None] == jnp.transpose(key_seg)[:, None, :]
    usable_keys = jnp.transpose(usable)[:, None, :]
    if causal:
        before = (key_pos[None, :] <= query_pos[:, None])[None]
        itself = (key_pos[None, :] == query_pos[:, None])[None]
        return same & before & (usable_keys | itself)
    return same & usable_keys


def block_grads(query_heads, grad_heads, lambdas, key_heads, value_heads, permit):
    scores = (
        jnp.einsum("arhd,brhd->rhab", query_heads, key_heads, preferred_element_type=jnp.float32)
        * 0.125
    )
    weights = jnp.where(permit[:, None], jnp.exp(scores), 0.0)
    spread = jnp.einsum(
        "arhd,brhd->rhab", grad_heads, value_heads, preferred_element_type=jnp.float32
    )
    slopes = weights * (spread + jnp.transpose(lambdas, (1, 2, 0))[..., None])
    return (weights.astype(jnp.bfloat16), slopes.astype(jnp.bfloat16))


def local(
    tokens,
    memory,
    cotangent,
    tgt_lengths,
    src_lengths,
    tgt_mask,
    src_mask,
    attn_in,
    attn_out,
    w_up,
    w_down,
    biases,
    up_bias,
    norm_gain,
    norm_shift,
    omega,
):
    micro_count, tokens_here, rows_here, width = tokens.shape
    head_size = width // HEADS
    my_pos = lax.axis_index("seq") * tokens_here + jnp.arange(tokens_here, dtype=jnp.int32)
    my_first = my_pos[0]
    my_last = my_pos[tokens_here - 1]

    def split_heads(values):
        return values.reshape(values.shape[0], rows_here, HEADS, head_size)

    def zero_heads():
        return jnp.zeros((tokens_here, rows_here, HEADS, head_size), jnp.float32)

    results = []
    grads_words = []
    grads_sources = []
    shares_all = None
    for micro_index in range(micro_count):
        in_weights = lax.all_gather(attn_in, ("rows", "seq"), axis=2, tiled=True)
        out_weights = lax.all_gather(attn_out, ("rows", "seq"), axis=1, tiled=True)
        up_weights = lax.all_gather(w_up, ("rows", "seq"), axis=0, tiled=True)
        down_weights = lax.all_gather(w_down, ("rows", "seq"), axis=0, tiled=True)
        words = tokens[micro_index]
        sources = memory[micro_index]
        words_full = words.astype(jnp.float32)
        tgt_len = tgt_lengths[micro_index]
        src_len = src_lengths[micro_index]
        tgt_ends = jnp.cumsum(tgt_len, axis=-1)
        src_ends = jnp.cumsum(src_len, axis=-1)
        src_starts = src_ends - src_len
        query_seg = segment_of(my_pos, tgt_ends)
        query_bounds = segment_bounds(my_first, my_last, tgt_ends)
        tgt_real = tgt_mask[micro_index].astype(jnp.bfloat16)
        src_real = src_mask[micro_index].astype(jnp.bfloat16)

        def attend(queries, keys, values, real_marks, ends, starts, causal):
            full_keys, full_values, full_real = (
                lax.all_gather(keys, "seq", axis=0, tiled=True),
                lax.all_gather(values, "seq", axis=0, tiled=True),
                lax.all_gather(real_marks, "seq", axis=0, tiled=True),
            )
            length = full_keys.shape[0]
            block = math.gcd(length, 512)
            query_heads = split_heads(queries)

            def step(carry, block_index):
                begin = block_index * block
                shares = ranges_share(query_bounds, segment_bounds(begin, begin + block - 1, ends))

                def step_compute(state):
                    totals, accum = state
                    key_heads = split_heads(lax.dynamic_slice_in_dim(full_keys, begin, block, 0))
                    value_heads = split_heads(
                        lax.dynamic_slice_in_dim(full_values, begin, block, 0)
                    )
                    key_pos = begin + jnp.arange(block, dtype=jnp.int32)
                    key_seg, usable = key_status(
                        key_pos,
                        lax.dynamic_slice_in_dim(full_real, begin, block, 0),
                        ends,
                        starts,
                        causal,
                    )
                    permit = permitted(my_pos, query_seg, key_pos, key_seg, usable, causal)
                    scores = (
                        jnp.einsum(
                            "trhd,krhd->rhtk",
                            query_heads,
                            key_heads,
                            preferred_element_type=jnp.float32,
                        )
                        * 0.125
                    )
                    weights = jnp.where(permit[:, None], jnp.exp(scores), 0.0)
                    totals = totals + jnp.sum(weights, axis=-1)
                    accum = accum + jnp.einsum(
                        "rhtk,krhd->trhd",
                        weights.astype(jnp.bfloat16),
                        value_heads,
                        preferred_element_type=jnp.float32,
                    )
                    return (totals, accum)

                return (lax.cond(shares, step_compute, lambda unchanged: unchanged, carry), None)

            start_carry = (jnp.zeros((rows_here, HEADS, tokens_here), jnp.float32), zero_heads())
            (totals, accum), unused = lax.scan(
                step, start_carry, jnp.arange(length // block, dtype=jnp.int32)
            )
            sums = jnp.transpose(totals, (2, 0, 1))
            output = (accum / sums[..., None]).reshape(tokens_here, rows_here, width)
            return (output, sums, (full_keys, full_values, full_real))

        def attention_back(
            grad_out,
            output,
            sums,
            queries,
            keys,
            values,
            real_marks,
            gathered_set,
            ends,
            starts,
            causal,
        ):
            full_keys, full_values, full_real = gathered_set
            grad_heads = split_heads(grad_out)
            lambdas = -jnp.sum(grad_heads * split_heads(output), axis=-1) / sums
            scaled = (grad_heads / sums[..., None]).astype(jnp.bfloat16)
            query_heads = split_heads(queries)
            length = full_keys.shape[0]
            block = math.gcd(length, 512)

            def query_step(accum, block_index):
                begin = block_index * block
                shares = ranges_share(query_bounds, segment_bounds(begin, begin + block - 1, ends))

                def query_compute(state):
                    key_heads = split_heads(lax.dynamic_slice_in_dim(full_keys, begin, block, 0))
                    value_heads = split_heads(
                        lax.dynamic_slice_in_dim(full_values, begin, block, 0)
                    )
                    key_pos = begin + jnp.arange(block, dtype=jnp.int32)
                    key_seg, usable = key_status(
                        key_pos,
                        lax.dynamic_slice_in_dim(full_real, begin, block, 0),
                        ends,
                        starts,
                        causal,
                    )
                    permit = permitted(my_pos, query_seg, key_pos, key_seg, usable, causal)
                    weights, slopes = block_grads(
                        query_heads, scaled, lambdas, key_heads, value_heads, permit
                    )
                    return (
                        state
                        + jnp.einsum(
                            "rhab,brhd->arhd", slopes, key_heads, preferred_element_type=jnp.float32
                        )
                        * 0.125
                    )

                return (lax.cond(shares, query_compute, lambda unchanged: unchanged, accum), None)

            grad_query, unused = lax.scan(
                query_step, zero_heads(), jnp.arange(length // block, dtype=jnp.int32)
            )
            all_lambdas = lax.all_gather(lambdas, "seq", axis=0, tiled=True)
            local_seg, local_usable = key_status(my_pos, real_marks, ends, starts, causal)
            local_bounds = segment_bounds(my_first, my_last, ends)
            local_keys = split_heads(keys)
            local_values = split_heads(values)
            query_piece = lax.all_gather(queries, "seq", axis=0, tiled=True)
            scaled_piece = lax.all_gather(
                scaled.reshape(tokens_here, rows_here, width), "seq", axis=0, tiled=True
            )
            size = query_piece.shape[0]
            inner = math.gcd(size, 512)

            def inner_step(inner_carry, inner_index):
                offset = inner_index * inner
                piece_first = offset
                shares = ranges_share(
                    segment_bounds(piece_first, piece_first + inner - 1, tgt_ends), local_bounds
                )

                def inner_compute(state):
                    acc_key, acc_value = state
                    query_blk = split_heads(lax.dynamic_slice_in_dim(query_piece, offset, inner, 0))
                    scaled_blk = split_heads(
                        lax.dynamic_slice_in_dim(scaled_piece, offset, inner, 0)
                    )
                    lambda_blk = lax.dynamic_slice_in_dim(all_lambdas, piece_first, inner, 0)
                    query_pos = piece_first + jnp.arange(inner, dtype=jnp.int32)
                    permit = permitted(
                        query_pos,
                        segment_of(query_pos, tgt_ends),
                        my_pos,
                        local_seg,
                        local_usable,
                        causal,
                    )
                    weights, slopes = block_grads(
                        query_blk, scaled_blk, lambda_blk, local_keys, local_values, permit
                    )
                    acc_key = (
                        acc_key
                        + jnp.einsum(
                            "rhab,arhd->brhd", slopes, query_blk, preferred_element_type=jnp.float32
                        )
                        * 0.125
                    )
                    acc_value = acc_value + jnp.einsum(
                        "rhab,arhd->brhd", weights, scaled_blk, preferred_element_type=jnp.float32
                    )
                    return (acc_key, acc_value)

                return (
                    lax.cond(shares, inner_compute, lambda unchanged: unchanged, inner_carry),
                    None,
                )

            folded, unused_inner = lax.scan(
                inner_step, (zero_heads(), zero_heads()), jnp.arange(size // inner, dtype=jnp.int32)
            )
            grad_key, grad_value = folded
            grad_key = grad_key.reshape(tokens_here, rows_here, width)
            grad_value = grad_value.reshape(tokens_here, rows_here, width)
            return (grad_query.reshape(tokens_here, rows_here, width), grad_key, grad_value)

        self_query = (project(words, in_weights[0, 0]) + biases[0]).astype(jnp.bfloat16)
        self_key = project(words, in_weights[0, 1]).astype(jnp.bfloat16)
        self_value = (project(words, in_weights[0, 2]) + biases[1]).astype(jnp.bfloat16)
        heard, heard_sums, self_set = attend(
            self_query, self_key, self_value, tgt_real, tgt_ends, None, True
        )
        heard_low = heard.astype(jnp.bfloat16)
        branch_self = project(heard_low, out_weights[0]) + biases[2]
        hidden_one, pull_one = jax.vjp(
            norm_block, branch_self, words_full, omega[0], norm_gain[0], norm_shift[0]
        )
        hidden_one_low = hidden_one.astype(jnp.bfloat16)
        cross_query = (project(hidden_one_low, in_weights[1, 0]) + biases[3]).astype(jnp.bfloat16)
        cross_key = project(sources, in_weights[1, 1]).astype(jnp.bfloat16)
        cross_value = (project(sources, in_weights[1, 2]) + biases[4]).astype(jnp.bfloat16)
        recalled, recalled_sums, cross_set = attend(
            cross_query, cross_key, cross_value, src_real, src_ends, src_starts, False
        )
        recalled_low = recalled.astype(jnp.bfloat16)
        branch_cross = project(recalled_low, out_weights[1]) + biases[5]
        hidden_two, pull_two = jax.vjp(
            norm_block, branch_cross, hidden_one, omega[1], norm_gain[1], norm_shift[1]
        )
        hidden_two_low = hidden_two.astype(jnp.bfloat16)
        up_pre = project(hidden_two_low, up_weights) + up_bias
        active, pull_active = jax.vjp(jax.nn.gelu, up_pre)
        active_low = active.astype(jnp.bfloat16)
        branch_ffn = project(active_low, down_weights) + biases[6]
        outcome, pull_three = jax.vjp(
            norm_block, branch_ffn, hidden_two, omega[2], norm_gain[2], norm_shift[2]
        )
        grad_result = cotangent[micro_index].astype(jnp.float32)
        grad_ffn, grad_two, omega_three, gain_three, shift_three = pull_three(grad_result)
        grad_ffn_low = grad_ffn.astype(jnp.bfloat16)
        grad_down = matrix_grad(active_low, grad_ffn_low)
        bias_ffn = column_sum(grad_ffn_low)
        grad_up_pre = pull_active(project_back(grad_ffn_low, down_weights))[0].astype(jnp.bfloat16)
        grad_up = matrix_grad(hidden_two_low, grad_up_pre)
        bias_up = column_sum(grad_up_pre)
        grad_two = grad_two + project_back(grad_up_pre, up_weights)
        grad_cross, grad_one, omega_two, gain_two, shift_two = pull_two(grad_two)
        grad_cross_low = grad_cross.astype(jnp.bfloat16)
        grad_out_cross = matrix_grad(recalled_low, grad_cross_low)
        bias_out_cross = column_sum(grad_cross_low)
        grad_recalled = project_back(grad_cross_low, out_weights[1])
        cross_gq, cross_gk, cross_gv = attention_back(
            grad_recalled,
            recalled,
            recalled_sums,
            cross_query,
            cross_key,
            cross_value,
            src_real,
            cross_set,
            src_ends,
            src_starts,
            False,
        )
        cross_gq = cross_gq.astype(jnp.bfloat16)
        cross_gk = cross_gk.astype(jnp.bfloat16)
        cross_gv = cross_gv.astype(jnp.bfloat16)
        grad_cross_query = matrix_grad(hidden_one_low, cross_gq)
        grad_cross_key = matrix_grad(sources, cross_gk)
        grad_cross_value = matrix_grad(sources, cross_gv)
        grad_one = grad_one + project_back(cross_gq, in_weights[1, 0])
        grad_sources = project_back(cross_gk, in_weights[1, 1]) + project_back(
            cross_gv, in_weights[1, 2]
        )
        grad_self, grad_words, omega_one, gain_one, shift_one = pull_one(grad_one)
        grad_self_low = grad_self.astype(jnp.bfloat16)
        grad_out_self = matrix_grad(heard_low, grad_self_low)
        bias_out_self = column_sum(grad_self_low)
        grad_heard = project_back(grad_self_low, out_weights[0])
        self_gq, self_gk, self_gv = attention_back(
            grad_heard,
            heard,
            heard_sums,
            self_query,
            self_key,
            self_value,
            tgt_real,
            self_set,
            tgt_ends,
            None,
            True,
        )
        self_gq = self_gq.astype(jnp.bfloat16)
        self_gk = self_gk.astype(jnp.bfloat16)
        self_gv = self_gv.astype(jnp.bfloat16)
        grad_words = (
            grad_words
            + project_back(self_gq, in_weights[0, 0])
            + project_back(self_gk, in_weights[0, 1])
            + project_back(self_gv, in_weights[0, 2])
        )
        grad_in = jnp.stack(
            [
                jnp.stack(
                    [
                        matrix_grad(words, self_gq),
                        matrix_grad(words, self_gk),
                        matrix_grad(words, self_gv),
                    ]
                ),
                jnp.stack([grad_cross_query, grad_cross_key, grad_cross_value]),
            ]
        )
        grad_out = jnp.stack([grad_out_self, grad_out_cross])
        grad_bias = jnp.stack(
            [
                column_sum(self_gq),
                column_sum(self_gv),
                bias_out_self,
                column_sum(cross_gq),
                column_sum(cross_gv),
                bias_out_cross,
                bias_ffn,
            ]
        )
        grad_gain = jnp.stack([gain_one, gain_two, gain_three])
        grad_shift = jnp.stack([shift_one, shift_two, shift_three])
        grad_omega = jnp.stack([omega_one, omega_two, omega_three])
        grads = (
            grad_in,
            grad_out,
            grad_up,
            grad_down,
            grad_bias,
            bias_up,
            grad_gain,
            grad_shift,
            grad_omega,
        )
        outcome, grad_words, grad_sources, grads = (
            outcome.astype(jnp.bfloat16),
            grad_words.astype(jnp.bfloat16),
            grad_sources.astype(jnp.bfloat16),
            grads,
        )
        results.append(outcome)
        grads_words.append(grad_words)
        grads_sources.append(grad_sources)
        part_shares = (
            lax.psum_scatter(grads[0], ("rows", "seq"), scatter_dimension=2, tiled=True),
            lax.psum_scatter(grads[1], ("rows", "seq"), scatter_dimension=1, tiled=True),
            lax.psum_scatter(grads[2], ("rows", "seq"), scatter_dimension=0, tiled=True),
            lax.psum_scatter(grads[3], ("rows", "seq"), scatter_dimension=0, tiled=True),
            lax.psum_scatter(grads[4], ("rows", "seq"), scatter_dimension=1, tiled=True),
            lax.psum_scatter(grads[5], ("rows", "seq"), scatter_dimension=0, tiled=True),
            lax.psum_scatter(grads[6], ("rows", "seq"), scatter_dimension=1, tiled=True),
            lax.psum_scatter(grads[7], ("rows", "seq"), scatter_dimension=1, tiled=True),
            lax.psum_scatter(grads[8], ("rows", "seq"), scatter_dimension=1, tiled=True),
        )
        shares_all = (
            part_shares if shares_all is None else jax.tree.map(jnp.add, shares_all, part_shares)
        )
    return (jnp.stack(results), jnp.stack(grads_words), jnp.stack(grads_sources)) + tuple(
        shares_all
    )


def over(mesh, function):
    return jax.shard_map(
        function,
        mesh=mesh,
        in_specs=(
            P(None, "seq", "rows", None),
            P(None, "seq", "rows", None),
            P(None, "seq", "rows", None),
            P(None, "rows", None),
            P(None, "rows", None),
            P(None, "seq", "rows"),
            P(None, "seq", "rows"),
            P(None, None, ("rows", "seq"), None),
            P(None, ("rows", "seq"), None),
            P(("rows", "seq"), None),
            P(("rows", "seq"), None),
            P(),
            P(),
            P(),
            P(),
            P(),
        ),
        out_specs=(
            P(None, "seq", "rows", None),
            P(None, "seq", "rows", None),
            P(None, "seq", "rows", None),
            P(None, None, ("rows", "seq"), None),
            P(None, ("rows", "seq"), None),
            P(("rows", "seq"), None),
            P(("rows", "seq"), None),
            P(None, ("rows", "seq")),
            P(("rows", "seq")),
            P(None, ("rows", "seq")),
            P(None, ("rows", "seq")),
            P(None, ("rows", "seq")),
        ),
        check_vma=False,
    )


def general(mesh):
    return over(mesh, local)


MESH = pl.DeviceIdType.MESH
UNIT = 16 * 1024
BINS = 16
NAMES = 208
BETWEEN = ("dn0", "dn1")
BETWEEN_OUT = BETWEEN + ("up1", "out1")
ODD = ("marks", "w0p", "w1p", "u0p", "x3", "x5", "x7", "sa", "sb", "ta", "out11a", "out11b")
F32 = jnp.float32
BF16 = jnp.bfloat16
PLANES, YS, XS, CORES = 4, 2, 2, 2
GROUP = YS * XS * CORES


def nn(left, right):
    return lax.dot_general(left, right, (((1,), (0,)), ((), ())), preferred_element_type=F32)


def nt(left, right):
    return lax.dot_general(left, right, (((1,), (1,)), ((), ())), preferred_element_type=F32)


def tn(left, right):
    return lax.dot_general(left, right, (((0,), (0,)), ((), ())), preferred_element_type=F32)


def flip(value):
    return jnp.transpose(value.astype(F32))


def fused_kernel(
    tok, mem, cot, tgt_len, src_len, tgt_msk, src_msk, s_in, s_out, s_up, s_dn, h_biases, h_up_bias, h_gain, h_shift, h_omega,
    o_res, o_tok, o_mem, h_in, h_out, h_up, h_dn, h_bias, h_upb, h_gain_o, h_shift_o, h_omega_o,
    biases, up_bias, gain, shift, omega, o_in, o_out, o_up, o_dn, o_bias, o_upb, o_gain, o_shift, o_omega,
    w_q, w_out, w_up, w_dn, g_q, g_out, g_up, g_dn,
    c_q, c_out, c_up, c_dn,
    p_q, p_out, p_up, p_dn,
    q_q, q_out, q_up, q_dn,
    z_q, z_out, z_up, z_dn,
    ws0, ws1, gs0, gs1, cs0, cs1, zs0, zs1, fs0, fs1,
    all_tok, all_mem, in_cot, raw_tl, raw_sl, raw_tm, raw_sm, meta, in_meta, all_meta,
    dx0, dx1, dc0, dc1, dp0, dp1,
    a3, b3, a4, b4, a5, b5, a6, b6, a7, b7, a8, b8,
    out_res, out_tok, out_mem,
    sg0, sg1, sg2, sg3, sr0, sr1, sr2, sra, srb,
    tg0, tg1, tg2, tg3, tr0, tr1, tr2, tra,
    code_self, code_cross, key_pos, rows_f,
    qt0, kt0, vt0, k0, v0, pt0, l0, ot0,
    qt1, kt1, vt1, k1, v1, pt1, l1, ot1,
    dnt, acc_k, acc_v,
    act, slope, gul, xh0, xh1, xh2, h1_f, h2_f,
    wt, bias_cols, wz, dt0, dt1, gauge,
    f_q, f_out, f_up, f_dn, f_u0, f_u1, mid_far, mid_line,
    ss, rs,
):
    c = lax.axis_index("rows")
    seq = lax.axis_index("seq")
    z = seq // (YS * XS)
    yx = lax.rem(seq, YS * XS)
    y = yx // XS
    x = lax.rem(yx, XS)
    width = 512
    here = 2 * 64

    def at(zz, yy, xx):
        return zz * (YS * XS) + yy * XS + xx

    def slot(cc, yy, xx):
        return cc * 4 + yy * 2 + xx

    def head(cc, yy, xx):
        return (yy * 2 + xx) * 2 + cc

    me_slot, me_head = slot(c, y, x), head(c, y, x)
    plane_peers = []
    for k in range(1, GROUP):
        cc = 1 - c if k & 4 else c
        yy = 1 - y if k & 2 else y
        xx = 1 - x if k & 1 else x
        plane_peers.append((cc, yy, xx))
    trio = [(1 - y, x), (y, 1 - x), (1 - y, 1 - x)]
    z_peers = [lax.rem(z + k, PLANES) for k in (1, 2, 3)]

    names, expected_bytes = {}, {}
    pending = []
    edge = (z == 0) | (z == PLANES - 1)

    def sem(name):
        return names.setdefault(name, len(names))

    def wait(semaphore, ref):
        pltpu.make_async_copy(ref, ref, semaphore).wait()

    def size(ref):
        return math.prod(ref.shape) * jnp.dtype(ref.dtype).itemsize

    bins = [0]
    odd = {}

    def out_sem(name):
        return ss.at[odd.setdefault(name, BINS + 1 + len(odd))] if name in ODD else ss.at[len(bins) - 1]

    def send(name, src, dst, device, recv=None):
        pltpu.make_async_remote_copy(
            src_ref=src, dst_ref=dst, send_sem=out_sem(name), recv_sem=rs.at[sem(name)] if recv is None else recv,
            device_id=device, device_id_type=MESH,
        ).start()

    def keep(name, src, dst):
        pltpu.make_async_copy(src, dst, rs.at[sem(name)]).start()

    def landed(name, ref):
        wait(rs.at[sem(name)], ref)

    def sent_later(name, ref):
        if name in ODD:
            pending.append((ss.at[odd[name]], ref, None))
            return
        bins[-1] += size(ref)
        assert size(ref) % UNIT == 0, (name, size(ref))
        if bins[-1] > 1024 * UNIT // 16:
            bins.append(0)

    line_bytes = [0]

    def along_z(name, src, block):
        i, j = sem(name + "z"), sem(name + "f")
        for step in (1, -1, 2, -2):
            to = z + step
            far = (z == 0) if step == 2 else (z == PLANES - 1) if step == -2 else None

            @pl.when((to >= 0) & (to < PLANES))
            def _():
                pltpu.make_async_remote_copy(
                    src_ref=src, dst_ref=block(z), send_sem=ss.at[BINS],
                    recv_sem=rs.at[i] if far is None else rs.at[jnp.where(far, j, i)],
                    device_id=(c, at(to, y, x)), device_id_type=MESH,
                ).start()

        line_bytes[0] += size(src)

    def pass_on(name, block):
        for mine, origin, to in ((1, 3, 0), (2, 0, 3)):

            @pl.when(z == mine)
            def _():
                landed(name + "f", block(origin))
                pltpu.make_async_remote_copy(
                    src_ref=block(origin), dst_ref=block(origin), send_sem=ss.at[BINS], recv_sem=rs.at[sem(name + "z")],
                    device_id=(c, at(to, y, x)), device_id_type=MESH,
                ).start()

    fold_bytes = [0]

    def fold_send(name, block, target, to):
        pltpu.make_async_remote_copy(
            src_ref=block, dst_ref=target, send_sem=ss.at[BINS], recv_sem=rs.at[sem(name)],
            device_id=(c, at(to, y, x)), device_id_type=MESH,
        ).start()

    def fold_z(name, block, far, line):
        inner = jnp.where(edge, 0, 1)
        for origin, step, hops in ((0, 3, 1), (3, -3, -1)):

            @pl.when(z == origin)
            def _():
                fold_send(name + "a", block(origin + step), far, origin + hops)
                fold_send(name + "l", block(origin + 2 * hops), line.at[2], origin + 2 * hops)

        for step in (1, -1):
            to = z + step

            @pl.when((to >= 0) & (to < PLANES))
            def _():
                between = jnp.where((to == 0) | (to == PLANES - 1), 0, inner)
                fold_send(name + "l", block(to), line.at[between], to)

        fold_bytes[0] += size(far)

    def fold_f(name, block, far, line):
        for mine, to in ((1, 3), (2, 0)):

            @pl.when(z == mine)
            def _():
                landed(name + "a", far)
                add(block(to), far)
                fold_send(name + "l", block(to), line.at[1], to)

    def fold_sum(name, own, line, result):
        @pl.when(edge)
        def _():
            landed(name + "l", line.at[pl.ds(0, 2)])

        @pl.when(jnp.logical_not(edge))
        def _():
            landed(name + "l", line)

        total = own.astype(F32) + line[0].astype(F32) + line[1].astype(F32)

        @pl.when(edge)
        def _():
            result[...] = total.astype(result.dtype)

        @pl.when(jnp.logical_not(edge))
        def _():
            result[...] = (total + line[2].astype(F32)).astype(result.dtype)

    def line_landed(name, blocks, own):
        @pl.when(edge)
        def _():
            landed(name + "z", blocks(3 + own))

        @pl.when(jnp.logical_not(edge))
        def _():
            landed(name + "z", blocks(2 + own))

    def to_plane(name, src, dst, slotted=False):
        half = lax.rem(z, 2)
        core = z // 2
        if slotted:
            recv = rs.at[jnp.where(half == 0, sem(name + "h0"), sem(name + "h1"))]
            part = dst.at[slot(core, y, x), half]
        else:
            recv = rs.at[sem(name)]
            part = dst.at[half]
        for m in range(2):
            plane = 2 * m + c
            own = (plane == z) & (core == c)
            out = ss.at[odd.setdefault(name + str(m), BINS + 1 + len(odd))]

            @pl.when(own)
            def _():
                pltpu.make_async_copy(src.at[m], part, recv).start()

            @pl.when(jnp.logical_not(own))
            def _():
                pltpu.make_async_remote_copy(
                    src_ref=src.at[m], dst_ref=part, send_sem=out, recv_sem=recv,
                    device_id=(core, at(plane, y, x)), device_id_type=MESH,
                ).start()

            pending.append((out, src.at[m], jnp.logical_not(own)))

    def from_plane(name, src, dst):
        micro, core = z // 2, lax.rem(z, 2)
        recv = rs.at[sem(name)]
        for half in range(2):
            zz = 2 * c + half
            own = (core == c) & (zz == z)
            part = dst.at[micro]
            out = ss.at[odd.setdefault(name + str(half), BINS + 1 + len(odd))]

            @pl.when(own)
            def _():
                pltpu.make_async_copy(src.at[half], part, recv).start()

            @pl.when(jnp.logical_not(own))
            def _():
                pltpu.make_async_remote_copy(
                    src_ref=src.at[half], dst_ref=part, send_sem=out, recv_sem=recv,
                    device_id=(core, at(zz, y, x)), device_id_type=MESH,
                ).start()

            pending.append((out, src.at[half], jnp.logical_not(own)))

    def to_heads(name, src, dst):
        keep(name, src.at[me_head], dst.at[me_slot])
        for cc, yy, xx in plane_peers:
            send(name, src.at[head(cc, yy, xx)], dst.at[me_slot], (cc, at(z, yy, xx)))
        sent_later(name, src.at[pl.ds(0, GROUP - 1)])

    def to_slot(name, src, dst, s):
        device = (s // 4, at(z, (s % 4) // 2, s % 2))
        i = sem(name)
        out = out_sem(name)

        @pl.when(me_slot == s)
        def _():
            pltpu.make_async_copy(src.at[s], dst.at[me_head], rs.at[i]).start()

        @pl.when(me_slot != s)
        def _():
            pltpu.make_async_remote_copy(
                src_ref=src.at[s], dst_ref=dst.at[me_head], send_sem=out, recv_sem=rs.at[i],
                device_id=device, device_id_type=MESH,
            ).start()

    weights = {
        "q": (w_q, s_in.at[1, pl.ds(0, 1)], g_q, c_q, p_q, q_q, z_q, o_in.at[1, pl.ds(0, 1)]),
    }

    for i in range(2):
        one = pl.ds(i, 1)
        refs = (w_out, s_out, g_out, c_out, p_out, q_out, z_out, o_out)
        weights["out" + str(i)] = tuple(
            ref.at[:, one] if ref is p_out or ref is q_out or ref is z_out else ref.at[one] for ref in refs
        )
        refs = (w_up, s_up, g_up, c_up, p_up, q_up, z_up, o_up)
        cols = pl.ds(i * 1024, 1024)
        weights["up" + str(i)] = tuple(
            ref.at[:, one] if ref is p_up or ref is q_up or ref is z_up
            else ref.at[:, :, cols] if ref is s_up or ref is o_up else ref.at[one]
            for ref in refs
        )
        refs = (w_dn, s_dn, g_dn, c_dn, p_dn, q_dn, z_dn, o_dn)
        cols = pl.ds(i * 256, 256)
        weights["dn" + str(i)] = tuple(
            ref.at[:, one] if ref is p_dn or ref is q_dn or ref is z_dn
            else ref.at[:, :, cols] if ref is s_dn or ref is o_dn else ref.at[one]
            for ref in refs
        )

    mids = {g: (mid_far.at[i], mid_line.at[i]) for i, g in enumerate(BETWEEN)}
    fars = {"q": f_q, "u0": f_u0, "u1": f_u1}
    for i in range(2):
        one = pl.ds(i, 1)
        fars["out" + str(i)], fars["up" + str(i)], fars["dn" + str(i)] = f_out.at[one], f_up.at[one], f_dn.at[one]

    def halves(ref):
        cols = ref.shape[-1] // 2
        return pl.ds(0, cols), pl.ds(cols, cols)

    x_next, y_next, core_next = (c, at(z, y, 1 - x)), (c, at(z, 1 - y, x)), (1 - c, seq)

    def gather_z(g):
        full, shard = weights[g][:2]
        if g in BETWEEN_OUT:
            first, second = halves(full)
            whole = s_dn if g[:2] == "dn" else s_up if g[:2] == "up" else shard
            keep(g + "o", shard, full.at[:, c, z, y, x])
            for which, cols, device in (("1a", first, x_next), ("1b", second, y_next)):
                part = full.at[:, c, z, y, x, :, cols]
                send(g + which, whole.at[:, :, shard_cols(g, cols)], part, device)
                sent_later(g + which, part)
            return
        keep(g + "z", shard, full.at[:, c, z, y, x])
        along_z(g, shard, lambda zz: full.at[:, c, zz, y, x])

    def gather_f(g):
        full = weights[g][0]
        if g in BETWEEN_OUT:
            first, second = halves(full)
            pass_on(g + "A", lambda zz: full.at[:, c, zz, y, :, :, first])
            pass_on(g + "B", lambda zz: full.at[:, c, zz, :, x, :, second])
            return
        pass_on(g, lambda zz: full.at[:, c, zz, y, x])

    def gather_1(g):
        full = weights[g][0]
        first, second = halves(full)
        if g in BETWEEN_OUT:
            landed(g + "o", full.at[:, c, z, y, x])
            landed(g + "1a", full.at[:, c, z, y, 1 - x, :, first])
            along_z(g + "A", full.at[:, c, z, y, :, :, first], lambda zz: full.at[:, c, zz, y, :, :, first])
            landed(g + "1b", full.at[:, c, z, 1 - y, x, :, second])
            along_z(g + "B", full.at[:, c, z, :, x, :, second], lambda zz: full.at[:, c, zz, :, x, :, second])
            return
        line_landed(g, lambda n: full.at[:, c, pl.ds(0, n), y, x], 1)
        part = full.at[:, c, :, y, x, :, first]
        send(g + "1a", part, part, x_next)
        sent_later(g + "1a", part)
        part = full.at[:, c, :, y, x, :, second]
        send(g + "1b", part, part, y_next)
        sent_later(g + "1b", part)

    def gather_2(g):
        full = weights[g][0]
        first, second = halves(full)
        if g in BETWEEN_OUT:
            line_landed(g + "A", lambda n: full.at[:, c, pl.ds(0, n), y, :, :, first], 0)
        else:
            landed(g + "1a", full.at[:, c, :, y, 1 - x, :, first])
        part = full.at[:, c, :, y, :, :, first]
        send(g + "2a", part, part, y_next)
        sent_later(g + "2a", part)
        if g in BETWEEN_OUT:
            line_landed(g + "B", lambda n: full.at[:, c, pl.ds(0, n), :, x, :, second], 0)
        else:
            landed(g + "1b", full.at[:, c, :, 1 - y, x, :, second])
        part = full.at[:, c, :, :, x, :, second]
        send(g + "2b", part, part, x_next)
        sent_later(g + "2b", part)

    def shard_cols(g, cols):
        start = int(g[-1]) * {"dn": 256, "up": 1024, "ou": 0}[g[:2]]
        return pl.ds(start + cols.start, cols.size)

    def gather_3(g):
        full = weights[g][0]
        first, second = halves(full)
        landed(g + "2a", full.at[:, c, :, 1 - y, :, :, first])
        landed(g + "2b", full.at[:, c, :, :, 1 - x, :, second])
        send(g + "3", full.at[:, c], full.at[:, c], core_next)
        sent_later(g + "3", full.at[:, c])

    def gathered(g):
        landed(g + "3", weights[g][0].at[:, 1 - c])

    def add(target, other):
        target[...] = (target[...].astype(F32) + other[...].astype(F32)).astype(BF16)

    def scatter_0(g):
        grad, across = weights[g][2:4]
        send(g + "r0", grad.at[:, 1 - c], across, core_next)
        sent_later(g + "r0", across)

    def scatter_1(g):
        grad, across, part = weights[g][2:5]
        first, second = halves(grad)
        landed(g + "r0", across)
        for lead in range(grad.shape[0]):

            @pl.loop(0, PLANES)
            def _(zz):
                add(grad.at[lead, c, zz], across.at[lead, zz])

        send(g + "r1a", grad.at[:, c, :, 1 - y, :, :, first], part.at[0], y_next)
        sent_later(g + "r1a", part.at[0])
        send(g + "r1b", grad.at[:, c, :, :, 1 - x, :, second], part.at[1], x_next)
        sent_later(g + "r1b", part.at[1])

    def scatter_2(g):
        grad, _, part, piece = weights[g][2:6]
        first, second = halves(grad)
        landed(g + "r1a", part.at[0])
        landed(g + "r1b", part.at[1])
        for lead in range(grad.shape[0]):

            @pl.loop(0, PLANES)
            def _(zz):
                add(grad.at[lead, c, zz, y, :, :, first], part.at[0, lead, zz])
                add(grad.at[lead, c, zz, :, x, :, second], part.at[1, lead, zz])

        if g in BETWEEN:
            fold_z(g + "A", lambda zz: grad.at[:, c, zz, y, :, :, first], mids[g][0].at[0, 0], mids[g][1].at[:, 0])
            fold_z(g + "B", lambda zz: grad.at[:, c, zz, :, x, :, second], mids[g][0].at[1, 0], mids[g][1].at[:, 1])
            return
        send(g + "r2a", grad.at[:, c, :, y, 1 - x, :, first], piece.at[0], x_next)
        sent_later(g + "r2a", piece.at[0])
        send(g + "r2b", grad.at[:, c, :, 1 - y, x, :, second], piece.at[1], y_next)
        sent_later(g + "r2b", piece.at[1])

    def scatter_3(g):
        grad, _, _, piece, line = weights[g][2:7]
        first, second = halves(grad)
        if g in BETWEEN:
            fold_sum(g + "A", grad[:, c, z, y, :, :, first], mids[g][1].at[:, 0], grad.at[:, c, z, y, :, :, first])
            send(g + "r2a", grad.at[:, c, z, y, 1 - x, :, first], piece.at[0, :, 0], x_next)
            sent_later(g + "r2a", piece.at[0, :, 0])
            fold_sum(g + "B", grad[:, c, z, :, x, :, second], mids[g][1].at[:, 1], grad.at[:, c, z, :, x, :, second])
            send(g + "r2b", grad.at[:, c, z, 1 - y, x, :, second], piece.at[1, :, 0], y_next)
            sent_later(g + "r2b", piece.at[1, :, 0])
            return
        landed(g + "r2a", piece.at[0])
        landed(g + "r2b", piece.at[1])
        for lead in range(grad.shape[0]):

            @pl.loop(0, PLANES)
            def _(zz):
                add(grad.at[lead, c, zz, y, x, :, first], piece.at[0, lead, zz])
                add(grad.at[lead, c, zz, y, x, :, second], piece.at[1, lead, zz])

        fold_z(g, lambda zz: grad.at[:, c, zz, y, x], fars[g], line)

    def scatter_f(g):
        grad, line = weights[g][2], weights[g][6]
        if g in BETWEEN:
            first, second = halves(grad)
            fold_f(g + "A", lambda zz: grad.at[:, c, zz, y, :, :, first], mids[g][0].at[0, 0], mids[g][1].at[:, 0])
            fold_f(g + "B", lambda zz: grad.at[:, c, zz, :, x, :, second], mids[g][0].at[1, 0], mids[g][1].at[:, 1])
            return
        fold_f(g, lambda zz: grad.at[:, c, zz, y, x], fars[g], line)

    def scattered(g):
        grad, _, _, piece, line, result = weights[g][2:8]
        if g in BETWEEN:
            landed(g + "r2a", piece.at[0, :, 0])
            landed(g + "r2b", piece.at[1, :, 0])
            across = jnp.concatenate([piece[0, :, 0], piece[1, :, 0]], axis=-1)
            result[...] = grad[:, c, z, y, x].astype(F32) + across.astype(F32)
            return
        fold_sum(g, grad[:, c, z, y, x], line, result)

    left, right = pl.ds(0, 256), pl.ds(256, 256)
    y_slot, x_slot, far_slot = slot(c, 1 - y, x), slot(c, y, 1 - x), slot(c, 1 - y, 1 - x)

    def spread_1(name, full, half):
        own = full.at[me_slot, half]
        landed(name + "h" + str(half), own)
        for which, device in (("y", y_next), ("x", x_next), ("c", core_next)):
            which = which if which == "c" else which + str(half)
            send(name + which, own, own, device)
            sent_later(name + which, own)

    def spread_2(name, full, half):
        for which, place, cols, device in (("y", y_slot, right, x_next), ("x", x_slot, left, y_next)):
            part = full.at[place, half]
            landed(name + which + str(half), part)
            half_of = full.at[place, half, :, cols]
            send(name + "q" + which + str(half), half_of, half_of, device)
            sent_later(name + "q" + which + str(half), half_of)
            send(name + "d", part, part, core_next)
            sent_later(name + "d", part)

    def spread_4(name, full, half):
        part = full.at[far_slot, half]
        landed(name + "qy" + str(half), full.at[far_slot, half, :, right])
        landed(name + "qx" + str(half), full.at[far_slot, half, :, left])
        send(name + "d", part, part, core_next)
        sent_later(name + "d", part)

    def spread_3(name, full):
        landed(name + "c", full.at[0])
        landed(name + "d", full.at[pl.ds(0, 3)])

    def merge_0(name, full, across):
        send(name + "c", full.at[pl.ds((1 - c) * 4, 4)], across, core_next)
        sent_later(name + "c", across)

    def merge_1(name, full, across, parts):
        landed(name + "c", across)
        add(full.at[far_slot], across.at[(1 - y) * 2 + 1 - x])
        send(name + "qx", full.at[far_slot, :, :, left], parts.at[2, :, :, left], y_next)
        send(name + "qy", full.at[far_slot, :, :, right], parts.at[2, :, :, right], x_next)
        sent_later(name + "q", parts.at[2])
        add(full.at[x_slot], across.at[y * 2 + 1 - x])
        add(full.at[y_slot], across.at[(1 - y) * 2 + x])
        add(full.at[me_slot], across.at[yx])

    def merge_3(name, full, parts):
        landed(name + "qx", parts.at[2, :, :, left])
        add(full.at[x_slot, :, :, left], parts.at[2, :, :, left])
        send(name + "px", full.at[x_slot], parts.at[0], x_next)
        sent_later(name + "px", parts.at[0])
        landed(name + "qy", parts.at[2, :, :, right])
        add(full.at[y_slot, :, :, right], parts.at[2, :, :, right])
        send(name + "py", full.at[y_slot], parts.at[1], y_next)
        sent_later(name + "py", parts.at[1])

    def merge_2(name, full, parts):
        landed(name + "px", parts.at[0])
        landed(name + "py", parts.at[1])
        total = full[me_slot].astype(F32)
        for k in range(2):
            total = total + parts[k].astype(F32)
        return total.reshape(here, width)

    def tile(index):
        return pl.ds(pl.multiple_of(index * 128, 128), 128)

    def slice_1(name, shard, full):
        keep(name + "p", shard.at[:, :, tile(yx)], full.at[:, c, z, yx])
        for yy, xx in trio:
            send(name + "p", shard.at[:, :, tile(yy * 2 + xx)], full.at[:, c, z, yx], (c, at(z, yy, xx)))
        sent_later(name + "p", full.at[:, c, z, pl.ds(0, 3)])

    def slice_2(name, full):
        landed(name + "p", full.at[:, c, z])
        along_z(name, full.at[:, c, z], lambda zz: full.at[:, c, zz])

    def slice_f(name, full):
        pass_on(name, lambda zz: full.at[:, c, zz])

    def slice_3(name, full):
        line_landed(name, lambda n: full.at[:, c, pl.ds(0, n)], 0)
        send(name + "c", full.at[:, c], full.at[:, c], core_next)
        sent_later(name + "c", full.at[:, c])

    def slice_4(name, full):
        landed(name + "c", full.at[:, 1 - c])

    def unslice_0(name, grad, across):
        send(name + "c", grad.at[:, 1 - c], across, core_next)
        sent_later(name + "c", across)

    def unslice_1(name, grad, across, line):
        landed(name + "c", across)
        for lead in range(grad.shape[0]):
            add(grad.at[lead, c], across.at[lead])
        fold_z(name, lambda zz: grad.at[:, c, zz], fars[name], line)

    def unslice_f(name, grad, line):
        fold_f(name, lambda zz: grad.at[:, c, zz], fars[name], line)

    def unslice_2(name, grad, line, total, result):
        fold_sum(name, grad[:, c, z], line, total)
        for yy, xx in trio:
            send(name + "p", total.at[:, yy * 2 + xx], result.at[:, :, tile(yx)], (c, at(z, yy, xx)))
        sent_later(name + "p", total.at[:, pl.ds(0, 3)])
        result[:, :, tile(yx)] = total[:, yx]

    def unslice_3(name, result):
        landed(name + "p", result.at[:, :, pl.ds(0, 384)])

    def matrix(ref):
        return ref[...].reshape(-1, ref.shape[-1])

    def put(ref, value):
        ref[...] = value.astype(BF16).reshape(ref.shape)

    def norm(r, i, kept):
        centered = r - jnp.mean(r, axis=1, keepdims=True)
        scale = lax.rsqrt(jnp.mean(centered * centered, axis=1, keepdims=True) + 1e-05)
        xhat = centered * scale
        kept[...] = xhat
        return xhat * gain[i : i + 1, :] + shift[i : i + 1, :], scale

    def column(row, value):
        sg0[row : row + 1, :] = jnp.sum(value, axis=0, keepdims=True)

    def norm_back(grad, i, kept, scale, skip):
        xhat = kept[...]
        column(12 + i, grad * xhat)
        column(15 + i, grad)
        dxhat = grad * gain[i : i + 1, :]
        dr = dxhat - jnp.mean(dxhat, axis=1, keepdims=True)
        dr = (dr - xhat * jnp.mean(dxhat * xhat, axis=1, keepdims=True)) * scale
        column(18 + i, dr * skip)
        return dr, dr * omega[i : i + 1, :]

    BLOCK = 256

    def attend(b, queries, keys, values_t, weights_t, sums, outputs, causal, name, target, arrives):
        extent = 512 if causal and b < 2 else 1024
        cols = slice(b * BLOCK, (b + 1) * BLOCK)
        scores = nn(keys[:extent, :], queries[:, cols])
        seg = rows_f[0:1, cols]
        code = (code_self if causal else code_cross)[:extent, :]
        permit = jnp.concatenate([code, code], axis=1) == seg
        if causal:
            pos = key_pos[:extent, :]
            pos = jnp.concatenate([pos, pos], axis=1)
            mine = rows_f[1:2, cols]
            permit = (permit & (pos <= mine)) | (pos == mine)
        weight = jnp.where(permit, jnp.exp(scores), 0.0)
        total = jnp.sum(weight, axis=0, keepdims=True)
        low = weight.astype(BF16)
        weights_t[:extent, cols] = low
        out = nn(values_t[:, :extent], low) / total
        sums[0:1, cols] = total
        outputs[:, cols] = out
        for k in range(2):
            target[2 * b + k] = out[:, k * here : (k + 1) * here].astype(BF16)
            to_slot(name, target, arrives, 2 * b + k)
        if b == 3:
            sent_later(name, target.at[pl.ds(0, GROUP - 1)])

    def attend_start(buffer, sums, outputs):
        acc_k[...] = jnp.zeros_like(acc_k)
        acc_v[...] = jnp.zeros_like(acc_v)
        for s in range(GROUP):
            cols = slice(s * here, (s + 1) * here)
            grad = buffer[s].astype(F32)
            inverse = 1.0 / sums[0:1, cols]
            dnt[:, cols] = (grad * inverse).astype(BF16)
            rows_f[2:3, cols] = -jnp.sum(grad * outputs[:, cols], axis=0, keepdims=True) * inverse

    def attend_back(b, queries, keys_t, values, weights_t, causal, name, target, arrives):
        extent = 512 if causal and b < 2 else 1024
        cols = slice(b * BLOCK, (b + 1) * BLOCK)
        low = weights_t[:extent, cols]
        dn = dnt[:, cols]
        spread = nn(values[:extent, :], dn)
        slopes = (low.astype(F32) * (spread + rows_f[2:3, cols])).astype(BF16)
        block = (nn(keys_t[:, :extent], slopes) * 0.125).astype(BF16)
        if name is None:
            dt0[0:64, cols] = block
        else:
            for k in range(2):
                target[2 * b + k] = block[:, k * here : (k + 1) * here]
                to_slot(name, target, arrives, 2 * b + k)
            if b == 3:
                sent_later(name, target.at[pl.ds(0, GROUP - 1)])
        acc_k[:, :extent] += nt(queries[:, cols], slopes)
        acc_v[:, :extent] += nt(dn, low)

    def by_head(target, value):
        target[...] = flip(value).astype(BF16).reshape(GROUP, 64, here)

    def heads_weights(first, full):
        for j in range(full.shape[0]):
            wt[first + j] = flip(matrix(full.at[j])).astype(BF16)

    own_rows = pl.ds(pl.multiple_of(c * 64, 64), 64)
    own_head = pl.ds(pl.multiple_of(me_head * 64, 64), 64)

    def own_weights(first, count):
        return jnp.concatenate([wt[first + j, own_rows, :] for j in range(count)], axis=0)

    def wide_bias(i):
        col = bias_cols[i, own_head, :]
        return jnp.concatenate([col, col], axis=1)

    def project_heads(rows, first, queries, keys, keys_t, values, values_t):
        count = 2 if queries is None else 3
        own = own_weights(first, count)
        for b in range(4):
            cols = slice(b * 256, (b + 1) * 256)
            out = nt(own, rows[2 * b : 2 * b + 2].reshape(256, width))
            if queries is not None:
                queries[:, cols] = ((out[0:64] + wide_bias(0)).astype(BF16).astype(F32) * 0.125).astype(BF16)
            at_k = 64 * (count - 2)
            block = out[at_k : at_k + 64].astype(BF16)
            keys_t[:, cols] = block
            keys[cols, :] = flip(block).astype(BF16)
            block = (out[at_k + 64 : at_k + 128] + wide_bias(1 if count == 3 else 2)).astype(BF16)
            values_t[:, cols] = block
            values[cols, :] = flip(block).astype(BF16)

    def rows_back(grads_t, first, target, core):
        count = grads_t.shape[0] // 64
        own = own_weights(first, count)
        for b in range(2):
            cols = pl.ds(pl.multiple_of(core * 512 + b * 256, 256), 256)
            out = tn(grads_t[:, cols], own)
            target[pl.ds(core * 4 + b * 2, 2)] = out.astype(BF16).reshape(2, 2, 64, width)

    def slices_back(grads_t, rows, grad):
        count = grads_t.shape[0] // 64
        out = nn(grads_t[...], rows[...].reshape(1024, width))
        wz[...] = jnp.zeros_like(wz)
        for j in range(count):
            wz[j, own_rows, :] = out[j * 64 : (j + 1) * 64]
            put(grad.at[j], jnp.transpose(wz[j]))

    def bias(i):
        return biases[i : i + 1, :]

    def make_masks():
        landed("marks", all_meta.at[pl.ds(0, 7)])
        order = lax.broadcasted_iota(jnp.int32, (1, 1024), 1)
        place = (order // 512) * 512 + lax.rem(order // 64, 2) * 256 + lax.rem(order // 128, 4) * 64 + lax.rem(order, 64)
        place = place.astype(F32)
        marks = [all_meta[s].astype(F32) for s in range(GROUP)]
        tgt_real = jnp.concatenate([mark[0:1, :] for mark in marks], axis=1)
        src_real = jnp.concatenate([mark[1:2, :] for mark in marks], axis=1)
        lower = lax.broadcasted_iota(jnp.int32, (32, 128), 1)
        later = lax.broadcasted_iota(jnp.int32, (32, 128), 0)

        def ends_of(row):
            lengths = jnp.broadcast_to(row, (32, 128))
            ends = jnp.sum(jnp.where(lower <= later, lengths, 0.0), axis=1, keepdims=True)
            starts = jnp.sum(jnp.where(lower < later, lengths, 0.0), axis=1, keepdims=True)
            return ends, starts

        def count(flags):
            return jnp.sum(jnp.where(flags, 1.0, 0.0), axis=0, keepdims=True)

        tgt_ends, _ = ends_of(marks[0][2:3, :])
        src_ends, src_starts = ends_of(marks[0][3:4, :])
        tgt_seg = count(tgt_ends <= place)
        src_seg = count(src_ends <= place)
        src_first = count(src_starts == place)
        self_row = jnp.where(tgt_real > 0.5, tgt_seg, -1.0)
        cross_row = jnp.where((src_real > 0.5) | (src_first > 0.5), src_seg, -1.0)
        rows_f[0:1, :] = tgt_seg
        rows_f[1:2, :] = place
        code_self[...] = jnp.transpose(jnp.broadcast_to(self_row, (128, 1024)))
        code_cross[...] = jnp.transpose(jnp.broadcast_to(cross_row, (128, 1024)))
        key_pos[...] = jnp.transpose(jnp.broadcast_to(place, (128, 1024)))

    def feed_up(rows, i):
        for k in (2 * i, 2 * i + 1):
            cols = slice(k * width, (k + 1) * width)
            inner = slice((k % 2) * width, (k % 2 + 1) * width)
            u = nn(rows, matrix(w_up.at[i, :, :, :, :, :, inner])) + up_bias[0:1, cols]
            square = u * u
            t = jnp.tanh(u * (0.7978845608028654 + 0.035677408136300125 * square))
            act[:, cols] = (0.5 * u * (1.0 + t)).astype(BF16)
            inner = 0.7978845608028654 + 0.10703222440890037 * square
            slope[:, cols] = 0.5 * (1.0 + t) + 0.5 * u * (1.0 - t * t) * inner

    def feed_back(gf, back):
        for k in range(4):
            cols = slice(k * width, (k + 1) * width)
            inner = slice((k % 2) * width, (k % 2 + 1) * width)
            rows = pl.ds(2 * (k % 2), 2)
            gu = nt(gf[:, 0:256], matrix(w_dn.at[0, k // 2, rows]))
            gu = gu + nt(gf[:, 256:512], matrix(w_dn.at[1, k // 2, rows]))
            gu = (gu * slope[:, cols]).astype(BF16)
            gul[:, cols] = gu
            column(8 + k, gu.astype(F32))
            back = back + nt(gu, matrix(w_up.at[k // 2, :, :, :, :, :, inner]))
        return back

    def value_sums(grads_t):
        total = jnp.sum(grads_t[64:128, :].astype(F32), axis=1, keepdims=True)
        bias_cols[0] = jnp.zeros((width, 128), F32)
        bias_cols[0, own_head, :] = jnp.broadcast_to(total, (64, 128))
        sg0[4:5, :] = jnp.transpose(bias_cols[0])[0:1, :]

    def head_sums(grads_t):
        lanes = lax.broadcasted_iota(jnp.int32, (64, 128), 1)
        dq_sum = jnp.sum(grads_t[0:64, :].astype(F32), axis=1, keepdims=True)
        dv_sum = jnp.sum(grads_t[128:192, :].astype(F32), axis=1, keepdims=True)
        bias_cols[0] = jnp.zeros((width, 128), F32)
        bias_cols[0, own_head, :] = jnp.where(lanes == 0, dq_sum, dv_sum)
        tg0[...] = jnp.transpose(bias_cols[0])[0:8, :]

    def small(name, src, dst, device):
        send(name, src, dst, device)
        sent_later(name, dst)

    def small_add(name, arrived, mine, total):
        landed(name, arrived)
        total[...] = mine[...] + arrived[...]

    def small_z(name, src, rows, tile_at, dst):
        for k, zz in enumerate(z_peers):
            send(name, src.at[rows, tile(tile_at(zz))], dst.at[2 - k], (c, at(zz, y, x)))
        sent_later(name, dst)

    def tile_own(zz):
        return c * 2 + zz // 2

    def tile_up(zz):
        return lax.rem(zz, 2) * 2 + y

    def small_sum(name, src, rows, tile_at, dst):
        landed(name, dst)
        return src[rows, tile(tile_at(z))] + dst[0] + dst[1] + dst[2]

    def small_out():
        block = c * 16 + seq
        shift_by = lax.rem(128 - lax.rem(block, 8) * 16, 128)
        turned = pltpu.roll(small_sum("sa", sg3, slice(None), tile_own, sra), shift_by, 1)
        o_bias[...] = turned[0:7, 0:16]
        o_gain[...] = turned[12:15, 0:16]
        o_shift[...] = turned[15:18, 0:16]
        o_omega[...] = turned[18:21, 0:16]
        turned = pltpu.roll(small_sum("ta", tg3, slice(None), tile_own, tra), shift_by, 1)
        o_bias[0:2, :] = turned[0:2, 0:16]
        turned = pltpu.roll(small_sum("sb", sg3, pl.ds(8, 8), tile_up, srb), lax.rem(block, 2) * 64, 1)
        wanted = block // 8
        row = jnp.zeros((1, 64), F32)
        for k in range(4):
            row = row + turned[k : k + 1, 0:64] * (wanted == k).astype(F32)
        o_upb[...] = row
        ends = ((o_bias, h_bias), (o_upb, h_upb), (o_gain, h_gain_o), (o_shift, h_shift_o), (o_omega, h_omega_o))
        for i, (src, dst) in enumerate(ends):
            keep("e" + str(4 + i), src, dst)

    raw = ((raw_tm, tgt_msk), (raw_sm, src_msk), (raw_tl, tgt_len), (raw_sl, src_len))
    for i, (ref, given) in enumerate(raw):
        keep("raw" + str(i), given, ref)
    given = ((h_biases, biases), (h_up_bias, up_bias), (h_gain, gain), (h_shift, shift), (h_omega, omega))
    for i, (src, ref) in enumerate(given):
        keep("given" + str(i), src, ref)
    barrier = pltpu.get_barrier_semaphore()
    greet = [(cc, at(z, yy, xx)) for cc, yy, xx in plane_peers]
    greet += [(cc, at(zz, y, x)) for zz in z_peers for cc in (c, 1 - c)]
    for device in greet:
        pl.semaphore_signal(barrier, inc=1, device_id=device, device_id_type=MESH)
    pl.semaphore_wait(barrier, len(greet))
    gather_z("out0")
    gather_z("up1")
    gather_z("dn1")
    to_plane("x", tok, all_tok, True)
    for i, (ref, _) in enumerate(raw):
        landed("raw" + str(i), ref)
        span = ref.shape[2]
        for m in range(2):
            for start in (0, 64):
                meta[m, i : i + 1, start : start + span] = ref[m]
    gather_z("q")
    slice_1("w0", s_in.at[0], ws0)
    gather_f("out0")
    to_plane("meta", meta, in_meta)
    gather_z("dn0")
    to_plane("m", mem, all_mem, True)
    spread_1("x", all_tok, 0)
    gather_z("up0")
    gather_z("out1")
    spread_1("x", all_tok, 1)
    gather_f("q")
    gather_1("out0")
    landed("meta", in_meta)
    slice_2("w0", ws0)
    lane = lax.broadcasted_iota(jnp.int32, (8, 128), 1)
    all_meta[me_slot] = jnp.where(lane < 64, in_meta[0], in_meta[1])
    gather_1("dn0")
    for cc, yy, xx in plane_peers:
        send("marks", all_meta.at[me_slot], all_meta.at[me_slot], (cc, at(z, yy, xx)))
    spread_1("m", all_mem, 0)
    spread_2("x", all_tok, 0)
    spread_2("x", all_tok, 1)
    spread_1("m", all_mem, 1)
    gather_1("out1")
    gather_f("up0")
    gather_2("out0")
    spread_4("x", all_tok, 0)
    spread_4("x", all_tok, 1)
    gather_1("q")
    slice_1("w1", s_in.at[1, pl.ds(1, 2)], ws1)
    spread_2("m", all_mem, 0)
    slice_f("w0", ws0)
    sent_later("marks", all_meta.at[pl.ds(0, 7)])
    for i, (_, ref) in enumerate(given):
        landed("given" + str(i), ref)
    for i, row in enumerate((0, 1, 4)):
        bias_cols[i] = jnp.transpose(jnp.broadcast_to(bias(row), (128, width)))
    gather_1("up1")
    gather_1("up0")
    gather_2("q")
    slice_2("w1", ws1)
    slice_3("w0", ws0)
    spread_2("m", all_mem, 1)
    make_masks()
    spread_3("x", all_tok)
    gather_3("out0")
    gather_f("dn0")
    gather_2("up0")
    slice_4("w0", ws0)
    gather_1("dn1")
    heads_weights(0, ws0)
    project_heads(all_tok, 0, qt0, k0, kt0, v0, vt0)
    attend(0, qt0, k0, vt0, pt0, l0, ot0, True, "x3", a3, b3)
    gather_f("out1")
    attend(1, qt0, k0, vt0, pt0, l0, ot0, True, "x3", a3, b3)
    attend(2, qt0, k0, vt0, pt0, l0, ot0, True, "x3", a3, b3)
    gather_2("dn0")
    attend(3, qt0, k0, vt0, pt0, l0, ot0, True, "x3", a3, b3)
    spread_4("m", all_mem, 0)
    spread_4("m", all_mem, 1)
    gathered("out0")
    gather_3("up0")
    gather_f("up1")
    gather_3("q")
    gather_2("out1")
    gather_2("up1")
    landed("x3", b3)
    words_f = all_tok[me_slot].reshape(here, width).astype(F32)
    gathered("q")
    slice_f("w1", ws1)
    branch = tn(b3[...].reshape(width, here), matrix(w_out.at[0])) + bias(2)
    spread_3("m", all_mem)
    h1, scale0 = norm(words_f * omega[0:1, :] + branch, 0, xh0)
    h1_f[...] = h1
    gather_f("dn1")
    h1_low = h1.astype(BF16)
    by_head(a4, nn(h1_low, matrix(w_q.at[0])) + bias(3))
    to_heads("x4", a4, b4)
    to_plane("cot", cot, in_cot)
    slice_3("w1", ws1)
    gather_3("dn0")
    gather_2("dn1")
    slice_4("w1", ws1)
    heads_weights(3, ws1)
    project_heads(all_mem, 3, None, k1, kt1, v1, vt1)
    gather_3("out1")
    gathered("up0")
    gather_3("up1")
    landed("x4", b4)
    for s in range(GROUP):
        qt1[:, s * here : (s + 1) * here] = (b4[s].astype(F32) * 0.125).astype(BF16)
    attend(0, qt1, k1, vt1, pt1, l1, ot1, False, "x5", a5, b5)
    attend(1, qt1, k1, vt1, pt1, l1, ot1, False, "x5", a5, b5)
    attend(2, qt1, k1, vt1, pt1, l1, ot1, False, "x5", a5, b5)
    attend(3, qt1, k1, vt1, pt1, l1, ot1, False, "x5", a5, b5)
    gathered("dn0")
    gathered("out1")
    gathered("up1")
    gather_3("dn1")
    gathered("dn1")
    landed("x5", b5)
    branch = tn(b5[...].reshape(width, here), matrix(w_out.at[1])) + bias(5)
    h2, scale1 = norm(h1_f[...] * omega[1:2, :] + branch, 1, xh1)
    h2_f[...] = h2
    h2_low = h2.astype(BF16)
    feed_up(h2_low, 0)
    feed_up(h2_low, 1)
    first = nn(act[...], matrix(w_dn.at[0]))
    second = nn(act[...], matrix(w_dn.at[1]))
    h3, scale2 = norm(h2_f[...] * omega[2:3, :] + jnp.concatenate([first, second], axis=1) + bias(6), 2, xh2)
    out_res[...] = h3.astype(BF16).reshape(2, 64, width)
    landed("cot", in_cot)
    grad = in_cot[...].reshape(here, width).astype(F32)
    dr, skip = norm_back(grad, 2, xh2, scale2, h2_f[...])
    gf = dr.astype(BF16)
    column(6, gf.astype(F32))
    back = feed_back(gf, skip)
    put(g_up.at[0], tn(h2_low, gul[:, 0:1024]))
    scatter_0("up0")
    dr, skip = norm_back(back, 1, xh1, scale1, h1_f[...])
    gc = dr.astype(BF16)
    column(5, gc.astype(F32))
    by_head(a6, nt(gc, matrix(w_out.at[1])))
    to_heads("x6", a6, b6)
    put(g_dn.at[0], tn(act[...], gf[:, 0:256]))
    from_plane("res", out_res, o_res)
    scatter_1("up0")
    put(g_dn.at[1], tn(act[...], gf[:, 256:512]))
    scatter_0("dn1")
    put(g_out.at[1], nn(b5[...].reshape(width, here), gc))
    scatter_0("out1")
    put(g_up.at[1], tn(h2_low, gul[:, 1024:2048]))
    scatter_0("up1")
    back = skip
    landed("x6", b6)
    attend_start(b6, l1, ot1)
    scatter_1("dn1")
    attend_back(0, qt1, kt1, v1, pt1, False, "x7", a7, b7)
    attend_back(1, qt1, kt1, v1, pt1, False, "x7", a7, b7)
    scatter_0("dn0")
    attend_back(2, qt1, kt1, v1, pt1, False, "x7", a7, b7)
    attend_back(3, qt1, kt1, v1, pt1, False, "x7", a7, b7)
    scatter_2("up0")
    scatter_1("dn0")
    dt1[0:64, :] = acc_k[...].astype(BF16)
    scatter_2("dn1")
    dt1[64:128, :] = acc_v[...].astype(BF16)
    scatter_1("out1")
    rows_back(dt1, 3, dx1, 1 - c)
    merge_0("dm", dx1, dc1)
    rows_back(dt1, 3, dx1, c)
    landed("x7", b7)
    dq = b7[...].reshape(width, here)
    slices_back(dt1, all_mem, gs1)
    unslice_0("u1", gs1, cs1)
    dq_row = flip(dq)
    column(3, dq_row)
    value_sums(dt1)
    back = back + nt(dq_row.astype(BF16), matrix(w_q.at[0]))
    dr, skip = norm_back(back, 0, xh0, scale0, words_f)
    ga = dr.astype(BF16)
    column(2, ga.astype(F32))
    scatter_3("up0")
    by_head(a8, nt(ga, matrix(w_out.at[0])))
    to_heads("x8", a8, b8)
    last = skip
    scatter_1("up1")
    put(g_q.at[0], nt(flip(h1_low).astype(BF16), dq))
    scatter_2("dn0")
    merge_1("dm", dx1, dc1, dp1)
    scatter_2("out1")
    small("s0", sg0, sr0, core_next)
    scatter_f("up0")
    put(g_out.at[0], nn(b3[...].reshape(width, here), ga))
    landed("x8", b8)
    attend_start(b8, l0, ot0)
    attend_back(0, qt0, kt0, v0, pt0, True, None, None, None)
    scatter_f("dn1")
    attend_back(1, qt0, kt0, v0, pt0, True, None, None, None)
    unslice_1("u1", gs1, cs1, zs1)
    attend_back(2, qt0, kt0, v0, pt0, True, None, None, None)
    scatter_2("up1")
    scatter_0("q")
    small_add("s0", sr0, sg0, sg1)
    scatter_0("out0")
    scatter_f("dn0")
    small("s1", sg1, sr1, y_next)
    merge_3("dm", dx1, dp1)
    attend_back(3, qt0, kt0, v0, pt0, True, None, None, None)
    dt0[64:128, :] = acc_k[...].astype(BF16)
    dt0[128:192, :] = acc_v[...].astype(BF16)
    scatter_3("out1")
    head_sums(dt0)
    small("t0", tg0, tr0, core_next)
    scatter_3("up1")
    slices_back(dt0, all_tok, gs0)
    unslice_0("u0", gs0, cs0)
    scatter_1("q")
    unslice_f("u1", gs1, zs1)
    small_add("t0", tr0, tg0, tg1)
    small_add("s1", sr1, sg1, sg2)
    small("s2", sg2, sr2, x_next)
    rows_back(dt0, 0, dx0, 1 - c)
    unslice_1("u0", gs0, cs0, zs0)
    merge_0("dx", dx0, dc0)
    small("t1", tg1, tr1, y_next)
    rows_back(dt0, 0, dx0, c)
    scatter_1("out0")
    out_mem[...] = merge_2("dm", dx1, dp1).astype(BF16).reshape(2, 64, width)
    scatter_f("out1")
    from_plane("gmem", out_mem, o_mem)
    merge_1("dx", dx0, dc0, dp0)
    scatter_2("q")
    scattered("up0")
    small_add("t1", tr1, tg1, tg2)
    landed("res", o_res)
    scatter_2("out0")
    scatter_f("up1")
    unslice_f("u0", gs0, zs0)
    small("t2", tg2, tr2, x_next)
    merge_3("dx", dx0, dp0)
    scatter_3("q")
    scatter_3("out0")
    small_add("s2", sr2, sg2, sg3)
    landed("gmem", o_mem)
    small_z("sa", sg3, slice(None), tile_own, sra)
    small_z("sb", sg3, pl.ds(8, 8), tile_up, srb)
    scatter_3("dn0")
    scattered("out1")
    unslice_2("u1", gs1, zs1, fs1, o_in.at[1, pl.ds(1, 2)])
    scatter_3("dn1")
    scattered("up1")
    small_add("t2", tr2, tg2, tg3)
    small_z("ta", tg3, slice(None), tile_own, tra)
    scatter_f("q")
    scatter_f("out0")
    out_tok[...] = (merge_2("dx", dx0, dp0) + last).astype(BF16).reshape(2, 64, width)
    from_plane("gtok", out_tok, o_tok)
    unslice_2("u0", gs0, zs0, fs0, o_in.at[0])
    scattered("q")
    scattered("out0")
    scattered("dn1")
    unslice_3("u1", o_in.at[1, pl.ds(1, 2)])
    scattered("dn0")
    keep("e3", o_dn, h_dn)
    small_out()
    unslice_3("u0", o_in.at[0])
    keep("e2", o_up, h_up)
    keep("e1", o_out, h_out)
    keep("e0", o_in, h_in)
    landed("gtok", o_tok)
    for i, ref in enumerate((h_in, h_out, h_up, h_dn, h_bias, h_upb, h_gain_o, h_shift_o, h_omega_o)):
        landed("e" + str(i), ref)
    for semaphore, ref, when in pending:
        if when is None:
            wait(semaphore, ref)
        else:

            @pl.when(when)
            def _():
                wait(semaphore, ref)

    for i, total in enumerate(bins):
        if total:
            wait(ss.at[i], gauge.at[pl.ds(0, total // 1024)])
    spans = [2 * line_bytes[0] + 3 * fold_bytes[0], 4 * line_bytes[0] + 3 * fold_bytes[0]]
    assert spans[0] % UNIT == 0 and spans[1] % UNIT == 0

    @pl.when(edge)
    def _():
        wait(ss.at[BINS], gauge.at[pl.ds(0, spans[0] // 1024)])

    @pl.when(jnp.logical_not(edge))
    def _():
        wait(ss.at[BINS], gauge.at[pl.ds(0, spans[1] // 1024)])

    assert len(names) <= NAMES and len(bins) <= BINS and BINS + 1 + len(odd) <= ss.shape[0]


def copy_kernel(*refs):
    count = len(refs) // 3
    given, results, held = (refs[i * count : (i + 1) * count] for i in range(3))
    arrived, left = refs[3 * count :]
    for i in range(count):
        pltpu.make_async_copy(given[i], held[i], arrived.at[i]).start()
    for i in range(count):
        pltpu.make_async_copy(given[i], held[i], arrived.at[i]).wait()
        pltpu.make_async_copy(held[i], results[i], left.at[i]).start()
    for i in range(count):
        pltpu.make_async_copy(held[i], results[i], left.at[i]).wait()


def fused_local(
    tokens, memory, cotangent, tgt_lengths, src_lengths, tgt_mask, src_mask, attn_in, attn_out, w_up, w_down,
    biases, up_bias, norm_gain, norm_shift, omega,
):
    any_space = pl.BlockSpec(memory_space=pl.ANY)
    vmem = pl.BlockSpec(memory_space=pltpu.VMEM)
    lines = (CORES, PLANES, YS, XS)
    leads = {"q": 1, "out": 2, "up": 2, "dn": 2}
    shards = {"q": (16, 512), "out": (16, 512), "up": (16, 1024), "dn": (64, 256)}
    kinds = tuple(leads)

    def low(*shape):
        return pltpu.VMEM(shape, BF16)

    def full(*shape):
        return pltpu.VMEM(shape, F32)

    def whole(k):
        return low(leads[k], *lines, *shards[k])

    def halved(k, *middle):
        return low(2, leads[k], *middle, shards[k][0], shards[k][1] // 2)

    params = [full(7, 512), full(1, 2048), full(3, 512), full(3, 512), full(3, 512)]
    results = [(2, 3, 16, 512), (2, 16, 512), (1, 16, 2048), (1, 64, 512), (7, 16), (1, 64), (3, 16), (3, 16), (3, 16)]
    scratch = params + [full(*shape) for shape in results]
    scratch += [whole(k) for k in kinds] * 2
    scratch += [low(leads[k], *lines[1:], *shards[k]) for k in kinds]
    scratch += [halved(k, PLANES, 2) for k in kinds] + [halved(k, PLANES) for k in kinds]
    scratch += [low(3, leads[k], *shards[k]) for k in kinds]
    scratch += [low(n, CORES, PLANES, 4, 16, 128) for n in (3, 2)] * 2
    scratch += [low(n, PLANES, 4, 16, 128) for n in (3, 2)] + [low(3, n, 4, 16, 128) for n in (3, 2)]
    scratch += [full(n, 4, 16, 128) for n in (3, 2)]
    local_rows = low(2, 64, 512)
    marks = [pltpu.VMEM((2, 1, n), jnp.int32) for n in (32, 32, 64, 64)] + [pltpu.VMEM((2, 8, 128), jnp.int32)] * 2
    scratch += [low(GROUP, 2, 64, 512)] * 2 + [local_rows] + marks + [pltpu.VMEM((GROUP, 8, 128), jnp.int32)]
    scratch += [low(GROUP, 2, 64, 512)] * 2 + [low(4, 2, 64, 512)] * 2 + [low(3, 2, 64, 512)] * 2
    scratch += [low(GROUP, 64, 128)] * 12 + [local_rows] * 3
    scratch += [full(24, 512)] * 7 + [full(3, 24, 128), full(3, 8, 128)]
    scratch += [full(8, 512)] * 7 + [full(3, 8, 128)]
    scratch += [full(1024, 128)] * 3 + [full(8, 1024)]
    scratch += ([low(64, 1024)] * 3 + [low(1024, 64)] * 2 + [low(1024, 1024), full(1, 1024), full(64, 1024)]) * 2
    scratch += [low(64, 1024)] + [full(64, 1024)] * 2
    scratch += [low(128, 2048), full(128, 2048), low(128, 2048)] + [full(128, 512)] * 5
    scratch += [low(5, 128, 512), full(3, 512, 128), full(3, 128, 512), low(192, 1024), low(128, 1024), low(2560, 512)]
    scratch += [low(leads[k], *shards[k]) for k in kinds] + [low(n, 4, 16, 128) for n in (3, 2)]
    scratch += [low(2, 2, 1, 1, 2, 64, 128), low(2, 3, 2, 1, 2, 64, 128)]
    scratch += [pltpu.SemaphoreType.DMA((46,)), pltpu.SemaphoreType.DMA((NAMES,))]
    rows = jax.ShapeDtypeStruct((2, 64, 512), BF16)

    def wide_out(*shape):
        return jax.ShapeDtypeStruct(shape, F32)

    outs = pl.pallas_call(
        fused_kernel,
        name="layer",
        out_shape=(rows, rows, rows, *(wide_out(*shape) for shape in results)),
        in_specs=[any_space] * 16,
        out_specs=(any_space,) * 12,
        scratch_shapes=scratch,
        compiler_params=pltpu.CompilerParams(collective_id=0, has_side_effects=True, vmem_limit_bytes=60 * 1024 * 1024),
    )(
        tokens.reshape(2, 64, 512), memory.reshape(2, 64, 512), cotangent.reshape(2, 64, 512),
        tgt_lengths, src_lengths, jnp.transpose(tgt_mask, (0, 2, 1)), jnp.transpose(src_mask, (0, 2, 1)),
        attn_in, attn_out, w_up.reshape(1, 16, 2048), w_down.reshape(1, 64, 512),
        biases, up_bias.reshape(1, 2048), norm_gain, norm_shift, omega,
    )
    outs = pl.pallas_call(
        copy_kernel,
        name="hand_over",
        out_shape=tuple(jax.ShapeDtypeStruct(out.shape, out.dtype) for out in outs),
        in_specs=[any_space] * len(outs),
        out_specs=(any_space,) * len(outs),
        scratch_shapes=[pltpu.VMEM(out.shape, out.dtype) for out in outs] + [pltpu.SemaphoreType.DMA((len(outs),))] * 2,
    )(*outs)
    shaped = [out.reshape(2, 64, 1, 512) for out in outs[:3]]
    return (
        *shaped, outs[3], outs[4], outs[5].reshape(16, 2048), outs[6].reshape(64, 512), outs[7], outs[8].reshape(64),
        outs[9], outs[10], outs[11],
    )


def solution(mesh):
    if mesh.shape["seq"] != PLANES * YS * XS or mesh.shape["rows"] != CORES:
        return general(mesh)
    return over(mesh, fused_local)
```
